32 devices in a mesh: seq: 16 (over z, y, x), tp: 2 (over core).
Axes of the slice: x: 2, y: 2, z: 4, core: 2. Of those that a mesh axis runs over, the one named last changes fastest.
Arguments:
- hidden_in: bfloat16 [4096, 2048], P('seq', 'tp'), may hold values from -6 to 6
- w_query: bfloat16 [2048, 2048], P(None, 'tp'), may hold values from -0.375 to 0.375
- w_keyval: bfloat16 [2048, 2, 2048], P(None, None, 'tp'), may hold values from -0.125 to 0.125
- w_out: bfloat16 [2048, 2048], P('tp'), may hold values from -0.125 to 0.125
- prompt_cache: bfloat16 [2048, 2, 2048], P('seq', None, 'tp'), may hold values from -160 to 160
- tail_cache: bfloat16 [32, 128, 2, 2048], P('seq', None, None, 'tp'), may hold values from -6 to 6
- tail_table: int32 [8, 4], replicated, may hold values from 0 to 31, as said below
- tail_len: int32 [8], replicated, may hold values from 1 to 512
- shared_len: int32 [1], replicated, may hold values from 1024 to 2048
Outputs:
- hidden_out: bfloat16 [4096, 2048], P('seq', 'tp')
- new_cache: bfloat16 [4096, 2, 2048], P('seq', None, 'tp')
The draws below stay inside these ranges and needn't reach their ends.
Inputs may be any that keep to these rules, and one draw needn't show every extreme that they name: Row r lists each of the slots r * 4 to (r + 1) * 4 - 1 once; block j of request r's tail is held in slot tail_table[r, j].
All inputs are finite; a program needn't handle non-finite values.
Results may differ from the reference program's by a relative error of at most 0.013.
Values may be sent and summed in bfloat16 or wider, within the bound.
No kernel may reach another device: no remote copies, remote signals or barrier semaphores. Data moves between devices by JAX's collectives and lax.ppermute only.
A program may use at most 128 MiB of HBM per device.

```python
import jax
import jax.numpy as jnp
from jax import lax

D = 2048
HEADS = 16
HD = 128
REQ = 8
BLK = 128
FRESH = 512
TOKENS = 4096
PROMPT = 2048
SLOTS = 32
TBLK = 4
TAIL = 512


def draw_prompt_cache(key, part):
    base = jnp.clip(jax.random.normal(key, (PROMPT, 2, HEADS * HD), jnp.float32), -6.0, 6.0)
    return base.astype(jnp.bfloat16)


def order_slots(subkey):
    return jax.random.permutation(subkey, TBLK)


def draw_tail_table(key, part):
    orders = jax.vmap(order_slots)(jax.random.split(key, REQ))
    return (jnp.arange(REQ, dtype=jnp.int32)[:, None] * TBLK + orders).astype(jnp.int32)


def set_ends(values, own_key, smallest, high):
    shape = values.shape
    index_at = [jax.random.randint(jax.random.fold_in(own_key, axis), (), 0, shape[axis]) for axis in range(len(shape))]
    values = values.at[tuple(index_at)].set(smallest)
    longest = shape.index(max(shape))
    index_at[longest] = (index_at[longest] + 1) % shape[longest]
    return values.at[tuple(index_at)].set(high)


def levels(key, shape, shards, smallest, high):
    def one(dim, parts):
        draws = jax.random.uniform(jax.random.fold_in(jax.random.fold_in(key, 6), dim), (parts,), jnp.float32, smallest / len(shards), high / len(shards))
        return jnp.repeat(jnp.exp(draws), shape[dim] // parts).reshape((-1,) + (1,) * (len(shape) - dim - 1))

    gain = one(*shards[0])
    for cut in shards[1:]:
        gain = gain * one(*cut)
    return gain


def scatter_about(stream_key, shape, scale, most, cuts=(), kind=jnp.bfloat16):
    entries = scale * jax.random.normal(stream_key, shape, jnp.float32)
    if cuts:
        entries = entries * levels(stream_key, shape, cuts, -0.22, 0.18)
    return jnp.clip(entries, -most, most).astype(kind)


def setup_inputs(seed: int = 0) -> dict:
    seeds = jax.random.split(jax.random.key(seed), 10)
    return {
        "hidden_in": scatter_about(seeds[0], (TOKENS, D), 1.0, 6.0, ((0, 16), (1, 2))),
        "w_query": scatter_about(seeds[1], (D, HEADS * HD), (D // 9) ** -0.5, 0.375, ((1, 2),)),
        "w_keyval": scatter_about(seeds[2], (D, 2, HEADS * HD), D ** -0.5, 0.125, ((2, 2),)),
        "w_out": scatter_about(seeds[3], (HEADS * HD, D), (HEADS * HD) ** -0.5, 0.125, ((0, 2),)),
        "prompt_cache": draw_prompt_cache(jax.random.fold_in(seeds[9], 71), 0),
        "tail_cache": scatter_about(seeds[5], (SLOTS, BLK, 2, HEADS * HD), 1.0, 6.0, ((0, 16), (3, 2))),
        "tail_table": draw_tail_table(jax.random.fold_in(seeds[9], 71), 0),
        "tail_len": set_ends(jax.random.randint(seeds[7], (REQ,), 1, TAIL + 1), jax.random.fold_in(seeds[7], 1), 1, TAIL).astype(jnp.int32),
        "shared_len": jax.random.randint(seeds[8], (1,), PROMPT // 2, PROMPT + 1).astype(jnp.int32),
    }


def layer_norm(inputs):
    values = inputs.astype(jnp.float32)
    mean = lax.optimization_barrier(jnp.mean(values, axis=-1, keepdims=True))
    centred = values - mean
    spread = lax.optimization_barrier(jnp.mean(centred * centred, axis=-1, keepdims=True))
    return (centred * lax.rsqrt(spread + 1e-05)).astype(jnp.bfloat16)

def rotate(vectors, positions):
    half = vectors.shape[-1] // 2
    freqs = 10000.0 ** (-jnp.arange(half, dtype=jnp.float32) / half)
    angles = positions.astype(jnp.float32)[:, None, None] * freqs
    cosine = jnp.cos(angles)
    sine = jnp.sin(angles)
    first = vectors[..., :half]
    second = vectors[..., half:]
    return jnp.concatenate([first * cosine - second * sine, second * cosine + first * sine], axis=-1)

def attend_head(query, keys, values, allowed):
    scores = jnp.dot(query, keys.T, preferred_element_type=jnp.float32) * HD ** (-0.5)
    scores = jnp.where(allowed, scores, -jnp.inf)
    top = lax.optimization_barrier(jnp.max(scores, axis=1, keepdims=True))
    weights = jnp.exp(scores - top)
    total = lax.optimization_barrier(jnp.sum(weights, axis=1, keepdims=True))
    mixed = jnp.dot(weights.astype(jnp.bfloat16), values, preferred_element_type=jnp.float32)
    return (mixed / total).astype(jnp.bfloat16)

def reference(hidden_in, w_query, w_keyval, w_out, prompt_cache, tail_cache, tail_table, tail_len, shared_len):
    normed = layer_norm(hidden_in)
    query = jnp.dot(normed, w_query, preferred_element_type=jnp.float32).reshape(TOKENS, HEADS, HD)
    projected = jnp.dot(normed, w_keyval.reshape(D, 2 * HEADS * HD), preferred_element_type=jnp.float32)
    projected = projected.reshape(TOKENS, 2, HEADS, HD)
    token = jnp.arange(TOKENS, dtype=jnp.int32)
    request = token // FRESH
    prompt_length = shared_len[0]
    positions = prompt_length + tail_len[request] + token % FRESH
    query = rotate(query, positions).astype(jnp.bfloat16)
    new_keys = rotate(projected[:, 0], positions).astype(jnp.bfloat16)
    new_values = projected[:, 1].astype(jnp.bfloat16)
    new_cache = jnp.stack([new_keys.reshape(TOKENS, HEADS * HD), new_values.reshape(TOKENS, HEADS * HD)], axis=1)
    tails = tail_cache[tail_table].reshape(REQ, TAIL, 2, HEADS, HD)
    prompt = prompt_cache.reshape(PROMPT, 2, HEADS, HD)
    fresh = new_cache.reshape(REQ, FRESH, 2, HEADS, HD)
    queries = query.reshape(REQ, FRESH, HEADS, HD)
    prompt_ok = jnp.arange(PROMPT, dtype=jnp.int32) < prompt_length
    causal = jnp.arange(FRESH, dtype=jnp.int32)[None, :] <= jnp.arange(FRESH, dtype=jnp.int32)[:, None]

    def one_request(operands):
        own_queries, own_tail, own_fresh, own_length = operands
        keyvals = jnp.concatenate([prompt, own_tail, own_fresh], axis=0)
        tail_ok = jnp.arange(TAIL, dtype=jnp.int32) < own_length
        allowed = jnp.concatenate([jnp.broadcast_to(prompt_ok[None, :], (FRESH, PROMPT)), jnp.broadcast_to(tail_ok[None, :], (FRESH, TAIL)), causal], axis=1)

        def one_head(head_operands):
            head_query, head_keys, head_values = head_operands
            return attend_head(head_query, head_keys, head_values, allowed)
        mixed = lax.map(one_head, (own_queries.transpose(1, 0, 2), keyvals[:, 0].transpose(1, 0, 2), keyvals[:, 1].transpose(1, 0, 2)))
        return mixed.transpose(1, 0, 2).reshape(FRESH, HEADS * HD)
    attended = lax.map(one_request, (queries, tails, fresh, tail_len)).reshape(TOKENS, HEADS * HD)
    summed = jnp.dot(attended, w_out, preferred_element_type=jnp.float32)
    hidden_out = (hidden_in.astype(jnp.float32) + summed).astype(jnp.bfloat16)
    return (hidden_out, new_cache)
```

```python
import functools

import jax
import jax.numpy as jnp
import numpy as np
from jax import lax
from jax.experimental import pallas as pl
from jax.experimental.pallas import tpu as pltpu
from jax.sharding import PartitionSpec as P

HD = 128
REQ = 8
NEGATIVE = -1e30
SCALE = float(HD**-0.5 * np.log2(np.e))
STAT_ROWS = 16


def params(mib=48):
    return pltpu.CompilerParams(vmem_limit_bytes=mib * 2**20)


def cost(flops, moved, exps=0):
    return pl.CostEstimate(flops=int(flops), bytes_accessed=int(moved), transcendentals=int(exps))


def cycle_of(group):
    if group == 2:
        return [0, 2, 4, 6, 7, 5, 3, 1]
    return list(range(REQ))


def pick(table, index):
    result = jnp.int32(table[0])
    for place, value in enumerate(table):
        result = jnp.where(index == place, jnp.int32(value), result)
    return result


def swap(value, axis, mask):
    pairs = [(source, source ^ mask) for source in range(lax.axis_size(axis))]
    return lax.ppermute(value, axis, pairs)


def turn(value, cycle, group, way):
    count = len(cycle)
    pairs = []
    for place in range(count):
        source, target = cycle[place], cycle[(place + way) % count]
        pairs += [(source * group + m, target * group + m) for m in range(group)]
    return lax.ppermute(value, "seq", pairs)


def rotated(vectors, cosine, sine):
    return vectors * cosine + pltpu.roll(vectors, HD // 2, 1) * sine


def angles(positions):
    half = HD // 2
    freqs = 10000.0 ** (-jnp.arange(half, dtype=jnp.float32) / half)
    angle = positions.astype(jnp.float32)[:, None] * freqs
    cosine, sine = jnp.cos(angle), jnp.sin(angle)
    return (
        jnp.concatenate([cosine, cosine], axis=1),
        jnp.concatenate([-sine, sine], axis=1),
    )


def query_kernel(count, *refs):
    pieces = refs[:count]
    weight, cosine, sine, query, normed = refs[count:]
    columns = pieces[0].shape[1]

    @pl.when(pl.program_id(0) == 0)
    def _():
        index = lax.axis_index("tp")
        values = [piece[...].astype(jnp.float32) for piece in pieces]
        features = columns * count
        mean = sum(jnp.sum(v, axis=1, keepdims=True) for v in values) / features
        values = [v - mean for v in values]
        spread = sum(jnp.sum(v * v, axis=1, keepdims=True) for v in values) / features
        inverse = lax.rsqrt(spread + 1e-05)
        for shift, v in enumerate(values):
            start = pl.multiple_of((index ^ shift) * columns, columns)
            normed[:, pl.ds(start, columns)] = (v * inverse).astype(jnp.bfloat16)

    product = jnp.dot(normed[...], weight[...], preferred_element_type=jnp.float32)
    for start in range(0, product.shape[1], HD):
        query[:, start : start + HD] = rotated(
            product[:, start : start + HD], cosine[...], sine[...]
        ).astype(jnp.bfloat16)


def project_query(pieces, w_query, cosine, sine):
    rows, columns = pieces[0].shape
    depth, width = w_query.shape
    wide = min(width, 2 * HD)
    whole = lambda shape: pl.BlockSpec(shape, lambda i: (0, 0))
    return pl.pallas_call(
        functools.partial(query_kernel, len(pieces)),
        grid=(width // wide,),
        in_specs=[whole((rows, columns))] * len(pieces)
        + [pl.BlockSpec((depth, wide), lambda i: (0, i)), whole((rows, HD)), whole((rows, HD))],
        out_specs=[pl.BlockSpec((rows, wide), lambda i: (0, i)), whole((rows, depth))],
        out_shape=[
            jax.ShapeDtypeStruct((rows, width), jnp.bfloat16),
            jax.ShapeDtypeStruct((rows, depth), jnp.bfloat16),
        ],
        compiler_params=params(),
        cost_estimate=cost(2 * rows * depth * width, 2 * depth * width),
        name="project_query",
    )(*pieces, w_query, cosine, sine)


def keyval_kernel(normed, weight, cosine, sine, keys, values, cache, apart, woven):
    rows, depth = normed.shape
    chunk = apart.shape[0] // 2
    flat = weight.reshape(2 * depth, HD)
    total = jnp.zeros((rows, 2 * HD), jnp.float32)
    for start in range(0, depth, chunk):
        apart[...] = flat[2 * start : 2 * (start + chunk), :].astype(jnp.float32)
        both = jnp.concatenate(
            [apart[pl.ds(0, chunk, stride=2), :], apart[pl.ds(1, chunk, stride=2), :]], axis=1
        ).astype(jnp.bfloat16)
        total += jnp.dot(
            normed[:, start : start + chunk], both, preferred_element_type=jnp.float32
        )
    key = rotated(total[:, :HD], cosine[...], sine[...]).astype(jnp.bfloat16)
    value = total[:, HD:].astype(jnp.bfloat16)
    keys[...] = key
    values[...] = value
    woven[pl.ds(0, rows, stride=2), :] = key.astype(jnp.float32)
    woven[pl.ds(1, rows, stride=2), :] = value.astype(jnp.float32)
    cache.reshape(2 * rows, HD)[...] = woven[...].astype(jnp.bfloat16)


def project_keyval(normed, w_keyval, cosine, sine):
    rows, depth = normed.shape
    width = w_keyval.shape[2]
    chunk = min(depth, 512)
    whole = lambda shape: pl.BlockSpec(shape, lambda i: (0, 0))
    column = pl.BlockSpec((rows, HD), lambda i: (0, i))
    return pl.pallas_call(
        keyval_kernel,
        grid=(width // HD,),
        in_specs=[
            whole((rows, depth)),
            pl.BlockSpec((depth, 2, HD), lambda i: (0, 0, i)),
            whole((rows, HD)),
            whole((rows, HD)),
        ],
        out_specs=[column, column, pl.BlockSpec((rows, 2, HD), lambda i: (0, 0, i))],
        out_shape=[
            jax.ShapeDtypeStruct((rows, width), jnp.bfloat16),
            jax.ShapeDtypeStruct((rows, width), jnp.bfloat16),
            jax.ShapeDtypeStruct((rows, 2, width), jnp.bfloat16),
        ],
        scratch_shapes=[
            pltpu.VMEM((2 * chunk, HD), jnp.float32),
            pltpu.VMEM((2 * rows, HD), jnp.float32),
        ],
        compiler_params=params(),
        cost_estimate=cost(4 * rows * depth * width, 4 * depth * width),
        name="project_keyval",
    )(normed, w_keyval, cosine, sine)


def part_apart(block, apart, keys, values, start):
    count = block.shape[0]
    apart[: 2 * count, :] = block.reshape(2 * count, HD)[...].astype(jnp.float32)
    keys[start : start + count, :] = apart[pl.ds(0, count, stride=2), :].astype(jnp.bfloat16)
    values[start : start + count, :HD] = apart[pl.ds(1, count, stride=2), :].astype(jnp.bfloat16)


def column_of(stats, lane):
    place = lax.broadcasted_iota(jnp.int32, stats.shape, 1)
    return jnp.sum(jnp.where(place == lane, stats, 0.0), axis=1, keepdims=True)


def with_column(stats, lane, column):
    place = lax.broadcasted_iota(jnp.int32, stats.shape, 1)
    return jnp.where(place == lane, column, stats)


def row_of(column):
    count = column.shape[0]
    eye = lax.broadcasted_iota(jnp.int32, (HD, HD), 0) == lax.broadcasted_iota(
        jnp.int32, (HD, HD), 1
    )
    return [
        jnp.sum(jnp.where(eye, column[start : start + HD], 0.0), axis=0, keepdims=True)
        for start in range(0, count, HD)
    ]


def column_from(rows):
    eye = lax.broadcasted_iota(jnp.int32, (HD, HD), 0) == lax.broadcasted_iota(
        jnp.int32, (HD, HD), 1
    )
    return jnp.concatenate(
        [jnp.sum(jnp.where(eye, row, 0.0), axis=1, keepdims=True) for row in rows], axis=0
    )


def attend_kernel(spec, *refs):
    group, steps, piece, own, first, last = spec
    refs = list(refs)
    take = lambda count: [refs.pop(0) for _ in range(count)]
    lengths, shared, table = take(3)
    queries = take(group)
    blocks = take(len(steps))
    if own:
        tail, fresh_keys, fresh_values = take(3)
    if not first:
        old_total, old_stats = take(2)
    if last:
        result, result_stats = take(2)
        parts = take(group - 1)
    else:
        new_total, new_stats = take(2)
    keys, values, bias, apart = take(4)
    head = pl.program_id(0)
    rows = queries[0].shape[0]
    cycle = cycle_of(group)
    seq = lax.axis_index("seq")
    request, member = seq // group, seq % group
    place = pick(list(np.argsort(cycle)), request)
    count = 0
    edges = []
    if own:
        block_size = 128
        slots = tail.shape[0] // block_size
        for i in range(slots):
            wanted = seq * slots + i
            number = jnp.int32(0)
            for j in range(table.shape[1]):
                number = jnp.where(table[request, j] == wanted, jnp.int32(j), number)
            edges.append((count + i * block_size, block_size, number * block_size, lengths[request]))
        part_apart(tail, apart, keys, values, count)
        count += tail.shape[0]
    for (step, begin), block in zip(steps, blocks):
        origin = pick(cycle, lax.rem(place + step + REQ, REQ))
        size = block.shape[0]
        start = (origin * group + member) * piece + begin
        edges.append((count, size, start, shared[0]))
        part_apart(block, apart, keys, values, count)
        count += size
    plain = count
    if own:
        keys[count : count + rows, :] = fresh_keys[...]
        values[count : count + rows, :HD] = fresh_values[...]
        count += rows

    @pl.when(head == 0)
    def _():
        values[:, HD:] = jnp.ones((values.shape[0], HD), jnp.bfloat16)
        for begin, size, start, length in edges:
            positions = start + lax.broadcasted_iota(jnp.int32, (1, size), 1)
            bias[:, begin : begin + size] = jnp.broadcast_to(
                jnp.where(positions < length, 0.0, NEGATIVE), (8, size)
            )
        if last:
            result_stats[...] = jnp.zeros_like(result_stats)
        else:
            new_stats[...] = jnp.zeros_like(new_stats)

    across = (((1,), (1,)), ((), ()))
    for shift in range(group):
        scores = lax.dot_general(
            queries[shift][...], keys[...], across, preferred_element_type=jnp.float32
        )
        seen = scores[:, :plain] + bias[0:1, :]
        if own:
            mine = (member ^ shift) * rows + lax.broadcasted_iota(jnp.int32, (rows, rows), 0)
            theirs = member * rows + lax.broadcasted_iota(jnp.int32, (rows, rows), 1)
            causal = jnp.where(theirs <= mine, scores[:, plain:], NEGATIVE)
            seen = jnp.concatenate([seen, causal], axis=1)
        top = jnp.max(seen, axis=1, keepdims=True)
        span = slice(shift * rows, (shift + 1) * rows)
        if not first:
            stats = old_stats[span, :]
            old_top = column_of(stats, head)
            top = jnp.maximum(top, old_top)
        weights = jnp.exp2((seen - top) * SCALE).astype(jnp.bfloat16)
        mixed = jnp.dot(weights, values[...], preferred_element_type=jnp.float32)
        total, summed = mixed[:, :HD], mixed[:, HD:]
        if not first:
            factor = jnp.exp2((old_top - top) * SCALE)
            total = total + old_total[shift] * factor
            summed = summed + column_of(stats, head + 64) * factor
        if last:
            even = total / summed
            extent = top * SCALE + jnp.log2(summed)
            if shift == 0:
                result[...] = even
                result_stats[...] = with_column(result_stats[...], head, extent)
            else:
                part = parts[shift - 1]
                part[:rows, :] = even.astype(jnp.bfloat16)
                lines = row_of(extent)
                packed = []
                for _ in range(3):
                    rounded = [line.astype(jnp.bfloat16).astype(jnp.float32) for line in lines]
                    packed += rounded
                    lines = [line - r for line, r in zip(lines, rounded)]
                line_number = lax.broadcasted_iota(jnp.int32, (STAT_ROWS, HD), 0)
                tile = jnp.zeros((STAT_ROWS, HD), jnp.float32)
                for i, line in enumerate(packed):
                    tile = jnp.where(line_number == i, line, tile)
                part[rows:, :] = tile.astype(jnp.bfloat16)
        else:
            new_total[shift] = total
            marked = with_column(new_stats[span, :], head, top)
            new_stats[span, :] = with_column(marked, head + 64, summed)


def attend(tail_len, shared_len, tail_table, queries, steps, blocks, own, old, last, name):
    group = len(queries)
    rows, width = queries[0].shape
    column = pl.BlockSpec((rows, HD), lambda i: (0, i))
    smem = pl.BlockSpec(memory_space=pltpu.SMEM)
    triple = lambda value: pl.BlockSpec((value.shape[0], 2, HD), lambda i: (0, 0, i))
    total_spec = pl.BlockSpec((group, rows, HD), lambda i: (0, 0, i))
    stats_spec = pl.BlockSpec((group * rows, HD), lambda i: (0, 0))
    in_specs = [smem] * 3 + [column] * group + [triple(block) for block in blocks]
    operands = [tail_len, shared_len, tail_table, *queries, *blocks]
    plain = sum(block.shape[0] for block in blocks)
    longest = max(block.shape[0] for block in blocks)
    count = plain
    if own:
        in_specs += [triple(own[0]), column, column]
        operands += own
        plain += own[0].shape[0]
        longest = max(longest, own[0].shape[0])
        count = plain + rows
    if old:
        in_specs += [total_spec, stats_spec]
        operands += old
    if last:
        out_specs = [column, pl.BlockSpec((rows, HD), lambda i: (0, 0))]
        out_shape = [
            jax.ShapeDtypeStruct((rows, width), jnp.float32),
            jax.ShapeDtypeStruct((rows, HD), jnp.float32),
        ]
        out_specs += [pl.BlockSpec((rows + STAT_ROWS, HD), lambda i: (0, i))] * (group - 1)
        out_shape += [jax.ShapeDtypeStruct((rows + STAT_ROWS, width), jnp.bfloat16)] * (group - 1)
    else:
        out_specs = [total_spec, stats_spec]
        out_shape = [
            jax.ShapeDtypeStruct((group, rows, width), jnp.float32),
            jax.ShapeDtypeStruct((group * rows, HD), jnp.float32),
        ]
    scores = group * rows * count * (width // HD)
    return pl.pallas_call(
        functools.partial(attend_kernel, (group, steps, blocks[0].shape[0], bool(own), not old, last)),
        grid=(width // HD,),
        in_specs=in_specs,
        out_specs=out_specs,
        out_shape=out_shape,
        scratch_shapes=[
            pltpu.VMEM((count, HD), jnp.bfloat16),
            pltpu.VMEM((count, 2 * HD), jnp.bfloat16),
            pltpu.VMEM((8, plain), jnp.float32),
            pltpu.VMEM((2 * longest, HD), jnp.float32),
        ],
        compiler_params=params(),
        cost_estimate=cost(4 * scores * HD, 4 * count * width, scores),
        name=name,
    )(*operands)


def output_kernel(group, heads, *refs):
    refs = list(refs)
    result, result_stats = refs[:2]
    parts = refs[2 : 1 + group]
    weight, hidden = refs[1 + group : 3 + group]
    kept = refs[3 + group]
    sent = refs[4 + group : -1]
    attended = refs[-1]
    rows = result.shape[0]
    lines = rows // HD
    for head in range(heads):
        span = slice(head * HD, (head + 1) * HD)
        extents = [result_stats[:, head : head + 1]]
        mixes = [result[:, span]]
        for part in parts:
            tile = part[rows:, span].astype(jnp.float32)
            extents.append(
                column_from(
                    [
                        tile[i : i + 1] + tile[lines + i : lines + i + 1]
                        + tile[2 * lines + i : 2 * lines + i + 1]
                        for i in range(lines)
                    ]
                )
            )
            mixes.append(part[:rows, span].astype(jnp.float32))
        top = functools.reduce(jnp.maximum, extents)
        shares = [jnp.exp2(extent - top) for extent in extents]
        mixed = sum(mix * share for mix, share in zip(mixes, shares)) / sum(shares)
        attended[:, span] = mixed.astype(jnp.bfloat16)
    index = lax.axis_index("tp")
    columns = hidden.shape[1]
    wide = min(columns, 256)
    for shift in range(len(sent), -1, -1):
        for start in range(0, columns, wide):
            place = pl.multiple_of((index ^ shift) * columns + start, wide)
            product = jnp.dot(
                attended[...], weight[:, pl.ds(place, wide)], preferred_element_type=jnp.float32
            )
            if shift:
                sent[shift - 1][:, start : start + wide] = product.astype(jnp.bfloat16)
            else:
                kept[:, start : start + wide] = product + hidden[:, start : start + wide].astype(
                    jnp.float32
                )


def project_output(result, stats, parts, w_out, hidden, ways):
    rows, width = result.shape
    columns = hidden.shape[1]
    vmem = pl.BlockSpec(memory_space=pltpu.VMEM)
    return pl.pallas_call(
        functools.partial(output_kernel, 1 + len(parts), width // HD),
        in_specs=[vmem] * (4 + len(parts)),
        out_specs=[vmem] * ways,
        out_shape=[jax.ShapeDtypeStruct((rows, columns), jnp.float32)]
        + [jax.ShapeDtypeStruct((rows, columns), jnp.bfloat16)] * (ways - 1),
        scratch_shapes=[pltpu.VMEM((rows, width), jnp.bfloat16)],
        compiler_params=params(),
        cost_estimate=cost(2 * rows * width * columns * ways, 2 * width * columns * ways),
        name="project_output",
    )(result, stats, *parts, w_out, hidden)


def local(
    hidden_in, w_query, w_keyval, w_out, prompt_cache, tail_cache, tail_table, tail_len, shared_len
):
    rows = hidden_in.shape[0]
    group = lax.axis_size("seq") // REQ
    ways = lax.axis_size("tp")
    cycle = cycle_of(group)
    seq = lax.axis_index("seq")
    request = seq // group
    member = seq % group

    pieces = [hidden_in] + [swap(hidden_in, "tp", shift) for shift in range(1, ways)]
    ahead, behind = [prompt_cache], [prompt_cache]
    half = REQ // 2
    for _ in range(half - 1):
        ahead.append(turn(ahead[-1], cycle, group, 1))
        behind.append(turn(behind[-1], cycle, group, -1))
    middle = prompt_cache.shape[0] // 2
    far_low = turn(ahead[-1][:middle], cycle, group, 1)
    far_high = turn(behind[-1][middle:], cycle, group, -1)

    own_length = lax.dynamic_index_in_dim(tail_len, request, 0, keepdims=False)
    positions = (
        shared_len[0] + own_length + member * rows + jnp.arange(rows, dtype=jnp.int32)
    )
    cosine, sine = angles(positions)
    query, normed = project_query(pieces, w_query, cosine, sine)
    queries = [query] + [swap(query, "seq", shift) for shift in range(1, group)]
    fresh_keys, fresh_values, new_cache = project_keyval(normed, w_keyval, cosine, sine)

    tail = tail_cache.reshape(-1, 2, tail_cache.shape[3])
    numbers = (tail_len, shared_len, tail_table, queries)
    near = [(0, 0)] + [(way * step, 0) for step in (1, 2) for way in (-1, 1)]
    near_blocks = [prompt_cache, ahead[1], behind[1], ahead[2], behind[2]]
    state = attend(
        *numbers, near, near_blocks, [tail, fresh_keys, fresh_values], None, False, "attend_near"
    )
    far = [(-3, 0), (3, 0), (-half, 0), (half, middle)]
    far_blocks = [ahead[3], behind[3], far_low, far_high]
    result, stats, *parts = attend(*numbers, far, far_blocks, None, state, True, "attend_far")
    parts = [swap(part, "seq", shift + 1) for shift, part in enumerate(parts)]
    kept, *sent = project_output(result, stats, parts, w_out, hidden_in, ways)
    total = kept
    for shift, part in enumerate(sent):
        total = total + swap(part, "tp", shift + 1).astype(jnp.float32)
    return (total.astype(jnp.bfloat16), new_cache)


def solution(mesh):
    return jax.shard_map(
        local,
        mesh=mesh,
        in_specs=(
            P("seq", "tp"),
            P(None, "tp"),
            P(None, None, "tp"),
            P("tp", None),
            P("seq", None, "tp"),
            P("seq", None, None, "tp"),
            P(),
            P(),
            P(),
        ),
        out_specs=(P("seq", "tp"), P("seq", None, "tp")),
        check_vma=False,
    )
```

```python
import functools

import jax
import jax.numpy as jnp
import numpy as np
from jax import lax
from jax.experimental import pallas as pl
from jax.experimental.pallas import tpu as pltpu
from jax.sharding import PartitionSpec as P

HD = 128
REQ = 8
NEGATIVE = -1e30
SCALE = float(HD**-0.5 * np.log2(np.e))
STAT_ROWS = 16


def params(mib=24):
    return pltpu.CompilerParams(vmem_limit_bytes=mib * 2**20)


def cost(flops, moved, exps=0):
    return pl.CostEstimate(flops=int(flops), bytes_accessed=int(moved), transcendentals=int(exps))


def cycle_of(group):
    if group == 2:
        return [0, 2, 4, 6, 7, 5, 3, 1]
    return list(range(REQ))


def pick(table, index):
    result = jnp.int32(table[0])
    for place, value in enumerate(table):
        result = jnp.where(index == place, jnp.int32(value), result)
    return result


def swap(value, axis, mask):
    pairs = [(source, source ^ mask) for source in range(lax.axis_size(axis))]
    return lax.ppermute(value, axis, pairs)


def turn(value, cycle, group, way):
    count = len(cycle)
    pairs = []
    for place in range(count):
        source, target = cycle[place], cycle[(place + way) % count]
        pairs += [(source * group + m, target * group + m) for m in range(group)]
    return lax.ppermute(value, "seq", pairs)


def rotated(vectors, cosine, sine):
    return vectors * cosine + pltpu.roll(vectors, HD // 2, 1) * sine


def angles(positions):
    half = HD // 2
    freqs = 10000.0 ** (-jnp.arange(half, dtype=jnp.float32) / half)
    angle = positions.astype(jnp.float32)[:, None] * freqs
    cosine, sine = jnp.cos(angle), jnp.sin(angle)
    return (
        jnp.concatenate([cosine, cosine], axis=1),
        jnp.concatenate([-sine, sine], axis=1),
    )


def lanes(start, count=HD):
    return pl.ds(pl.multiple_of(start, HD), count)


def after(value, *others):
    return lax.optimization_barrier((value, *others))[0]


VMEM = pl.BlockSpec(memory_space=pltpu.VMEM)
SMEM = pl.BlockSpec(memory_space=pltpu.SMEM)


def part_kernel(*refs):
    *pieces, apart, result_scratch = refs
    result = apart
    for i, piece in enumerate(pieces):
        count = piece.shape[0]
        scratch = result_scratch.at[i]
        scratch[...] = piece.reshape(2 * count, HD)[...].astype(jnp.float32)
        span = slice(i * HD, (i + 1) * HD)
        for j in range(2):
            result[j, :, span] = scratch[pl.ds(j, count, stride=2), :].astype(jnp.bfloat16)


def part_keyval(block, name):
    count, _, width = block.shape
    heads = width // HD
    specs = [
        pl.BlockSpec((count, 2, HD), functools.partial(lambda i, _: (0, 0, i), i))
        for i in range(heads)
    ]
    return pl.pallas_call(
        part_kernel,
        grid=(1,),
        in_specs=specs,
        out_specs=pl.BlockSpec((2, count, width), lambda _: (0, 0, 0)),
        out_shape=jax.ShapeDtypeStruct((2, count, width), jnp.bfloat16),
        scratch_shapes=[pltpu.VMEM((heads, 2 * count, HD), jnp.float32)],
        compiler_params=params(16),
        cost_estimate=cost(0, 8 * count * width),
        name=name,
    )(*[block] * heads)


def query_kernel(*refs):
    *pieces, weight, cosine, sine, query, normed = refs
    rows, columns = pieces[0].shape
    index = lax.axis_index("tp")
    features = columns * len(pieces)
    values = [piece[...].astype(jnp.float32) for piece in pieces]
    mean = sum(jnp.sum(v, axis=1, keepdims=True) for v in values) / features
    values = [v - mean for v in values]
    spread = sum(jnp.sum(v * v, axis=1, keepdims=True) for v in values) / features
    inverse = lax.rsqrt(spread + 1e-05)
    for shift, v in enumerate(values):
        normed[:, lanes((index ^ shift) * columns, columns)] = (v * inverse).astype(jnp.bfloat16)
    width = weight.shape[1]
    wide = min(width, 2 * HD)
    for base in range(0, width, wide):
        product = jnp.dot(
            normed[...], weight[:, base : base + wide], preferred_element_type=jnp.float32
        )
        for start in range(0, wide, HD):
            query[:, base + start : base + start + HD] = rotated(
                product[:, start : start + HD], cosine[...], sine[...]
            ).astype(jnp.bfloat16)


def project_query(pieces, w_query, cosine, sine):
    rows, columns = pieces[0].shape
    depth, width = w_query.shape
    return pl.pallas_call(
        query_kernel,
        in_specs=[VMEM] * (len(pieces) + 3),
        out_specs=[VMEM] * 2,
        out_shape=[
            jax.ShapeDtypeStruct((rows, width), jnp.bfloat16),
            jax.ShapeDtypeStruct((rows, depth), jnp.bfloat16),
        ],
        compiler_params=params(24),
        cost_estimate=cost(2 * rows * depth * width, 2 * depth * width),
        name="project_query",
    )(*pieces, w_query, cosine, sine)


def keyval_kernel(together, *refs):
    normed = refs[0]
    weights = refs[1 : 1 + together]
    cosine, sine, keys, values, cache, spaced = refs[1 + together : 7 + together]
    woven = refs[7 + together]
    rows, depth = normed.shape

    @pl.when(pl.program_id(0) == 0)
    def _():
        source = lax.broadcasted_iota(jnp.int32, (HD, 2 * HD), 0)
        target = lax.broadcasted_iota(jnp.int32, (HD, 2 * HD), 1)
        for j in range(2):
            spread = jnp.where(target == 2 * source + j, 1.0, 0.0).astype(jnp.bfloat16)
            for start in range(0, depth, HD):
                spaced[j * rows : (j + 1) * rows, 2 * start : 2 * (start + HD)] = jnp.dot(
                    normed[:, start : start + HD], spread, preferred_element_type=jnp.float32
                ).astype(jnp.bfloat16)

    flat = [weight.reshape(2 * depth, HD)[...] for weight in weights]
    total = jnp.dot(
        spaced[...], jnp.concatenate(flat, axis=1), preferred_element_type=jnp.float32
    )
    for i in range(together):
        span = slice(i * HD, (i + 1) * HD)
        key = rotated(total[:rows, span], cosine[...], sine[...]).astype(jnp.bfloat16)
        value = total[rows:, span].astype(jnp.bfloat16)
        keys[:, span] = key
        values[:, span] = value
        place = woven.at[i]
        place[pl.ds(0, rows, stride=2), :] = key.astype(jnp.float32)
        place[pl.ds(1, rows, stride=2), :] = value.astype(jnp.float32)
        cache[:, :, span] = place[...].astype(jnp.bfloat16).reshape(rows, 2, HD)


def project_keyval(normed, w_keyval, cosine, sine):
    rows, depth = normed.shape
    width = w_keyval.shape[2]
    together = min(2, width // HD)
    wide = together * HD
    whole = lambda shape: pl.BlockSpec(shape, lambda i: (0, 0))
    column = pl.BlockSpec((rows, wide), lambda i: (0, i))
    weights = [
        pl.BlockSpec((depth, 2, HD), functools.partial(lambda j, i: (0, 0, together * i + j), j))
        for j in range(together)
    ]
    return pl.pallas_call(
        functools.partial(keyval_kernel, together),
        grid=(width // wide,),
        in_specs=[whole((rows, depth)), *weights, whole((rows, HD)), whole((rows, HD))],
        out_specs=[column, column, pl.BlockSpec((rows, 2, wide), lambda i: (0, 0, i))],
        out_shape=[
            jax.ShapeDtypeStruct((rows, width), jnp.bfloat16),
            jax.ShapeDtypeStruct((rows, width), jnp.bfloat16),
            jax.ShapeDtypeStruct((rows, 2, width), jnp.bfloat16),
        ],
        scratch_shapes=[
            pltpu.VMEM((2 * rows, 2 * depth), jnp.bfloat16),
            pltpu.VMEM((together, 2 * rows, HD), jnp.float32),
        ],
        compiler_params=params(24),
        cost_estimate=cost(4 * rows * depth * width, 4 * depth * width),
        name="project_keyval",
    )(normed, *[w_keyval] * together, cosine, sine)


def column_of(stats, lane):
    place = lax.broadcasted_iota(jnp.int32, stats.shape, 1)
    return jnp.sum(jnp.where(place == lane, stats, 0.0), axis=1, keepdims=True)


def with_column(stats, lane, column):
    place = lax.broadcasted_iota(jnp.int32, stats.shape, 1)
    return jnp.where(place == lane, column, stats)


def attend_kernel(spec, *refs):
    group, steps, piece, own, first, last = spec
    refs = list(refs)
    take = lambda count: [refs.pop(0) for _ in range(count)]
    lengths, shared, table = take(3)
    queries = take(group)
    blocks = take(len(steps))
    if own:
        tail, fresh_keys, fresh_values = take(3)
    if not first:
        old_mix, old_stats = take(2)
    if last:
        result, result_stats = take(2)
        parts = take(group - 1)
        stats = take(1)[0]
    else:
        mix, stats = take(2)
    bias = take(1)[0]
    if own:
        causal = take(1)[0]
    rows, width = queries[0].shape
    heads = width // HD
    cycle = cycle_of(group)
    seq = lax.axis_index("seq")
    request, member = seq // group, seq % group
    place = pick(list(np.argsort(cycle)), request)
    edges = []
    count = 0
    if own:
        block_size = 128
        slots = tail.shape[1] // block_size
        for i in range(slots):
            wanted = seq * slots + i
            number = jnp.int32(0)
            for j in range(table.shape[1]):
                number = jnp.where(table[request, j] == wanted, jnp.int32(j), number)
            edges.append((count, block_size, number * block_size, lengths[request]))
            count += block_size
    for (step, begin), block in zip(steps, blocks):
        origin = pick(cycle, lax.rem(place + step + REQ, REQ))
        size = block.shape[1]
        edges.append((count, size, (origin * group + member) * piece + begin, shared[0]))
        count += size
    for begin, size, start, length in edges:
        positions = start + lax.broadcasted_iota(jnp.int32, (size, HD), 0)
        lane = lax.broadcasted_iota(jnp.int32, (size, HD), 1)
        bias[begin : begin + size, :] = jnp.where(
            (positions >= length) & (lane == 0), NEGATIVE, 0.0
        ).astype(jnp.bfloat16)
    if own:
        bias[count : count + rows, :] = jnp.zeros((rows, HD), jnp.bfloat16)
        theirs = member * rows + lax.broadcasted_iota(jnp.int32, (rows, rows), 1)
        for shift in range(group):
            mine = (member ^ shift) * rows + lax.broadcasted_iota(jnp.int32, (rows, rows), 0)
            causal[shift * rows : (shift + 1) * rows, :] = jnp.where(theirs <= mine, 0.0, NEGATIVE)
    stats[...] = jnp.zeros_like(stats)
    unit = jnp.where(
        lax.broadcasted_iota(jnp.int32, (group * rows, HD), 1) == 0, 1.0, 0.0
    ).astype(jnp.bfloat16)
    across = (((1,), (1,)), ((), ()))

    def one_head(head):
        span = lanes(head * HD)
        query = jnp.concatenate([q[:, span] for q in queries], axis=0)
        keys = [block[0, :, span] for block in blocks]
        values = [block[1, :, span] for block in blocks]
        if own:
            keys = [tail[0, :, span], *keys, fresh_keys[:, span]]
            values = [tail[1, :, span], *values, fresh_values[:, span]]
        keys = jnp.concatenate(keys, axis=0)
        values = jnp.concatenate(values, axis=0)
        scores = lax.dot_general(
            jnp.concatenate([query, unit], axis=1),
            jnp.concatenate([keys, bias[...]], axis=1),
            across,
            preferred_element_type=jnp.float32,
        )
        if own:
            scores = jnp.concatenate([scores[:, :count], scores[:, count:] + causal[...]], axis=1)
        top = jnp.max(scores, axis=1, keepdims=True)
        if not first:
            old = column_of(old_stats[...], head)
            top = jnp.maximum(top, old * (1.0 / SCALE))
        weights = jnp.exp2((scores - top) * SCALE).astype(jnp.bfloat16)
        mixed = jnp.dot(
            weights,
            jnp.concatenate([values, jnp.ones_like(values)], axis=1),
            preferred_element_type=jnp.float32,
        )
        total, summed = mixed[:, :HD], mixed[:, HD:]
        if not first:
            factor = jnp.exp2(old - top * SCALE)
            total = total + old_mix[:, span] * factor
            summed = summed + factor
        even = total / summed
        stats[...] = with_column(stats[...], head, top * SCALE + jnp.log2(summed))
        if last:
            result[:, span] = even[:rows]
            for shift in range(1, group):
                parts[shift - 1][:rows, span] = even[shift * rows : (shift + 1) * rows].astype(
                    jnp.bfloat16
                )
        else:
            mix[:, span] = even

    together = min(2, heads)

    def some_heads(i, _):
        for j in range(together):
            one_head(together * i + j)
        return 0

    lax.fori_loop(0, heads // together, some_heads, 0)
    if last:
        result_stats[...] = stats[:rows, :]
        for shift in range(1, group):
            line = jnp.transpose(stats[shift * rows : (shift + 1) * rows, :])[:heads, :]
            packed = []
            for _ in range(3):
                rounded = line.astype(jnp.bfloat16).astype(jnp.float32)
                packed.append(rounded)
                line = line - rounded
            gap = -3 * heads % STAT_ROWS
            if gap:
                packed.append(jnp.zeros((gap, rows), jnp.float32))
            packed = jnp.concatenate(packed, axis=0).astype(jnp.bfloat16)
            for j in range(packed.shape[0] // STAT_ROWS):
                parts[shift - 1][rows:, j * rows : (j + 1) * rows] = packed[
                    j * STAT_ROWS : (j + 1) * STAT_ROWS
                ]


def attend(tail_len, shared_len, tail_table, queries, steps, blocks, own, old, last, name):
    group = len(queries)
    rows, width = queries[0].shape
    operands = [tail_len, shared_len, tail_table, *queries, *blocks]
    piece = blocks[0].shape[1]
    plain = sum(block.shape[1] for block in blocks)
    if own:
        operands += own
        plain += own[0].shape[1]
    if old:
        operands += old
    count = plain + (rows if own else 0)
    flat_stats = jax.ShapeDtypeStruct((group * rows, HD), jnp.float32)
    scratch = [pltpu.VMEM((count, HD), jnp.bfloat16)]
    if own:
        scratch.append(pltpu.VMEM((group * rows, rows), jnp.float32))
    if last:
        out_shape = [
            jax.ShapeDtypeStruct((rows, width), jnp.float32),
            jax.ShapeDtypeStruct((rows, HD), jnp.float32),
        ] + [jax.ShapeDtypeStruct((rows + STAT_ROWS, width), jnp.bfloat16)] * (group - 1)
        scratch.insert(0, pltpu.VMEM((group * rows, HD), jnp.float32))
    else:
        out_shape = [jax.ShapeDtypeStruct((group * rows, width), jnp.float32), flat_stats]
    scores = group * rows * count * (width // HD)
    return pl.pallas_call(
        functools.partial(
            attend_kernel, (group, steps, piece, bool(own), not old, last)
        ),
        in_specs=[SMEM] * 3 + [VMEM] * (len(operands) - 3),
        out_specs=[VMEM] * len(out_shape),
        out_shape=out_shape,
        scratch_shapes=scratch,
        compiler_params=params(32),
        cost_estimate=cost(4 * scores * HD, 4 * count * width, scores),
        name=name,
    )(*operands)


def combine_kernel(*refs):
    result, stats, *refs = refs
    *parts, weight, attended, sent = refs[: len(refs)]
    rows, width = result.shape
    heads = width // HD
    extents = [stats[...]]
    for part in parts:
        tile = part[rows:, :].astype(jnp.float32)
        groups = -(-3 * heads // STAT_ROWS)
        lines = jnp.concatenate(
            [tile[:, j * rows : (j + 1) * rows] for j in range(groups)], axis=0
        )
        line = sum(lines[i * heads : (i + 1) * heads] for i in range(3))
        line = jnp.concatenate([line, jnp.zeros((HD - heads, rows), jnp.float32)], axis=0)
        extents.append(jnp.transpose(line))
    top = functools.reduce(jnp.maximum, extents)
    shares = [jnp.exp2(extent - top) for extent in extents]
    whole = sum(shares)
    shares = [share / whole for share in shares]
    for head in range(heads):
        span = slice(head * HD, (head + 1) * HD)
        mixes = [result[:, span]] + [part[:rows, span].astype(jnp.float32) for part in parts]
        mixed = sum(mix * share[:, head : head + 1] for mix, share in zip(mixes, shares))
        attended[:, span] = mixed.astype(jnp.bfloat16)
    index = lax.axis_index("tp")
    ways = sent.shape[0] + 1
    columns = weight.shape[1] // ways
    for shift in range(1, ways):
        sent[shift - 1] = jnp.dot(
            attended[...],
            weight[:, lanes((index ^ shift) * columns, columns)],
            preferred_element_type=jnp.float32,
        ).astype(jnp.bfloat16)


def combine(result, stats, parts, w_out, ways):
    rows, width = result.shape
    columns = w_out.shape[1] // ways
    return pl.pallas_call(
        combine_kernel,
        in_specs=[VMEM] * (3 + len(parts)),
        out_specs=[VMEM] * 2,
        out_shape=[
            jax.ShapeDtypeStruct((rows, width), jnp.bfloat16),
            jax.ShapeDtypeStruct((ways - 1, rows, columns), jnp.bfloat16),
        ],
        compiler_params=params(20),
        cost_estimate=cost(2 * rows * width * columns * (ways - 1), 2 * width * w_out.shape[1]),
        name="combine_send",
    )(result, stats, *parts, w_out)


def keep_kernel(attended, weight, hidden, kept):
    columns = hidden.shape[1]
    product = jnp.dot(
        attended[...],
        weight[:, lanes(lax.axis_index("tp") * columns, columns)],
        preferred_element_type=jnp.float32,
    )
    kept[...] = product + hidden[...].astype(jnp.float32)


def keep(attended, w_out, hidden):
    rows, width = attended.shape
    return pl.pallas_call(
        keep_kernel,
        in_specs=[VMEM] * 3,
        out_specs=VMEM,
        out_shape=jax.ShapeDtypeStruct(hidden.shape, jnp.float32),
        compiler_params=params(20),
        cost_estimate=cost(2 * rows * width * hidden.shape[1], 2 * width * w_out.shape[1]),
        name="keep_own",
    )(attended, w_out, hidden)


def local(
    hidden_in, w_query, w_keyval, w_out, prompt_cache, tail_cache, tail_table, tail_len, shared_len
):
    rows = hidden_in.shape[0]
    group = lax.axis_size("seq") // REQ
    ways = lax.axis_size("tp")
    cycle = cycle_of(group)
    seq = lax.axis_index("seq")
    request = seq // group
    member = seq % group
    half = REQ // 2
    middle = prompt_cache.shape[0] // 2

    pieces = [hidden_in] + [swap(hidden_in, "tp", shift) for shift in range(1, ways)]
    prompt = part_keyval(prompt_cache, "part_prompt")
    ahead, behind = [prompt], [prompt]

    def step(*others):
        for blocks, way in ((ahead, 1), (behind, -1)):
            blocks.append(turn(after(blocks[-1], *others), cycle, group, way))

    step()
    own_length = lax.dynamic_index_in_dim(tail_len, request, 0, keepdims=False)
    positions = shared_len[0] + own_length + member * rows + jnp.arange(rows, dtype=jnp.int32)
    cosine, sine = angles(positions)
    query, normed = project_query(pieces, w_query, cosine, sine)
    queries = [query] + [swap(query, "seq", shift) for shift in range(1, group)]
    fresh_keys, fresh_values, new_cache = project_keyval(normed, w_keyval, cosine, sine)
    step(fresh_keys)
    tail = part_keyval(tail_cache.reshape(-1, 2, tail_cache.shape[3]), "part_tail")

    numbers = (tail_len, shared_len, tail_table, queries)
    near = [(0, 0), (-1, 0), (1, 0)]
    state = attend(
        *numbers,
        near,
        [prompt, ahead[1], behind[1]],
        [tail, fresh_keys, fresh_values],
        None,
        False,
        "attend_near",
    )
    step(state[1])
    state = attend(
        *numbers, [(-2, 0), (2, 0)], [ahead[2], behind[2]], None, state, False, "attend_mid"
    )
    far_low = turn(after(ahead[3], state[1])[:, :middle], cycle, group, 1)
    far_high = turn(after(behind[3], state[1])[:, middle:], cycle, group, -1)
    far = [(-3, 0), (3, 0), (-half, 0), (half, middle)]
    far_blocks = [ahead[3], behind[3], far_low, far_high]
    result, stats, *parts = attend(*numbers, far, far_blocks, None, state, True, "attend_far")
    parts = [swap(part, "seq", shift + 1) for shift, part in enumerate(parts)]
    attended, sent = combine(result, stats, parts, w_out, ways)
    received = [swap(sent[shift - 1], "tp", shift) for shift in range(1, ways)]
    total = keep(attended, w_out, hidden_in)
    for part in received:
        total = total + part.astype(jnp.float32)
    return (total.astype(jnp.bfloat16), new_cache)


def solution(mesh):
    return jax.shard_map(
        local,
        mesh=mesh,
        in_specs=(
            P("seq", "tp"),
            P(None, "tp"),
            P(None, None, "tp"),
            P("tp", None),
            P("seq", None, "tp"),
            P("seq", None, None, "tp"),
            P(),
            P(),
            P(),
        ),
        out_specs=(P("seq", "tp"), P("seq", None, "tp")),
        check_vma=False,
    )
```

```python
import functools

import jax
import jax.numpy as jnp
import numpy as np
from jax import lax
from jax.experimental import pallas as pl
from jax.experimental.pallas import tpu as pltpu
from jax.sharding import PartitionSpec as P

HD = 128
REQ = 8
NEGATIVE = -1e30
SCALE = float(HD**-0.5 * np.log2(np.e))
STAT_ROWS = 16


def params(mib=24):
    return pltpu.CompilerParams(vmem_limit_bytes=mib * 2**20)


def cost(flops, moved, exps=0):
    return pl.CostEstimate(flops=int(flops), bytes_accessed=int(moved), transcendentals=int(exps))


def cycle_of(group):
    if group == 2:
        return [0, 2, 4, 6, 7, 5, 3, 1]
    return list(range(REQ))


def pick(table, index):
    result = jnp.int32(table[0])
    for place, value in enumerate(table):
        result = jnp.where(index == place, jnp.int32(value), result)
    return result


def swap(value, axis, mask):
    pairs = [(source, source ^ mask) for source in range(lax.axis_size(axis))]
    return lax.ppermute(value, axis, pairs)


def turn(value, cycle, group, way):
    count = len(cycle)
    pairs = []
    for place in range(count):
        source, target = cycle[place], cycle[(place + way) % count]
        pairs += [(source * group + m, target * group + m) for m in range(group)]
    return lax.ppermute(value, "seq", pairs)


def rotated(vectors, cosine, sine):
    return vectors * cosine + pltpu.roll(vectors, HD // 2, 1) * sine


def angles(positions):
    half = HD // 2
    freqs = 10000.0 ** (-jnp.arange(half, dtype=jnp.float32) / half)
    angle = positions.astype(jnp.float32)[:, None] * freqs
    cosine, sine = jnp.cos(angle), jnp.sin(angle)
    return (
        jnp.concatenate([cosine, cosine], axis=1),
        jnp.concatenate([-sine, sine], axis=1),
    )


def lanes(start, count=HD):
    return pl.ds(pl.multiple_of(start, HD), count)


def after(value, *others):
    return lax.optimization_barrier((value, *others))[0]


VMEM = pl.BlockSpec(memory_space=pltpu.VMEM)
HBM = pl.BlockSpec(memory_space=pltpu.HBM)
SMEM = pl.BlockSpec(memory_space=pltpu.SMEM)


def viewed(block):
    count, pair, width = block.shape
    return block.reshape(count, pair, width // HD, HD).transpose(0, 2, 1, 3)


def take_apart(block, apart, begin, result, offset):
    count, heads = block.shape[:2]
    stride = 2 * heads
    flat = block.reshape(count * stride, HD)
    apart[begin * stride : (begin + count) * stride, :] = flat[...].astype(jnp.float32)
    for head in range(heads):
        for j in range(2):
            result[j, offset : offset + count, head * HD : (head + 1) * HD] = apart[
                pl.ds(begin * stride + 2 * head + j, count, stride=stride), :
            ].astype(jnp.bfloat16)


def part_kernel(*refs):
    *blocks, result, apart = refs
    offset = 0
    for block in blocks:
        take_apart(block, apart, offset, result, offset)
        offset += block.shape[0]


def part_keyval(blocks, name):
    count = sum(block.shape[0] for block in blocks)
    heads = blocks[0].shape[1]
    return pl.pallas_call(
        part_kernel,
        in_specs=[VMEM] * len(blocks),
        out_specs=VMEM,
        out_shape=jax.ShapeDtypeStruct((2, count, heads * HD), jnp.bfloat16),
        scratch_shapes=[pltpu.VMEM((2 * heads * count, HD), jnp.float32)],
        compiler_params=params(16),
        cost_estimate=cost(0, 8 * count * heads * HD),
        name=name,
    )(*blocks)


def query_kernel(*refs):
    *pieces, weight, cosine, sine, query, normed, near, arrived = refs
    count, _, wide = near.shape
    copies = [
        pltpu.make_async_copy(
            weight.at[:, pl.ds(i * wide, wide)], near.at[i], arrived.at[i]
        )
        for i in range(count)
    ]
    for copy in copies:
        copy.start()
    rows, columns = pieces[0].shape
    index = lax.axis_index("tp")
    features = columns * len(pieces)
    values = [piece[...].astype(jnp.float32) for piece in pieces]
    mean = sum(jnp.sum(v, axis=1, keepdims=True) for v in values) / features
    values = [v - mean for v in values]
    spread = sum(jnp.sum(v * v, axis=1, keepdims=True) for v in values) / features
    inverse = lax.rsqrt(spread + 1e-05)
    for shift, v in enumerate(values):
        normed[:, lanes((index ^ shift) * columns, columns)] = (v * inverse).astype(jnp.bfloat16)
    for i, copy in enumerate(copies):
        copy.wait()
        product = jnp.dot(normed[...], near[i], preferred_element_type=jnp.float32)
        for start in range(0, wide, HD):
            query[:, i * wide + start : i * wide + start + HD] = rotated(
                product[:, start : start + HD], cosine[...], sine[...]
            ).astype(jnp.bfloat16)


def project_query(pieces, w_query, cosine, sine):
    rows, columns = pieces[0].shape
    depth, width = w_query.shape
    wide = min(width, 2 * HD)
    return pl.pallas_call(
        query_kernel,
        in_specs=[VMEM] * len(pieces) + [HBM, VMEM, VMEM],
        out_specs=[VMEM] * 2,
        out_shape=[
            jax.ShapeDtypeStruct((rows, width), jnp.bfloat16),
            jax.ShapeDtypeStruct((rows, depth), jnp.bfloat16),
        ],
        scratch_shapes=[
            pltpu.VMEM((width // wide, depth, wide), jnp.bfloat16),
            pltpu.SemaphoreType.DMA((width // wide,)),
        ],
        compiler_params=params(60),
        cost_estimate=cost(2 * rows * depth * width, 2 * depth * width),
        name="project_query",
    )(*pieces, w_query, cosine, sine)


def keyval_kernel(
    normed, weight, cosine, sine, keys, values, cache, near, arrived, apart, total, woven
):
    parts, chunk, heads = near.shape[:3]
    rows = normed.shape[0]
    stride = 2 * heads
    copies = [
        pltpu.make_async_copy(weight.at[pl.ds(i * chunk, chunk)], near.at[i], arrived.at[i])
        for i in range(parts)
    ]
    for copy in copies:
        copy.start()
    for i, copy in enumerate(copies):
        copy.wait()
        flat = apart.at[i % 2]
        flat[...] = near.at[i].reshape(chunk * stride, HD)[...].astype(jnp.float32)
        for head in range(heads):
            both = [
                flat[pl.ds(2 * head + j, chunk, stride=stride), :].astype(jnp.bfloat16)
                for j in range(2)
            ]
            product = jnp.dot(
                normed[:, i * chunk : (i + 1) * chunk],
                jnp.concatenate(both, axis=1),
                preferred_element_type=jnp.float32,
            )
            span = slice(2 * head * HD, 2 * (head + 1) * HD)
            if i == 0:
                total[:, span] = product
            else:
                total[:, span] += product
    for head in range(heads):
        span = slice(head * HD, (head + 1) * HD)
        begin = 2 * head * HD
        key = rotated(total[:, begin : begin + HD], cosine[...], sine[...]).astype(jnp.bfloat16)
        value = total[:, begin + HD : begin + 2 * HD].astype(jnp.bfloat16)
        keys[:, span] = key
        values[:, span] = value
        woven[pl.ds(2 * head, rows, stride=stride), :] = key.astype(jnp.float32)
        woven[pl.ds(2 * head + 1, rows, stride=stride), :] = value.astype(jnp.float32)
    cache.reshape(rows * stride, HD)[...] = woven[...].astype(jnp.bfloat16)


def project_keyval(normed, w_keyval, cosine, sine):
    rows, depth = normed.shape
    weight = viewed(w_keyval)
    heads = weight.shape[1]
    width = heads * HD
    chunk = min(depth, 256)
    keys, values, cache = pl.pallas_call(
        keyval_kernel,
        in_specs=[VMEM, HBM, VMEM, VMEM],
        out_specs=[VMEM] * 3,
        out_shape=[
            jax.ShapeDtypeStruct((rows, width), jnp.bfloat16),
            jax.ShapeDtypeStruct((rows, width), jnp.bfloat16),
            jax.ShapeDtypeStruct((rows, heads, 2, HD), jnp.bfloat16),
        ],
        scratch_shapes=[
            pltpu.VMEM((depth // chunk, chunk, heads, 2, HD), jnp.bfloat16),
            pltpu.SemaphoreType.DMA((depth // chunk,)),
            pltpu.VMEM((2, 2 * heads * chunk, HD), jnp.float32),
            pltpu.VMEM((rows, 2 * width), jnp.float32),
            pltpu.VMEM((2 * heads * rows, HD), jnp.float32),
        ],
        compiler_params=params(57),
        cost_estimate=cost(4 * rows * depth * width, 4 * depth * width),
        name="project_keyval",
    )(normed, weight, cosine, sine)
    return keys, values, cache.transpose(0, 2, 1, 3).reshape(rows, 2, width)


def column_of(stats, lane):
    place = lax.broadcasted_iota(jnp.int32, stats.shape, 1)
    return jnp.sum(jnp.where(place == lane, stats, 0.0), axis=1, keepdims=True)


def with_column(stats, lane, column):
    place = lax.broadcasted_iota(jnp.int32, stats.shape, 1)
    return jnp.where(place == lane, column, stats)


def attend_kernel(spec, *refs):
    group, shifts, rings, slots, piece, fresh, first, last = spec
    refs = list(refs)
    take = lambda count: [refs.pop(0) for _ in range(count)]
    lengths, shared, table = take(3)
    queries = take(len(shifts))
    if fresh:
        block, fresh_keys, fresh_values = take(3)
    else:
        raw = take(len(rings))
    if not first:
        old_mixes, old_stats = take(len(shifts)), take(len(shifts))
    if last:
        results = take(len(shifts))
        mine_stats = take(1) if 0 in shifts else []
    else:
        results, new_stats = take(len(shifts)), take(len(shifts))
    bias, stats = take(2)
    if fresh:
        causal = take(1)[0]
    else:
        block, apart = take(2)
    rows, width = queries[0].shape
    heads = width // HD
    cycle = cycle_of(group)
    seq = lax.axis_index("seq")
    request, member = seq // group, seq % group
    place = pick(list(np.argsort(cycle)), request)
    edges = []
    count = 0
    block_size = 128
    for i in range(slots):
        wanted = seq * slots + i
        number = jnp.int32(0)
        for j in range(table.shape[1]):
            number = jnp.where(table[request, j] == wanted, jnp.int32(j), number)
        edges.append((count, block_size, number * block_size, lengths[request]))
        count += block_size
    for step, begin, size in rings:
        origin = pick(cycle, lax.rem(place + step + REQ, REQ))
        edges.append((count, size, (origin * group + member) * piece + begin, shared[0]))
        count += size
    for begin, size, start, length in edges:
        positions = start + lax.broadcasted_iota(jnp.int32, (size, HD), 0)
        lane = lax.broadcasted_iota(jnp.int32, (size, HD), 1)
        bias[begin : begin + size, :] = jnp.where(
            (positions >= length) & (lane == 0), NEGATIVE, 0.0
        ).astype(jnp.bfloat16)
    if fresh:
        bias[count : count + rows, :] = jnp.zeros((rows, HD), jnp.bfloat16)
        theirs = member * rows + lax.broadcasted_iota(jnp.int32, (rows, rows), 1)
        for i, shift in enumerate(shifts):
            mine = (member ^ shift) * rows + lax.broadcasted_iota(jnp.int32, (rows, rows), 0)
            causal[i * rows : (i + 1) * rows, :] = jnp.where(theirs <= mine, 0.0, NEGATIVE)
    else:
        offset = 0
        for piece_ref in raw:
            take_apart(piece_ref, apart, offset, block, offset)
            offset += piece_ref.shape[0]
    stats[...] = jnp.zeros_like(stats)
    unit = jnp.where(
        lax.broadcasted_iota(jnp.int32, (len(shifts) * rows, HD), 1) == 0, 1.0, 0.0
    ).astype(jnp.bfloat16)
    across = (((1,), (1,)), ((), ()))

    def stacked(values):
        return values[0] if len(values) == 1 else jnp.concatenate(values, axis=0)

    def one_head(head):
        span = lanes(head * HD)
        query = stacked([q[:, span] for q in queries])
        keys = [block[0, :, span]]
        values = [block[1, :, span]]
        if fresh:
            keys.append(fresh_keys[:, span])
            values.append(fresh_values[:, span])
        keys, values = stacked(keys), stacked(values)
        scores = lax.dot_general(
            jnp.concatenate([query, unit], axis=1),
            jnp.concatenate([keys, bias[...]], axis=1),
            across,
            preferred_element_type=jnp.float32,
        )
        if fresh:
            scores = jnp.concatenate([scores[:, :count], scores[:, count:] + causal[...]], axis=1)
        top = jnp.max(scores, axis=1, keepdims=True)
        if not first:
            old = stacked([column_of(s[...], head) for s in old_stats])
            top = jnp.maximum(top, old * (1.0 / SCALE))
        weights = jnp.exp2((scores - top) * SCALE).astype(jnp.bfloat16)
        mixed = jnp.dot(
            weights,
            jnp.concatenate([values, jnp.ones_like(values)], axis=1),
            preferred_element_type=jnp.float32,
        )
        total, summed = mixed[:, :HD], mixed[:, HD:]
        if not first:
            factor = jnp.exp2(old - top * SCALE)
            total = total + stacked([mix[:, span] for mix in old_mixes]) * factor
            summed = summed + factor
        even = total / summed
        stats[...] = with_column(stats[...], head, top * SCALE + jnp.log2(summed))
        for i, result in enumerate(results):
            result[:rows, span] = even[i * rows : (i + 1) * rows].astype(result.dtype)

    together = min(2, heads)

    def some_heads(i, _):
        for j in range(together):
            one_head(together * i + j)
        return 0

    lax.fori_loop(0, heads // together, some_heads, 0)
    for i, shift in enumerate(shifts):
        own_rows = stats[i * rows : (i + 1) * rows, :]
        if not last:
            new_stats[i][...] = own_rows
        elif shift == 0:
            mine_stats[0][...] = own_rows
        else:
            line = jnp.transpose(own_rows)[:heads, :]
            packed = []
            for _ in range(3):
                rounded = line.astype(jnp.bfloat16).astype(jnp.float32)
                packed.append(rounded)
                line = line - rounded
            gap = -3 * heads % STAT_ROWS
            if gap:
                packed.append(jnp.zeros((gap, rows), jnp.float32))
            packed = jnp.concatenate(packed, axis=0).astype(jnp.bfloat16)
            for j in range(packed.shape[0] // STAT_ROWS):
                results[i][rows:, j * rows : (j + 1) * rows] = packed[
                    j * STAT_ROWS : (j + 1) * STAT_ROWS
                ]


def attend(facts, queries, shifts, rings, slots, piece, blocks, old, last, name):
    group = len(queries)
    queries = [queries[shift] for shift in shifts]
    rows, width = queries[0].shape
    heads = width // HD
    fresh = blocks[0].ndim == 3
    operands = [*facts, *queries, *blocks]
    if old:
        operands += [old[shift][0] for shift in shifts] + [old[shift][1] for shift in shifts]
    plain = blocks[0].shape[1] if fresh else sum(block.shape[0] for block in blocks)
    count = plain + (rows if fresh else 0)
    many = len(shifts) * rows
    scratch = [pltpu.VMEM((count, HD), jnp.bfloat16), pltpu.VMEM((many, HD), jnp.float32)]
    if fresh:
        scratch.append(pltpu.VMEM((many, rows), jnp.float32))
    else:
        scratch.append(pltpu.VMEM((2, count, width), jnp.bfloat16))
        scratch.append(pltpu.VMEM((2 * heads * count, HD), jnp.float32))
    state = jax.ShapeDtypeStruct((rows, width), jnp.float32)
    state_stats = jax.ShapeDtypeStruct((rows, HD), jnp.float32)
    sent = jax.ShapeDtypeStruct((rows + STAT_ROWS, width), jnp.bfloat16)
    if last:
        out_shape = [sent if shift else state for shift in shifts]
        out_shape += [state_stats] * (0 in shifts)
    else:
        out_shape = [state] * len(shifts) + [state_stats] * len(shifts)
    scores = many * count * heads
    results = pl.pallas_call(
        functools.partial(
            attend_kernel, (group, shifts, rings, slots, piece, fresh, not old, last)
        ),
        in_specs=[SMEM] * 3 + [VMEM] * (len(operands) - 3),
        out_specs=[VMEM] * len(out_shape),
        out_shape=out_shape,
        scratch_shapes=scratch,
        compiler_params=params(28),
        cost_estimate=cost(4 * scores * HD, 4 * count * width, scores),
        name=name,
    )(*operands)
    if last:
        return results
    return {
        shift: (results[i], results[len(shifts) + i]) for i, shift in enumerate(shifts)
    }


def combine_kernel(*refs):
    result, stats, *refs = refs
    *parts, weight, attended, sent = refs[: len(refs)]
    rows, width = result.shape
    heads = width // HD
    extents = [stats[...]]
    for part in parts:
        tile = part[rows:, :].astype(jnp.float32)
        groups = -(-3 * heads // STAT_ROWS)
        lines = jnp.concatenate(
            [tile[:, j * rows : (j + 1) * rows] for j in range(groups)], axis=0
        )
        line = sum(lines[i * heads : (i + 1) * heads] for i in range(3))
        line = jnp.concatenate([line, jnp.zeros((HD - heads, rows), jnp.float32)], axis=0)
        extents.append(jnp.transpose(line))
    top = functools.reduce(jnp.maximum, extents)
    shares = [jnp.exp2(extent - top) for extent in extents]
    whole = sum(shares)
    shares = [share / whole for share in shares]
    for head in range(heads):
        span = slice(head * HD, (head + 1) * HD)
        mixes = [result[:, span]] + [part[:rows, span].astype(jnp.float32) for part in parts]
        mixed = sum(mix * share[:, head : head + 1] for mix, share in zip(mixes, shares))
        attended[:, span] = mixed.astype(jnp.bfloat16)
    index = lax.axis_index("tp")
    ways = sent.shape[0] + 1
    columns = weight.shape[1] // ways
    for shift in range(1, ways):
        sent[shift - 1] = jnp.dot(
            attended[...],
            weight[:, lanes((index ^ shift) * columns, columns)],
            preferred_element_type=jnp.float32,
        ).astype(jnp.bfloat16)


def combine(result, stats, parts, w_out, ways):
    rows, width = result.shape
    columns = w_out.shape[1] // ways
    return pl.pallas_call(
        combine_kernel,
        in_specs=[VMEM] * (3 + len(parts)),
        out_specs=[VMEM] * 2,
        out_shape=[
            jax.ShapeDtypeStruct((rows, width), jnp.bfloat16),
            jax.ShapeDtypeStruct((ways - 1, rows, columns), jnp.bfloat16),
        ],
        compiler_params=params(20),
        cost_estimate=cost(2 * rows * width * columns * (ways - 1), 2 * width * w_out.shape[1]),
        name="combine_send",
    )(result, stats, *parts, w_out)


def keep_kernel(attended, weight, hidden, kept):
    columns = hidden.shape[1]
    product = jnp.dot(
        attended[...],
        weight[:, lanes(lax.axis_index("tp") * columns, columns)],
        preferred_element_type=jnp.float32,
    )
    kept[...] = product + hidden[...].astype(jnp.float32)


def keep(attended, w_out, hidden):
    rows, width = attended.shape
    return pl.pallas_call(
        keep_kernel,
        in_specs=[VMEM] * 3,
        out_specs=VMEM,
        out_shape=jax.ShapeDtypeStruct(hidden.shape, jnp.float32),
        compiler_params=params(20),
        cost_estimate=cost(2 * rows * width * hidden.shape[1], 2 * width * w_out.shape[1]),
        name="keep_own",
    )(attended, w_out, hidden)


def local(
    hidden_in, w_query, w_keyval, w_out, prompt_cache, tail_cache, tail_table, tail_len, shared_len
):
    rows = hidden_in.shape[0]
    group = lax.axis_size("seq") // REQ
    ways = lax.axis_size("tp")
    cycle = cycle_of(group)
    seq = lax.axis_index("seq")
    request = seq // group
    member = seq % group
    half = REQ // 2
    piece = prompt_cache.shape[0]
    middle = piece // 2

    pieces = [hidden_in] + [swap(hidden_in, "tp", shift) for shift in range(1, ways)]
    prompt = viewed(prompt_cache)
    ahead, behind = [prompt], [prompt]

    def step(*others):
        for blocks, way in ((ahead, 1), (behind, -1)):
            blocks.append(turn(after(blocks[-1], *others), cycle, group, way))

    step()
    own_length = lax.dynamic_index_in_dim(tail_len, request, 0, keepdims=False)
    positions = shared_len[0] + own_length + member * rows + jnp.arange(rows, dtype=jnp.int32)
    cosine, sine = angles(positions)
    query, normed = project_query(pieces, w_query, cosine, sine)
    queries = [query] + [swap(query, "seq", shift) for shift in range(1, group)]
    fresh_keys, fresh_values, new_cache = project_keyval(normed, w_keyval, cosine, sine)
    step(fresh_keys)
    tail = viewed(tail_cache.reshape(-1, 2, tail_cache.shape[3]))
    slots = tail_cache.shape[0]
    near_block = part_keyval([tail, prompt, ahead[1], behind[1]], "part_near")

    facts = (tail_len, shared_len, tail_table)
    others = list(range(1, group))
    near = (
        [(0, 0, piece), (-1, 0, piece), (1, 0, piece)],
        slots,
        piece,
        [near_block, fresh_keys, fresh_values],
        None,
        False,
    )
    state = attend(facts, queries, [0], *near, "attend_near_own")
    ready = after(queries[1], state[0][1])
    state |= attend(facts, [query, ready, *queries[2:]], others, *near, "attend_near_others")
    step(state[1][1])
    rings = [(-2, 0, piece), (2, 0, piece)]
    state = attend(
        facts, queries, [0, *others], rings, 0, piece, [ahead[2], behind[2]], state, False, "attend_mid"
    )
    far_low = turn(after(ahead[3], state[1][1])[:middle], cycle, group, 1)
    far_high = turn(after(behind[3], state[1][1])[middle:], cycle, group, -1)
    rings = [(-3, 0, piece), (3, 0, piece), (-half, 0, middle), (half, middle, piece - middle)]
    far_blocks = [ahead[3], behind[3], far_low, far_high]
    far = (rings, 0, piece, far_blocks, state, True)
    parts = attend(facts, queries, others, *far, "attend_far_others")
    ready = after(query, parts[0])
    result, stats = attend(facts, [ready, *queries[1:]], [0], *far, "attend_far_own")
    parts = [swap(part, "seq", shift + 1) for shift, part in enumerate(parts)]
    attended, sent = combine(result, stats, parts, w_out, ways)
    received = [swap(sent[shift - 1], "tp", shift) for shift in range(1, ways)]
    total = keep(attended, w_out, hidden_in)
    for part in received:
        total = total + part.astype(jnp.float32)
    return (total.astype(jnp.bfloat16), new_cache)


def solution(mesh):
    return jax.shard_map(
        local,
        mesh=mesh,
        in_specs=(
            P("seq", "tp"),
            P(None, "tp"),
            P(None, None, "tp"),
            P("tp", None),
            P("seq", None, "tp"),
            P("seq", None, None, "tp"),
            P(),
            P(),
            P(),
        ),
        out_specs=(P("seq", "tp"), P("seq", None, "tp")),
        check_vma=False,
    )
```

```python
import functools

import jax
import jax.numpy as jnp
import numpy as np
from jax import lax
from jax.experimental import pallas as pl
from jax.experimental.pallas import tpu as pltpu
from jax.sharding import PartitionSpec as P

HD = 128
REQ = 8
BLK = 128
NEGATIVE = -1e30
SCALE = float(HD**-0.5 * np.log2(np.e))
STAT_ROWS = 16


def params(mib=24):
    return pltpu.CompilerParams(vmem_limit_bytes=mib * 2**20)


def cost(flops, moved, exps=0):
    return pl.CostEstimate(flops=int(flops), bytes_accessed=int(moved), transcendentals=int(exps))


def cycle_of(group):
    if group == 2:
        return [0, 2, 4, 6, 7, 5, 3, 1]
    return list(range(REQ))


def pick(table, index):
    result = jnp.int32(table[0])
    for place, value in enumerate(table):
        result = jnp.where(index == place, jnp.int32(value), result)
    return result


def swap(value, axis, mask):
    pairs = [(source, source ^ mask) for source in range(lax.axis_size(axis))]
    return lax.ppermute(value, axis, pairs)


def turn(value, cycle, group, way):
    count = len(cycle)
    pairs = []
    for place in range(count):
        source, target = cycle[place], cycle[(place + way) % count]
        pairs += [(source * group + m, target * group + m) for m in range(group)]
    return lax.ppermute(value, "seq", pairs)


def rotated(vectors, cosine, sine):
    return vectors * cosine + pltpu.roll(vectors, HD // 2, 1) * sine


def angles(positions):
    half = HD // 2
    freqs = 10000.0 ** (-jnp.arange(half, dtype=jnp.float32) / half)
    angle = positions.astype(jnp.float32)[:, None] * freqs
    cosine, sine = jnp.cos(angle), jnp.sin(angle)
    return (
        jnp.concatenate([cosine, cosine], axis=1),
        jnp.concatenate([-sine, sine], axis=1),
    )


def lanes(start, count=HD):
    return pl.ds(pl.multiple_of(start, HD), count)


def after(value, *others):
    return lax.optimization_barrier((value, *others))[0]


VMEM = pl.BlockSpec(memory_space=pltpu.VMEM)
HBM = pl.BlockSpec(memory_space=pltpu.HBM)
SMEM = pl.BlockSpec(memory_space=pltpu.SMEM)


def viewed(block):
    count, pair, width = block.shape
    return block.reshape(count, pair, width // HD, HD).transpose(0, 2, 1, 3)


def order_rows(stride, back):
    rows = 2 * HD
    places = rows // stride
    row = lax.broadcasted_iota(jnp.int32, (rows, rows), 1 if back else 0)
    column = lax.broadcasted_iota(jnp.int32, (rows, rows), 0 if back else 1)
    source = lax.rem(row, places) * stride + lax.div(row, places)
    return jnp.where(column == source, 1.0, 0.0).astype(jnp.bfloat16)


def reordered(order, tiles):
    both = tiles[0] if len(tiles) == 1 else jnp.concatenate(tiles, axis=1)
    mixed = jnp.dot(order, both, preferred_element_type=jnp.float32).astype(jnp.bfloat16)
    return [mixed[:, i * HD : (i + 1) * HD] for i in range(len(tiles))]


def take_apart(block, order, result, offset):
    count, heads = block.shape[:2]
    stride = 2 * heads
    places = 2 * HD // stride
    flat = block.reshape(count * stride, HD)
    for start in range(0, count, 2 * places):
        starts = [at for at in (start, start + places) if at < count]
        tiles = [flat[at * stride : (at + places) * stride, :] for at in starts]
        for at, tile in zip(starts, reordered(order, tiles)):
            for head in range(heads):
                for j in range(2):
                    line = (2 * head + j) * places
                    result[
                        j, offset + at : offset + at + places, head * HD : (head + 1) * HD
                    ] = tile[line : line + places]


def part_kernel(*refs):
    *blocks, result = refs
    order = order_rows(2 * blocks[0].shape[1], False)
    offset = 0
    for block in blocks:
        take_apart(block, order, result, offset)
        offset += block.shape[0]


def part_keyval(blocks, name):
    count = sum(block.shape[0] for block in blocks)
    heads = blocks[0].shape[1]
    return pl.pallas_call(
        part_kernel,
        in_specs=[VMEM] * len(blocks),
        out_specs=VMEM,
        out_shape=jax.ShapeDtypeStruct((2, count, heads * HD), jnp.bfloat16),
        compiler_params=params(16),
        cost_estimate=cost(0, 8 * count * heads * HD),
        name=name,
    )(*blocks)


def query_kernel(*refs):
    *pieces, weight, cosine, sine, query, normed, near, total, arrived = refs
    count, depth, width = near.shape
    copies = [
        pltpu.make_async_copy(weight.at[pl.ds(i * depth, depth)], near.at[i], arrived.at[i])
        for i in range(count)
    ]
    for copy in copies:
        copy.start()
    rows, columns = pieces[0].shape
    index = lax.axis_index("tp")
    features = columns * len(pieces)
    values = [piece[...].astype(jnp.float32) for piece in pieces]
    mean = sum(jnp.sum(v, axis=1, keepdims=True) for v in values) / features
    values = [v - mean for v in values]
    spread = sum(jnp.sum(v * v, axis=1, keepdims=True) for v in values) / features
    inverse = lax.rsqrt(spread + 1e-05)
    for shift, v in enumerate(values):
        normed[:, lanes((index ^ shift) * columns, columns)] = (v * inverse).astype(jnp.bfloat16)
    wide = min(width, 2 * HD)
    for i, copy in enumerate(copies):
        copy.wait()
        for base in range(0, width, wide):
            span = slice(base, base + wide)
            product = jnp.dot(
                normed[:, i * depth : (i + 1) * depth],
                near[i, :, span],
                preferred_element_type=jnp.float32,
            )
            if i:
                product += total[:, span]
            if i < count - 1:
                total[:, span] = product
                continue
            for start in range(0, wide, HD):
                query[:, base + start : base + start + HD] = rotated(
                    product[:, start : start + HD], cosine[...], sine[...]
                ).astype(jnp.bfloat16)


def project_query(pieces, w_query, cosine, sine):
    rows, columns = pieces[0].shape
    depth, width = w_query.shape
    return pl.pallas_call(
        query_kernel,
        in_specs=[VMEM] * len(pieces) + [HBM, VMEM, VMEM],
        out_specs=[VMEM] * 2,
        out_shape=[
            jax.ShapeDtypeStruct((rows, width), jnp.bfloat16),
            jax.ShapeDtypeStruct((rows, depth), jnp.bfloat16),
        ],
        scratch_shapes=[
            pltpu.VMEM((2, depth // 2, width), jnp.bfloat16),
            pltpu.VMEM((rows, width), jnp.float32),
            pltpu.SemaphoreType.DMA((2,)),
        ],
        compiler_params=params(60),
        cost_estimate=cost(2 * rows * depth * width, 2 * depth * width),
        name="project_query",
    )(*pieces, w_query, cosine, sine)


def keyval_kernel(
    normed, weight, cosine, sine, keys, values, cache, near, arrived, apart, total
):
    parts, chunk, heads = near.shape[:3]
    rows = normed.shape[0]
    stride = 2 * heads
    copies = [
        pltpu.make_async_copy(weight.at[pl.ds(i * chunk, chunk)], near.at[i], arrived.at[i])
        for i in range(parts)
    ]
    for copy in copies:
        copy.start()
    order = order_rows(stride, False)
    for i, copy in enumerate(copies):
        copy.wait()
        here = apart.at[i % 2]
        take_apart(near.at[i], order, here, 0)
        for head in range(heads):
            span = slice(head * HD, (head + 1) * HD)
            product = jnp.dot(
                normed[:, i * chunk : (i + 1) * chunk],
                jnp.concatenate([here[0, :, span], here[1, :, span]], axis=1),
                preferred_element_type=jnp.float32,
            )
            span = slice(2 * head * HD, 2 * (head + 1) * HD)
            if i == 0:
                total[:, span] = product
            else:
                total[:, span] += product
    for head in range(heads):
        span = slice(head * HD, (head + 1) * HD)
        begin = 2 * head * HD
        key = rotated(total[:, begin : begin + HD], cosine[...], sine[...]).astype(jnp.bfloat16)
        value = total[:, begin + HD : begin + 2 * HD].astype(jnp.bfloat16)
        keys[:, span] = key
        values[:, span] = value
    order = order_rows(stride, True)
    places = 2 * HD // stride
    flat = cache.reshape(rows * stride, HD)
    for start in range(0, rows, 2 * places):
        starts = [at for at in (start, start + places) if at < rows]
        tiles = [
            jnp.concatenate(
                [
                    pair[at : at + places, head * HD : (head + 1) * HD]
                    for head in range(heads)
                    for pair in (keys, values)
                ],
                axis=0,
            )
            for at in starts
        ]
        for at, tile in zip(starts, reordered(order, tiles)):
            flat[at * stride : (at + places) * stride, :] = tile


def project_keyval(normed, w_keyval, cosine, sine):
    rows, depth = normed.shape
    weight = viewed(w_keyval)
    heads = weight.shape[1]
    width = heads * HD
    chunk = min(depth, 512)
    keys, values, cache = pl.pallas_call(
        keyval_kernel,
        in_specs=[VMEM, HBM, VMEM, VMEM],
        out_specs=[VMEM] * 3,
        out_shape=[
            jax.ShapeDtypeStruct((rows, width), jnp.bfloat16),
            jax.ShapeDtypeStruct((rows, width), jnp.bfloat16),
            jax.ShapeDtypeStruct((rows, heads, 2, HD), jnp.bfloat16),
        ],
        scratch_shapes=[
            pltpu.VMEM((depth // chunk, chunk, heads, 2, HD), jnp.bfloat16),
            pltpu.SemaphoreType.DMA((depth // chunk,)),
            pltpu.VMEM((2, 2, chunk, width), jnp.bfloat16),
            pltpu.VMEM((rows, 2 * width), jnp.float32),
        ],
        compiler_params=params(57),
        cost_estimate=cost(4 * rows * depth * width, 4 * depth * width),
        name="project_keyval",
    )(normed, weight, cosine, sine)
    return keys, values, cache.transpose(0, 2, 1, 3).reshape(rows, 2, width)


def column_of(stats, lane):
    place = lax.broadcasted_iota(jnp.int32, stats.shape, 1)
    return jnp.sum(jnp.where(place == lane, stats, 0.0), axis=1, keepdims=True)


def with_column(stats, lane, column):
    place = lax.broadcasted_iota(jnp.int32, stats.shape, 1)
    return jnp.where(place == lane, column, stats)


def attend_kernel(spec, *refs):
    group, shifts, rings, slots, piece, fresh, first, last = spec
    refs = list(refs)
    take = lambda count: [refs.pop(0) for _ in range(count)]
    lengths, shared, table = take(3)
    queries = take(len(shifts))
    if fresh:
        *parted, fresh_keys, fresh_values = take(fresh)
    else:
        raw = take(len(rings))
    if not first:
        old_mixes, old_stats = take(len(shifts)), take(len(shifts))
    if last:
        results = take(len(shifts))
        mine_stats = take(1) if 0 in shifts else []
    else:
        results, new_stats = take(len(shifts)), take(len(shifts))
    bias, stats = take(2)
    if fresh:
        causal = take(1)[0]
    else:
        parted = take(1)
    rows, width = queries[0].shape
    heads = width // HD
    cycle = cycle_of(group)
    seq = lax.axis_index("seq")
    request, member = seq // group, seq % group
    place = pick(list(np.argsort(cycle)), request)
    edges = []
    count = 0
    block_size = BLK
    for i in range(slots):
        wanted = seq * slots + i
        number = jnp.int32(0)
        for j in range(table.shape[1]):
            number = jnp.where(table[request, j] == wanted, jnp.int32(j), number)
        edges.append((count, block_size, number * block_size, lengths[request]))
        count += block_size
    for step, begin, size in rings:
        origin = pick(cycle, lax.rem(place + step + REQ, REQ))
        edges.append((count, size, (origin * group + member) * piece + begin, shared[0]))
        count += size
    for begin, size, start, length in edges:
        positions = start + lax.broadcasted_iota(jnp.int32, (size, HD), 0)
        lane = lax.broadcasted_iota(jnp.int32, (size, HD), 1)
        bias[begin : begin + size, :] = jnp.where(
            (positions >= length) & (lane == 0), NEGATIVE, 0.0
        ).astype(jnp.bfloat16)
    if fresh:
        bias[count : count + rows, :] = jnp.zeros((rows, HD), jnp.bfloat16)
        theirs = member * rows + lax.broadcasted_iota(jnp.int32, (rows, rows), 1)
        for i, shift in enumerate(shifts):
            mine = (member ^ shift) * rows + lax.broadcasted_iota(jnp.int32, (rows, rows), 0)
            causal[i * rows : (i + 1) * rows, :] = jnp.where(theirs <= mine, 0.0, NEGATIVE)
    else:
        offset = 0
        order = order_rows(2 * heads, False)
        for piece_ref in raw:
            take_apart(piece_ref, order, parted[0], offset)
            offset += piece_ref.shape[0]
    stats[...] = jnp.zeros_like(stats)
    unit = jnp.where(
        lax.broadcasted_iota(jnp.int32, (len(shifts) * rows, HD), 1) == 0, 1.0, 0.0
    ).astype(jnp.bfloat16)
    across = (((1,), (1,)), ((), ()))

    def stacked(values):
        return values[0] if len(values) == 1 else jnp.concatenate(values, axis=0)

    def one_head(head):
        span = lanes(head * HD)
        query = stacked([q[:, span] for q in queries])
        keys = [block[0, :, span] for block in parted]
        values = [block[1, :, span] for block in parted]
        if fresh:
            keys.append(fresh_keys[:, span])
            values.append(fresh_values[:, span])
        keys, values = stacked(keys), stacked(values)
        scores = lax.dot_general(
            jnp.concatenate([query, unit], axis=1),
            jnp.concatenate([keys, bias[...]], axis=1),
            across,
            preferred_element_type=jnp.float32,
        )
        if fresh:
            scores = jnp.concatenate([scores[:, :count], scores[:, count:] + causal[...]], axis=1)
        top = jnp.max(scores, axis=1, keepdims=True)
        if not first:
            old = stacked([column_of(s[...], head) for s in old_stats])
            top = jnp.maximum(top, old * (1.0 / SCALE))
        weights = jnp.exp2((scores - top) * SCALE).astype(jnp.bfloat16)
        mixed = jnp.dot(
            weights,
            jnp.concatenate([values, jnp.ones_like(values)], axis=1),
            preferred_element_type=jnp.float32,
        )
        total, summed = mixed[:, :HD], mixed[:, HD:]
        if not first:
            factor = jnp.exp2(old - top * SCALE)
            total = total + stacked([mix[:, span] for mix in old_mixes]) * factor
            summed = summed + factor
        even = total / summed
        stats[...] = with_column(stats[...], head, top * SCALE + jnp.log2(summed))
        for i, result in enumerate(results):
            result[:rows, span] = even[i * rows : (i + 1) * rows].astype(result.dtype)

    together = min(2, heads)

    def some_heads(i, _):
        for j in range(together):
            one_head(together * i + j)
        return 0

    lax.fori_loop(0, heads // together, some_heads, 0)
    for i, shift in enumerate(shifts):
        own_rows = stats[i * rows : (i + 1) * rows, :]
        if not last:
            new_stats[i][...] = own_rows
        elif shift == 0:
            mine_stats[0][...] = own_rows
        else:
            line = jnp.transpose(own_rows)[:heads, :]
            packed = []
            for _ in range(3):
                rounded = line.astype(jnp.bfloat16).astype(jnp.float32)
                packed.append(rounded)
                line = line - rounded
            gap = -3 * heads % STAT_ROWS
            if gap:
                packed.append(jnp.zeros((gap, rows), jnp.float32))
            packed = jnp.concatenate(packed, axis=0).astype(jnp.bfloat16)
            for j in range(packed.shape[0] // STAT_ROWS):
                results[i][rows:, j * rows : (j + 1) * rows] = packed[
                    j * STAT_ROWS : (j + 1) * STAT_ROWS
                ]


def attend(facts, queries, shifts, rings, slots, piece, blocks, old, last, name):
    group = len(queries)
    queries = [queries[shift] for shift in shifts]
    rows, width = queries[0].shape
    heads = width // HD
    fresh = len(blocks) if blocks[0].ndim == 3 else 0
    operands = [*facts, *queries, *blocks]
    if old:
        operands += [old[shift][0] for shift in shifts] + [old[shift][1] for shift in shifts]
    plain = sum(size for _, _, size in rings) + BLK * slots
    count = plain + (rows if fresh else 0)
    many = len(shifts) * rows
    scratch = [pltpu.VMEM((count, HD), jnp.bfloat16), pltpu.VMEM((many, HD), jnp.float32)]
    if fresh:
        scratch.append(pltpu.VMEM((many, rows), jnp.float32))
    else:
        scratch.append(pltpu.VMEM((2, count, width), jnp.bfloat16))
    state = jax.ShapeDtypeStruct((rows, width), jnp.float32)
    state_stats = jax.ShapeDtypeStruct((rows, HD), jnp.float32)
    sent = jax.ShapeDtypeStruct((rows + STAT_ROWS, width), jnp.bfloat16)
    if last:
        out_shape = [sent if shift else state for shift in shifts]
        out_shape += [state_stats] * (0 in shifts)
    else:
        out_shape = [state] * len(shifts) + [state_stats] * len(shifts)
    scores = many * count * heads
    results = pl.pallas_call(
        functools.partial(
            attend_kernel, (group, shifts, rings, slots, piece, fresh, not old, last)
        ),
        in_specs=[SMEM] * 3 + [VMEM] * (len(operands) - 3),
        out_specs=[VMEM] * len(out_shape),
        out_shape=out_shape,
        scratch_shapes=scratch,
        compiler_params=params(28),
        cost_estimate=cost(4 * scores * HD, 4 * count * width, scores),
        name=name,
    )(*operands)
    if last:
        return results
    return {
        shift: (results[i], results[len(shifts) + i]) for i, shift in enumerate(shifts)
    }


def combine_kernel(*refs):
    result, stats, *refs = refs
    *parts, weight, attended, sent = refs[: len(refs)]
    rows, width = result.shape
    heads = width // HD
    extents = [stats[...]]
    for part in parts:
        tile = part[rows:, :].astype(jnp.float32)
        groups = -(-3 * heads // STAT_ROWS)
        lines = jnp.concatenate(
            [tile[:, j * rows : (j + 1) * rows] for j in range(groups)], axis=0
        )
        line = sum(lines[i * heads : (i + 1) * heads] for i in range(3))
        line = jnp.concatenate([line, jnp.zeros((HD - heads, rows), jnp.float32)], axis=0)
        extents.append(jnp.transpose(line))
    top = functools.reduce(jnp.maximum, extents)
    shares = [jnp.exp2(extent - top) for extent in extents]
    whole = sum(shares)
    shares = [share / whole for share in shares]
    for head in range(heads):
        span = slice(head * HD, (head + 1) * HD)
        mixes = [result[:, span]] + [part[:rows, span].astype(jnp.float32) for part in parts]
        mixed = sum(mix * share[:, head : head + 1] for mix, share in zip(mixes, shares))
        attended[:, span] = mixed.astype(jnp.bfloat16)
    index = lax.axis_index("tp")
    ways = sent.shape[0] + 1
    columns = weight.shape[1] // ways
    for shift in range(1, ways):
        sent[shift - 1] = jnp.dot(
            attended[...],
            weight[:, lanes((index ^ shift) * columns, columns)],
            preferred_element_type=jnp.float32,
        ).astype(jnp.bfloat16)


def combine(result, stats, parts, w_out, ways):
    rows, width = result.shape
    columns = w_out.shape[1] // ways
    return pl.pallas_call(
        combine_kernel,
        in_specs=[VMEM] * (3 + len(parts)),
        out_specs=[VMEM] * 2,
        out_shape=[
            jax.ShapeDtypeStruct((rows, width), jnp.bfloat16),
            jax.ShapeDtypeStruct((ways - 1, rows, columns), jnp.bfloat16),
        ],
        compiler_params=params(20),
        cost_estimate=cost(2 * rows * width * columns * (ways - 1), 2 * width * w_out.shape[1]),
        name="combine_send",
    )(result, stats, *parts, w_out)


def keep_kernel(attended, weight, hidden, kept):
    columns = hidden.shape[1]
    product = jnp.dot(
        attended[...],
        weight[:, lanes(lax.axis_index("tp") * columns, columns)],
        preferred_element_type=jnp.float32,
    )
    kept[...] = product + hidden[...].astype(jnp.float32)


def keep(attended, w_out, hidden):
    rows, width = attended.shape
    return pl.pallas_call(
        keep_kernel,
        in_specs=[VMEM] * 3,
        out_specs=VMEM,
        out_shape=jax.ShapeDtypeStruct(hidden.shape, jnp.float32),
        compiler_params=params(20),
        cost_estimate=cost(2 * rows * width * hidden.shape[1], 2 * width * w_out.shape[1]),
        name="keep_own",
    )(attended, w_out, hidden)


def local(
    hidden_in, w_query, w_keyval, w_out, prompt_cache, tail_cache, tail_table, tail_len, shared_len
):
    rows = hidden_in.shape[0]
    group = lax.axis_size("seq") // REQ
    ways = lax.axis_size("tp")
    cycle = cycle_of(group)
    seq = lax.axis_index("seq")
    request = seq // group
    member = seq % group
    half = REQ // 2
    piece = prompt_cache.shape[0]
    middle = piece // 2

    pieces = [hidden_in] + [swap(hidden_in, "tp", shift) for shift in range(1, ways)]
    prompt = viewed(prompt_cache)
    ahead, behind = [prompt], [prompt]

    def step(*others):
        for blocks, way in ((ahead, 1), (behind, -1)):
            blocks.append(turn(after(blocks[-1], *others), cycle, group, way))

    step()
    own_length = lax.dynamic_index_in_dim(tail_len, request, 0, keepdims=False)
    positions = shared_len[0] + own_length + member * rows + jnp.arange(rows, dtype=jnp.int32)
    cosine, sine = angles(positions)
    query, normed = project_query(pieces, w_query, cosine, sine)
    queries = [query] + [swap(query, "seq", shift) for shift in range(1, group)]
    tail = viewed(tail_cache.reshape(-1, 2, tail_cache.shape[3]))
    slots = tail_cache.shape[0]
    own_block = part_keyval([after(tail, query), prompt], "part_own")
    step(own_block)
    ready = after(normed, ahead[1], behind[1])
    fresh_keys, fresh_values, new_cache = project_keyval(ready, w_keyval, cosine, sine)
    near_block = part_keyval([ahead[1], behind[1]], "part_near")

    facts = (tail_len, shared_len, tail_table)
    others = list(range(1, group))
    near = (
        [(0, 0, piece), (-1, 0, piece), (1, 0, piece)],
        slots,
        piece,
        [own_block, near_block, fresh_keys, fresh_values],
        None,
        False,
    )
    state = attend(facts, queries, [0], *near, "attend_near_own")
    ready = after(queries[1], state[0][1], ahead[2], behind[2])
    state |= attend(facts, [query, ready, *queries[2:]], others, *near, "attend_near_others")
    step(state[0][1])
    rings = [(-2, 0, piece), (2, 0, piece)]
    state = attend(
        facts, queries, [0, *others], rings, 0, piece, [ahead[2], behind[2]], state, False, "attend_mid"
    )
    far_low = turn(after(ahead[3], state[1][1])[:middle], cycle, group, 1)
    far_high = turn(after(behind[3], state[1][1])[middle:], cycle, group, -1)
    rings = [(-3, 0, piece), (3, 0, piece), (-half, 0, middle), (half, middle, piece - middle)]
    far_blocks = [ahead[3], behind[3], far_low, far_high]
    far = (rings, 0, piece, far_blocks, state, True)
    parts = attend(facts, queries, others, *far, "attend_far_others")
    ready = after(query, parts[0])
    result, stats = attend(facts, [ready, *queries[1:]], [0], *far, "attend_far_own")
    parts = [swap(part, "seq", shift + 1) for shift, part in enumerate(parts)]
    attended, sent = combine(result, stats, parts, w_out, ways)
    received = [swap(sent[shift - 1], "tp", shift) for shift in range(1, ways)]
    total = keep(attended, w_out, hidden_in)
    for part in received:
        total = total + part.astype(jnp.float32)
    return (total.astype(jnp.bfloat16), new_cache)


def solution(mesh):
    return jax.shard_map(
        local,
        mesh=mesh,
        in_specs=(
            P("seq", "tp"),
            P(None, "tp"),
            P(None, None, "tp"),
            P("tp", None),
            P("seq", None, "tp"),
            P("seq", None, None, "tp"),
            P(),
            P(),
            P(),
        ),
        out_specs=(P("seq", "tp"), P("seq", None, "tp")),
        check_vma=False,
    )
```

```python
import functools

import jax
import jax.numpy as jnp
import numpy as np
from jax import lax
from jax.experimental import pallas as pl
from jax.experimental.pallas import tpu as pltpu
from jax.sharding import PartitionSpec as P

HD = 128
REQ = 8
BLK = 128
NEGATIVE = -1e30
SCALE = float(HD**-0.5 * np.log2(np.e))
STAT_ROWS = 16


def params(mib=24):
    return pltpu.CompilerParams(vmem_limit_bytes=mib * 2**20)


def cost(flops, moved, exps=0):
    return pl.CostEstimate(flops=int(flops), bytes_accessed=int(moved), transcendentals=int(exps))


def cycle_of(group):
    if group == 2:
        return [0, 2, 4, 6, 7, 5, 3, 1]
    return list(range(REQ))


def pick(table, index):
    result = jnp.int32(table[0])
    for place, value in enumerate(table):
        result = jnp.where(index == place, jnp.int32(value), result)
    return result


def swap(value, axis, mask):
    pairs = [(source, source ^ mask) for source in range(lax.axis_size(axis))]
    return lax.ppermute(value, axis, pairs)


def turn(value, cycle, group, way):
    count = len(cycle)
    pairs = []
    for place in range(count):
        source, target = cycle[place], cycle[(place + way) % count]
        pairs += [(source * group + m, target * group + m) for m in range(group)]
    return lax.ppermute(value, "seq", pairs)


def rotated(vectors, cosine, sine):
    return vectors * cosine + pltpu.roll(vectors, HD // 2, 1) * sine


def angles(positions):
    half = HD // 2
    freqs = 10000.0 ** (-jnp.arange(half, dtype=jnp.float32) / half)
    angle = positions.astype(jnp.float32)[:, None] * freqs
    cosine, sine = jnp.cos(angle), jnp.sin(angle)
    return (
        jnp.concatenate([cosine, cosine], axis=1),
        jnp.concatenate([-sine, sine], axis=1),
    )


def lanes(start, count=HD):
    return pl.ds(pl.multiple_of(start, HD), count)


def after(value, *others):
    return lax.optimization_barrier((value, *others))[0]


VMEM = pl.BlockSpec(memory_space=pltpu.VMEM)
HBM = pl.BlockSpec(memory_space=pltpu.HBM)
SMEM = pl.BlockSpec(memory_space=pltpu.SMEM)


def viewed(block):
    count, pair, width = block.shape
    return block.reshape(count, pair, width // HD, HD).transpose(0, 2, 1, 3)


def order_rows(stride, back):
    rows = 2 * HD
    places = rows // stride
    row = lax.broadcasted_iota(jnp.int32, (rows, rows), 1 if back else 0)
    column = lax.broadcasted_iota(jnp.int32, (rows, rows), 0 if back else 1)
    source = lax.rem(row, places) * stride + lax.div(row, places)
    return jnp.where(column == source, 1.0, 0.0).astype(jnp.bfloat16)


def reordered(order, tiles):
    both = tiles[0] if len(tiles) == 1 else jnp.concatenate(tiles, axis=1)
    mixed = jnp.dot(order, both, preferred_element_type=jnp.float32).astype(jnp.bfloat16)
    return [mixed[:, i * HD : (i + 1) * HD] for i in range(len(tiles))]


def take_apart(block, order, result, offset):
    count, heads = block.shape[:2]
    stride = 2 * heads
    places = 2 * HD // stride
    flat = block.reshape(count * stride, HD)
    for start in range(0, count, 2 * places):
        starts = [at for at in (start, start + places) if at < count]
        tiles = [flat[at * stride : (at + places) * stride, :] for at in starts]
        for at, tile in zip(starts, reordered(order, tiles)):
            for head in range(heads):
                for j in range(2):
                    line = (2 * head + j) * places
                    result[
                        j, offset + at : offset + at + places, head * HD : (head + 1) * HD
                    ] = tile[line : line + places]


def part_kernel(*refs):
    *blocks, result = refs
    order = order_rows(2 * blocks[0].shape[1], False)
    offset = 0
    for block in blocks:
        take_apart(block, order, result, offset)
        offset += block.shape[0]


def part_keyval(blocks, name):
    count = sum(block.shape[0] for block in blocks)
    heads = blocks[0].shape[1]
    return pl.pallas_call(
        part_kernel,
        in_specs=[VMEM] * len(blocks),
        out_specs=VMEM,
        out_shape=jax.ShapeDtypeStruct((2, count, heads * HD), jnp.bfloat16),
        compiler_params=params(16),
        cost_estimate=cost(0, 8 * count * heads * HD),
        name=name,
    )(*blocks)


def query_kernel(*refs):
    *pieces, weight, cosine, sine, query, normed = refs
    columns = pieces[0].shape[1]
    index = lax.axis_index("tp")
    features = columns * len(pieces)
    values = [piece[...].astype(jnp.float32) for piece in pieces]
    mean = sum(jnp.sum(v, axis=1, keepdims=True) for v in values) / features
    values = [v - mean for v in values]
    spread = sum(jnp.sum(v * v, axis=1, keepdims=True) for v in values) / features
    inverse = lax.rsqrt(spread + 1e-05)
    for shift, v in enumerate(values):
        normed[:, lanes((index ^ shift) * columns, columns)] = (v * inverse).astype(jnp.bfloat16)
    width = weight.shape[1]
    wide = min(width, 2 * HD)
    for base in range(0, width, wide):
        product = jnp.dot(
            normed[...], weight[:, base : base + wide], preferred_element_type=jnp.float32
        )
        for start in range(0, wide, HD):
            query[:, base + start : base + start + HD] = rotated(
                product[:, start : start + HD], cosine[...], sine[...]
            ).astype(jnp.bfloat16)


def project_query(pieces, w_query, cosine, sine):
    rows, columns = pieces[0].shape
    depth, width = w_query.shape
    return pl.pallas_call(
        query_kernel,
        in_specs=[VMEM] * (len(pieces) + 3),
        out_specs=[VMEM] * 2,
        out_shape=[
            jax.ShapeDtypeStruct((rows, width), jnp.bfloat16),
            jax.ShapeDtypeStruct((rows, depth), jnp.bfloat16),
        ],
        compiler_params=params(20),
        cost_estimate=cost(2 * rows * depth * width, 2 * depth * width),
        name="project_query",
    )(*pieces, w_query, cosine, sine)


def weight_kernel(weight, result, near, arrived):
    slots, chunk, heads = near.shape[:3]
    count = weight.shape[0] // chunk
    copies = [
        pltpu.make_async_copy(
            weight.at[pl.ds(i * chunk, chunk)], near.at[i % slots], arrived.at[i]
        )
        for i in range(count)
    ]
    for copy in copies[:slots]:
        copy.start()
    order = order_rows(2 * heads, False)
    for i, copy in enumerate(copies):
        copy.wait()
        take_apart(near.at[i % slots], order, result, i * chunk)
        if i + slots < count:
            copies[i + slots].start()


def part_weights(w_keyval):
    weight = viewed(w_keyval)
    depth, heads = weight.shape[:2]
    chunk = min(depth, 256)
    count = depth // chunk
    return pl.pallas_call(
        weight_kernel,
        in_specs=[HBM],
        out_specs=VMEM,
        out_shape=jax.ShapeDtypeStruct((2, depth, heads * HD), jnp.bfloat16),
        scratch_shapes=[
            pltpu.VMEM((min(4, count), chunk, heads, 2, HD), jnp.bfloat16),
            pltpu.SemaphoreType.DMA((count,)),
        ],
        compiler_params=params(38),
        cost_estimate=cost(2**12 * depth * heads * HD, 8 * depth * heads * HD),
        name="part_weights",
    )(weight)


def keyval_kernel(normed, weight, cosine, sine, keys, values, cache):
    rows = normed.shape[0]
    heads = weight.shape[2] // HD
    stride = 2 * heads
    for head in range(heads):
        span = slice(head * HD, (head + 1) * HD)
        product = jnp.dot(
            normed[...],
            jnp.concatenate([weight[0, :, span], weight[1, :, span]], axis=1),
            preferred_element_type=jnp.float32,
        )
        keys[:, span] = rotated(product[:, :HD], cosine[...], sine[...]).astype(jnp.bfloat16)
        values[:, span] = product[:, HD:].astype(jnp.bfloat16)
    order = order_rows(stride, True)
    places = 2 * HD // stride
    flat = cache.reshape(rows * stride, HD)
    for start in range(0, rows, 2 * places):
        starts = [at for at in (start, start + places) if at < rows]
        tiles = [
            jnp.concatenate(
                [
                    pair[at : at + places, head * HD : (head + 1) * HD]
                    for head in range(heads)
                    for pair in (keys, values)
                ],
                axis=0,
            )
            for at in starts
        ]
        for at, tile in zip(starts, reordered(order, tiles)):
            flat[at * stride : (at + places) * stride, :] = tile


def project_keyval(normed, weight, cosine, sine):
    rows, depth = normed.shape
    width = weight.shape[2]
    heads = width // HD
    keys, values, cache = pl.pallas_call(
        keyval_kernel,
        in_specs=[VMEM] * 4,
        out_specs=[VMEM] * 3,
        out_shape=[
            jax.ShapeDtypeStruct((rows, width), jnp.bfloat16),
            jax.ShapeDtypeStruct((rows, width), jnp.bfloat16),
            jax.ShapeDtypeStruct((rows, heads, 2, HD), jnp.bfloat16),
        ],
        compiler_params=params(20),
        cost_estimate=cost(4 * rows * depth * width, 4 * depth * width),
        name="project_keyval",
    )(normed, weight, cosine, sine)
    return keys, values, cache.transpose(0, 2, 1, 3).reshape(rows, 2, width)


def with_column(stats, lane, column):
    place = lax.broadcasted_iota(jnp.int32, stats.shape, 1)
    return jnp.where(place == lane, column, stats)


def attend_kernel(spec, *refs):
    group, shifts, rings, slots, piece, fresh, first, last = spec
    refs = list(refs)
    take = lambda count: [refs.pop(0) for _ in range(count)]
    lengths, shared, table = take(3)
    queries = take(len(shifts))
    if fresh:
        *parted, fresh_keys, fresh_values = take(fresh)
    else:
        raw = take(len(rings))
    if not first:
        old_mixes, old_stats = take(len(shifts)), take(len(shifts))
    results = take(len(shifts))
    if last:
        mine_stats = take(1) if 0 in shifts else []
        bias, stats = take(2)
        stats[...] = jnp.zeros_like(stats)
    else:
        new_stats = take(len(shifts))
        bias = take(1)[0]
    if fresh:
        causal = take(1)[0]
    else:
        parted = take(1)
    rows, width = queries[0].shape
    heads = width // HD
    cycle = cycle_of(group)
    seq = lax.axis_index("seq")
    request, member = seq // group, seq % group
    place = pick(list(np.argsort(cycle)), request)
    edges = []
    count = 0
    block_size = BLK
    for i in range(slots):
        wanted = seq * slots + i
        number = jnp.int32(0)
        for j in range(table.shape[1]):
            number = jnp.where(table[request, j] == wanted, jnp.int32(j), number)
        edges.append((count, block_size, number * block_size, lengths[request]))
        count += block_size
    for step, begin, size in rings:
        origin = pick(cycle, lax.rem(place + step + REQ, REQ))
        edges.append((count, size, (origin * group + member) * piece + begin, shared[0]))
        count += size
    for begin, size, start, length in edges:
        positions = start + lax.broadcasted_iota(jnp.int32, (size, HD), 0)
        lane = lax.broadcasted_iota(jnp.int32, (size, HD), 1)
        bias[begin : begin + size, :] = jnp.where(
            (positions >= length) & (lane == 0), NEGATIVE, 0.0
        ).astype(jnp.bfloat16)
    if fresh:
        bias[count : count + rows, :] = jnp.zeros((rows, HD), jnp.bfloat16)
        theirs = member * rows + lax.broadcasted_iota(jnp.int32, (rows, rows), 1)
        for i, shift in enumerate(shifts):
            mine = (member ^ shift) * rows + lax.broadcasted_iota(jnp.int32, (rows, rows), 0)
            causal[i * rows : (i + 1) * rows, :] = jnp.where(theirs <= mine, 0.0, NEGATIVE)
    else:
        offset = 0
        order = order_rows(2 * heads, False)
        for piece_ref in raw:
            take_apart(piece_ref, order, parted[0], offset)
            offset += piece_ref.shape[0]
    unit = jnp.where(
        lax.broadcasted_iota(jnp.int32, (len(shifts) * rows, HD), 1) == 0, 1.0, 0.0
    ).astype(jnp.bfloat16)
    across = (((1,), (1,)), ((), ()))

    def stacked(values):
        return values[0] if len(values) == 1 else jnp.concatenate(values, axis=0)

    def one_head(head):
        span = lanes(head * HD)
        query = stacked([q[:, span] for q in queries])
        keys = [block[0, :, span] for block in parted]
        values = [block[1, :, span] for block in parted]
        if fresh:
            keys.append(fresh_keys[:, span])
            values.append(fresh_values[:, span])
        keys, values = stacked(keys), stacked(values)
        scores = lax.dot_general(
            jnp.concatenate([query, unit], axis=1),
            jnp.concatenate([keys, bias[...]], axis=1),
            across,
            preferred_element_type=jnp.float32,
        )
        if fresh:
            scores = jnp.concatenate([scores[:, :count], scores[:, count:] + causal[...]], axis=1)
        top = jnp.max(scores, axis=1, keepdims=True)
        if not first:
            old = stacked([s[:, span] for s in old_stats])
            top = jnp.maximum(top, old[:, :1] * (1.0 / SCALE))
        weights = jnp.exp2((scores - top) * SCALE).astype(jnp.bfloat16)
        mixed = jnp.dot(
            weights,
            jnp.concatenate([values, jnp.ones_like(values)], axis=1),
            preferred_element_type=jnp.float32,
        )
        total, summed = mixed[:, :HD], mixed[:, HD:]
        if not first:
            factor = jnp.exp2(old - top * SCALE)
            total = total + stacked([mix[:, span] for mix in old_mixes]) * factor
            summed = summed + factor
        even = total / summed
        extent = top * SCALE + jnp.log2(summed)
        if last:
            stats[...] = with_column(stats[...], head, extent)
        else:
            for i, new in enumerate(new_stats):
                new[:, span] = extent[i * rows : (i + 1) * rows]
        for i, result in enumerate(results):
            result[:rows, span] = even[i * rows : (i + 1) * rows].astype(result.dtype)

    together = min(4, heads)

    def some_heads(i, _):
        for j in range(together):
            one_head(together * i + j)
        return 0

    lax.fori_loop(0, heads // together, some_heads, 0)
    if not last:
        return
    for i, shift in enumerate(shifts):
        own_rows = stats[i * rows : (i + 1) * rows, :]
        if shift == 0:
            mine_stats[0][...] = own_rows
        else:
            line = jnp.transpose(own_rows)[:heads, :]
            packed = []
            for _ in range(3):
                rounded = line.astype(jnp.bfloat16).astype(jnp.float32)
                packed.append(rounded)
                line = line - rounded
            gap = -3 * heads % STAT_ROWS
            if gap:
                packed.append(jnp.zeros((gap, rows), jnp.float32))
            packed = jnp.concatenate(packed, axis=0).astype(jnp.bfloat16)
            for j in range(packed.shape[0] // STAT_ROWS):
                results[i][rows:, j * rows : (j + 1) * rows] = packed[
                    j * STAT_ROWS : (j + 1) * STAT_ROWS
                ]


def attend(facts, queries, shifts, rings, slots, piece, blocks, old, last, name):
    group = len(queries)
    queries = [queries[shift] for shift in shifts]
    rows, width = queries[0].shape
    heads = width // HD
    fresh = len(blocks) if blocks[0].ndim == 3 else 0
    operands = [*facts, *queries, *blocks]
    if old:
        operands += [old[shift][0] for shift in shifts] + [old[shift][1] for shift in shifts]
    plain = sum(size for _, _, size in rings) + BLK * slots
    count = plain + (rows if fresh else 0)
    many = len(shifts) * rows
    scratch = [pltpu.VMEM((count, HD), jnp.bfloat16)]
    if last:
        scratch.append(pltpu.VMEM((many, HD), jnp.float32))
    if fresh:
        scratch.append(pltpu.VMEM((many, rows), jnp.float32))
    else:
        scratch.append(pltpu.VMEM((2, count, width), jnp.bfloat16))
    state = jax.ShapeDtypeStruct((rows, width), jnp.float32)
    state_stats = jax.ShapeDtypeStruct((rows, HD), jnp.float32)
    sent = jax.ShapeDtypeStruct((rows + STAT_ROWS, width), jnp.bfloat16)
    if last:
        out_shape = [sent if shift else state for shift in shifts]
        out_shape += [state_stats] * (0 in shifts)
    else:
        out_shape = [state] * (2 * len(shifts))
    scores = many * count * heads
    results = pl.pallas_call(
        functools.partial(
            attend_kernel, (group, shifts, rings, slots, piece, fresh, not old, last)
        ),
        in_specs=[SMEM] * 3 + [VMEM] * (len(operands) - 3),
        out_specs=[VMEM] * len(out_shape),
        out_shape=out_shape,
        scratch_shapes=scratch,
        compiler_params=params(28),
        cost_estimate=cost(4 * scores * HD, 4 * count * width, scores),
        name=name,
    )(*operands)
    if last:
        return results
    return {
        shift: (results[i], results[len(shifts) + i]) for i, shift in enumerate(shifts)
    }


def combine_kernel(*refs):
    result, stats, *refs = refs
    *parts, weight, attended, sent = refs[: len(refs)]
    rows, width = result.shape
    heads = width // HD
    extents = [stats[...]]
    for part in parts:
        tile = part[rows:, :].astype(jnp.float32)
        groups = -(-3 * heads // STAT_ROWS)
        lines = jnp.concatenate(
            [tile[:, j * rows : (j + 1) * rows] for j in range(groups)], axis=0
        )
        line = sum(lines[i * heads : (i + 1) * heads] for i in range(3))
        line = jnp.concatenate([line, jnp.zeros((HD - heads, rows), jnp.float32)], axis=0)
        extents.append(jnp.transpose(line))
    top = functools.reduce(jnp.maximum, extents)
    shares = [jnp.exp2(extent - top) for extent in extents]
    whole = sum(shares)
    shares = [share / whole for share in shares]
    for head in range(heads):
        span = slice(head * HD, (head + 1) * HD)
        mixes = [result[:, span]] + [part[:rows, span].astype(jnp.float32) for part in parts]
        mixed = sum(mix * share[:, head : head + 1] for mix, share in zip(mixes, shares))
        attended[:, span] = mixed.astype(jnp.bfloat16)
    index = lax.axis_index("tp")
    ways = sent.shape[0] + 1
    columns = weight.shape[1] // ways
    for shift in range(1, ways):
        sent[shift - 1] = jnp.dot(
            attended[...],
            weight[:, lanes((index ^ shift) * columns, columns)],
            preferred_element_type=jnp.float32,
        ).astype(jnp.bfloat16)


def combine(result, stats, parts, w_out, ways):
    rows, width = result.shape
    columns = w_out.shape[1] // ways
    return pl.pallas_call(
        combine_kernel,
        in_specs=[VMEM] * (3 + len(parts)),
        out_specs=[VMEM] * 2,
        out_shape=[
            jax.ShapeDtypeStruct((rows, width), jnp.bfloat16),
            jax.ShapeDtypeStruct((ways - 1, rows, columns), jnp.bfloat16),
        ],
        compiler_params=params(20),
        cost_estimate=cost(2 * rows * width * columns * (ways - 1), 2 * width * w_out.shape[1]),
        name="combine_send",
    )(result, stats, *parts, w_out)


def keep_kernel(attended, weight, hidden, kept):
    columns = hidden.shape[1]
    product = jnp.dot(
        attended[...],
        weight[:, lanes(lax.axis_index("tp") * columns, columns)],
        preferred_element_type=jnp.float32,
    )
    kept[...] = product + hidden[...].astype(jnp.float32)


def keep(attended, w_out, hidden):
    rows, width = attended.shape
    return pl.pallas_call(
        keep_kernel,
        in_specs=[VMEM] * 3,
        out_specs=VMEM,
        out_shape=jax.ShapeDtypeStruct(hidden.shape, jnp.float32),
        compiler_params=params(20),
        cost_estimate=cost(2 * rows * width * hidden.shape[1], 2 * width * w_out.shape[1]),
        name="keep_own",
    )(attended, w_out, hidden)


def local(
    hidden_in, w_query, w_keyval, w_out, prompt_cache, tail_cache, tail_table, tail_len, shared_len
):
    rows = hidden_in.shape[0]
    group = lax.axis_size("seq") // REQ
    ways = lax.axis_size("tp")
    cycle = cycle_of(group)
    seq = lax.axis_index("seq")
    request = seq // group
    member = seq % group
    half = REQ // 2
    piece = prompt_cache.shape[0]
    middle = piece // 2

    weight = part_weights(w_keyval)
    pieces = [hidden_in] + [swap(hidden_in, "tp", shift) for shift in range(1, ways)]
    prompt = viewed(prompt_cache)
    ahead, behind = [prompt], [prompt]

    def step(*others):
        for blocks, way in ((ahead, 1), (behind, -1)):
            blocks.append(turn(after(blocks[-1], *others), cycle, group, way))

    step()
    own_length = lax.dynamic_index_in_dim(tail_len, request, 0, keepdims=False)
    positions = shared_len[0] + own_length + member * rows + jnp.arange(rows, dtype=jnp.int32)
    cosine, sine = angles(positions)
    pieces[0] = after(pieces[0], weight)
    query, normed = project_query(pieces, w_query, cosine, sine)
    queries = [query] + [swap(query, "seq", shift) for shift in range(1, group)]
    tail = viewed(tail_cache.reshape(-1, 2, tail_cache.shape[3]))
    slots = tail_cache.shape[0]
    own_block = part_keyval([after(tail, query), prompt], "part_own")
    step(own_block)
    ready = after(normed, ahead[1], behind[1])
    fresh_keys, fresh_values, new_cache = project_keyval(ready, weight, cosine, sine)
    near_block = part_keyval([ahead[1], behind[1]], "part_near")

    facts = (tail_len, shared_len, tail_table)
    others = list(range(1, group))
    near = (
        [(0, 0, piece), (-1, 0, piece), (1, 0, piece)],
        slots,
        piece,
        [own_block, near_block, fresh_keys, fresh_values],
        None,
        False,
    )
    state = attend(facts, queries, [0], *near, "attend_near_own")
    ready = after(queries[1], state[0][1], ahead[2], behind[2])
    state |= attend(facts, [query, ready, *queries[2:]], others, *near, "attend_near_others")
    step(state[0][1])
    rings = [(-2, 0, piece), (2, 0, piece)]
    mid = (rings, 0, piece, [ahead[2], behind[2]], state, False, "attend_second")
    state = attend(facts, queries, [0, *others], *mid)
    far_low = turn(after(ahead[3], state[1][1])[:middle], cycle, group, 1)
    far_high = turn(after(behind[3], state[1][1])[middle:], cycle, group, -1)
    rings = [(-3, 0, piece), (3, 0, piece)]
    mid = (rings, 0, piece, [ahead[3], behind[3]], state, False, "attend_third")
    state = attend(facts, queries, [0, *others], *mid)
    rings = [(-half, 0, middle), (half, middle, piece - middle)]
    far = (rings, 0, piece, [far_low, far_high], state, True)
    parts = attend(facts, queries, others, *far, "attend_far_others")
    ready = after(query, parts[0])
    result, stats = attend(facts, [ready, *queries[1:]], [0], *far, "attend_far_own")
    parts = [swap(part, "seq", shift + 1) for shift, part in enumerate(parts)]
    attended, sent = combine(result, stats, parts, w_out, ways)
    received = [swap(sent[shift - 1], "tp", shift) for shift in range(1, ways)]
    total = keep(attended, w_out, hidden_in)
    for part in received:
        total = total + part.astype(jnp.float32)
    return (total.astype(jnp.bfloat16), new_cache)


def solution(mesh):
    return jax.shard_map(
        local,
        mesh=mesh,
        in_specs=(
            P("seq", "tp"),
            P(None, "tp"),
            P(None, None, "tp"),
            P("tp", None),
            P("seq", None, "tp"),
            P("seq", None, None, "tp"),
            P(),
            P(),
            P(),
        ),
        out_specs=(P("seq", "tp"), P("seq", None, "tp")),
        check_vma=False,
    )
```

```python
import functools

import jax
import jax.numpy as jnp
import numpy as np
from jax import lax
from jax.experimental import pallas as pl
from jax.experimental.pallas import tpu as pltpu
from jax.sharding import PartitionSpec as P

HD = 128
REQ = 8
BLK = 128
NEGATIVE = -1e30
SCALE = float(HD**-0.5 * np.log2(np.e))


def params(mib=24):
    return pltpu.CompilerParams(vmem_limit_bytes=mib * 2**20)


def cost(flops, moved, exps=0):
    return pl.CostEstimate(flops=int(flops), bytes_accessed=int(moved), transcendentals=int(exps))


def cycle_of(group):
    if group == 2:
        return [0, 2, 4, 6, 7, 5, 3, 1]
    return list(range(REQ))


def pick(table, index):
    result = jnp.int32(table[0])
    for place, value in enumerate(table):
        result = jnp.where(index == place, jnp.int32(value), result)
    return result


def swap(value, axis, mask):
    pairs = [(source, source ^ mask) for source in range(lax.axis_size(axis))]
    return lax.ppermute(value, axis, pairs)


def turn(value, cycle, group, way):
    count = len(cycle)
    pairs = []
    for place in range(count):
        source, target = cycle[place], cycle[(place + way) % count]
        pairs += [(source * group + m, target * group + m) for m in range(group)]
    return lax.ppermute(value, "seq", pairs)


def rotated(vectors, cosine, sine):
    return vectors * cosine + pltpu.roll(vectors, HD // 2, 1) * sine


def position_kernel(lengths, shared, positions):
    rows = positions.shape[0]
    group = lax.axis_size("seq") // REQ
    seq = lax.axis_index("seq")
    start = shared[0] + lengths[seq // group] + (seq % group) * rows
    places = start + lax.broadcasted_iota(jnp.int32, positions.shape, 0)
    positions[...] = places.astype(jnp.float32)


def angles(tail_len, shared_len, rows):
    half = HD // 2
    positions = pl.pallas_call(
        position_kernel,
        in_specs=[SMEM] * 2,
        out_specs=VMEM,
        out_shape=jax.ShapeDtypeStruct((rows, HD), jnp.float32),
        compiler_params=params(8),
        cost_estimate=cost(rows * HD, 4 * rows * HD),
        name="positions",
    )(tail_len, shared_len)
    lane = jnp.arange(HD, dtype=jnp.int32)
    freqs = 10000.0 ** (-(lane % half).astype(jnp.float32) / half)
    angle = positions * freqs
    return jnp.cos(angle), jnp.sin(angle) * jnp.where(lane < half, -1.0, 1.0)


def lanes(start, count=HD):
    return pl.ds(pl.multiple_of(start, HD), count)


def after(value, *others):
    return lax.optimization_barrier((value, *others))[0]


VMEM = pl.BlockSpec(memory_space=pltpu.VMEM)
HBM = pl.BlockSpec(memory_space=pltpu.HBM)
SMEM = pl.BlockSpec(memory_space=pltpu.SMEM)


def viewed(block):
    count, pair, width = block.shape
    return block.reshape(count, pair, width // HD, HD).transpose(0, 2, 1, 3)


def order_rows(stride, back):
    rows = 2 * HD
    places = rows // stride
    row = lax.broadcasted_iota(jnp.int32, (rows, rows), 1 if back else 0)
    column = lax.broadcasted_iota(jnp.int32, (rows, rows), 0 if back else 1)
    source = lax.rem(row, places) * stride + lax.div(row, places)
    return jnp.where(column == source, 1.0, 0.0).astype(jnp.bfloat16)


def reordered(order, tiles):
    both = tiles[0] if len(tiles) == 1 else jnp.concatenate(tiles, axis=1)
    mixed = jnp.dot(order, both, preferred_element_type=jnp.float32).astype(jnp.bfloat16)
    return [mixed[:, i * HD : (i + 1) * HD] for i in range(len(tiles))]


def take_apart(block, order, keys, values, offset):
    count, heads = block.shape[:2]
    stride = 2 * heads
    places = 2 * HD // stride
    flat = block.reshape(count * stride, HD)
    for start in range(0, count, 2 * places):
        starts = [at for at in (start, start + places) if at < count]
        tiles = [flat[at * stride : (at + places) * stride, :] for at in starts]
        for at, tile in zip(starts, reordered(order, tiles)):
            for head in range(heads):
                for j, result in enumerate((keys, values)):
                    line = (2 * head + j) * places
                    result[offset + at : offset + at + places, head * HD : (head + 1) * HD] = tile[
                        line : line + places
                    ]


ACROSS = (((1,), (1,)), ((), ()))


def unit_matrix(size):
    row = lax.broadcasted_iota(jnp.int32, (size, size), 0)
    column = lax.broadcasted_iota(jnp.int32, (size, size), 1)
    return jnp.where(row == column, 1.0, 0.0).astype(jnp.bfloat16)


def turned_over(unit, value):
    return lax.dot_general(unit, value, ACROSS, preferred_element_type=jnp.float32).astype(
        jnp.bfloat16
    )


def turn_heads(values, result):
    unit = unit_matrix(HD)
    for start in range(0, values.shape[1], HD):
        result[start : start + HD, :] = turned_over(unit, values[:, start : start + HD])


def part_kernel(*refs):
    *blocks, keys, turned, token, values = refs
    order = order_rows(2 * blocks[0].shape[1], False)
    offset = 0
    for block in blocks:
        take_apart(block, order, keys, values, offset)
        offset += block.shape[0]
    turn_heads(values, turned)
    token[...] = jnp.zeros_like(token)


TOKEN = jax.ShapeDtypeStruct((8, HD), jnp.float32)


def part_keyval(blocks, name):
    count = sum(block.shape[0] for block in blocks)
    width = blocks[0].shape[1] * HD
    return pl.pallas_call(
        part_kernel,
        in_specs=[VMEM] * len(blocks),
        out_specs=[VMEM] * 3,
        out_shape=[
            jax.ShapeDtypeStruct((count, width), jnp.bfloat16),
            jax.ShapeDtypeStruct((width, count), jnp.bfloat16),
            TOKEN,
        ],
        scratch_shapes=[pltpu.VMEM((count, width), jnp.bfloat16)],
        compiler_params=params(16),
        cost_estimate=cost(2**10 * count * width, 8 * count * width),
        name=name,
    )(*blocks)


def query_kernel(*refs):
    *pieces, weight, cosine, sine, query, normed = refs
    columns = pieces[0].shape[1]
    index = lax.axis_index("tp")
    features = columns * len(pieces)
    values = [piece[...].astype(jnp.float32) for piece in pieces]
    mean = sum(jnp.sum(v, axis=1, keepdims=True) for v in values) / features
    values = [v - mean for v in values]
    spread = sum(jnp.sum(v * v, axis=1, keepdims=True) for v in values) / features
    inverse = lax.rsqrt(spread + 1e-05)
    for shift, v in enumerate(values):
        normed[:, lanes((index ^ shift) * columns, columns)] = (v * inverse).astype(jnp.bfloat16)
    width = weight.shape[1]
    wide = min(width, 2 * HD)
    for base in range(0, width, wide):
        product = jnp.dot(
            normed[...], weight[:, base : base + wide], preferred_element_type=jnp.float32
        )
        for start in range(0, wide, HD):
            query[:, base + start : base + start + HD] = rotated(
                product[:, start : start + HD], cosine[...], sine[...]
            ).astype(jnp.bfloat16)


def project_query(pieces, w_query, cosine, sine):
    rows, columns = pieces[0].shape
    depth, width = w_query.shape
    return pl.pallas_call(
        query_kernel,
        in_specs=[VMEM] * (len(pieces) + 3),
        out_specs=[VMEM] * 2,
        out_shape=[
            jax.ShapeDtypeStruct((rows, width), jnp.bfloat16),
            jax.ShapeDtypeStruct((rows, depth), jnp.bfloat16),
        ],
        compiler_params=params(20),
        cost_estimate=cost(2 * rows * depth * width, 2 * depth * width),
        name="project_query",
    )(*pieces, w_query, cosine, sine)


def weight_kernel(weight, result, token, near, arrived):
    slots, chunk, heads = near.shape[:3]
    count = weight.shape[0] // chunk
    copies = [
        pltpu.make_async_copy(
            weight.at[pl.ds(i * chunk, chunk)], near.at[i % slots], arrived.at[i]
        )
        for i in range(count)
    ]
    for copy in copies[:slots]:
        copy.start()
    order = order_rows(2 * heads, False)
    for i, copy in enumerate(copies):
        copy.wait()
        take_apart(near.at[i % slots], order, result.at[0], result.at[1], i * chunk)
        if i + slots < count:
            copies[i + slots].start()
    token[...] = jnp.zeros_like(token)


def part_weights(w_keyval):
    weight = viewed(w_keyval)
    depth, heads = weight.shape[:2]
    chunk = min(depth, 256)
    count = depth // chunk
    return pl.pallas_call(
        weight_kernel,
        in_specs=[HBM],
        out_specs=[VMEM] * 2,
        out_shape=[jax.ShapeDtypeStruct((2, depth, heads * HD), jnp.bfloat16), TOKEN],
        scratch_shapes=[
            pltpu.VMEM((count, chunk, heads, 2, HD), jnp.bfloat16),
            pltpu.SemaphoreType.DMA((count,)),
        ],
        compiler_params=params(38),
        cost_estimate=cost(2**12 * depth * heads * HD, 8 * depth * heads * HD),
        name="part_weights",
    )(weight)


def keyval_kernel(normed, weight, cosine, sine, keys, turned, cache, values):
    rows = normed.shape[0]
    heads = weight.shape[2] // HD
    stride = 2 * heads
    for head in range(heads):
        span = slice(head * HD, (head + 1) * HD)
        product = jnp.dot(
            normed[...],
            jnp.concatenate([weight[0, :, span], weight[1, :, span]], axis=1),
            preferred_element_type=jnp.float32,
        )
        keys[:, span] = rotated(product[:, :HD], cosine[...], sine[...]).astype(jnp.bfloat16)
        values[:, span] = product[:, HD:].astype(jnp.bfloat16)
    turn_heads(values, turned)
    order = order_rows(stride, True)
    places = 2 * HD // stride
    flat = cache.reshape(rows * stride, HD)
    for start in range(0, rows, 2 * places):
        starts = [at for at in (start, start + places) if at < rows]
        tiles = [
            jnp.concatenate(
                [
                    pair[at : at + places, head * HD : (head + 1) * HD]
                    for head in range(heads)
                    for pair in (keys, values)
                ],
                axis=0,
            )
            for at in starts
        ]
        for at, tile in zip(starts, reordered(order, tiles)):
            flat[at * stride : (at + places) * stride, :] = tile


def project_keyval(normed, weight, cosine, sine):
    rows, depth = normed.shape
    width = weight.shape[2]
    heads = width // HD
    keys, turned, cache = pl.pallas_call(
        keyval_kernel,
        in_specs=[VMEM] * 4,
        out_specs=[VMEM] * 3,
        out_shape=[
            jax.ShapeDtypeStruct((rows, width), jnp.bfloat16),
            jax.ShapeDtypeStruct((width, rows), jnp.bfloat16),
            jax.ShapeDtypeStruct((rows, heads, 2, HD), jnp.bfloat16),
        ],
        scratch_shapes=[pltpu.VMEM((rows, width), jnp.bfloat16)],
        compiler_params=params(20),
        cost_estimate=cost(4 * rows * depth * width, 4 * depth * width),
        name="project_keyval",
    )(normed, weight, cosine, sine)
    return keys, turned, cache.transpose(0, 2, 1, 3).reshape(rows, 2, width)


def attend_kernel(spec, *refs):
    group, shifts, rings, slots, piece, parted, first, last = spec
    refs = list(refs)
    take = lambda count: [refs.pop(0) for _ in range(count)]
    lengths, shared, table = take(3)
    queries = take(len(shifts))
    if parted:
        blocks = take(2 * parted)
        many_keys, many_turned = blocks[::2], blocks[1::2]
    else:
        raw = take(len(rings))
    if not first:
        old_mixes, old_extents = take(len(shifts)), take(len(shifts))
    results = take(len(shifts))
    extents = [None if last and shift else take(1)[0] for shift in shifts]
    token, bias = take(2)
    extents = [take(1)[0] if extent is None else extent for extent in extents]
    if parted:
        causal = take(1)[0]
    else:
        keys_here, turned_here, values_here = take(3)
        many_keys, many_turned = [keys_here], [turned_here]
    rows, width = queries[0].shape
    heads = width // HD
    cycle = cycle_of(group)
    seq = lax.axis_index("seq")
    request, member = seq // group, seq % group
    place = pick(list(np.argsort(cycle)), request)
    edges = []
    count = 0
    for i in range(slots):
        wanted = seq * slots + i
        number = jnp.int32(0)
        for j in range(table.shape[0]):
            number = jnp.where(table[j, request] == wanted, jnp.int32(j), number)
        edges.append((count, BLK, number * BLK, lengths[request]))
        count += BLK
    for step, begin, size in rings:
        origin = pick(cycle, lax.rem(place + step + REQ, REQ))
        edges.append((count, size, (origin * group + member) * piece + begin, shared[0]))
        count += size
    for begin, size, start, length in edges:
        positions = start + lax.broadcasted_iota(jnp.int32, (size, HD), 0)
        lane = lax.broadcasted_iota(jnp.int32, (size, HD), 1)
        bias[begin : begin + size, :] = jnp.where(
            (positions >= length) & (lane == 0), NEGATIVE, 0.0
        ).astype(jnp.bfloat16)
    if parted:
        bias[count : count + rows, :] = jnp.zeros((rows, HD), jnp.bfloat16)
        theirs = member * rows + lax.broadcasted_iota(jnp.int32, (rows, rows), 0)
        for i, shift in enumerate(shifts):
            mine = (member ^ shift) * rows + lax.broadcasted_iota(jnp.int32, (rows, rows), 1)
            causal[i] = jnp.where(theirs <= mine, 0.0, NEGATIVE)
    else:
        offset = 0
        order = order_rows(2 * heads, False)
        for block in raw:
            take_apart(block, order, keys_here, values_here, offset)
            offset += block.shape[0]
        turn_heads(values_here, turned_here)
    token[...] = jnp.zeros_like(token)
    unit = jnp.where(lax.broadcasted_iota(jnp.int32, (rows, HD), 1) == 0, 1.0, 0.0)
    unit = unit.astype(jnp.bfloat16)

    def one_head(head):
        span = lanes(head * HD)
        line = pl.ds(head, 1)
        keys = jnp.concatenate([keys[:, span] for keys in many_keys], axis=0)
        keys = jnp.concatenate([keys, bias[...]], axis=1)
        values = jnp.concatenate([turned[span, :] for turned in many_turned], axis=1)
        for i in range(len(shifts)):
            query = jnp.concatenate([queries[i][:, span], unit], axis=1)
            scores = lax.dot_general(keys, query, ACROSS, preferred_element_type=jnp.float32)
            if parted:
                scores = jnp.concatenate([scores[:count], scores[count:] + causal[i]], axis=0)
            top = jnp.max(scores, axis=0, keepdims=True)
            if not first:
                old = old_extents[i][line, :]
                top = jnp.maximum(top, old * (1.0 / SCALE))
            weights = jnp.exp2((scores - top) * SCALE)
            summed = jnp.sum(weights, axis=0, keepdims=True)
            mixed = jnp.dot(
                values, weights.astype(jnp.bfloat16), preferred_element_type=jnp.float32
            )
            if not first:
                factor = jnp.exp2(old - top * SCALE)
                summed = summed + factor
                mixed = mixed + old_mixes[i][span, :] * factor
            mixed = mixed * (1.0 / summed)
            extents[i][line, :] = top * SCALE + jnp.log2(summed)
            results[i][span, :] = mixed.astype(results[i].dtype)

    together = min(4, heads)

    def some_heads(i, _):
        for j in range(together):
            one_head(together * i + j)
        return 0

    lax.fori_loop(0, heads // together, some_heads, 0)
    for i, shift in enumerate(shifts):
        if last and shift:
            line = extents[i][:heads, :]
            packed = []
            for _ in range(3):
                rounded = line.astype(jnp.bfloat16).astype(jnp.float32)
                packed.append(rounded)
                line = line - rounded
            gap = stat_rows(heads) - 3 * heads
            if gap:
                packed.append(jnp.zeros((gap, rows), jnp.float32))
            results[i][width:, :] = jnp.concatenate(packed, axis=0).astype(jnp.bfloat16)


def stat_rows(heads):
    return -(-3 * heads // 16) * 16


def attend(facts, queries, shifts, rings, slots, piece, blocks, old, last, name):
    group = len(queries)
    queries = [queries[shift] for shift in shifts]
    rows, width = queries[0].shape
    heads = width // HD
    parted = len(blocks) // 2 if blocks[0].ndim == 2 else 0
    operands = [*facts, *queries, *blocks]
    if old:
        operands += [old[shift][0] for shift in shifts] + [old[shift][1] for shift in shifts]
    count = sum(size for _, _, size in rings) + BLK * slots + (rows if parted else 0)
    scratch = [pltpu.VMEM((count, HD), jnp.bfloat16)]
    lines = (max(heads, 8), rows)
    scratch += [pltpu.VMEM(lines, jnp.float32) for shift in shifts if last and shift]
    if parted:
        scratch.append(pltpu.VMEM((len(shifts), rows, rows), jnp.float32))
    else:
        scratch += [
            pltpu.VMEM((count, width), jnp.bfloat16),
            pltpu.VMEM((width, count), jnp.bfloat16),
            pltpu.VMEM((count, width), jnp.bfloat16),
        ]
    mixes = [
        jax.ShapeDtypeStruct((width + stat_rows(heads), rows), jnp.bfloat16)
        if last and shift
        else jax.ShapeDtypeStruct((width, rows), jnp.float32)
        for shift in shifts
    ]
    extents = [
        jax.ShapeDtypeStruct(lines, jnp.float32) for shift in shifts if not (last and shift)
    ]
    scores = len(shifts) * rows * count * heads
    results = pl.pallas_call(
        functools.partial(
            attend_kernel, (group, shifts, rings, slots, piece, parted, not old, last)
        ),
        in_specs=[SMEM] * 3 + [VMEM] * (len(operands) - 3),
        out_specs=[VMEM] * (len(mixes) + len(extents) + 1),
        out_shape=[*mixes, *extents, TOKEN],
        scratch_shapes=scratch,
        compiler_params=params(24),
        cost_estimate=cost(4 * scores * HD, 4 * count * width, scores),
        name=name,
    )(*operands)
    if last:
        return results
    state = {shift: (results[i], results[len(shifts) + i]) for i, shift in enumerate(shifts)}
    return state, results[-1]


def combine_kernel(*refs):
    result, extent, *parts, weight, attended, sent = refs
    width, rows = result.shape
    heads = width // HD
    extents = [extent[:heads, :]]
    for part in parts:
        lines = part[width:, :].astype(jnp.float32)
        extents.append(sum(lines[i * heads : (i + 1) * heads] for i in range(3)))
    top = functools.reduce(jnp.maximum, extents)
    shares = [jnp.exp2(extent - top) for extent in extents]
    whole = sum(shares)
    shares = [share / whole for share in shares]
    unit = unit_matrix(rows)
    for head in range(heads):
        span = slice(head * HD, (head + 1) * HD)
        mixes = [result[span, :]] + [part[span, :].astype(jnp.float32) for part in parts]
        mixed = sum(mix * share[head : head + 1] for mix, share in zip(mixes, shares))
        attended[:, span] = turned_over(unit, mixed.astype(jnp.bfloat16))
    index = lax.axis_index("tp")
    ways = sent.shape[0] + 1
    columns = weight.shape[1] // ways
    for shift in range(1, ways):
        sent[shift - 1] = jnp.dot(
            attended[...],
            weight[:, lanes((index ^ shift) * columns, columns)],
            preferred_element_type=jnp.float32,
        ).astype(jnp.bfloat16)


def combine(result, extent, parts, w_out, ways):
    width, rows = result.shape
    columns = w_out.shape[1] // ways
    return pl.pallas_call(
        combine_kernel,
        in_specs=[VMEM] * (3 + len(parts)),
        out_specs=[VMEM] * 2,
        out_shape=[
            jax.ShapeDtypeStruct((rows, width), jnp.bfloat16),
            jax.ShapeDtypeStruct((ways - 1, rows, columns), jnp.bfloat16),
        ],
        compiler_params=params(20),
        cost_estimate=cost(2 * rows * width * columns * (ways - 1), 2 * width * w_out.shape[1]),
        name="combine_send",
    )(result, extent, *parts, w_out)


def keep_kernel(attended, weight, hidden, kept):
    columns = hidden.shape[1]
    product = jnp.dot(
        attended[...],
        weight[:, lanes(lax.axis_index("tp") * columns, columns)],
        preferred_element_type=jnp.float32,
    )
    kept[...] = product + hidden[...].astype(jnp.float32)


def keep(attended, w_out, hidden):
    rows, width = attended.shape
    return pl.pallas_call(
        keep_kernel,
        in_specs=[VMEM] * 3,
        out_specs=VMEM,
        out_shape=jax.ShapeDtypeStruct(hidden.shape, jnp.float32),
        compiler_params=params(20),
        cost_estimate=cost(2 * rows * width * hidden.shape[1], 2 * width * w_out.shape[1]),
        name="keep_own",
    )(attended, w_out, hidden)


def local(
    hidden_in, w_query, w_keyval, w_out, prompt_cache, tail_cache, tail_table, tail_len, shared_len
):
    rows = hidden_in.shape[0]
    group = lax.axis_size("seq") // REQ
    ways = lax.axis_size("tp")
    cycle = cycle_of(group)
    half = REQ // 2
    piece = prompt_cache.shape[0]
    middle = piece // 2

    pieces = [hidden_in] + [swap(hidden_in, "tp", shift) for shift in range(1, ways)]
    prompt = viewed(prompt_cache)
    ahead, behind = [prompt], [prompt]

    def step(*others):
        for blocks, way in ((ahead, 1), (behind, -1)):
            blocks.append(turn(after(blocks[-1], *others), cycle, group, way))

    step()
    cosine, sine = angles(tail_len, shared_len, rows)
    weight, token = part_weights(w_keyval)
    pieces[0] = after(pieces[0], token)
    query, normed = project_query(pieces, w_query, cosine, sine)
    queries = [query] + [swap(query, "seq", shift) for shift in range(1, group)]
    tail = viewed(tail_cache.reshape(-1, 2, tail_cache.shape[3]))
    slots = tail_cache.shape[0]
    *own_block, token = part_keyval([tail, prompt], "part_own")
    step(token)
    *near_block, token = part_keyval([ahead[1], behind[1]], "part_near")
    fresh_keys, fresh_turned, new_cache = project_keyval(normed, weight, cosine, sine)

    table = tail_table.T
    facts = (tail_len, shared_len, table)
    others = list(range(1, group))
    near = (
        [(0, 0, piece), (-1, 0, piece), (1, 0, piece)],
        slots,
        piece,
        [*own_block, *near_block, fresh_keys, fresh_turned],
        None,
        False,
    )
    state, token = attend(facts, queries, [0], *near, "attend_near_own")
    step(token)
    ready = (after(tail_len, token), shared_len, table)
    state_others, token = attend(ready, queries, others, *near, "attend_near_others")
    state |= state_others
    rings = [(-2, 0, piece), (2, 0, piece)]
    second = (rings, 0, piece, [ahead[2], behind[2]], state, False, "attend_second")
    state, token = attend(facts, queries, [0, *others], *second)
    far_low = turn(after(ahead[3], token)[:middle], cycle, group, 1)
    far_high = turn(after(behind[3], token)[middle:], cycle, group, -1)
    rings = [(-3, 0, piece), (3, 0, piece)]
    third = (rings, 0, piece, [ahead[3], behind[3]], state, False, "attend_third")
    state, token = attend(facts, queries, [0, *others], *third)
    rings = [(-half, 0, middle), (half, middle, piece - middle)]
    far = (rings, 0, piece, [far_low, far_high], state, True)
    *parts, token = attend(facts, queries, others, *far, "attend_far_others")
    ready = (after(tail_len, token), shared_len, table)
    result, extent, token = attend(ready, queries, [0], *far, "attend_far_own")
    parts = [swap(part, "seq", shift + 1) for shift, part in enumerate(parts)]
    attended, sent = combine(result, extent, parts, w_out, ways)
    received = [swap(sent[shift - 1], "tp", shift) for shift in range(1, ways)]
    total = keep(attended, w_out, hidden_in)
    for part in received:
        total = total + part.astype(jnp.float32)
    return (total.astype(jnp.bfloat16), new_cache)


def solution(mesh):
    return jax.shard_map(
        local,
        mesh=mesh,
        in_specs=(
            P("seq", "tp"),
            P(None, "tp"),
            P(None, None, "tp"),
            P("tp", None),
            P("seq", None, "tp"),
            P("seq", None, None, "tp"),
            P(),
            P(),
            P(),
        ),
        out_specs=(P("seq", "tp"), P("seq", None, "tp")),
        check_vma=False,
    )
```

```python
import functools

import jax
import jax.numpy as jnp
import numpy as np
from jax import lax
from jax.experimental import pallas as pl
from jax.experimental.pallas import tpu as pltpu
from jax.sharding import PartitionSpec as P

HD = 128
REQ = 8
BLK = 128
NEGATIVE = -1e30
SCALE = float(HD**-0.5 * np.log2(np.e))


def params(mib=24):
    return pltpu.CompilerParams(vmem_limit_bytes=mib * 2**20)


def cost(flops, moved, exps=0):
    return pl.CostEstimate(flops=int(flops), bytes_accessed=int(moved), transcendentals=int(exps))


def cycle_of(group):
    if group == 2:
        return [0, 2, 4, 6, 7, 5, 3, 1]
    return list(range(REQ))


def pick(table, index):
    result = jnp.int32(table[0])
    for place, value in enumerate(table):
        result = jnp.where(index == place, jnp.int32(value), result)
    return result


def swap(value, axis, mask):
    pairs = [(source, source ^ mask) for source in range(lax.axis_size(axis))]
    return lax.ppermute(value, axis, pairs)


def turn(value, cycle, group, way):
    count = len(cycle)
    pairs = []
    for place in range(count):
        source, target = cycle[place], cycle[(place + way) % count]
        pairs += [(source * group + m, target * group + m) for m in range(group)]
    return lax.ppermute(value, "seq", pairs)


def rotated(vectors, cosine, sine):
    return vectors * cosine + pltpu.roll(vectors, HD // 2, 1) * sine


def position_kernel(lengths, shared, positions):
    rows = positions.shape[0]
    group = lax.axis_size("seq") // REQ
    seq = lax.axis_index("seq")
    start = shared[0] + lengths[seq // group] + (seq % group) * rows
    places = start + lax.broadcasted_iota(jnp.int32, positions.shape, 0)
    positions[...] = places.astype(jnp.float32)


def angles(tail_len, shared_len, rows):
    half = HD // 2
    positions = pl.pallas_call(
        position_kernel,
        in_specs=[SMEM] * 2,
        out_specs=VMEM,
        out_shape=jax.ShapeDtypeStruct((rows, HD), jnp.float32),
        compiler_params=params(8),
        cost_estimate=cost(rows * HD, 4 * rows * HD),
        name="positions",
    )(tail_len, shared_len)
    lane = jnp.arange(HD, dtype=jnp.int32)
    freqs = 10000.0 ** (-(lane % half).astype(jnp.float32) / half)
    angle = positions * freqs
    return jnp.cos(angle), jnp.sin(angle) * jnp.where(lane < half, -1.0, 1.0)


def lanes(start, count=HD):
    return pl.ds(pl.multiple_of(start, HD), count)


def after(value, *others):
    return lax.optimization_barrier((value, *others))[0]


VMEM = pl.BlockSpec(memory_space=pltpu.VMEM)
HBM = pl.BlockSpec(memory_space=pltpu.HBM)
SMEM = pl.BlockSpec(memory_space=pltpu.SMEM)


def viewed(block):
    count, pair, width = block.shape
    heads = width // HD
    return block.reshape(count, pair, heads, HD).transpose(0, 2, 1, 3).reshape(-1, HD)


def order_rows(stride, back):
    rows = 2 * HD
    places = rows // stride
    row = lax.broadcasted_iota(jnp.int32, (rows, rows), 1 if back else 0)
    column = lax.broadcasted_iota(jnp.int32, (rows, rows), 0 if back else 1)
    source = lax.rem(row, places) * stride + lax.div(row, places)
    return jnp.where(column == source, 1.0, 0.0).astype(jnp.bfloat16)


def reordered(order, tiles):
    both = tiles[0] if len(tiles) == 1 else jnp.concatenate(tiles, axis=1)
    mixed = jnp.dot(order, both, preferred_element_type=jnp.float32).astype(jnp.bfloat16)
    return [mixed[:, i * HD : (i + 1) * HD] for i in range(len(tiles))]


def take_apart(block, order, keys, values, offset):
    heads = keys.shape[1] // HD
    stride = 2 * heads
    count = block.shape[0] // stride
    places = 2 * HD // stride
    for start in range(0, count, 2 * places):
        starts = [at for at in (start, start + places) if at < count]
        tiles = [block[at * stride : (at + places) * stride, :] for at in starts]
        for at, tile in zip(starts, reordered(order, tiles)):
            for head in range(heads):
                for j, result in enumerate((keys, values)):
                    line = (2 * head + j) * places
                    result[offset + at : offset + at + places, head * HD : (head + 1) * HD] = tile[
                        line : line + places
                    ]


ACROSS = (((1,), (1,)), ((), ()))


def unit_matrix(size):
    row = lax.broadcasted_iota(jnp.int32, (size, size), 0)
    column = lax.broadcasted_iota(jnp.int32, (size, size), 1)
    return jnp.where(row == column, 1.0, 0.0).astype(jnp.bfloat16)


def turned_over(unit, value):
    return lax.dot_general(unit, value, ACROSS, preferred_element_type=jnp.float32).astype(
        jnp.bfloat16
    )


def turn_heads(values, result):
    unit = unit_matrix(HD)
    for start in range(0, values.shape[1], HD):
        result[start : start + HD, :] = turned_over(unit, values[:, start : start + HD])


def part_kernel(*refs):
    *blocks, keys, turned, token, values = refs
    stride = keys.shape[1] * 2 // HD
    order = order_rows(stride, False)
    offset = 0
    for block in blocks:
        take_apart(block, order, keys, values, offset)
        offset += block.shape[0] // stride
    turn_heads(values, turned)
    token[...] = jnp.zeros_like(token)


TOKEN = jax.ShapeDtypeStruct((8, HD), jnp.float32)


def part_keyval(blocks, width, name):
    count = sum(block.shape[0] for block in blocks) * HD // (2 * width)
    return pl.pallas_call(
        part_kernel,
        in_specs=[VMEM] * len(blocks),
        out_specs=[VMEM] * 3,
        out_shape=[
            jax.ShapeDtypeStruct((count, width), jnp.bfloat16),
            jax.ShapeDtypeStruct((width, count), jnp.bfloat16),
            TOKEN,
        ],
        scratch_shapes=[pltpu.VMEM((count, width), jnp.bfloat16)],
        compiler_params=params(16),
        cost_estimate=cost(2**10 * count * width, 8 * count * width),
        name=name,
    )(*blocks)


def query_kernel(*refs):
    *pieces, weight, cosine, sine, query, normed, token = refs
    token[...] = jnp.zeros_like(token)
    columns = pieces[0].shape[1]
    index = lax.axis_index("tp")
    features = columns * len(pieces)
    values = [piece[...].astype(jnp.float32) for piece in pieces]
    mean = sum(jnp.sum(v, axis=1, keepdims=True) for v in values) / features
    values = [v - mean for v in values]
    spread = sum(jnp.sum(v * v, axis=1, keepdims=True) for v in values) / features
    inverse = lax.rsqrt(spread + 1e-05)
    for shift, v in enumerate(values):
        normed[:, lanes((index ^ shift) * columns, columns)] = (v * inverse).astype(jnp.bfloat16)
    width = weight.shape[1]
    wide = min(width, 2 * HD)
    for base in range(0, width, wide):
        product = jnp.dot(
            normed[...], weight[:, base : base + wide], preferred_element_type=jnp.float32
        )
        for start in range(0, wide, HD):
            query[:, base + start : base + start + HD] = rotated(
                product[:, start : start + HD], cosine[...], sine[...]
            ).astype(jnp.bfloat16)


def project_query(pieces, w_query, cosine, sine):
    rows, columns = pieces[0].shape
    depth, width = w_query.shape
    return pl.pallas_call(
        query_kernel,
        in_specs=[VMEM] * (len(pieces) + 3),
        out_specs=[VMEM] * 3,
        out_shape=[
            jax.ShapeDtypeStruct((rows, width), jnp.bfloat16),
            jax.ShapeDtypeStruct((rows, depth), jnp.bfloat16),
            TOKEN,
        ],
        compiler_params=params(20),
        cost_estimate=cost(2 * rows * depth * width, 2 * depth * width),
        name="project_query",
    )(*pieces, w_query, cosine, sine)


def weight_kernel(weight, result, token, near, arrived):
    slots, chunk = near.shape[:2]
    count = weight.shape[0] // chunk
    stride = result.shape[2] * 2 // HD
    copies = [
        pltpu.make_async_copy(
            weight.at[pl.ds(i * chunk, chunk)], near.at[i % slots], arrived.at[i]
        )
        for i in range(count)
    ]
    for copy in copies[:slots]:
        copy.start()
    order = order_rows(stride, False)
    for i, copy in enumerate(copies):
        copy.wait()
        take_apart(near.at[i % slots], order, result.at[0], result.at[1], i * chunk // stride)
        if i + slots < count:
            copies[i + slots].start()
    token[...] = jnp.zeros_like(token)


def part_weights(w_keyval):
    depth, _, width = w_keyval.shape
    weight = viewed(w_keyval)
    count = max(depth // 256, 1)
    chunk = weight.shape[0] // count
    return pl.pallas_call(
        weight_kernel,
        in_specs=[HBM],
        out_specs=[VMEM] * 2,
        out_shape=[jax.ShapeDtypeStruct((2, depth, width), jnp.bfloat16), TOKEN],
        scratch_shapes=[
            pltpu.VMEM((count, chunk, HD), jnp.bfloat16),
            pltpu.SemaphoreType.DMA((count,)),
        ],
        compiler_params=params(38),
        cost_estimate=cost(2**10 * depth * width, 8 * depth * width),
        name="part_weights",
    )(weight)


def keyval_kernel(normed, weight, cosine, sine, keys, turned, cache, values):
    rows = normed.shape[0]
    heads = weight.shape[2] // HD
    stride = 2 * heads
    for head in range(heads):
        span = slice(head * HD, (head + 1) * HD)
        product = jnp.dot(
            normed[...],
            jnp.concatenate([weight[0, :, span], weight[1, :, span]], axis=1),
            preferred_element_type=jnp.float32,
        )
        keys[:, span] = rotated(product[:, :HD], cosine[...], sine[...]).astype(jnp.bfloat16)
        values[:, span] = product[:, HD:].astype(jnp.bfloat16)
    turn_heads(values, turned)
    order = order_rows(stride, True)
    places = 2 * HD // stride
    for start in range(0, rows, 2 * places):
        starts = [at for at in (start, start + places) if at < rows]
        tiles = [
            jnp.concatenate(
                [
                    pair[at : at + places, head * HD : (head + 1) * HD]
                    for head in range(heads)
                    for pair in (keys, values)
                ],
                axis=0,
            )
            for at in starts
        ]
        for at, tile in zip(starts, reordered(order, tiles)):
            cache[at * stride : (at + places) * stride, :] = tile


def project_keyval(normed, weight, cosine, sine):
    rows, depth = normed.shape
    width = weight.shape[2]
    heads = width // HD
    keys, turned, cache = pl.pallas_call(
        keyval_kernel,
        in_specs=[VMEM] * 4,
        out_specs=[VMEM] * 3,
        out_shape=[
            jax.ShapeDtypeStruct((rows, width), jnp.bfloat16),
            jax.ShapeDtypeStruct((width, rows), jnp.bfloat16),
            jax.ShapeDtypeStruct((rows * heads * 2, HD), jnp.bfloat16),
        ],
        scratch_shapes=[pltpu.VMEM((rows, width), jnp.bfloat16)],
        compiler_params=params(20),
        cost_estimate=cost(4 * rows * depth * width, 4 * depth * width),
        name="project_keyval",
    )(normed, weight, cosine, sine)
    cache = cache.reshape(rows, heads, 2, HD).transpose(0, 2, 1, 3)
    return keys, turned, cache.reshape(rows, 2, width)


def attend_kernel(spec, *refs):
    group, shifts, rings, slots, piece, parted, first, last = spec
    refs = list(refs)
    take = lambda count: [refs.pop(0) for _ in range(count)]
    lengths, shared, table = take(3)
    queries = take(len(shifts))
    if parted:
        blocks = take(2 * parted)
        sources = list(zip(blocks[::2], blocks[1::2]))
    else:
        raw = take(len(rings))
    if not first:
        old_mixes, old_extents = take(len(shifts)), take(len(shifts))
    results = take(len(shifts))
    extents = [None if last and shift else take(1)[0] for shift in shifts]
    token, bias, first_scores, second_scores = take(4)
    extents = [take(1)[0] if extent is None else extent for extent in extents]
    if parted:
        causal = take(1)[0]
    else:
        keys_here, turned_here, values_here = take(3)
        sources = [(keys_here, turned_here)]
    rows, width = queries[0].shape
    heads = width // HD
    cycle = cycle_of(group)
    seq = lax.axis_index("seq")
    request, member = seq // group, seq % group
    place = pick(list(np.argsort(cycle)), request)
    edges = []
    count = 0
    for i in range(slots):
        wanted = seq * slots + i
        number = jnp.int32(0)
        for j in range(table.shape[0]):
            number = jnp.where(table[j, request] == wanted, jnp.int32(j), number)
        edges.append((count, BLK, number * BLK, lengths[request]))
        count += BLK
    for step, begin, size in rings:
        origin = pick(cycle, lax.rem(place + step + REQ, REQ))
        edges.append((count, size, (origin * group + member) * piece + begin, shared[0]))
        count += size
    for begin, size, start, length in edges:
        positions = start + lax.broadcasted_iota(jnp.int32, (size, HD), 0)
        lane = lax.broadcasted_iota(jnp.int32, (size, HD), 1)
        bias[begin : begin + size, :] = jnp.where(
            (positions >= length) & (lane == 0), NEGATIVE, 0.0
        ).astype(jnp.bfloat16)
    if parted:
        bias[count : count + rows, :] = jnp.zeros((rows, HD), jnp.bfloat16)
        theirs = member * rows + lax.broadcasted_iota(jnp.int32, (rows, rows), 0)
        for i, shift in enumerate(shifts):
            mine = (member ^ shift) * rows + lax.broadcasted_iota(jnp.int32, (rows, rows), 1)
            causal[:, i * rows : (i + 1) * rows] = jnp.where(theirs <= mine, 0.0, NEGATIVE)
    else:
        offset = 0
        order = order_rows(2 * heads, False)
        for block in raw:
            take_apart(block, order, keys_here, values_here, offset)
            offset += block.shape[0] // (2 * heads)
        turn_heads(values_here, turned_here)
    token[...] = jnp.zeros_like(token)
    many = len(shifts) * rows
    unit = jnp.where(lax.broadcasted_iota(jnp.int32, (many, HD), 1) == 0, 1.0, 0.0)
    unit = unit.astype(jnp.bfloat16)
    chunks = []
    begin = 0
    for source in sources:
        length = source[0].shape[0]
        for start in range(0, length, 2 * HD):
            size = min(2 * HD, length - start)
            chunks.append((source, start, size, begin + start, parted and begin == count))
        begin += length

    def beside(values, axis):
        return values[0] if len(values) == 1 else jnp.concatenate(values, axis=axis)

    def start_head(head):
        span = lanes(head * HD)
        query = jnp.concatenate([beside([q[:, span] for q in queries], 0), unit], axis=1)
        return span, query

    def score(state, chunk, scores, top):
        span, query = state
        (keys, _), start, size, at, masked = chunk
        keys = jnp.concatenate([keys[start : start + size, span], bias[at : at + size, :]], axis=1)
        part = lax.dot_general(keys, query, ACROSS, preferred_element_type=jnp.float32)
        if masked:
            part = part + causal[start : start + size, :]
        scores[at : at + size, :] = part
        here = jnp.max(part, axis=0, keepdims=True)
        return here if top is None else jnp.maximum(top, here)

    def mix(span, chunk, scores, top, summed, mixed):
        (_, turned), start, size, at, _ = chunk
        weights = jnp.exp2((scores[at : at + size, :] - top) * SCALE)
        here = jnp.sum(weights, axis=0, keepdims=True)
        product = jnp.dot(
            turned[span, start : start + size],
            weights.astype(jnp.bfloat16),
            preferred_element_type=jnp.float32,
        )
        return (here, product) if summed is None else (summed + here, mixed + product)

    def one_head(head, scores, top, following, next_scores):
        span = lanes(head * HD)
        line = pl.ds(head, 1)
        if not first:
            old = beside([extent[line, :] for extent in old_extents], 1)
            top = jnp.maximum(top, old * (1.0 / SCALE))
        state = start_head(following)
        next_top = summed = mixed = None
        for chunk in chunks:
            next_top = score(state, chunk, next_scores, next_top)
            summed, mixed = mix(span, chunk, scores, top, summed, mixed)
        if not first:
            factor = jnp.exp2(old - top * SCALE)
            summed = summed + factor
            mixed = mixed + beside([old_mix[span, :] for old_mix in old_mixes], 1) * factor
        mixed = mixed * (1.0 / summed)
        extent = top * SCALE + jnp.log2(summed)
        for i, result in enumerate(results):
            columns = slice(i * rows, (i + 1) * rows)
            extents[i][line, :] = extent[:, columns]
            result[span, :] = mixed[:, columns].astype(result.dtype)
        return next_top

    def two_heads(i, top):
        top = one_head(2 * i, first_scores, top, 2 * i + 1, second_scores)
        following = jnp.minimum(2 * i + 2, heads - 1)
        return one_head(2 * i + 1, second_scores, top, following, first_scores)

    state = start_head(0)
    top = None
    for chunk in chunks:
        top = score(state, chunk, first_scores, top)
    lax.fori_loop(0, heads // 2, two_heads, top)
    for i, shift in enumerate(shifts):
        if last and shift:
            line = extents[i][:heads, :]
            packed = []
            for _ in range(3):
                rounded = line.astype(jnp.bfloat16).astype(jnp.float32)
                packed.append(rounded)
                line = line - rounded
            gap = stat_rows(heads) - 3 * heads
            if gap:
                packed.append(jnp.zeros((gap, rows), jnp.float32))
            results[i][width:, :] = jnp.concatenate(packed, axis=0).astype(jnp.bfloat16)


def stat_rows(heads):
    return -(-3 * heads // 16) * 16


def attend(facts, queries, shifts, rings, slots, piece, blocks, parted, old, last, name):
    group = len(queries)
    queries = [queries[shift] for shift in shifts]
    rows, width = queries[0].shape
    heads = width // HD
    parted = len(blocks) // 2 if parted else 0
    operands = [*facts, *queries, *blocks]
    if old:
        operands += [old[shift][0] for shift in shifts] + [old[shift][1] for shift in shifts]
    count = sum(size for _, _, size in rings) + BLK * slots + (rows if parted else 0)
    many = len(shifts) * rows
    scratch = [pltpu.VMEM((count, HD), jnp.bfloat16)]
    scratch += [pltpu.VMEM((count, many), jnp.float32)] * 2
    lines = (max(heads, 8), rows)
    scratch += [pltpu.VMEM(lines, jnp.float32) for shift in shifts if last and shift]
    if parted:
        scratch.append(pltpu.VMEM((rows, many), jnp.float32))
    else:
        scratch += [
            pltpu.VMEM((count, width), jnp.bfloat16),
            pltpu.VMEM((width, count), jnp.bfloat16),
            pltpu.VMEM((count, width), jnp.bfloat16),
        ]
    mixes = [
        jax.ShapeDtypeStruct((width + stat_rows(heads), rows), jnp.bfloat16)
        if last and shift
        else jax.ShapeDtypeStruct((width, rows), jnp.float32)
        for shift in shifts
    ]
    extents = [
        jax.ShapeDtypeStruct(lines, jnp.float32) for shift in shifts if not (last and shift)
    ]
    scores = len(shifts) * rows * count * heads
    results = pl.pallas_call(
        functools.partial(
            attend_kernel, (group, shifts, rings, slots, piece, parted, not old, last)
        ),
        in_specs=[SMEM] * 3 + [VMEM] * (len(operands) - 3),
        out_specs=[VMEM] * (len(mixes) + len(extents) + 1),
        out_shape=[*mixes, *extents, TOKEN],
        scratch_shapes=scratch,
        compiler_params=params(24),
        cost_estimate=cost(4 * scores * HD, 4 * count * width, scores),
        name=name,
    )(*operands)
    if last:
        return results
    state = {shift: (results[i], results[len(shifts) + i]) for i, shift in enumerate(shifts)}
    return state, results[-1]


def combine_kernel(*refs):
    result, extent, *parts, weight, attended, sent = refs
    width, rows = result.shape
    heads = width // HD
    extents = [extent[:heads, :]]
    for part in parts:
        lines = part[width:, :].astype(jnp.float32)
        extents.append(sum(lines[i * heads : (i + 1) * heads] for i in range(3)))
    top = functools.reduce(jnp.maximum, extents)
    shares = [jnp.exp2(extent - top) for extent in extents]
    whole = sum(shares)
    shares = [share / whole for share in shares]
    unit = unit_matrix(rows)
    for head in range(heads):
        span = slice(head * HD, (head + 1) * HD)
        mixes = [result[span, :]] + [part[span, :].astype(jnp.float32) for part in parts]
        mixed = sum(mix * share[head : head + 1] for mix, share in zip(mixes, shares))
        attended[:, span] = turned_over(unit, mixed.astype(jnp.bfloat16))
    index = lax.axis_index("tp")
    ways = sent.shape[0] + 1
    columns = weight.shape[1] // ways
    for shift in range(1, ways):
        sent[shift - 1] = jnp.dot(
            attended[...],
            weight[:, lanes((index ^ shift) * columns, columns)],
            preferred_element_type=jnp.float32,
        ).astype(jnp.bfloat16)


def combine(result, extent, parts, w_out, ways):
    width, rows = result.shape
    columns = w_out.shape[1] // ways
    return pl.pallas_call(
        combine_kernel,
        in_specs=[VMEM] * (3 + len(parts)),
        out_specs=[VMEM] * 2,
        out_shape=[
            jax.ShapeDtypeStruct((rows, width), jnp.bfloat16),
            jax.ShapeDtypeStruct((ways - 1, rows, columns), jnp.bfloat16),
        ],
        compiler_params=params(20),
        cost_estimate=cost(2 * rows * width * columns * (ways - 1), 2 * width * w_out.shape[1]),
        name="combine_send",
    )(result, extent, *parts, w_out)


def keep_kernel(attended, weight, hidden, kept):
    columns = hidden.shape[1]
    product = jnp.dot(
        attended[...],
        weight[:, lanes(lax.axis_index("tp") * columns, columns)],
        preferred_element_type=jnp.float32,
    )
    kept[...] = product + hidden[...].astype(jnp.float32)


def keep(attended, w_out, hidden):
    rows, width = attended.shape
    return pl.pallas_call(
        keep_kernel,
        in_specs=[VMEM] * 3,
        out_specs=VMEM,
        out_shape=jax.ShapeDtypeStruct(hidden.shape, jnp.float32),
        compiler_params=params(20),
        cost_estimate=cost(2 * rows * width * hidden.shape[1], 2 * width * w_out.shape[1]),
        name="keep_own",
    )(attended, w_out, hidden)


def local(
    hidden_in, w_query, w_keyval, w_out, prompt_cache, tail_cache, tail_table, tail_len, shared_len
):
    rows = hidden_in.shape[0]
    group = lax.axis_size("seq") // REQ
    ways = lax.axis_size("tp")
    cycle = cycle_of(group)
    half = REQ // 2
    piece = prompt_cache.shape[0]
    middle = piece // 2
    width = w_query.shape[1]
    stride = 2 * width // HD

    pieces = [hidden_in] + [swap(hidden_in, "tp", shift) for shift in range(1, ways)]
    prompt = viewed(prompt_cache)
    ahead, behind = [prompt], [prompt]

    def step(*others):
        for blocks, way in ((ahead, 1), (behind, -1)):
            blocks.append(turn(after(blocks[-1], *others), cycle, group, way))

    step()
    cosine, sine = angles(tail_len, shared_len, rows)
    weight, weight_token = part_weights(w_keyval)
    pieces[0] = after(pieces[0], weight_token)
    query, normed, query_token = project_query(pieces, w_query, cosine, sine)
    queries = [query] + [swap(query, "seq", shift) for shift in range(1, group)]
    tail = viewed(tail_cache.reshape(-1, 2, tail_cache.shape[3]))
    slots = tail_cache.shape[0]
    *own_block, token = part_keyval([tail, prompt], width, "part_own")
    step(token, weight_token, query_token)
    *near_block, token = part_keyval([ahead[1], behind[1]], width, "part_near")
    fresh_keys, fresh_turned, new_cache = project_keyval(normed, weight, cosine, sine)

    table = tail_table.T
    facts = (tail_len, shared_len, table)
    others = list(range(1, group))
    near = (
        [(0, 0, piece), (-1, 0, piece), (1, 0, piece)],
        slots,
        piece,
        [*own_block, *near_block, fresh_keys, fresh_turned],
        True,
        None,
        False,
    )
    state, token = attend(facts, queries, [0], *near, "attend_near_own")
    step(token)
    ready = (after(tail_len, token), shared_len, table)
    state_others, token = attend(ready, queries, others, *near, "attend_near_others")
    state |= state_others
    rings = [(-2, 0, piece), (2, 0, piece)]
    second = (rings, 0, piece, [ahead[2], behind[2]], False, state, False, "attend_second")
    state, token = attend(facts, queries, [0, *others], *second)
    far_low = turn(after(ahead[3], token)[: middle * stride], cycle, group, 1)
    far_high = turn(after(behind[3], token)[middle * stride :], cycle, group, -1)
    rings = [(-3, 0, piece), (3, 0, piece)]
    third = (rings, 0, piece, [ahead[3], behind[3]], False, state, False, "attend_third")
    state, token = attend(facts, queries, [0, *others], *third)
    rings = [(-half, 0, middle), (half, middle, piece - middle)]
    far = (rings, 0, piece, [far_low, far_high], False, state, True)
    *parts, token = attend(facts, queries, others, *far, "attend_far_others")
    ready = (after(tail_len, token), shared_len, table)
    result, extent, token = attend(ready, queries, [0], *far, "attend_far_own")
    parts = [swap(part, "seq", shift + 1) for shift, part in enumerate(parts)]
    attended, sent = combine(result, extent, parts, w_out, ways)
    received = [swap(sent[shift - 1], "tp", shift) for shift in range(1, ways)]
    total = keep(attended, w_out, hidden_in)
    for part in received:
        total = total + part.astype(jnp.float32)
    return (total.astype(jnp.bfloat16), new_cache)


def solution(mesh):
    return jax.shard_map(
        local,
        mesh=mesh,
        in_specs=(
            P("seq", "tp"),
            P(None, "tp"),
            P(None, None, "tp"),
            P("tp", None),
            P("seq", None, "tp"),
            P("seq", None, None, "tp"),
            P(),
            P(),
            P(),
        ),
        out_specs=(P("seq", "tp"), P("seq", None, "tp")),
        check_vma=False,
    )
```

```python
import functools

import jax
import jax.numpy as jnp
import numpy as np
from jax import lax
from jax.experimental import pallas as pl
from jax.experimental.pallas import tpu as pltpu
from jax.sharding import PartitionSpec as P

HD = 128
REQ = 8
BLK = 128
NEGATIVE = -1e30
SCALE = float(HD**-0.5 * np.log2(np.e))


def params(mib=24):
    return pltpu.CompilerParams(vmem_limit_bytes=mib * 2**20)


def cost(flops, moved, exps=0):
    return pl.CostEstimate(flops=int(flops), bytes_accessed=int(moved), transcendentals=int(exps))


def cycle_of(group):
    if group == 2:
        return [0, 2, 4, 6, 7, 5, 3, 1]
    return list(range(REQ))


def pick(table, index):
    result = jnp.int32(table[0])
    for place, value in enumerate(table):
        result = jnp.where(index == place, jnp.int32(value), result)
    return result


def swap(value, axis, mask):
    pairs = [(source, source ^ mask) for source in range(lax.axis_size(axis))]
    return lax.ppermute(value, axis, pairs)


def turn(value, cycle, group, way):
    count = len(cycle)
    pairs = []
    for place in range(count):
        source, target = cycle[place], cycle[(place + way) % count]
        pairs += [(source * group + m, target * group + m) for m in range(group)]
    return lax.ppermute(value, "seq", pairs)


def rotated(vectors, cosine, sine):
    return vectors * cosine + pltpu.roll(vectors, HD // 2, 1) * sine


def position_kernel(lengths, shared, positions):
    rows = positions.shape[0]
    group = lax.axis_size("seq") // REQ
    seq = lax.axis_index("seq")
    start = shared[0] + lengths[seq // group] + (seq % group) * rows
    places = start + lax.broadcasted_iota(jnp.int32, positions.shape, 0)
    positions[...] = places.astype(jnp.float32)


def angles(tail_len, shared_len, rows):
    half = HD // 2
    positions = pl.pallas_call(
        position_kernel,
        in_specs=[SMEM] * 2,
        out_specs=VMEM,
        out_shape=jax.ShapeDtypeStruct((rows, HD), jnp.float32),
        compiler_params=params(8),
        cost_estimate=cost(rows * HD, 4 * rows * HD),
        name="positions",
    )(tail_len, shared_len)
    lane = jnp.arange(HD, dtype=jnp.int32)
    freqs = 10000.0 ** (-(lane % half).astype(jnp.float32) / half)
    angle = positions * freqs
    return jnp.cos(angle), jnp.sin(angle) * jnp.where(lane < half, -1.0, 1.0)


def lanes(start, count=HD):
    if isinstance(start, int):
        return pl.ds(start, count)
    return pl.ds(pl.multiple_of(start, HD), count)


def after(value, *others):
    return lax.optimization_barrier((value, *others))[0]


VMEM = pl.BlockSpec(memory_space=pltpu.VMEM)
HBM = pl.BlockSpec(memory_space=pltpu.HBM)
SMEM = pl.BlockSpec(memory_space=pltpu.SMEM)


def viewed(block):
    count, pair, width = block.shape
    heads = width // HD
    return block.reshape(count, pair, heads, HD).transpose(0, 2, 1, 3).reshape(-1, HD)


def order_rows(stride, back):
    rows = 2 * HD
    places = rows // stride
    row = lax.broadcasted_iota(jnp.int32, (rows, rows), 1 if back else 0)
    column = lax.broadcasted_iota(jnp.int32, (rows, rows), 0 if back else 1)
    source = lax.rem(row, places) * stride + lax.div(row, places)
    return jnp.where(column == source, 1.0, 0.0).astype(jnp.bfloat16)


def reordered(order, tiles):
    both = tiles[0] if len(tiles) == 1 else jnp.concatenate(tiles, axis=1)
    mixed = jnp.dot(order, both, preferred_element_type=jnp.float32).astype(jnp.bfloat16)
    return [mixed[:, i * HD : (i + 1) * HD] for i in range(len(tiles))]


def take_apart(block, order, keys, values, offset):
    heads = keys.shape[1] // HD
    stride = 2 * heads
    count = block.shape[0] // stride
    places = 2 * HD // stride
    for start in range(0, count, 2 * places):
        starts = [at for at in (start, start + places) if at < count]
        tiles = [block[at * stride : (at + places) * stride, :] for at in starts]
        for at, tile in zip(starts, reordered(order, tiles)):
            for head in range(heads):
                for j, result in enumerate((keys, values)):
                    line = (2 * head + j) * places
                    result[offset + at : offset + at + places, head * HD : (head + 1) * HD] = tile[
                        line : line + places
                    ]


ACROSS = (((1,), (1,)), ((), ()))


def unit_matrix(size):
    row = lax.broadcasted_iota(jnp.int32, (size, size), 0)
    column = lax.broadcasted_iota(jnp.int32, (size, size), 1)
    return jnp.where(row == column, 1.0, 0.0).astype(jnp.bfloat16)


def turned_over(unit, value):
    return lax.dot_general(unit, value, ACROSS, preferred_element_type=jnp.float32).astype(
        jnp.bfloat16
    )


def turn_heads(values, result):
    unit = unit_matrix(HD)
    for start in range(0, values.shape[1], HD):
        result[start : start + HD, :] = turned_over(unit, values[:, start : start + HD])


def part_kernel(*refs):
    *blocks, keys, turned, values = refs
    stride = keys.shape[1] * 2 // HD
    order = order_rows(stride, False)
    offset = 0
    for block in blocks:
        take_apart(block, order, keys, values, offset)
        offset += block.shape[0] // stride
    turn_heads(values, turned)


def part_keyval(blocks, width, name):
    count = sum(block.shape[0] for block in blocks) * HD // (2 * width)
    return pl.pallas_call(
        part_kernel,
        in_specs=[VMEM] * len(blocks),
        out_specs=[VMEM] * 2,
        out_shape=[
            jax.ShapeDtypeStruct((count, width), jnp.bfloat16),
            jax.ShapeDtypeStruct((width, count), jnp.bfloat16),
        ],
        scratch_shapes=[pltpu.VMEM((count, width), jnp.bfloat16)],
        compiler_params=params(16),
        cost_estimate=cost(2**10 * count * width, 8 * count * width),
        name=name,
    )(*blocks)


def query_kernel(*refs):
    *pieces, weight, cosine, sine, query, normed = refs
    columns = pieces[0].shape[1]
    index = lax.axis_index("tp")
    features = columns * len(pieces)
    values = [piece[...].astype(jnp.float32) for piece in pieces]
    mean = sum(jnp.sum(v, axis=1, keepdims=True) for v in values) / features
    values = [v - mean for v in values]
    spread = sum(jnp.sum(v * v, axis=1, keepdims=True) for v in values) / features
    inverse = lax.rsqrt(spread + 1e-05)
    for shift, v in enumerate(values):
        normed[:, lanes((index ^ shift) * columns, columns)] = (v * inverse).astype(jnp.bfloat16)
    width = weight.shape[1]
    wide = min(width, 2 * HD)
    for base in range(0, width, wide):
        product = jnp.dot(
            normed[...], weight[:, base : base + wide], preferred_element_type=jnp.float32
        )
        for start in range(0, wide, HD):
            query[:, base + start : base + start + HD] = rotated(
                product[:, start : start + HD], cosine[...], sine[...]
            ).astype(jnp.bfloat16)


def project_query(pieces, w_query, cosine, sine):
    rows, columns = pieces[0].shape
    depth, width = w_query.shape
    return pl.pallas_call(
        query_kernel,
        in_specs=[VMEM] * (len(pieces) + 3),
        out_specs=[VMEM] * 2,
        out_shape=[
            jax.ShapeDtypeStruct((rows, width), jnp.bfloat16),
            jax.ShapeDtypeStruct((rows, depth), jnp.bfloat16),
        ],
        compiler_params=params(20),
        cost_estimate=cost(2 * rows * depth * width, 2 * depth * width),
        name="project_query",
    )(*pieces, w_query, cosine, sine)


def weight_kernel(weight, result, near, arrived):
    slots, chunk = near.shape[:2]
    count = weight.shape[0] // chunk
    stride = result.shape[2] * 2 // HD
    copies = [
        pltpu.make_async_copy(
            weight.at[pl.ds(i * chunk, chunk)], near.at[i % slots], arrived.at[i]
        )
        for i in range(count)
    ]
    for copy in copies[:slots]:
        copy.start()
    order = order_rows(stride, False)
    for i, copy in enumerate(copies):
        copy.wait()
        take_apart(near.at[i % slots], order, result.at[0], result.at[1], i * chunk // stride)
        if i + slots < count:
            copies[i + slots].start()


def part_weights(w_keyval):
    depth, _, width = w_keyval.shape
    weight = viewed(w_keyval)
    count = max(depth // 256, 1)
    chunk = weight.shape[0] // count
    return pl.pallas_call(
        weight_kernel,
        in_specs=[HBM],
        out_specs=VMEM,
        out_shape=jax.ShapeDtypeStruct((2, depth, width), jnp.bfloat16),
        scratch_shapes=[
            pltpu.VMEM((count, chunk, HD), jnp.bfloat16),
            pltpu.SemaphoreType.DMA((count,)),
        ],
        compiler_params=params(38),
        cost_estimate=cost(2**10 * depth * width, 8 * depth * width),
        name="part_weights",
    )(weight)


def keyval_kernel(normed, weight, cosine, sine, keys, turned, cache, values):
    rows = normed.shape[0]
    heads = weight.shape[2] // HD
    stride = 2 * heads
    for head in range(heads):
        span = slice(head * HD, (head + 1) * HD)
        product = jnp.dot(
            normed[...],
            jnp.concatenate([weight[0, :, span], weight[1, :, span]], axis=1),
            preferred_element_type=jnp.float32,
        )
        keys[:, span] = rotated(product[:, :HD], cosine[...], sine[...]).astype(jnp.bfloat16)
        values[:, span] = product[:, HD:].astype(jnp.bfloat16)
    turn_heads(values, turned)
    order = order_rows(stride, True)
    places = 2 * HD // stride
    for start in range(0, rows, 2 * places):
        starts = [at for at in (start, start + places) if at < rows]
        tiles = [
            jnp.concatenate(
                [
                    pair[at : at + places, head * HD : (head + 1) * HD]
                    for head in range(heads)
                    for pair in (keys, values)
                ],
                axis=0,
            )
            for at in starts
        ]
        for at, tile in zip(starts, reordered(order, tiles)):
            cache[at * stride : (at + places) * stride, :] = tile


def project_keyval(normed, weight, cosine, sine):
    rows, depth = normed.shape
    width = weight.shape[2]
    heads = width // HD
    keys, turned, cache = pl.pallas_call(
        keyval_kernel,
        in_specs=[VMEM] * 4,
        out_specs=[VMEM] * 3,
        out_shape=[
            jax.ShapeDtypeStruct((rows, width), jnp.bfloat16),
            jax.ShapeDtypeStruct((width, rows), jnp.bfloat16),
            jax.ShapeDtypeStruct((rows * heads * 2, HD), jnp.bfloat16),
        ],
        scratch_shapes=[pltpu.VMEM((rows, width), jnp.bfloat16)],
        compiler_params=params(20),
        cost_estimate=cost(4 * rows * depth * width, 4 * depth * width),
        name="project_keyval",
    )(normed, weight, cosine, sine)
    cache = cache.reshape(rows, heads, 2, HD).transpose(0, 2, 1, 3)
    return keys, turned, cache.reshape(rows, 2, width)


def attend_kernel(spec, *refs):
    group, shifts, rings, slots, piece, parted, first, last = spec
    fresh = slots > 0
    refs = list(refs)
    take = lambda count: [refs.pop(0) for _ in range(count)]
    lengths, shared, table = take(3)
    queries = take(len(shifts))
    if parted:
        blocks = take(2 * parted)
        sources = list(zip(blocks[::2], blocks[1::2]))
    else:
        raw = take(len(rings))
    if not first:
        old_mixes, old_extents = take(len(shifts)), take(len(shifts))
    results = take(len(shifts))
    extents = [None if last and shift else take(1)[0] for shift in shifts]
    if not parted:
        sources = [tuple(take(2))]
    bias, first_scores, second_scores = take(3)
    extents = [take(1)[0] if extent is None else extent for extent in extents]
    if fresh:
        causal = take(1)[0]
    if not parted:
        values_here = take(1)[0]
        keys_here, turned_here = sources[0]
    rows, width = queries[0].shape
    heads = width // HD
    cycle = cycle_of(group)
    seq = lax.axis_index("seq")
    request, member = seq // group, seq % group
    place = pick(list(np.argsort(cycle)), request)
    edges = []
    count = 0
    for i in range(slots):
        wanted = seq * slots + i
        number = jnp.int32(0)
        for j in range(table.shape[0]):
            number = jnp.where(table[j, request] == wanted, jnp.int32(j), number)
        edges.append((count, BLK, number * BLK, lengths[request]))
        count += BLK
    for step, begin, size in rings:
        origin = pick(cycle, lax.rem(place + step + REQ, REQ))
        edges.append((count, size, (origin * group + member) * piece + begin, shared[0]))
        count += size
    for begin, size, start, length in edges:
        positions = start + lax.broadcasted_iota(jnp.int32, (size, HD), 0)
        lane = lax.broadcasted_iota(jnp.int32, (size, HD), 1)
        bias[begin : begin + size, :] = jnp.where(
            (positions >= length) & (lane == 0), NEGATIVE, 0.0
        ).astype(jnp.bfloat16)
    if fresh:
        bias[count : count + rows, :] = jnp.zeros((rows, HD), jnp.bfloat16)
        theirs = member * rows + lax.broadcasted_iota(jnp.int32, (rows, rows), 0)
        for i, shift in enumerate(shifts):
            mine = (member ^ shift) * rows + lax.broadcasted_iota(jnp.int32, (rows, rows), 1)
            causal[:, i * rows : (i + 1) * rows] = jnp.where(theirs <= mine, 0.0, NEGATIVE)
    if not parted:
        offset = 0
        order = order_rows(2 * heads, False)
        for block in raw:
            take_apart(block, order, keys_here, values_here, offset)
            offset += block.shape[0] // (2 * heads)
        turn_heads(values_here, turned_here)
    many = len(shifts) * rows
    unit = jnp.where(lax.broadcasted_iota(jnp.int32, (many, HD), 1) == 0, 1.0, 0.0)
    unit = unit.astype(jnp.bfloat16)
    chunks = []
    begin = 0
    for source in sources:
        length = source[0].shape[0]
        for start in range(0, length, 2 * HD):
            size = min(2 * HD, length - start)
            chunks.append((source, start, size, begin + start, fresh and begin == count))
        begin += length

    def beside(values, axis):
        return values[0] if len(values) == 1 else jnp.concatenate(values, axis=axis)

    def query_of(head):
        return jnp.concatenate([beside([q[:, lanes(head * HD)] for q in queries], 0), unit], axis=1)

    def score(head, query, chunk, scores, top):
        (keys, _), start, size, at, masked = chunk
        keys = keys[start : start + size, lanes(head * HD)]
        keys = jnp.concatenate([keys, bias[at : at + size, :]], axis=1)
        part = lax.dot_general(keys, query, ACROSS, preferred_element_type=jnp.float32)
        if masked:
            part = part + causal[start : start + size, :]
        scores[at : at + size, :] = part
        here = jnp.max(part, axis=0, keepdims=True)
        return here if top is None else jnp.maximum(top, here)

    def mix(head, chunk, scores, top, sums):
        (_, turned), start, size, at, _ = chunk
        weights = jnp.exp2((scores[at : at + size, :] - top) * SCALE)
        here = jnp.sum(weights, axis=0, keepdims=True)
        product = jnp.dot(
            turned[lanes(head * HD), start : start + size],
            weights.astype(jnp.bfloat16),
            preferred_element_type=jnp.float32,
        )
        return (here, product) if sums is None else (sums[0] + here, sums[1] + product)

    together = min(heads // 2, 4 if count <= 256 else 1)

    def some_heads(base, scores, tops, following, next_scores):
        span = lambda k: lanes((base + k) * HD)
        line = lambda k: pl.ds(base + k, 1)
        each = range(together)
        if not first:
            olds = [beside([extent[line(k), :] for extent in old_extents], 1) for k in each]
            tops = [jnp.maximum(top, old * (1.0 / SCALE)) for top, old in zip(tops, olds)]
        next_tops = [None] * together
        sums = [None] * together
        if following is not None:
            next_queries = [query_of(following + k) for k in each]
        for chunk in chunks:
            for k in each:
                if following is not None:
                    next_tops[k] = score(
                        following + k, next_queries[k], chunk, next_scores.at[k], next_tops[k]
                    )
                sums[k] = mix(base + k, chunk, scores.at[k], tops[k], sums[k])
        for k in each:
            summed, mixed = sums[k]
            if not first:
                factor = jnp.exp2(olds[k] - tops[k] * SCALE)
                summed = summed + factor
                old_mix = beside([old_mix[span(k), :] for old_mix in old_mixes], 1)
                mixed = mixed + old_mix * factor
            mixed = mixed * (1.0 / summed)
            extent = tops[k] * SCALE + jnp.log2(summed)
            for i, result in enumerate(results):
                columns = slice(i * rows, (i + 1) * rows)
                extents[i][line(k), :] = extent[:, columns]
                result[span(k), :] = mixed[:, columns].astype(result.dtype)
        return next_tops

    def two_parts(i, tops):
        base = 2 * together * i
        tops = some_heads(base, first_scores, tops, base + together, second_scores)
        following = jnp.minimum(base + 2 * together, heads - together)
        return some_heads(base + together, second_scores, tops, following, first_scores)

    tops = []
    for k in range(together):
        query, top = query_of(k), None
        for chunk in chunks:
            top = score(k, query, chunk, first_scores.at[k], top)
        tops.append(top)
    if heads == 2 * together:
        tops = some_heads(0, first_scores, tops, together, second_scores)
        some_heads(together, second_scores, tops, None, None)
    else:
        lax.fori_loop(0, heads // (2 * together), two_parts, tops)
    for i, shift in enumerate(shifts):
        if last and shift:
            line = extents[i][:heads, :]
            packed = []
            for _ in range(3):
                rounded = line.astype(jnp.bfloat16).astype(jnp.float32)
                packed.append(rounded)
                line = line - rounded
            gap = stat_rows(heads) - 3 * heads
            if gap:
                packed.append(jnp.zeros((gap, rows), jnp.float32))
            results[i][width:, :] = jnp.concatenate(packed, axis=0).astype(jnp.bfloat16)


def stat_rows(heads):
    return -(-3 * heads // 16) * 16


def attend(facts, queries, shifts, rings, slots, piece, blocks, parted, old, last, name):
    group = len(queries)
    queries = [queries[shift] for shift in shifts]
    rows, width = queries[0].shape
    heads = width // HD
    parted = len(blocks) // 2 if parted else 0
    operands = [*facts, *queries, *blocks]
    if old:
        operands += [old[shift][0] for shift in shifts] + [old[shift][1] for shift in shifts]
    count = sum(size for _, _, size in rings) + BLK * slots + (rows if slots else 0)
    many = len(shifts) * rows
    scratch = [pltpu.VMEM((count, HD), jnp.bfloat16)]
    together = min(heads // 2, 4 if count <= 256 else 1)
    scratch += [pltpu.VMEM((together, count, many), jnp.float32)] * 2
    lines = (max(heads, 8), rows)
    scratch += [pltpu.VMEM(lines, jnp.float32) for shift in shifts if last and shift]
    if slots:
        scratch.append(pltpu.VMEM((rows, many), jnp.float32))
    if not parted:
        scratch.append(pltpu.VMEM((count, width), jnp.bfloat16))
    mixes = [
        jax.ShapeDtypeStruct((width + stat_rows(heads), rows), jnp.bfloat16)
        if last and shift
        else jax.ShapeDtypeStruct((width, rows), jnp.float32)
        for shift in shifts
    ]
    extents = [
        jax.ShapeDtypeStruct(lines, jnp.float32) for shift in shifts if not (last and shift)
    ]
    scores = many * count * heads
    shapes = [*mixes, *extents]
    if not parted:
        shapes += [
            jax.ShapeDtypeStruct((count, width), jnp.bfloat16),
            jax.ShapeDtypeStruct((width, count), jnp.bfloat16),
        ]
    results = pl.pallas_call(
        functools.partial(
            attend_kernel, (group, shifts, rings, slots, piece, parted, not old, last)
        ),
        in_specs=[SMEM] * 3 + [VMEM] * (len(operands) - 3),
        out_specs=[VMEM] * len(shapes),
        out_shape=shapes,
        scratch_shapes=scratch,
        compiler_params=params(24),
        cost_estimate=cost(4 * scores * HD, 4 * count * width, scores),
        name=name,
    )(*operands)
    mixes = results[: len(shifts)]
    extents = [*results[len(shifts) : len(shapes) - (0 if parted else 2)]]
    if last:
        extents = [extents.pop(0) if shift == 0 else None for shift in shifts]
    state = {shift: pair for shift, *pair in zip(shifts, mixes, extents)}
    return state, results[len(results) - 2 :]


def combine_kernel(*refs):
    result, extent, *parts, weight, attended, sent = refs
    width, rows = result.shape
    heads = width // HD
    extents = [extent[:heads, :]]
    for part in parts:
        lines = part[width:, :].astype(jnp.float32)
        extents.append(sum(lines[i * heads : (i + 1) * heads] for i in range(3)))
    top = functools.reduce(jnp.maximum, extents)
    shares = [jnp.exp2(extent - top) for extent in extents]
    whole = sum(shares)
    shares = [share / whole for share in shares]
    unit = unit_matrix(rows)
    for head in range(heads):
        span = slice(head * HD, (head + 1) * HD)
        mixes = [result[span, :]] + [part[span, :].astype(jnp.float32) for part in parts]
        mixed = sum(mix * share[head : head + 1] for mix, share in zip(mixes, shares))
        attended[:, span] = turned_over(unit, mixed.astype(jnp.bfloat16))
    index = lax.axis_index("tp")
    ways = sent.shape[0] + 1
    columns = weight.shape[1] // ways
    for shift in range(1, ways):
        sent[shift - 1] = jnp.dot(
            attended[...],
            weight[:, lanes((index ^ shift) * columns, columns)],
            preferred_element_type=jnp.float32,
        ).astype(jnp.bfloat16)


def combine(result, extent, parts, w_out, ways):
    width, rows = result.shape
    columns = w_out.shape[1] // ways
    return pl.pallas_call(
        combine_kernel,
        in_specs=[VMEM] * (3 + len(parts)),
        out_specs=[VMEM] * 2,
        out_shape=[
            jax.ShapeDtypeStruct((rows, width), jnp.bfloat16),
            jax.ShapeDtypeStruct((ways - 1, rows, columns), jnp.bfloat16),
        ],
        compiler_params=params(20),
        cost_estimate=cost(2 * rows * width * columns * (ways - 1), 2 * width * w_out.shape[1]),
        name="combine_send",
    )(result, extent, *parts, w_out)


def keep_kernel(attended, weight, hidden, kept):
    columns = hidden.shape[1]
    product = jnp.dot(
        attended[...],
        weight[:, lanes(lax.axis_index("tp") * columns, columns)],
        preferred_element_type=jnp.float32,
    )
    kept[...] = product + hidden[...].astype(jnp.float32)


def keep(attended, w_out, hidden):
    rows, width = attended.shape
    return pl.pallas_call(
        keep_kernel,
        in_specs=[VMEM] * 3,
        out_specs=VMEM,
        out_shape=jax.ShapeDtypeStruct(hidden.shape, jnp.float32),
        compiler_params=params(20),
        cost_estimate=cost(2 * rows * width * hidden.shape[1], 2 * width * w_out.shape[1]),
        name="keep_own",
    )(attended, w_out, hidden)


def local(
    hidden_in, w_query, w_keyval, w_out, prompt_cache, tail_cache, tail_table, tail_len, shared_len
):
    rows = hidden_in.shape[0]
    group = lax.axis_size("seq") // REQ
    ways = lax.axis_size("tp")
    cycle = cycle_of(group)
    half = REQ // 2
    piece = prompt_cache.shape[0]
    middle = piece // 2
    width = w_query.shape[1]
    stride = 2 * width // HD

    pieces = [hidden_in] + [swap(hidden_in, "tp", shift) for shift in range(1, ways)]
    prompt = viewed(prompt_cache)
    halves = [prompt[: middle * stride], prompt[middle * stride :]]
    ahead = {0: [halves[0]], 1: [halves[1]]}
    behind = {0: [halves[0]], 1: [halves[1]]}

    def step(which, *others):
        for blocks, part, way in ((ahead, which, 1), (behind, 1 - which, -1)):
            block = blocks[part][-1]
            if others:
                block = after(block, *others)
            blocks[part].append(turn(block, cycle, group, way))

    def arrived(hop):
        blocks = [way[part][hop] for way in (ahead, behind) for part in (0, 1)]
        rings = [(sign * hop, part * middle, middle) for sign in (-1, 1) for part in (0, 1)]
        return blocks, rings

    step(0)
    step(1)
    cosine, sine = angles(tail_len, shared_len, rows)
    weight = part_weights(w_keyval)
    step(0, weight)
    pieces[0] = after(pieces[0], weight)
    query, normed = project_query(pieces, w_query, cosine, sine)
    queries = [query] + [swap(query, "seq", shift) for shift in range(1, group)]
    tail = viewed(tail_cache.reshape(-1, 2, tail_cache.shape[3]))
    slots = tail_cache.shape[0]
    own_block = part_keyval([tail, prompt], width, "part_own")
    step(1, own_block[0], query)
    fresh_keys, fresh_turned, new_cache = project_keyval(normed, weight, cosine, sine)
    step(0, fresh_keys)
    blocks, rings = arrived(1)
    near_block = part_keyval(blocks, width, "part_near")

    table = tail_table.T
    facts = (tail_len, shared_len, table)
    others = list(range(1, group))
    near = (
        [(0, 0, piece), *rings],
        slots,
        piece,
        [*own_block, *near_block, fresh_keys, fresh_turned],
        True,
        None,
        False,
    )
    own, _ = attend(facts, queries, [0], *near, "attend_near_own")
    step(1, own[0][1])
    ready = (after(tail_len, own[0][1]), shared_len, table)
    theirs, _ = attend(ready, queries, others, *near, "attend_near_others")
    step(0, theirs[1][1])
    rest = []
    rest_rings = []
    for hop in range(2, half):
        blocks, rings = arrived(hop)
        name = f"attend_hop{hop}_others"
        theirs, parted = attend(
            facts, queries, others, rings, 0, piece, blocks, False, theirs, False, name
        )
        rest += parted
        rest_rings += rings
    rings = [(-half, 0, middle), (half, middle, piece - middle)]
    blocks = [ahead[0][half], behind[1][half]]
    theirs, parted = attend(
        facts, queries, others, rings, 0, piece, blocks, False, theirs, True, "attend_far_others"
    )
    rest += parted
    rest_rings += rings
    ready = (after(tail_len, theirs[1][0]), shared_len, table)
    own, _ = attend(
        ready, queries, [0], rest_rings, 0, piece, rest, True, own, True, "attend_rest_own"
    )
    parts = [swap(theirs[shift][0], "seq", shift) for shift in others]
    attended, sent = combine(*own[0], parts, w_out, ways)
    received = [swap(sent[shift - 1], "tp", shift) for shift in range(1, ways)]
    total = keep(attended, w_out, hidden_in)
    for part in received:
        total = total + part.astype(jnp.float32)
    return (total.astype(jnp.bfloat16), new_cache)


def solution(mesh):
    return jax.shard_map(
        local,
        mesh=mesh,
        in_specs=(
            P("seq", "tp"),
            P(None, "tp"),
            P(None, None, "tp"),
            P("tp", None),
            P("seq", None, "tp"),
            P("seq", None, None, "tp"),
            P(),
            P(),
            P(),
        ),
        out_specs=(P("seq", "tp"), P("seq", None, "tp")),
        check_vma=False,
    )
```

```python
import functools

import jax
import jax.numpy as jnp
import numpy as np
from jax import lax
from jax.experimental import pallas as pl
from jax.experimental.pallas import tpu as pltpu
from jax.sharding import PartitionSpec as P

HD = 128
REQ = 8
BLK = 128
NEGATIVE = -1e30
SCALE = float(HD**-0.5 * np.log2(np.e))


def params(mib=24):
    return pltpu.CompilerParams(vmem_limit_bytes=mib * 2**20)


def cost(flops, moved, exps=0):
    return pl.CostEstimate(flops=int(flops), bytes_accessed=int(moved), transcendentals=int(exps))


def cycle_of(group):
    if group == 2:
        return [0, 2, 4, 6, 7, 5, 3, 1]
    return list(range(REQ))


def pick(table, index):
    result = jnp.int32(table[0])
    for place, value in enumerate(table):
        result = jnp.where(index == place, jnp.int32(value), result)
    return result


def swap(value, axis, mask):
    pairs = [(source, source ^ mask) for source in range(lax.axis_size(axis))]
    return lax.ppermute(value, axis, pairs)


def turn(value, cycle, group, way):
    count = len(cycle)
    pairs = []
    for place in range(count):
        source, target = cycle[place], cycle[(place + way) % count]
        pairs += [(source * group + m, target * group + m) for m in range(group)]
    return lax.ppermute(value, "seq", pairs)


def rotated(vectors, cosine, sine):
    return vectors * cosine + pltpu.roll(vectors, HD // 2, 1) * sine


def position_kernel(lengths, shared, positions):
    rows = positions.shape[0]
    group = lax.axis_size("seq") // REQ
    seq = lax.axis_index("seq")
    start = shared[0] + lengths[seq // group] + (seq % group) * rows
    places = start + lax.broadcasted_iota(jnp.int32, positions.shape, 0)
    positions[...] = places.astype(jnp.float32)


def angles(tail_len, shared_len, rows):
    half = HD // 2
    positions = pl.pallas_call(
        position_kernel,
        in_specs=[SMEM] * 2,
        out_specs=VMEM,
        out_shape=jax.ShapeDtypeStruct((rows, HD), jnp.float32),
        compiler_params=params(8),
        cost_estimate=cost(rows * HD, 4 * rows * HD),
        name="positions",
    )(tail_len, shared_len)
    lane = jnp.arange(HD, dtype=jnp.int32)
    freqs = 10000.0 ** (-(lane % half).astype(jnp.float32) / half)
    angle = positions * freqs
    return jnp.cos(angle), jnp.sin(angle) * jnp.where(lane < half, -1.0, 1.0)


def lanes(start, count=HD):
    if isinstance(start, int):
        return pl.ds(start, count)
    return pl.ds(pl.multiple_of(start, HD), count)


def after(value, *others):
    return lax.optimization_barrier((value, *others))[0]


VMEM = pl.BlockSpec(memory_space=pltpu.VMEM)
HBM = pl.BlockSpec(memory_space=pltpu.HBM)
SMEM = pl.BlockSpec(memory_space=pltpu.SMEM)


def viewed(block):
    count, pair, width = block.shape
    heads = width // HD
    return block.reshape(count, pair, heads, HD).transpose(0, 2, 1, 3).reshape(-1, HD)


def order_rows(stride, back):
    rows = 2 * HD
    places = rows // stride
    row = lax.broadcasted_iota(jnp.int32, (rows, rows), 1 if back else 0)
    column = lax.broadcasted_iota(jnp.int32, (rows, rows), 0 if back else 1)
    source = lax.rem(row, places) * stride + lax.div(row, places)
    return jnp.where(column == source, 1.0, 0.0).astype(jnp.bfloat16)


def reordered(order, tiles):
    both = tiles[0] if len(tiles) == 1 else jnp.concatenate(tiles, axis=1)
    mixed = jnp.dot(order, both, preferred_element_type=jnp.float32).astype(jnp.bfloat16)
    return [mixed[:, i * HD : (i + 1) * HD] for i in range(len(tiles))]


def take_apart(block, order, keys, values, offset):
    heads = keys.shape[1] // HD
    stride = 2 * heads
    count = block.shape[0] // stride
    places = 2 * HD // stride
    for start in range(0, count, 2 * places):
        starts = [at for at in (start, start + places) if at < count]
        tiles = [block[at * stride : (at + places) * stride, :] for at in starts]
        for at, tile in zip(starts, reordered(order, tiles)):
            for head in range(heads):
                for j, result in enumerate((keys, values)):
                    line = (2 * head + j) * places
                    result[offset + at : offset + at + places, head * HD : (head + 1) * HD] = tile[
                        line : line + places
                    ]


ACROSS = (((1,), (1,)), ((), ()))


def unit_matrix(size):
    row = lax.broadcasted_iota(jnp.int32, (size, size), 0)
    column = lax.broadcasted_iota(jnp.int32, (size, size), 1)
    return jnp.where(row == column, 1.0, 0.0).astype(jnp.bfloat16)


def turned_over(unit, value):
    return lax.dot_general(unit, value, ACROSS, preferred_element_type=jnp.float32).astype(
        jnp.bfloat16
    )


def turn_heads(values, result):
    unit = unit_matrix(HD)
    for start in range(0, values.shape[1], HD):
        result[start : start + HD, :] = turned_over(unit, values[:, start : start + HD])


def part_kernel(*refs):
    *blocks, keys, turned, values = refs
    stride = keys.shape[1] * 2 // HD
    order = order_rows(stride, False)
    offset = 0
    for block in blocks:
        take_apart(block, order, keys, values, offset)
        offset += block.shape[0] // stride
    turn_heads(values, turned)


def part_keyval(blocks, width, name):
    count = sum(block.shape[0] for block in blocks) * HD // (2 * width)
    return pl.pallas_call(
        part_kernel,
        in_specs=[VMEM] * len(blocks),
        out_specs=[VMEM] * 2,
        out_shape=[
            jax.ShapeDtypeStruct((count, width), jnp.bfloat16),
            jax.ShapeDtypeStruct((width, count), jnp.bfloat16),
        ],
        scratch_shapes=[pltpu.VMEM((count, width), jnp.bfloat16)],
        compiler_params=params(16),
        cost_estimate=cost(2**10 * count * width, 8 * count * width),
        name=name,
    )(*blocks)


def query_kernel(*refs):
    *pieces, weight, cosine, sine, query, normed = refs
    columns = pieces[0].shape[1]
    index = lax.axis_index("tp")
    features = columns * len(pieces)
    values = [piece[...].astype(jnp.float32) for piece in pieces]
    mean = sum(jnp.sum(v, axis=1, keepdims=True) for v in values) / features
    values = [v - mean for v in values]
    spread = sum(jnp.sum(v * v, axis=1, keepdims=True) for v in values) / features
    inverse = lax.rsqrt(spread + 1e-05)
    for shift, v in enumerate(values):
        normed[:, lanes((index ^ shift) * columns, columns)] = (v * inverse).astype(jnp.bfloat16)
    width = weight.shape[1]
    wide = min(width, 2 * HD)
    for base in range(0, width, wide):
        product = jnp.dot(
            normed[...], weight[:, base : base + wide], preferred_element_type=jnp.float32
        )
        for start in range(0, wide, HD):
            query[:, base + start : base + start + HD] = rotated(
                product[:, start : start + HD], cosine[...], sine[...]
            ).astype(jnp.bfloat16)


def project_query(pieces, w_query, cosine, sine):
    rows, columns = pieces[0].shape
    depth, width = w_query.shape
    return pl.pallas_call(
        query_kernel,
        in_specs=[VMEM] * (len(pieces) + 3),
        out_specs=[VMEM] * 2,
        out_shape=[
            jax.ShapeDtypeStruct((rows, width), jnp.bfloat16),
            jax.ShapeDtypeStruct((rows, depth), jnp.bfloat16),
        ],
        compiler_params=params(20),
        cost_estimate=cost(2 * rows * depth * width, 2 * depth * width),
        name="project_query",
    )(*pieces, w_query, cosine, sine)


def weight_kernel(weight, result, near, arrived):
    slots, chunk = near.shape[:2]
    count = weight.shape[0] // chunk
    stride = result.shape[2] * 2 // HD
    copies = [
        pltpu.make_async_copy(
            weight.at[pl.ds(i * chunk, chunk)], near.at[i % slots], arrived.at[i]
        )
        for i in range(count)
    ]
    for copy in copies[:slots]:
        copy.start()
    order = order_rows(stride, False)
    for i, copy in enumerate(copies):
        copy.wait()
        take_apart(near.at[i % slots], order, result.at[0], result.at[1], i * chunk // stride)
        if i + slots < count:
            copies[i + slots].start()


def part_weights(w_keyval):
    depth, _, width = w_keyval.shape
    weight = viewed(w_keyval)
    count = max(depth // 256, 1)
    chunk = weight.shape[0] // count
    return pl.pallas_call(
        weight_kernel,
        in_specs=[HBM],
        out_specs=VMEM,
        out_shape=jax.ShapeDtypeStruct((2, depth, width), jnp.bfloat16),
        scratch_shapes=[
            pltpu.VMEM((count, chunk, HD), jnp.bfloat16),
            pltpu.SemaphoreType.DMA((count,)),
        ],
        compiler_params=params(38),
        cost_estimate=cost(2**10 * depth * width, 8 * depth * width),
        name="part_weights",
    )(weight)


def keyval_kernel(normed, weight, cosine, sine, keys, values, turned):
    heads = weight.shape[2] // HD
    for head in range(heads):
        span = slice(head * HD, (head + 1) * HD)
        product = jnp.dot(
            normed[...],
            jnp.concatenate([weight[0, :, span], weight[1, :, span]], axis=1),
            preferred_element_type=jnp.float32,
        )
        keys[:, span] = rotated(product[:, :HD], cosine[...], sine[...]).astype(jnp.bfloat16)
        values[:, span] = product[:, HD:].astype(jnp.bfloat16)
    turn_heads(values, turned)


def project_keyval(normed, weight, cosine, sine):
    rows, depth = normed.shape
    width = weight.shape[2]
    flat = jax.ShapeDtypeStruct((rows, width), jnp.bfloat16)
    return pl.pallas_call(
        keyval_kernel,
        in_specs=[VMEM] * 4,
        out_specs=[VMEM] * 3,
        out_shape=[flat, flat, jax.ShapeDtypeStruct((width, rows), jnp.bfloat16)],
        compiler_params=params(20),
        cost_estimate=cost(4 * rows * depth * width, 4 * depth * width),
        name="project_keyval",
    )(normed, weight, cosine, sine)


def weave_kernel(keys, values, *refs):
    cache, token = refs[-2:]
    token[...] = jnp.zeros_like(token)
    rows, width = keys.shape
    heads = width // HD
    stride = 2 * heads
    order = order_rows(stride, True)
    places = 2 * HD // stride
    for start in range(0, rows, 2 * places):
        starts = [at for at in (start, start + places) if at < rows]
        tiles = [
            jnp.concatenate(
                [
                    pair[at : at + places, head * HD : (head + 1) * HD]
                    for head in range(heads)
                    for pair in (keys, values)
                ],
                axis=0,
            )
            for at in starts
        ]
        for at, tile in zip(starts, reordered(order, tiles)):
            cache[at * stride : (at + places) * stride, :] = tile


def weave(keys, values, *earlier):
    rows, width = keys.shape
    heads = width // HD
    cache, token = pl.pallas_call(
        weave_kernel,
        in_specs=[VMEM] * (2 + len(earlier)),
        out_specs=[VMEM] * 2,
        out_shape=[
            jax.ShapeDtypeStruct((rows * heads * 2, HD), jnp.bfloat16),
            jax.ShapeDtypeStruct((8, HD), jnp.float32),
        ],
        compiler_params=params(16),
        cost_estimate=cost(2**10 * rows * width, 8 * rows * width),
        name="weave_cache",
    )(keys, values, *earlier)
    cache = cache.reshape(rows, heads, 2, HD).transpose(0, 2, 1, 3)
    return cache.reshape(rows, 2, width), token


def attend_kernel(spec, *refs):
    group, shifts, rings, slots, piece, parted, first, last = spec
    fresh = slots > 0
    refs = list(refs)
    take = lambda count: [refs.pop(0) for _ in range(count)]
    lengths, shared, table = take(3)
    queries = take(len(shifts))
    if parted:
        blocks = take(2 * parted)
        sources = list(zip(blocks[::2], blocks[1::2]))
    else:
        raw = take(len(rings))
    if not first:
        old_mixes, old_extents = take(len(shifts)), take(len(shifts))
    results = take(len(shifts))
    extents = [None if last and shift else take(1)[0] for shift in shifts]
    if not parted:
        sources = [tuple(take(2))]
    bias, first_scores, second_scores = take(3)
    extents = [take(1)[0] if extent is None else extent for extent in extents]
    if fresh:
        causal = take(1)[0]
    if not parted:
        values_here = take(1)[0]
        keys_here, turned_here = sources[0]
    rows, width = queries[0].shape
    heads = width // HD
    cycle = cycle_of(group)
    seq = lax.axis_index("seq")
    request, member = seq // group, seq % group
    place = pick(list(np.argsort(cycle)), request)
    edges = []
    count = 0
    for i in range(slots):
        wanted = seq * slots + i
        number = jnp.int32(0)
        for j in range(table.shape[0]):
            number = jnp.where(table[j, request] == wanted, jnp.int32(j), number)
        edges.append((count, BLK, number * BLK, lengths[request]))
        count += BLK
    for step, begin, size in rings:
        origin = pick(cycle, lax.rem(place + step + REQ, REQ))
        edges.append((count, size, (origin * group + member) * piece + begin, shared[0]))
        count += size
    for begin, size, start, length in edges:
        positions = start + lax.broadcasted_iota(jnp.int32, (size, HD), 0)
        lane = lax.broadcasted_iota(jnp.int32, (size, HD), 1)
        bias[begin : begin + size, :] = jnp.where(
            (positions >= length) & (lane == 0), NEGATIVE, 0.0
        ).astype(jnp.bfloat16)
    if fresh:
        bias[count : count + rows, :] = jnp.zeros((rows, HD), jnp.bfloat16)
        theirs = member * rows + lax.broadcasted_iota(jnp.int32, (rows, rows), 0)
        for i, shift in enumerate(shifts):
            mine = (member ^ shift) * rows + lax.broadcasted_iota(jnp.int32, (rows, rows), 1)
            causal[:, i * rows : (i + 1) * rows] = jnp.where(theirs <= mine, 0.0, NEGATIVE)
    if not parted:
        offset = 0
        order = order_rows(2 * heads, False)
        for block in raw:
            take_apart(block, order, keys_here, values_here, offset)
            offset += block.shape[0] // (2 * heads)
        turn_heads(values_here, turned_here)
    many = len(shifts) * rows
    unit = jnp.where(lax.broadcasted_iota(jnp.int32, (many, HD), 1) == 0, 1.0, 0.0)
    unit = unit.astype(jnp.bfloat16)
    chunks = []
    begin = 0
    for source in sources:
        length = source[0].shape[0]
        for start in range(0, length, 2 * HD):
            size = min(2 * HD, length - start)
            chunks.append((source, start, size, begin + start, fresh and begin == count))
        begin += length

    def beside(values, axis):
        return values[0] if len(values) == 1 else jnp.concatenate(values, axis=axis)

    def query_of(head):
        return jnp.concatenate([beside([q[:, lanes(head * HD)] for q in queries], 0), unit], axis=1)

    def score(head, query, chunk, scores, top):
        (keys, _), start, size, at, masked = chunk
        keys = keys[start : start + size, lanes(head * HD)]
        keys = jnp.concatenate([keys, bias[at : at + size, :]], axis=1)
        part = lax.dot_general(keys, query, ACROSS, preferred_element_type=jnp.float32)
        if masked:
            part = part + causal[start : start + size, :]
        scores[at : at + size, :] = part
        here = jnp.max(part, axis=0, keepdims=True)
        return here if top is None else jnp.maximum(top, here)

    def mix(head, chunk, scores, top, sums):
        (_, turned), start, size, at, _ = chunk
        weights = jnp.exp2((scores[at : at + size, :] - top) * SCALE)
        here = jnp.sum(weights, axis=0, keepdims=True)
        product = jnp.dot(
            turned[lanes(head * HD), start : start + size],
            weights.astype(jnp.bfloat16),
            preferred_element_type=jnp.float32,
        )
        return (here, product) if sums is None else (sums[0] + here, sums[1] + product)

    together = min(heads // 2, 4 if count <= 256 else 1)

    def some_heads(base, scores, tops, following, next_scores):
        span = lambda k: lanes((base + k) * HD)
        line = lambda k: pl.ds(base + k, 1)
        each = range(together)
        if not first:
            olds = [beside([extent[line(k), :] for extent in old_extents], 1) for k in each]
            tops = [jnp.maximum(top, old * (1.0 / SCALE)) for top, old in zip(tops, olds)]
        next_tops = [None] * together
        sums = [None] * together
        if following is not None:
            next_queries = [query_of(following + k) for k in each]
        for chunk in chunks:
            for k in each:
                if following is not None:
                    next_tops[k] = score(
                        following + k, next_queries[k], chunk, next_scores.at[k], next_tops[k]
                    )
                sums[k] = mix(base + k, chunk, scores.at[k], tops[k], sums[k])
        for k in each:
            summed, mixed = sums[k]
            if not first:
                factor = jnp.exp2(olds[k] - tops[k] * SCALE)
                summed = summed + factor
                old_mix = beside([old_mix[span(k), :] for old_mix in old_mixes], 1)
                mixed = mixed + old_mix * factor
            mixed = mixed * (1.0 / summed)
            extent = tops[k] * SCALE + jnp.log2(summed)
            for i, result in enumerate(results):
                columns = slice(i * rows, (i + 1) * rows)
                extents[i][line(k), :] = extent[:, columns]
                result[span(k), :] = mixed[:, columns].astype(result.dtype)
        return next_tops

    def two_parts(i, tops):
        base = 2 * together * i
        tops = some_heads(base, first_scores, tops, base + together, second_scores)
        following = jnp.minimum(base + 2 * together, heads - together)
        return some_heads(base + together, second_scores, tops, following, first_scores)

    tops = []
    for k in range(together):
        query, top = query_of(k), None
        for chunk in chunks:
            top = score(k, query, chunk, first_scores.at[k], top)
        tops.append(top)
    if heads == 2 * together:
        tops = some_heads(0, first_scores, tops, together, second_scores)
        some_heads(together, second_scores, tops, None, None)
    else:
        lax.fori_loop(0, heads // (2 * together), two_parts, tops)
    for i, shift in enumerate(shifts):
        if last and shift:
            line = extents[i][:heads, :]
            packed = []
            for _ in range(3):
                rounded = line.astype(jnp.bfloat16).astype(jnp.float32)
                packed.append(rounded)
                line = line - rounded
            gap = stat_rows(heads) - 3 * heads
            if gap:
                packed.append(jnp.zeros((gap, rows), jnp.float32))
            results[i][width:, :] = jnp.concatenate(packed, axis=0).astype(jnp.bfloat16)


def stat_rows(heads):
    return -(-3 * heads // 16) * 16


def attend(facts, queries, shifts, rings, slots, piece, blocks, parted, old, last, name):
    group = len(queries)
    queries = [queries[shift] for shift in shifts]
    rows, width = queries[0].shape
    heads = width // HD
    parted = len(blocks) // 2 if parted else 0
    operands = [*facts, *queries, *blocks]
    if old:
        operands += [old[shift][0] for shift in shifts] + [old[shift][1] for shift in shifts]
    count = sum(size for _, _, size in rings) + BLK * slots + (rows if slots else 0)
    many = len(shifts) * rows
    scratch = [pltpu.VMEM((count, HD), jnp.bfloat16)]
    together = min(heads // 2, 4 if count <= 256 else 1)
    scratch += [pltpu.VMEM((together, count, many), jnp.float32)] * 2
    lines = (max(heads, 8), rows)
    scratch += [pltpu.VMEM(lines, jnp.float32) for shift in shifts if last and shift]
    if slots:
        scratch.append(pltpu.VMEM((rows, many), jnp.float32))
    if not parted:
        scratch.append(pltpu.VMEM((count, width), jnp.bfloat16))
    mixes = [
        jax.ShapeDtypeStruct((width + stat_rows(heads), rows), jnp.bfloat16)
        if last and shift
        else jax.ShapeDtypeStruct((width, rows), jnp.float32)
        for shift in shifts
    ]
    extents = [
        jax.ShapeDtypeStruct(lines, jnp.float32) for shift in shifts if not (last and shift)
    ]
    scores = many * count * heads
    shapes = [*mixes, *extents]
    if not parted:
        shapes += [
            jax.ShapeDtypeStruct((count, width), jnp.bfloat16),
            jax.ShapeDtypeStruct((width, count), jnp.bfloat16),
        ]
    results = pl.pallas_call(
        functools.partial(
            attend_kernel, (group, shifts, rings, slots, piece, parted, not old, last)
        ),
        in_specs=[SMEM] * 3 + [VMEM] * (len(operands) - 3),
        out_specs=[VMEM] * len(shapes),
        out_shape=shapes,
        scratch_shapes=scratch,
        compiler_params=params(24),
        cost_estimate=cost(4 * scores * HD, 4 * count * width, scores),
        name=name,
    )(*operands)
    mixes = results[: len(shifts)]
    extents = [*results[len(shifts) : len(shapes) - (0 if parted else 2)]]
    if last:
        extents = [extents.pop(0) if shift == 0 else None for shift in shifts]
    state = {shift: pair for shift, *pair in zip(shifts, mixes, extents)}
    return state, results[len(results) - 2 :]


def combine_kernel(*refs):
    result, extent, *parts, weight, _, attended, sent = refs
    width, rows = result.shape
    heads = width // HD
    extents = [extent[:heads, :]]
    for part in parts:
        lines = part[width:, :].astype(jnp.float32)
        extents.append(sum(lines[i * heads : (i + 1) * heads] for i in range(3)))
    top = functools.reduce(jnp.maximum, extents)
    shares = [jnp.exp2(extent - top) for extent in extents]
    whole = sum(shares)
    shares = [share / whole for share in shares]
    unit = unit_matrix(rows)
    for head in range(heads):
        span = slice(head * HD, (head + 1) * HD)
        mixes = [result[span, :]] + [part[span, :].astype(jnp.float32) for part in parts]
        mixed = sum(mix * share[head : head + 1] for mix, share in zip(mixes, shares))
        attended[:, span] = turned_over(unit, mixed.astype(jnp.bfloat16))
    index = lax.axis_index("tp")
    ways = sent.shape[0] + 1
    columns = weight.shape[1] // ways
    for shift in range(1, ways):
        sent[shift - 1] = jnp.dot(
            attended[...],
            weight[:, lanes((index ^ shift) * columns, columns)],
            preferred_element_type=jnp.float32,
        ).astype(jnp.bfloat16)


def combine(result, extent, parts, w_out, token, ways):
    width, rows = result.shape
    columns = w_out.shape[1] // ways
    return pl.pallas_call(
        combine_kernel,
        in_specs=[VMEM] * (4 + len(parts)),
        out_specs=[VMEM] * 2,
        out_shape=[
            jax.ShapeDtypeStruct((rows, width), jnp.bfloat16),
            jax.ShapeDtypeStruct((ways - 1, rows, columns), jnp.bfloat16),
        ],
        compiler_params=params(20),
        cost_estimate=cost(2 * rows * width * columns * (ways - 1), 2 * width * w_out.shape[1]),
        name="combine_send",
    )(result, extent, *parts, w_out, token)


def keep_kernel(attended, weight, hidden, kept):
    columns = hidden.shape[1]
    product = jnp.dot(
        attended[...],
        weight[:, lanes(lax.axis_index("tp") * columns, columns)],
        preferred_element_type=jnp.float32,
    )
    kept[...] = product + hidden[...].astype(jnp.float32)


def keep(attended, w_out, hidden):
    rows, width = attended.shape
    return pl.pallas_call(
        keep_kernel,
        in_specs=[VMEM] * 3,
        out_specs=VMEM,
        out_shape=jax.ShapeDtypeStruct(hidden.shape, jnp.float32),
        compiler_params=params(20),
        cost_estimate=cost(2 * rows * width * hidden.shape[1], 2 * width * w_out.shape[1]),
        name="keep_own",
    )(attended, w_out, hidden)


def local(
    hidden_in, w_query, w_keyval, w_out, prompt_cache, tail_cache, tail_table, tail_len, shared_len
):
    rows = hidden_in.shape[0]
    group = lax.axis_size("seq") // REQ
    ways = lax.axis_size("tp")
    cycle = cycle_of(group)
    half = REQ // 2
    piece = prompt_cache.shape[0]
    middle = piece // 2
    width = w_query.shape[1]
    stride = 2 * width // HD

    pieces = [hidden_in] + [swap(hidden_in, "tp", shift) for shift in range(1, ways)]
    prompt = viewed(prompt_cache)
    halves = [prompt[: middle * stride], prompt[middle * stride :]]
    ahead = {0: [halves[0]], 1: [halves[1]]}
    behind = {0: [halves[0]], 1: [halves[1]]}

    def step(which, *others):
        for blocks, part, way in ((ahead, which, 1), (behind, 1 - which, -1)):
            block = blocks[part][-1]
            if others:
                block = after(block, *others)
            blocks[part].append(turn(block, cycle, group, way))

    def arrived(hop):
        blocks = [way[part][hop] for way in (ahead, behind) for part in (0, 1)]
        rings = [(sign * hop, part * middle, middle) for sign in (-1, 1) for part in (0, 1)]
        return blocks, rings

    step(0)
    step(1)
    weight = part_weights(w_keyval)
    step(0, weight)
    cosine, sine = angles(after(tail_len, weight), shared_len, rows)
    pieces[0] = after(pieces[0], weight, ahead[0][1], behind[1][1])
    query, normed = project_query(pieces, w_query, cosine, sine)
    queries = [query] + [swap(query, "seq", shift) for shift in range(1, group)]
    tail = viewed(tail_cache.reshape(-1, 2, tail_cache.shape[3]))
    slots = tail_cache.shape[0]
    own_block = part_keyval([tail, prompt], width, "part_own")
    step(1, query)
    ready = after(cosine, ahead[1][1], behind[0][1])
    fresh_keys, fresh_values, fresh_turned = project_keyval(normed, weight, ready, sine)
    step(0, fresh_keys)
    blocks, near_rings = arrived(1)
    near_block = part_keyval(blocks, width, "part_near")
    step(1, near_block[0])

    table = tail_table.T
    others = list(range(1, group))
    near_rings = [(0, 0, piece), *near_rings]
    near = [*own_block, *near_block]
    fresh = [fresh_keys, fresh_turned]
    facts = (after(tail_len, ahead[1][2], behind[0][2]), shared_len, table)
    theirs, _ = attend(
        facts,
        queries,
        others,
        near_rings,
        slots,
        piece,
        near + fresh,
        True,
        None,
        False,
        "attend_near_others",
    )
    step(0, theirs[1][1])
    facts = (tail_len, shared_len, table)
    rest = []
    rest_rings = []
    for hop in range(2, half):
        blocks, rings = arrived(hop)
        name = f"attend_hop{hop}_others"
        theirs, parted = attend(
            facts, queries, others, rings, 0, piece, blocks, False, theirs, False, name
        )
        rest += parted
        rest_rings += rings
    rings = [(-half, 0, middle), (half, middle, piece - middle)]
    blocks = [ahead[0][half], behind[1][half]]
    theirs, parted = attend(
        facts, queries, others, rings, 0, piece, blocks, False, theirs, True, "attend_far_others"
    )
    rest += parted
    rest_rings += rings
    facts = (after(tail_len, theirs[1][0]), shared_len, table)
    own, _ = attend(
        facts,
        queries,
        [0],
        near_rings + rest_rings,
        slots,
        piece,
        near + rest + fresh,
        True,
        None,
        True,
        "attend_own",
    )
    new_cache, token = weave(fresh_keys, fresh_values, theirs[1][0])
    parts = [swap(theirs[shift][0], "seq", shift) for shift in others]
    attended, sent = combine(*own[0], parts, w_out, token, ways)
    received = [swap(sent[shift - 1], "tp", shift) for shift in range(1, ways)]
    total = keep(attended, w_out, hidden_in)
    for part in received:
        total = total + part.astype(jnp.float32)
    return (total.astype(jnp.bfloat16), new_cache)


def solution(mesh):
    return jax.shard_map(
        local,
        mesh=mesh,
        in_specs=(
            P("seq", "tp"),
            P(None, "tp"),
            P(None, None, "tp"),
            P("tp", None),
            P("seq", None, "tp"),
            P("seq", None, None, "tp"),
            P(),
            P(),
            P(),
        ),
        out_specs=(P("seq", "tp"), P("seq", None, "tp")),
        check_vma=False,
    )
```

```python
import functools

import jax
import jax.numpy as jnp
import numpy as np
from jax import lax
from jax.experimental import pallas as pl
from jax.experimental.pallas import tpu as pltpu
from jax.sharding import PartitionSpec as P

HD = 128
REQ = 8
BLK = 128
NEGATIVE = -1e30
SCALE = float(HD**-0.5 * np.log2(np.e))


def params(mib=24):
    return pltpu.CompilerParams(vmem_limit_bytes=mib * 2**20)


def cost(flops, moved, exps=0):
    return pl.CostEstimate(flops=int(flops), bytes_accessed=int(moved), transcendentals=int(exps))


def cycle_of(group):
    if group == 2:
        return [0, 2, 4, 6, 7, 5, 3, 1]
    return list(range(REQ))


def pick(table, index):
    result = jnp.int32(table[0])
    for place, value in enumerate(table):
        result = jnp.where(index == place, jnp.int32(value), result)
    return result


def swap(value, axis, mask):
    pairs = [(source, source ^ mask) for source in range(lax.axis_size(axis))]
    return lax.ppermute(value, axis, pairs)


def turn(value, cycle, group, way):
    count = len(cycle)
    pairs = []
    for place in range(count):
        source, target = cycle[place], cycle[(place + way) % count]
        pairs += [(source * group + m, target * group + m) for m in range(group)]
    return lax.ppermute(value, "seq", pairs)


def rotated(vectors, cosine, sine):
    return vectors * cosine + pltpu.roll(vectors, HD // 2, 1) * sine


def position_kernel(lengths, shared, positions):
    rows = positions.shape[0]
    group = lax.axis_size("seq") // REQ
    seq = lax.axis_index("seq")
    start = shared[0] + lengths[seq // group] + (seq % group) * rows
    places = start + lax.broadcasted_iota(jnp.int32, positions.shape, 0)
    positions[...] = places.astype(jnp.float32)


def angles(tail_len, shared_len, rows):
    half = HD // 2
    positions = pl.pallas_call(
        position_kernel,
        in_specs=[SMEM] * 2,
        out_specs=VMEM,
        out_shape=jax.ShapeDtypeStruct((rows, HD), jnp.float32),
        compiler_params=params(8),
        cost_estimate=cost(rows * HD, 4 * rows * HD),
        name="positions",
    )(tail_len, shared_len)
    lane = jnp.arange(HD, dtype=jnp.int32)
    freqs = 10000.0 ** (-(lane % half).astype(jnp.float32) / half)
    angle = positions * freqs
    return jnp.cos(angle), jnp.sin(angle) * jnp.where(lane < half, -1.0, 1.0)


def lanes(start, count=HD):
    if isinstance(start, int):
        return pl.ds(start, count)
    return pl.ds(pl.multiple_of(start, HD), count)


def after(value, *others):
    return lax.optimization_barrier((value, *others))[0]


VMEM = pl.BlockSpec(memory_space=pltpu.VMEM)
HBM = pl.BlockSpec(memory_space=pltpu.HBM)
SMEM = pl.BlockSpec(memory_space=pltpu.SMEM)


def viewed(block):
    count, pair, width = block.shape
    heads = width // HD
    return block.reshape(count, pair, heads, HD).transpose(0, 2, 1, 3).reshape(-1, HD)


def order_rows(stride, back):
    rows = 2 * HD
    places = rows // stride
    row = lax.broadcasted_iota(jnp.int32, (rows, rows), 1 if back else 0)
    column = lax.broadcasted_iota(jnp.int32, (rows, rows), 0 if back else 1)
    source = lax.rem(row, places) * stride + lax.div(row, places)
    return jnp.where(column == source, 1.0, 0.0).astype(jnp.bfloat16)


def reordered(order, tiles):
    both = tiles[0] if len(tiles) == 1 else jnp.concatenate(tiles, axis=1)
    mixed = jnp.dot(order, both, preferred_element_type=jnp.float32).astype(jnp.bfloat16)
    return [mixed[:, i * HD : (i + 1) * HD] for i in range(len(tiles))]


def take_apart(block, order, keys, values, offset):
    heads = keys.shape[1] // HD
    stride = 2 * heads
    count = block.shape[0] // stride
    places = 2 * HD // stride
    for start in range(0, count, 2 * places):
        starts = [at for at in (start, start + places) if at < count]
        tiles = [block[at * stride : (at + places) * stride, :] for at in starts]
        for at, tile in zip(starts, reordered(order, tiles)):
            for head in range(heads):
                for j, result in enumerate((keys, values)):
                    line = (2 * head + j) * places
                    result[offset + at : offset + at + places, head * HD : (head + 1) * HD] = tile[
                        line : line + places
                    ]


ACROSS = (((1,), (1,)), ((), ()))


def unit_matrix(size):
    row = lax.broadcasted_iota(jnp.int32, (size, size), 0)
    column = lax.broadcasted_iota(jnp.int32, (size, size), 1)
    return jnp.where(row == column, 1.0, 0.0).astype(jnp.bfloat16)


def turned_over(unit, value):
    return lax.dot_general(unit, value, ACROSS, preferred_element_type=jnp.float32).astype(
        jnp.bfloat16
    )


def turn_heads(values, result):
    unit = unit_matrix(HD)
    for start in range(0, values.shape[1], HD):
        result[start : start + HD, :] = turned_over(unit, values[:, start : start + HD])


def part_kernel(*refs):
    *blocks, keys, turned, values = refs
    stride = keys.shape[1] * 2 // HD
    order = order_rows(stride, False)
    offset = 0
    for block in blocks:
        take_apart(block, order, keys, values, offset)
        offset += block.shape[0] // stride
    turn_heads(values, turned)


def part_keyval(blocks, width, name):
    count = sum(block.shape[0] for block in blocks) * HD // (2 * width)
    return pl.pallas_call(
        part_kernel,
        in_specs=[VMEM] * len(blocks),
        out_specs=[VMEM] * 2,
        out_shape=[
            jax.ShapeDtypeStruct((count, width), jnp.bfloat16),
            jax.ShapeDtypeStruct((width, count), jnp.bfloat16),
        ],
        scratch_shapes=[pltpu.VMEM((count, width), jnp.bfloat16)],
        compiler_params=params(16),
        cost_estimate=cost(2**10 * count * width, 8 * count * width),
        name=name,
    )(*blocks)


def query_kernel(*refs):
    *pieces, weight, cosine, sine, query, normed = refs
    columns = pieces[0].shape[1]
    index = lax.axis_index("tp")
    features = columns * len(pieces)
    values = [piece[...].astype(jnp.float32) for piece in pieces]
    mean = sum(jnp.sum(v, axis=1, keepdims=True) for v in values) / features
    values = [v - mean for v in values]
    spread = sum(jnp.sum(v * v, axis=1, keepdims=True) for v in values) / features
    inverse = lax.rsqrt(spread + 1e-05)
    for shift, v in enumerate(values):
        normed[:, lanes((index ^ shift) * columns, columns)] = (v * inverse).astype(jnp.bfloat16)
    width = weight.shape[1]
    wide = min(width, 2 * HD)
    for base in range(0, width, wide):
        product = jnp.dot(
            normed[...], weight[:, base : base + wide], preferred_element_type=jnp.float32
        )
        for start in range(0, wide, HD):
            query[:, base + start : base + start + HD] = rotated(
                product[:, start : start + HD], cosine[...], sine[...]
            ).astype(jnp.bfloat16)


def project_query(pieces, w_query, cosine, sine):
    rows, columns = pieces[0].shape
    depth, width = w_query.shape
    return pl.pallas_call(
        query_kernel,
        in_specs=[VMEM] * (len(pieces) + 3),
        out_specs=[VMEM] * 2,
        out_shape=[
            jax.ShapeDtypeStruct((rows, width), jnp.bfloat16),
            jax.ShapeDtypeStruct((rows, depth), jnp.bfloat16),
        ],
        compiler_params=params(20),
        cost_estimate=cost(2 * rows * depth * width, 2 * depth * width),
        name="project_query",
    )(*pieces, w_query, cosine, sine)


def weight_kernel(weight, result, near, arrived):
    slots, chunk = near.shape[:2]
    count = weight.shape[0] // chunk
    stride = result.shape[2] * 2 // HD
    copies = [
        pltpu.make_async_copy(
            weight.at[pl.ds(i * chunk, chunk)], near.at[i % slots], arrived.at[i]
        )
        for i in range(count)
    ]
    for copy in copies[:slots]:
        copy.start()
    order = order_rows(stride, False)
    for i, copy in enumerate(copies):
        copy.wait()
        take_apart(near.at[i % slots], order, result.at[0], result.at[1], i * chunk // stride)
        if i + slots < count:
            copies[i + slots].start()


def part_weights(w_keyval):
    depth, _, width = w_keyval.shape
    weight = viewed(w_keyval)
    count = max(depth // 256, 1)
    chunk = weight.shape[0] // count
    return pl.pallas_call(
        weight_kernel,
        in_specs=[HBM],
        out_specs=VMEM,
        out_shape=jax.ShapeDtypeStruct((2, depth, width), jnp.bfloat16),
        scratch_shapes=[
            pltpu.VMEM((count, chunk, HD), jnp.bfloat16),
            pltpu.SemaphoreType.DMA((count,)),
        ],
        compiler_params=params(38),
        cost_estimate=cost(2**10 * depth * width, 8 * depth * width),
        name="part_weights",
    )(weight)


def keyval_kernel(normed, weight, cosine, sine, keys, values, turned):
    heads = weight.shape[2] // HD
    for head in range(heads):
        span = slice(head * HD, (head + 1) * HD)
        product = jnp.dot(
            normed[...],
            jnp.concatenate([weight[0, :, span], weight[1, :, span]], axis=1),
            preferred_element_type=jnp.float32,
        )
        keys[:, span] = rotated(product[:, :HD], cosine[...], sine[...]).astype(jnp.bfloat16)
        values[:, span] = product[:, HD:].astype(jnp.bfloat16)
    turn_heads(values, turned)


def project_keyval(normed, weight, cosine, sine):
    rows, depth = normed.shape
    width = weight.shape[2]
    flat = jax.ShapeDtypeStruct((rows, width), jnp.bfloat16)
    return pl.pallas_call(
        keyval_kernel,
        in_specs=[VMEM] * 4,
        out_specs=[VMEM] * 3,
        out_shape=[flat, flat, jax.ShapeDtypeStruct((width, rows), jnp.bfloat16)],
        compiler_params=params(20),
        cost_estimate=cost(4 * rows * depth * width, 4 * depth * width),
        name="project_keyval",
    )(normed, weight, cosine, sine)


def weave_kernel(keys, values, *refs):
    cache, token = refs[-2:]
    token[...] = jnp.zeros_like(token)
    rows, width = keys.shape
    heads = width // HD
    stride = 2 * heads
    order = order_rows(stride, True)
    places = 2 * HD // stride
    for start in range(0, rows, 2 * places):
        starts = [at for at in (start, start + places) if at < rows]
        tiles = [
            jnp.concatenate(
                [
                    pair[at : at + places, head * HD : (head + 1) * HD]
                    for head in range(heads)
                    for pair in (keys, values)
                ],
                axis=0,
            )
            for at in starts
        ]
        for at, tile in zip(starts, reordered(order, tiles)):
            cache[at * stride : (at + places) * stride, :] = tile


def weave(keys, values, *earlier):
    rows, width = keys.shape
    heads = width // HD
    cache, token = pl.pallas_call(
        weave_kernel,
        in_specs=[VMEM] * (2 + len(earlier)),
        out_specs=[VMEM] * 2,
        out_shape=[
            jax.ShapeDtypeStruct((rows * heads * 2, HD), jnp.bfloat16),
            jax.ShapeDtypeStruct((8, HD), jnp.float32),
        ],
        compiler_params=params(16),
        cost_estimate=cost(2**10 * rows * width, 8 * rows * width),
        name="weave_cache",
    )(keys, values, *earlier)
    cache = cache.reshape(rows, heads, 2, HD).transpose(0, 2, 1, 3)
    return cache.reshape(rows, 2, width), token


def attend_kernel(spec, *refs):
    group, shifts, rings, slots, piece, parted, first, last = spec
    fresh = slots > 0
    refs = list(refs)
    take = lambda count: [refs.pop(0) for _ in range(count)]
    lengths, shared, table = take(3)
    queries = take(len(shifts))
    if parted:
        blocks = take(2 * parted)
        sources = list(zip(blocks[::2], blocks[1::2]))
    else:
        raw = take(len(rings))
    if not first:
        old_mixes, old_extents = take(len(shifts)), take(len(shifts))
    results = take(len(shifts))
    extents = [None if last and shift else take(1)[0] for shift in shifts]
    if not parted:
        sources = [tuple(take(2))]
    bias, first_scores, second_scores = take(3)
    extents = [take(1)[0] if extent is None else extent for extent in extents]
    if fresh:
        causal = take(1)[0]
    if not parted:
        values_here = take(1)[0]
        keys_here, turned_here = sources[0]
    rows, width = queries[0].shape
    heads = width // HD
    cycle = cycle_of(group)
    seq = lax.axis_index("seq")
    request, member = seq // group, seq % group
    place = pick(list(np.argsort(cycle)), request)
    edges = []
    count = 0
    for i in range(slots):
        wanted = seq * slots + i
        number = jnp.int32(0)
        for j in range(table.shape[0]):
            number = jnp.where(table[j, request] == wanted, jnp.int32(j), number)
        edges.append((count, BLK, number * BLK, lengths[request]))
        count += BLK
    for step, begin, size in rings:
        origin = pick(cycle, lax.rem(place + step + REQ, REQ))
        edges.append((count, size, (origin * group + member) * piece + begin, shared[0]))
        count += size
    for begin, size, start, length in edges:
        positions = start + lax.broadcasted_iota(jnp.int32, (size, HD), 0)
        lane = lax.broadcasted_iota(jnp.int32, (size, HD), 1)
        bias[begin : begin + size, :] = jnp.where(
            (positions >= length) & (lane == 0), NEGATIVE, 0.0
        ).astype(jnp.bfloat16)
    if fresh:
        bias[count : count + rows, :] = jnp.zeros((rows, HD), jnp.bfloat16)
        theirs = member * rows + lax.broadcasted_iota(jnp.int32, (rows, rows), 0)
        for i, shift in enumerate(shifts):
            mine = (member ^ shift) * rows + lax.broadcasted_iota(jnp.int32, (rows, rows), 1)
            causal[:, i * rows : (i + 1) * rows] = jnp.where(theirs <= mine, 0.0, NEGATIVE)
    if not parted:
        offset = 0
        order = order_rows(2 * heads, False)
        for block in raw:
            take_apart(block, order, keys_here, values_here, offset)
            offset += block.shape[0] // (2 * heads)
        turn_heads(values_here, turned_here)
    many = len(shifts) * rows
    unit = jnp.where(lax.broadcasted_iota(jnp.int32, (many, HD), 1) == 0, 1.0, 0.0)
    unit = unit.astype(jnp.bfloat16)
    chunks = []
    begin = 0
    for source in sources:
        length = source[0].shape[0]
        for start in range(0, length, 2 * HD):
            size = min(2 * HD, length - start)
            chunks.append((source, start, size, begin + start, fresh and begin == count))
        begin += length

    def beside(values, axis):
        return values[0] if len(values) == 1 else jnp.concatenate(values, axis=axis)

    def query_of(head):
        return jnp.concatenate([beside([q[:, lanes(head * HD)] for q in queries], 0), unit], axis=1)

    def score(head, query, chunk, scores, top):
        (keys, _), start, size, at, masked = chunk
        keys = keys[start : start + size, lanes(head * HD)]
        keys = jnp.concatenate([keys, bias[at : at + size, :]], axis=1)
        part = lax.dot_general(keys, query, ACROSS, preferred_element_type=jnp.float32)
        if masked:
            part = part + causal[start : start + size, :]
        scores[at : at + size, :] = part
        here = jnp.max(part, axis=0, keepdims=True)
        return here if top is None else jnp.maximum(top, here)

    def mix(head, chunk, scores, top, sums):
        (_, turned), start, size, at, _ = chunk
        weights = jnp.exp2((scores[at : at + size, :] - top) * SCALE)
        here = jnp.sum(weights, axis=0, keepdims=True)
        product = jnp.dot(
            turned[lanes(head * HD), start : start + size],
            weights.astype(jnp.bfloat16),
            preferred_element_type=jnp.float32,
        )
        return (here, product) if sums is None else (sums[0] + here, sums[1] + product)

    together = min(heads // 2, 4 if count <= 256 else 1)

    def some_heads(base, scores, tops, following, next_scores):
        span = lambda k: lanes((base + k) * HD)
        line = lambda k: pl.ds(base + k, 1)
        each = range(together)
        if not first:
            olds = [beside([extent[line(k), :] for extent in old_extents], 1) for k in each]
            tops = [jnp.maximum(top, old * (1.0 / SCALE)) for top, old in zip(tops, olds)]
        next_tops = [None] * together
        sums = [None] * together
        if following is not None:
            next_queries = [query_of(following + k) for k in each]
        for chunk in chunks:
            for k in each:
                if following is not None:
                    next_tops[k] = score(
                        following + k, next_queries[k], chunk, next_scores.at[k], next_tops[k]
                    )
                sums[k] = mix(base + k, chunk, scores.at[k], tops[k], sums[k])
        for k in each:
            summed, mixed = sums[k]
            if not first:
                factor = jnp.exp2(olds[k] - tops[k] * SCALE)
                summed = summed + factor
                old_mix = beside([old_mix[span(k), :] for old_mix in old_mixes], 1)
                mixed = mixed + old_mix * factor
            mixed = mixed * (1.0 / summed)
            extent = tops[k] * SCALE + jnp.log2(summed)
            for i, result in enumerate(results):
                columns = slice(i * rows, (i + 1) * rows)
                extents[i][line(k), :] = extent[:, columns]
                result[span(k), :] = mixed[:, columns].astype(result.dtype)
        return next_tops

    def two_parts(i, tops):
        base = 2 * together * i
        tops = some_heads(base, first_scores, tops, base + together, second_scores)
        following = jnp.minimum(base + 2 * together, heads - together)
        return some_heads(base + together, second_scores, tops, following, first_scores)

    tops = []
    for k in range(together):
        query, top = query_of(k), None
        for chunk in chunks:
            top = score(k, query, chunk, first_scores.at[k], top)
        tops.append(top)
    if heads == 2 * together:
        tops = some_heads(0, first_scores, tops, together, second_scores)
        some_heads(together, second_scores, tops, None, None)
    else:
        lax.fori_loop(0, heads // (2 * together), two_parts, tops)
    for i, shift in enumerate(shifts):
        if last and shift:
            line = extents[i][:heads, :]
            packed = []
            for _ in range(3):
                rounded = line.astype(jnp.bfloat16).astype(jnp.float32)
                packed.append(rounded)
                line = line - rounded
            gap = stat_rows(heads) - 3 * heads
            if gap:
                packed.append(jnp.zeros((gap, rows), jnp.float32))
            results[i][width:, :] = jnp.concatenate(packed, axis=0).astype(jnp.bfloat16)


def stat_rows(heads):
    return -(-3 * heads // 16) * 16


def attend(facts, queries, shifts, rings, slots, piece, blocks, parted, old, last, name):
    group = len(queries)
    queries = [queries[shift] for shift in shifts]
    rows, width = queries[0].shape
    heads = width // HD
    parted = len(blocks) // 2 if parted else 0
    operands = [*facts, *queries, *blocks]
    if old:
        operands += [old[shift][0] for shift in shifts] + [old[shift][1] for shift in shifts]
    count = sum(size for _, _, size in rings) + BLK * slots + (rows if slots else 0)
    many = len(shifts) * rows
    scratch = [pltpu.VMEM((count, HD), jnp.bfloat16)]
    together = min(heads // 2, 4 if count <= 256 else 1)
    scratch += [pltpu.VMEM((together, count, many), jnp.float32)] * 2
    lines = (max(heads, 8), rows)
    scratch += [pltpu.VMEM(lines, jnp.float32) for shift in shifts if last and shift]
    if slots:
        scratch.append(pltpu.VMEM((rows, many), jnp.float32))
    if not parted:
        scratch.append(pltpu.VMEM((count, width), jnp.bfloat16))
    mixes = [
        jax.ShapeDtypeStruct((width + stat_rows(heads), rows), jnp.bfloat16)
        if last and shift
        else jax.ShapeDtypeStruct((width, rows), jnp.float32)
        for shift in shifts
    ]
    extents = [
        jax.ShapeDtypeStruct(lines, jnp.float32) for shift in shifts if not (last and shift)
    ]
    scores = many * count * heads
    shapes = [*mixes, *extents]
    if not parted:
        shapes += [
            jax.ShapeDtypeStruct((count, width), jnp.bfloat16),
            jax.ShapeDtypeStruct((width, count), jnp.bfloat16),
        ]
    results = pl.pallas_call(
        functools.partial(
            attend_kernel, (group, shifts, rings, slots, piece, parted, not old, last)
        ),
        in_specs=[SMEM] * 3 + [VMEM] * (len(operands) - 3),
        out_specs=[VMEM] * len(shapes),
        out_shape=shapes,
        scratch_shapes=scratch,
        compiler_params=params(24),
        cost_estimate=cost(4 * scores * HD, 4 * count * width, scores),
        name=name,
    )(*operands)
    mixes = results[: len(shifts)]
    extents = [*results[len(shifts) : len(shapes) - (0 if parted else 2)]]
    if last:
        extents = [extents.pop(0) if shift == 0 else None for shift in shifts]
    state = {shift: pair for shift, *pair in zip(shifts, mixes, extents)}
    return state, results[len(results) - 2 :]


def combine_kernel(*refs):
    result, extent, *parts, weight, _, attended, sent = refs
    width, rows = result.shape
    heads = width // HD
    extents = [extent[:heads, :]]
    for part in parts:
        lines = part[width:, :].astype(jnp.float32)
        extents.append(sum(lines[i * heads : (i + 1) * heads] for i in range(3)))
    top = functools.reduce(jnp.maximum, extents)
    shares = [jnp.exp2(extent - top) for extent in extents]
    whole = sum(shares)
    shares = [share / whole for share in shares]
    unit = unit_matrix(rows)
    for head in range(heads):
        span = slice(head * HD, (head + 1) * HD)
        mixes = [result[span, :]] + [part[span, :].astype(jnp.float32) for part in parts]
        mixed = sum(mix * share[head : head + 1] for mix, share in zip(mixes, shares))
        attended[:, span] = turned_over(unit, mixed.astype(jnp.bfloat16))
    index = lax.axis_index("tp")
    ways = sent.shape[0] + 1
    columns = weight.shape[1] // ways
    for shift in range(1, ways):
        sent[shift - 1] = jnp.dot(
            attended[...],
            weight[:, lanes((index ^ shift) * columns, columns)],
            preferred_element_type=jnp.float32,
        ).astype(jnp.bfloat16)


def combine(result, extent, parts, w_out, token, ways):
    width, rows = result.shape
    columns = w_out.shape[1] // ways
    return pl.pallas_call(
        combine_kernel,
        in_specs=[VMEM] * (4 + len(parts)),
        out_specs=[VMEM] * 2,
        out_shape=[
            jax.ShapeDtypeStruct((rows, width), jnp.bfloat16),
            jax.ShapeDtypeStruct((ways - 1, rows, columns), jnp.bfloat16),
        ],
        compiler_params=params(20),
        cost_estimate=cost(2 * rows * width * columns * (ways - 1), 2 * width * w_out.shape[1]),
        name="combine_send",
    )(result, extent, *parts, w_out, token)


def keep_kernel(attended, weight, hidden, kept):
    columns = hidden.shape[1]
    product = jnp.dot(
        attended[...],
        weight[:, lanes(lax.axis_index("tp") * columns, columns)],
        preferred_element_type=jnp.float32,
    )
    kept[...] = product + hidden[...].astype(jnp.float32)


def keep(attended, w_out, hidden):
    rows, width = attended.shape
    return pl.pallas_call(
        keep_kernel,
        in_specs=[VMEM] * 3,
        out_specs=VMEM,
        out_shape=jax.ShapeDtypeStruct(hidden.shape, jnp.float32),
        compiler_params=params(20),
        cost_estimate=cost(2 * rows * width * hidden.shape[1], 2 * width * w_out.shape[1]),
        name="keep_own",
    )(attended, w_out, hidden)


def local(
    hidden_in, w_query, w_keyval, w_out, prompt_cache, tail_cache, tail_table, tail_len, shared_len
):
    rows = hidden_in.shape[0]
    group = lax.axis_size("seq") // REQ
    ways = lax.axis_size("tp")
    cycle = cycle_of(group)
    half = REQ // 2
    piece = prompt_cache.shape[0]
    middle = piece // 2
    width = w_query.shape[1]
    stride = 2 * width // HD

    pieces = [hidden_in] + [swap(hidden_in, "tp", shift) for shift in range(1, ways)]
    prompt = viewed(prompt_cache)
    ahead, behind = {0: [None], 1: [None]}, {0: [None], 1: [None]}
    nearest = []
    for blocks, way in ((ahead, 1), (behind, -1)):
        block = turn(prompt, cycle, group, way)
        nearest.append(block)
        blocks[0].append(block[: middle * stride])
        blocks[1].append(block[middle * stride :])

    def step(which, *others):
        for blocks, part, way in ((ahead, which, 1), (behind, 1 - which, -1)):
            block = blocks[part][-1]
            if others:
                block = after(block, *others)
            blocks[part].append(turn(block, cycle, group, way))

    def arrived(hop):
        blocks = [way[part][hop] for way in (ahead, behind) for part in (0, 1)]
        rings = [(sign * hop, part * middle, middle) for sign in (-1, 1) for part in (0, 1)]
        return blocks, rings

    weight = part_weights(w_keyval)
    cosine, sine = angles(after(tail_len, weight), shared_len, rows)
    pieces[0] = after(pieces[0], weight)
    query, normed = project_query(pieces, w_query, cosine, sine)
    queries = [query] + [swap(query, "seq", shift) for shift in range(1, group)]
    tail = viewed(tail_cache.reshape(-1, 2, tail_cache.shape[3]))
    slots = tail_cache.shape[0]
    own_block = part_keyval([tail, prompt], width, "part_own")
    step(0, weight, query)
    step(1, query)
    ready = after(cosine, ahead[1][1], behind[0][1])
    fresh_keys, fresh_values, fresh_turned = project_keyval(normed, weight, ready, sine)
    step(0, fresh_keys)
    near_block = part_keyval(nearest, width, "part_near")
    step(1, near_block[0])

    table = tail_table.T
    others = list(range(1, group))
    near_rings = [(0, 0, piece), (-1, 0, piece), (1, 0, piece)]
    near = [*own_block, *near_block]
    fresh = [fresh_keys, fresh_turned]
    facts = (tail_len, shared_len, table)
    theirs, _ = attend(
        facts,
        queries,
        others,
        near_rings,
        slots,
        piece,
        near + fresh,
        True,
        None,
        False,
        "attend_near_others",
    )
    step(0, theirs[1][1])
    facts = (tail_len, shared_len, table)
    rest = []
    rest_rings = []
    for hop in range(2, half):
        blocks, rings = arrived(hop)
        name = f"attend_hop{hop}_others"
        theirs, parted = attend(
            facts, queries, others, rings, 0, piece, blocks, False, theirs, False, name
        )
        rest += parted
        rest_rings += rings
    rings = [(-half, 0, middle), (half, middle, piece - middle)]
    blocks = [ahead[0][half], behind[1][half]]
    theirs, parted = attend(
        facts, queries, others, rings, 0, piece, blocks, False, theirs, True, "attend_far_others"
    )
    rest += parted
    rest_rings += rings
    facts = (after(tail_len, theirs[1][0]), shared_len, table)
    own, _ = attend(
        facts,
        queries,
        [0],
        near_rings + rest_rings,
        slots,
        piece,
        near + rest + fresh,
        True,
        None,
        True,
        "attend_own",
    )
    new_cache, token = weave(fresh_keys, fresh_values, theirs[1][0])
    parts = [swap(theirs[shift][0], "seq", shift) for shift in others]
    attended, sent = combine(*own[0], parts, w_out, token, ways)
    received = [swap(sent[shift - 1], "tp", shift) for shift in range(1, ways)]
    total = keep(attended, w_out, hidden_in)
    for part in received:
        total = total + part.astype(jnp.float32)
    return (total.astype(jnp.bfloat16), new_cache)


def solution(mesh):
    return jax.shard_map(
        local,
        mesh=mesh,
        in_specs=(
            P("seq", "tp"),
            P(None, "tp"),
            P(None, None, "tp"),
            P("tp", None),
            P("seq", None, "tp"),
            P("seq", None, None, "tp"),
            P(),
            P(),
            P(),
        ),
        out_specs=(P("seq", "tp"), P("seq", None, "tp")),
        check_vma=False,
    )
```

```python
import functools

import jax
import jax.numpy as jnp
import numpy as np
from jax import lax
from jax.experimental import pallas as pl
from jax.experimental.pallas import tpu as pltpu
from jax.sharding import PartitionSpec as P

HD = 128
REQ = 8
BLK = 128
NEGATIVE = -1e30
SCALE = float(HD**-0.5 * np.log2(np.e))


def params(mib=24):
    return pltpu.CompilerParams(vmem_limit_bytes=mib * 2**20)


def cost(flops, moved, exps=0):
    return pl.CostEstimate(flops=int(flops), bytes_accessed=int(moved), transcendentals=int(exps))


def cycle_of(group):
    if group == 2:
        return [0, 2, 4, 6, 7, 5, 3, 1]
    return list(range(REQ))


def pick(table, index):
    result = jnp.int32(table[0])
    for place, value in enumerate(table):
        result = jnp.where(index == place, jnp.int32(value), result)
    return result


def swap(value, axis, mask):
    pairs = [(source, source ^ mask) for source in range(lax.axis_size(axis))]
    return lax.ppermute(value, axis, pairs)


def turn(value, cycle, group, way):
    count = len(cycle)
    pairs = []
    for place in range(count):
        source, target = cycle[place], cycle[(place + way) % count]
        pairs += [(source * group + m, target * group + m) for m in range(group)]
    return lax.ppermute(value, "seq", pairs)


def rotated(vectors, cosine, sine):
    return vectors * cosine + pltpu.roll(vectors, HD // 2, 1) * sine


def position_kernel(lengths, shared, positions):
    rows = positions.shape[0]
    group = lax.axis_size("seq") // REQ
    seq = lax.axis_index("seq")
    start = shared[0] + lengths[seq // group] + (seq % group) * rows
    places = start + lax.broadcasted_iota(jnp.int32, positions.shape, 0)
    positions[...] = places.astype(jnp.float32)


def angles(tail_len, shared_len, rows):
    half = HD // 2
    positions = pl.pallas_call(
        position_kernel,
        in_specs=[SMEM] * 2,
        out_specs=VMEM,
        out_shape=jax.ShapeDtypeStruct((rows, HD), jnp.float32),
        compiler_params=params(8),
        cost_estimate=cost(rows * HD, 4 * rows * HD),
        name="positions",
    )(tail_len, shared_len)
    lane = jnp.arange(HD, dtype=jnp.int32)
    freqs = 10000.0 ** (-(lane % half).astype(jnp.float32) / half)
    angle = positions * freqs
    return jnp.cos(angle), jnp.sin(angle) * jnp.where(lane < half, -1.0, 1.0)


def lanes(start, count=HD):
    if isinstance(start, int):
        return pl.ds(start, count)
    return pl.ds(pl.multiple_of(start, HD), count)


def after(value, *others):
    return lax.optimization_barrier((value, *others))[0]


VMEM = pl.BlockSpec(memory_space=pltpu.VMEM)
HBM = pl.BlockSpec(memory_space=pltpu.HBM)
SMEM = pl.BlockSpec(memory_space=pltpu.SMEM)


def viewed(block):
    count, pair, width = block.shape
    heads = width // HD
    return block.reshape(count, pair, heads, HD).transpose(0, 2, 1, 3).reshape(-1, HD)


def order_rows(stride, back):
    rows = 2 * HD
    places = rows // stride
    row = lax.broadcasted_iota(jnp.int32, (rows, rows), 1 if back else 0)
    column = lax.broadcasted_iota(jnp.int32, (rows, rows), 0 if back else 1)
    source = lax.rem(row, places) * stride + lax.div(row, places)
    return jnp.where(column == source, 1.0, 0.0).astype(jnp.bfloat16)


def reordered(order, tiles):
    both = tiles[0] if len(tiles) == 1 else jnp.concatenate(tiles, axis=1)
    mixed = jnp.dot(order, both, preferred_element_type=jnp.float32).astype(jnp.bfloat16)
    return [mixed[:, i * HD : (i + 1) * HD] for i in range(len(tiles))]


def take_apart(block, order, keys, values, offset):
    heads = keys.shape[1] // HD
    stride = 2 * heads
    count = block.shape[0] // stride
    places = 2 * HD // stride
    for start in range(0, count, 2 * places):
        starts = [at for at in (start, start + places) if at < count]
        tiles = [block[at * stride : (at + places) * stride, :] for at in starts]
        for at, tile in zip(starts, reordered(order, tiles)):
            for head in range(heads):
                for j, result in enumerate((keys, values)):
                    line = (2 * head + j) * places
                    result[offset + at : offset + at + places, head * HD : (head + 1) * HD] = tile[
                        line : line + places
                    ]


ACROSS = (((1,), (1,)), ((), ()))


def unit_matrix(size):
    row = lax.broadcasted_iota(jnp.int32, (size, size), 0)
    column = lax.broadcasted_iota(jnp.int32, (size, size), 1)
    return jnp.where(row == column, 1.0, 0.0).astype(jnp.bfloat16)


def turned_over(unit, value):
    return lax.dot_general(unit, value, ACROSS, preferred_element_type=jnp.float32).astype(
        jnp.bfloat16
    )


def turn_heads(values, result):
    unit = unit_matrix(HD)
    for start in range(0, values.shape[1], HD):
        result[start : start + HD, :] = turned_over(unit, values[:, start : start + HD])


def part_kernel(*refs):
    *blocks, keys, turned, values = refs
    stride = keys.shape[1] * 2 // HD
    order = order_rows(stride, False)
    offset = 0
    for block in blocks:
        take_apart(block, order, keys, values, offset)
        offset += block.shape[0] // stride
    turn_heads(values, turned)


def part_keyval(blocks, width, name):
    count = sum(block.shape[0] for block in blocks) * HD // (2 * width)
    return pl.pallas_call(
        part_kernel,
        in_specs=[VMEM] * len(blocks),
        out_specs=[VMEM] * 2,
        out_shape=[
            jax.ShapeDtypeStruct((count, width), jnp.bfloat16),
            jax.ShapeDtypeStruct((width, count), jnp.bfloat16),
        ],
        scratch_shapes=[pltpu.VMEM((count, width), jnp.bfloat16)],
        compiler_params=params(16),
        cost_estimate=cost(2**10 * count * width, 8 * count * width),
        name=name,
    )(*blocks)


def query_kernel(*refs):
    *pieces, weight, cosine, sine, query, normed = refs
    columns = pieces[0].shape[1]
    index = lax.axis_index("tp")
    features = columns * len(pieces)
    values = [piece[...].astype(jnp.float32) for piece in pieces]
    mean = sum(jnp.sum(v, axis=1, keepdims=True) for v in values) / features
    values = [v - mean for v in values]
    spread = sum(jnp.sum(v * v, axis=1, keepdims=True) for v in values) / features
    inverse = lax.rsqrt(spread + 1e-05)
    for shift, v in enumerate(values):
        normed[:, lanes((index ^ shift) * columns, columns)] = (v * inverse).astype(jnp.bfloat16)
    width = weight.shape[1]
    wide = min(width, 2 * HD)
    for base in range(0, width, wide):
        product = jnp.dot(
            normed[...], weight[:, base : base + wide], preferred_element_type=jnp.float32
        )
        for start in range(0, wide, HD):
            query[:, base + start : base + start + HD] = rotated(
                product[:, start : start + HD], cosine[...], sine[...]
            ).astype(jnp.bfloat16)


def project_query(pieces, w_query, cosine, sine):
    rows, columns = pieces[0].shape
    depth, width = w_query.shape
    return pl.pallas_call(
        query_kernel,
        in_specs=[VMEM] * (len(pieces) + 3),
        out_specs=[VMEM] * 2,
        out_shape=[
            jax.ShapeDtypeStruct((rows, width), jnp.bfloat16),
            jax.ShapeDtypeStruct((rows, depth), jnp.bfloat16),
        ],
        compiler_params=params(20),
        cost_estimate=cost(2 * rows * depth * width, 2 * depth * width),
        name="project_query",
    )(*pieces, w_query, cosine, sine)


def weight_kernel(weight, result, near, arrived):
    slots, chunk = near.shape[:2]
    count = weight.shape[0] // chunk
    stride = result.shape[2] * 2 // HD
    copies = [
        pltpu.make_async_copy(
            weight.at[pl.ds(i * chunk, chunk)], near.at[i % slots], arrived.at[i]
        )
        for i in range(count)
    ]
    for copy in copies[:slots]:
        copy.start()
    order = order_rows(stride, False)
    for i, copy in enumerate(copies):
        copy.wait()
        take_apart(near.at[i % slots], order, result.at[0], result.at[1], i * chunk // stride)
        if i + slots < count:
            copies[i + slots].start()


def part_weights(w_keyval):
    depth, _, width = w_keyval.shape
    weight = viewed(w_keyval)
    count = max(depth // 256, 1)
    chunk = weight.shape[0] // count
    return pl.pallas_call(
        weight_kernel,
        in_specs=[HBM],
        out_specs=VMEM,
        out_shape=jax.ShapeDtypeStruct((2, depth, width), jnp.bfloat16),
        scratch_shapes=[
            pltpu.VMEM((count, chunk, HD), jnp.bfloat16),
            pltpu.SemaphoreType.DMA((count,)),
        ],
        compiler_params=params(38),
        cost_estimate=cost(2**10 * depth * width, 8 * depth * width),
        name="part_weights",
    )(weight)


def keyval_kernel(normed, weight, cosine, sine, keys, values, turned):
    heads = weight.shape[2] // HD
    for head in range(heads):
        span = slice(head * HD, (head + 1) * HD)
        product = jnp.dot(
            normed[...],
            jnp.concatenate([weight[0, :, span], weight[1, :, span]], axis=1),
            preferred_element_type=jnp.float32,
        )
        keys[:, span] = rotated(product[:, :HD], cosine[...], sine[...]).astype(jnp.bfloat16)
        values[:, span] = product[:, HD:].astype(jnp.bfloat16)
    turn_heads(values, turned)


def project_keyval(normed, weight, cosine, sine):
    rows, depth = normed.shape
    width = weight.shape[2]
    flat = jax.ShapeDtypeStruct((rows, width), jnp.bfloat16)
    return pl.pallas_call(
        keyval_kernel,
        in_specs=[VMEM] * 4,
        out_specs=[VMEM] * 3,
        out_shape=[flat, flat, jax.ShapeDtypeStruct((width, rows), jnp.bfloat16)],
        compiler_params=params(20),
        cost_estimate=cost(4 * rows * depth * width, 4 * depth * width),
        name="project_keyval",
    )(normed, weight, cosine, sine)


def weave_kernel(keys, values, *refs):
    cache, token = refs[-2:]
    token[...] = jnp.zeros_like(token)
    rows, width = keys.shape
    heads = width // HD
    stride = 2 * heads
    order = order_rows(stride, True)
    places = 2 * HD // stride
    for start in range(0, rows, 2 * places):
        starts = [at for at in (start, start + places) if at < rows]
        tiles = [
            jnp.concatenate(
                [
                    pair[at : at + places, head * HD : (head + 1) * HD]
                    for head in range(heads)
                    for pair in (keys, values)
                ],
                axis=0,
            )
            for at in starts
        ]
        for at, tile in zip(starts, reordered(order, tiles)):
            cache[at * stride : (at + places) * stride, :] = tile


def weave(keys, values, *earlier):
    rows, width = keys.shape
    heads = width // HD
    cache, token = pl.pallas_call(
        weave_kernel,
        in_specs=[VMEM] * (2 + len(earlier)),
        out_specs=[VMEM] * 2,
        out_shape=[
            jax.ShapeDtypeStruct((rows * heads * 2, HD), jnp.bfloat16),
            jax.ShapeDtypeStruct((8, HD), jnp.float32),
        ],
        compiler_params=params(16),
        cost_estimate=cost(2**10 * rows * width, 8 * rows * width),
        name="weave_cache",
    )(keys, values, *earlier)
    cache = cache.reshape(rows, heads, 2, HD).transpose(0, 2, 1, 3)
    return cache.reshape(rows, 2, width), token


def attend_kernel(spec, *refs):
    group, shifts, rings, slots, piece, parted, first, last = spec
    fresh = slots > 0
    refs = list(refs)
    take = lambda count: [refs.pop(0) for _ in range(count)]
    lengths, shared, table = take(3)
    queries = take(len(shifts))
    if parted:
        blocks = take(2 * parted)
        sources = list(zip(blocks[::2], blocks[1::2]))
    else:
        raw = take(len(rings))
    if not first:
        old_mixes, old_extents = take(len(shifts)), take(len(shifts))
    results = take(len(shifts))
    extents = [None if last and shift else take(1)[0] for shift in shifts]
    if not parted:
        sources = [tuple(take(2))]
    bias, first_scores, second_scores = take(3)
    extents = [take(1)[0] if extent is None else extent for extent in extents]
    if fresh:
        causal = take(1)[0]
    if not parted:
        values_here = take(1)[0]
        keys_here, turned_here = sources[0]
    rows, width = queries[0].shape
    heads = width // HD
    cycle = cycle_of(group)
    seq = lax.axis_index("seq")
    request, member = seq // group, seq % group
    place = pick(list(np.argsort(cycle)), request)
    edges = []
    count = 0
    for i in range(slots):
        wanted = seq * slots + i
        number = jnp.int32(0)
        for j in range(table.shape[0]):
            number = jnp.where(table[j, request] == wanted, jnp.int32(j), number)
        edges.append((count, BLK, number * BLK, lengths[request]))
        count += BLK
    for step, begin, size in rings:
        origin = pick(cycle, lax.rem(place + step + REQ, REQ))
        edges.append((count, size, (origin * group + member) * piece + begin, shared[0]))
        count += size
    for begin, size, start, length in edges:
        positions = start + lax.broadcasted_iota(jnp.int32, (size, HD), 0)
        lane = lax.broadcasted_iota(jnp.int32, (size, HD), 1)
        bias[begin : begin + size, :] = jnp.where(
            (positions >= length) & (lane == 0), NEGATIVE, 0.0
        ).astype(jnp.bfloat16)
    if fresh:
        bias[count : count + rows, :] = jnp.zeros((rows, HD), jnp.bfloat16)
        theirs = member * rows + lax.broadcasted_iota(jnp.int32, (rows, rows), 0)
        for i, shift in enumerate(shifts):
            mine = (member ^ shift) * rows + lax.broadcasted_iota(jnp.int32, (rows, rows), 1)
            causal[:, i * rows : (i + 1) * rows] = jnp.where(theirs <= mine, 0.0, NEGATIVE)
    if not parted:
        offset = 0
        order = order_rows(2 * heads, False)
        for block in raw:
            take_apart(block, order, keys_here, values_here, offset)
            offset += block.shape[0] // (2 * heads)
        turn_heads(values_here, turned_here)
    many = len(shifts) * rows
    unit = jnp.where(lax.broadcasted_iota(jnp.int32, (many, HD), 1) == 0, 1.0, 0.0)
    unit = unit.astype(jnp.bfloat16)
    chunks = []
    begin = 0
    for source in sources:
        length = source[0].shape[0]
        for start in range(0, length, 2 * HD):
            size = min(2 * HD, length - start)
            chunks.append((source, start, size, begin + start, fresh and begin == count))
        begin += length

    def beside(values, axis):
        return values[0] if len(values) == 1 else jnp.concatenate(values, axis=axis)

    def query_of(head):
        return jnp.concatenate([beside([q[:, lanes(head * HD)] for q in queries], 0), unit], axis=1)

    def score(head, query, chunk, scores, top):
        (keys, _), start, size, at, masked = chunk
        keys = keys[start : start + size, lanes(head * HD)]
        keys = jnp.concatenate([keys, bias[at : at + size, :]], axis=1)
        part = lax.dot_general(keys, query, ACROSS, preferred_element_type=jnp.float32)
        if masked:
            part = part + causal[start : start + size, :]
        scores[at : at + size, :] = part
        here = jnp.max(part, axis=0, keepdims=True)
        return here if top is None else jnp.maximum(top, here)

    def mix(head, chunk, scores, top, sums):
        (_, turned), start, size, at, _ = chunk
        weights = jnp.exp2((scores[at : at + size, :] - top) * SCALE)
        here = jnp.sum(weights, axis=0, keepdims=True)
        product = jnp.dot(
            turned[lanes(head * HD), start : start + size],
            weights.astype(jnp.bfloat16),
            preferred_element_type=jnp.float32,
        )
        return (here, product) if sums is None else (sums[0] + here, sums[1] + product)

    together = min(heads // 2, 4 if count <= 256 else 1)

    def some_heads(base, scores, tops, following, next_scores):
        span = lambda k: lanes((base + k) * HD)
        line = lambda k: pl.ds(base + k, 1)
        each = range(together)
        if not first:
            olds = [beside([extent[line(k), :] for extent in old_extents], 1) for k in each]
            tops = [jnp.maximum(top, old * (1.0 / SCALE)) for top, old in zip(tops, olds)]
        next_tops = [None] * together
        sums = [None] * together
        if following is not None:
            next_queries = [query_of(following + k) for k in each]
        for chunk in chunks:
            for k in each:
                if following is not None:
                    next_tops[k] = score(
                        following + k, next_queries[k], chunk, next_scores.at[k], next_tops[k]
                    )
                sums[k] = mix(base + k, chunk, scores.at[k], tops[k], sums[k])
        for k in each:
            summed, mixed = sums[k]
            if not first:
                factor = jnp.exp2(olds[k] - tops[k] * SCALE)
                summed = summed + factor
                old_mix = beside([old_mix[span(k), :] for old_mix in old_mixes], 1)
                mixed = mixed + old_mix * factor
            mixed = mixed * (1.0 / summed)
            extent = tops[k] * SCALE + jnp.log2(summed)
            for i, result in enumerate(results):
                columns = slice(i * rows, (i + 1) * rows)
                extents[i][line(k), :] = extent[:, columns]
                result[span(k), :] = mixed[:, columns].astype(result.dtype)
        return next_tops

    def two_parts(i, tops):
        base = 2 * together * i
        tops = some_heads(base, first_scores, tops, base + together, second_scores)
        following = jnp.minimum(base + 2 * together, heads - together)
        return some_heads(base + together, second_scores, tops, following, first_scores)

    tops = []
    for k in range(together):
        query, top = query_of(k), None
        for chunk in chunks:
            top = score(k, query, chunk, first_scores.at[k], top)
        tops.append(top)
    if heads == 2 * together:
        tops = some_heads(0, first_scores, tops, together, second_scores)
        some_heads(together, second_scores, tops, None, None)
    else:
        lax.fori_loop(0, heads // (2 * together), two_parts, tops)
    for i, shift in enumerate(shifts):
        if last and shift:
            line = extents[i][:heads, :]
            packed = []
            for _ in range(3):
                rounded = line.astype(jnp.bfloat16).astype(jnp.float32)
                packed.append(rounded)
                line = line - rounded
            gap = stat_rows(heads) - 3 * heads
            if gap:
                packed.append(jnp.zeros((gap, rows), jnp.float32))
            results[i][width:, :] = jnp.concatenate(packed, axis=0).astype(jnp.bfloat16)


def stat_rows(heads):
    return -(-3 * heads // 16) * 16


def attend(facts, queries, shifts, rings, slots, piece, blocks, parted, old, last, name):
    group = len(queries)
    queries = [queries[shift] for shift in shifts]
    rows, width = queries[0].shape
    heads = width // HD
    parted = len(blocks) // 2 if parted else 0
    operands = [*facts, *queries, *blocks]
    if old:
        operands += [old[shift][0] for shift in shifts] + [old[shift][1] for shift in shifts]
    count = sum(size for _, _, size in rings) + BLK * slots + (rows if slots else 0)
    many = len(shifts) * rows
    scratch = [pltpu.VMEM((count, HD), jnp.bfloat16)]
    together = min(heads // 2, 4 if count <= 256 else 1)
    scratch += [pltpu.VMEM((together, count, many), jnp.float32)] * 2
    lines = (max(heads, 8), rows)
    scratch += [pltpu.VMEM(lines, jnp.float32) for shift in shifts if last and shift]
    if slots:
        scratch.append(pltpu.VMEM((rows, many), jnp.float32))
    if not parted:
        scratch.append(pltpu.VMEM((count, width), jnp.bfloat16))
    mixes = [
        jax.ShapeDtypeStruct((width + stat_rows(heads), rows), jnp.bfloat16)
        if last and shift
        else jax.ShapeDtypeStruct((width, rows), jnp.float32)
        for shift in shifts
    ]
    extents = [
        jax.ShapeDtypeStruct(lines, jnp.float32) for shift in shifts if not (last and shift)
    ]
    scores = many * count * heads
    shapes = [*mixes, *extents]
    if not parted:
        shapes += [
            jax.ShapeDtypeStruct((count, width), jnp.bfloat16),
            jax.ShapeDtypeStruct((width, count), jnp.bfloat16),
        ]
    results = pl.pallas_call(
        functools.partial(
            attend_kernel, (group, shifts, rings, slots, piece, parted, not old, last)
        ),
        in_specs=[SMEM] * 3 + [VMEM] * (len(operands) - 3),
        out_specs=[VMEM] * len(shapes),
        out_shape=shapes,
        scratch_shapes=scratch,
        compiler_params=params(24),
        cost_estimate=cost(4 * scores * HD, 4 * count * width, scores),
        name=name,
    )(*operands)
    mixes = results[: len(shifts)]
    extents = [*results[len(shifts) : len(shapes) - (0 if parted else 2)]]
    if last:
        extents = [extents.pop(0) if shift == 0 else None for shift in shifts]
    state = {shift: pair for shift, *pair in zip(shifts, mixes, extents)}
    return state, results[len(results) - 2 :]


def combine_kernel(*refs):
    result, extent, *parts, weight, _, attended, sent = refs
    width, rows = result.shape
    heads = width // HD
    extents = [extent[:heads, :]]
    for part in parts:
        lines = part[width:, :].astype(jnp.float32)
        extents.append(sum(lines[i * heads : (i + 1) * heads] for i in range(3)))
    top = functools.reduce(jnp.maximum, extents)
    shares = [jnp.exp2(extent - top) for extent in extents]
    whole = sum(shares)
    shares = [share / whole for share in shares]
    unit = unit_matrix(rows)
    for head in range(heads):
        span = slice(head * HD, (head + 1) * HD)
        mixes = [result[span, :]] + [part[span, :].astype(jnp.float32) for part in parts]
        mixed = sum(mix * share[head : head + 1] for mix, share in zip(mixes, shares))
        attended[:, span] = turned_over(unit, mixed.astype(jnp.bfloat16))
    index = lax.axis_index("tp")
    ways = sent.shape[0] + 1
    columns = weight.shape[1] // ways
    for shift in range(1, ways):
        sent[shift - 1] = jnp.dot(
            attended[...],
            weight[:, lanes((index ^ shift) * columns, columns)],
            preferred_element_type=jnp.float32,
        ).astype(jnp.bfloat16)


def combine(result, extent, parts, w_out, token, ways):
    width, rows = result.shape
    columns = w_out.shape[1] // ways
    return pl.pallas_call(
        combine_kernel,
        in_specs=[VMEM] * (4 + len(parts)),
        out_specs=[VMEM] * 2,
        out_shape=[
            jax.ShapeDtypeStruct((rows, width), jnp.bfloat16),
            jax.ShapeDtypeStruct((ways - 1, rows, columns), jnp.bfloat16),
        ],
        compiler_params=params(20),
        cost_estimate=cost(2 * rows * width * columns * (ways - 1), 2 * width * w_out.shape[1]),
        name="combine_send",
    )(result, extent, *parts, w_out, token)


def keep_kernel(attended, weight, hidden, kept):
    columns = hidden.shape[1]
    product = jnp.dot(
        attended[...],
        weight[:, lanes(lax.axis_index("tp") * columns, columns)],
        preferred_element_type=jnp.float32,
    )
    kept[...] = product + hidden[...].astype(jnp.float32)


def keep(attended, w_out, hidden):
    rows, width = attended.shape
    return pl.pallas_call(
        keep_kernel,
        in_specs=[VMEM] * 3,
        out_specs=VMEM,
        out_shape=jax.ShapeDtypeStruct(hidden.shape, jnp.float32),
        compiler_params=params(20),
        cost_estimate=cost(2 * rows * width * hidden.shape[1], 2 * width * w_out.shape[1]),
        name="keep_own",
    )(attended, w_out, hidden)


def local(
    hidden_in, w_query, w_keyval, w_out, prompt_cache, tail_cache, tail_table, tail_len, shared_len
):
    rows = hidden_in.shape[0]
    group = lax.axis_size("seq") // REQ
    ways = lax.axis_size("tp")
    cycle = cycle_of(group)
    half = REQ // 2
    piece = prompt_cache.shape[0]
    middle = piece // 2
    width = w_query.shape[1]
    stride = 2 * width // HD

    pieces = [hidden_in] + [swap(hidden_in, "tp", shift) for shift in range(1, ways)]
    prompt = viewed(prompt_cache)
    ahead, behind = {0: [None], 1: [None]}, {0: [None], 1: [None]}
    nearest = []
    for blocks, way in ((ahead, 1), (behind, -1)):
        block = turn(prompt, cycle, group, way)
        nearest.append(block)
        blocks[0].append(block[: middle * stride])
        blocks[1].append(block[middle * stride :])

    def step(which, *others):
        for blocks, part, way in ((ahead, which, 1), (behind, 1 - which, -1)):
            block = blocks[part][-1]
            if others:
                block = after(block, *others)
            blocks[part].append(turn(block, cycle, group, way))

    def arrived(hop):
        blocks = [way[part][hop] for way in (ahead, behind) for part in (0, 1)]
        rings = [(sign * hop, part * middle, middle) for sign in (-1, 1) for part in (0, 1)]
        return blocks, rings

    weight = part_weights(w_keyval)
    cosine, sine = angles(after(tail_len, weight), shared_len, rows)
    pieces[0] = after(pieces[0], weight)
    query, normed = project_query(pieces, w_query, cosine, sine)
    queries = [query] + [swap(query, "seq", shift) for shift in range(1, group)]
    tail = viewed(tail_cache.reshape(-1, 2, tail_cache.shape[3]))
    slots = tail_cache.shape[0]
    own_block = part_keyval([tail, prompt], width, "part_own")
    step(0, weight, query)
    step(1, query)
    ready = after(cosine, ahead[1][1], behind[0][1])
    fresh_keys, fresh_values, fresh_turned = project_keyval(normed, weight, ready, sine)
    step(0, fresh_keys)
    near_block = part_keyval(nearest, width, "part_near")

    table = tail_table.T
    others = list(range(1, group))
    near_rings = [(0, 0, piece), (-1, 0, piece), (1, 0, piece)]
    near = [*own_block, *near_block]
    fresh = [fresh_keys, fresh_turned]
    facts = (tail_len, shared_len, table)
    theirs, _ = attend(
        facts,
        queries,
        others,
        near_rings,
        slots,
        piece,
        near + fresh,
        True,
        None,
        False,
        "attend_near_others",
    )
    step(1, theirs[1][1])
    step(0, theirs[1][1])
    facts = (tail_len, shared_len, table)
    rest = []
    rest_rings = []
    for hop in range(2, half):
        blocks, rings = arrived(hop)
        name = f"attend_hop{hop}_others"
        theirs, parted = attend(
            facts, queries, others, rings, 0, piece, blocks, False, theirs, False, name
        )
        rest += parted
        rest_rings += rings
    rings = [(-half, 0, middle), (half, middle, piece - middle)]
    blocks = [ahead[0][half], behind[1][half]]
    theirs, parted = attend(
        facts, queries, others, rings, 0, piece, blocks, False, theirs, True, "attend_far_others"
    )
    rest += parted
    rest_rings += rings
    facts = (after(tail_len, theirs[1][0]), shared_len, table)
    own, _ = attend(
        facts,
        queries,
        [0],
        near_rings + rest_rings,
        slots,
        piece,
        near + rest + fresh,
        True,
        None,
        True,
        "attend_own",
    )
    new_cache, token = weave(fresh_keys, fresh_values, theirs[1][0])
    parts = [swap(theirs[shift][0], "seq", shift) for shift in others]
    attended, sent = combine(*own[0], parts, w_out, token, ways)
    received = [swap(sent[shift - 1], "tp", shift) for shift in range(1, ways)]
    total = keep(attended, w_out, hidden_in)
    for part in received:
        total = total + part.astype(jnp.float32)
    return (total.astype(jnp.bfloat16), new_cache)


def solution(mesh):
    return jax.shard_map(
        local,
        mesh=mesh,
        in_specs=(
            P("seq", "tp"),
            P(None, "tp"),
            P(None, None, "tp"),
            P("tp", None),
            P("seq", None, "tp"),
            P("seq", None, None, "tp"),
            P(),
            P(),
            P(),
        ),
        out_specs=(P("seq", "tp"), P("seq", None, "tp")),
        check_vma=False,
    )
```

```python
import functools

import jax
import jax.numpy as jnp
import numpy as np
from jax import lax
from jax.experimental import pallas as pl
from jax.experimental.pallas import tpu as pltpu
from jax.sharding import PartitionSpec as P

HD = 128
REQ = 8
BLK = 128
NEGATIVE = -1e30
SCALE = float(HD**-0.5 * np.log2(np.e))


def params(mib=24):
    return pltpu.CompilerParams(vmem_limit_bytes=mib * 2**20)


def cost(flops, moved, exps=0):
    return pl.CostEstimate(flops=int(flops), bytes_accessed=int(moved), transcendentals=int(exps))


def cycle_of(group):
    if group == 2:
        return [0, 2, 4, 6, 7, 5, 3, 1]
    return list(range(REQ))


def pick(table, index):
    result = jnp.int32(table[0])
    for place, value in enumerate(table):
        result = jnp.where(index == place, jnp.int32(value), result)
    return result


def swap(value, axis, mask):
    pairs = [(source, source ^ mask) for source in range(lax.axis_size(axis))]
    return lax.ppermute(value, axis, pairs)


def turn(value, cycle, group, way):
    count = len(cycle)
    pairs = []
    for place in range(count):
        source, target = cycle[place], cycle[(place + way) % count]
        pairs += [(source * group + m, target * group + m) for m in range(group)]
    return lax.ppermute(value, "seq", pairs)


def rotated(vectors, cosine, sine):
    return vectors * cosine + pltpu.roll(vectors, HD // 2, 1) * sine


def position_kernel(lengths, shared, positions):
    rows = positions.shape[0]
    group = lax.axis_size("seq") // REQ
    seq = lax.axis_index("seq")
    start = shared[0] + lengths[seq // group] + (seq % group) * rows
    places = start + lax.broadcasted_iota(jnp.int32, positions.shape, 0)
    positions[...] = places.astype(jnp.float32)


def angles(tail_len, shared_len, rows):
    half = HD // 2
    positions = pl.pallas_call(
        position_kernel,
        in_specs=[SMEM] * 2,
        out_specs=VMEM,
        out_shape=jax.ShapeDtypeStruct((rows, HD), jnp.float32),
        compiler_params=params(8),
        cost_estimate=cost(rows * HD, 4 * rows * HD),
        name="positions",
    )(tail_len, shared_len)
    lane = jnp.arange(HD, dtype=jnp.int32)
    freqs = 10000.0 ** (-(lane % half).astype(jnp.float32) / half)
    angle = positions * freqs
    return jnp.cos(angle), jnp.sin(angle) * jnp.where(lane < half, -1.0, 1.0)


def lanes(start, count=HD):
    if isinstance(start, int):
        return pl.ds(start, count)
    return pl.ds(pl.multiple_of(start, HD), count)


def after(value, *others):
    return lax.optimization_barrier((value, *others))[0]


VMEM = pl.BlockSpec(memory_space=pltpu.VMEM)
HBM = pl.BlockSpec(memory_space=pltpu.HBM)
SMEM = pl.BlockSpec(memory_space=pltpu.SMEM)


def viewed(block):
    count, pair, width = block.shape
    heads = width // HD
    return block.reshape(count, pair, heads, HD).transpose(0, 2, 1, 3).reshape(-1, HD)


def order_rows(stride, back):
    rows = 2 * HD
    places = rows // stride
    row = lax.broadcasted_iota(jnp.int32, (rows, rows), 1 if back else 0)
    column = lax.broadcasted_iota(jnp.int32, (rows, rows), 0 if back else 1)
    source = lax.rem(row, places) * stride + lax.div(row, places)
    return jnp.where(column == source, 1.0, 0.0).astype(jnp.bfloat16)


def reordered(order, tiles):
    both = tiles[0] if len(tiles) == 1 else jnp.concatenate(tiles, axis=1)
    mixed = jnp.dot(order, both, preferred_element_type=jnp.float32).astype(jnp.bfloat16)
    return [mixed[:, i * HD : (i + 1) * HD] for i in range(len(tiles))]


def take_apart(block, order, keys, values, offset):
    heads = keys.shape[1] // HD
    stride = 2 * heads
    count = block.shape[0] // stride
    places = 2 * HD // stride
    for start in range(0, count, 2 * places):
        starts = [at for at in (start, start + places) if at < count]
        tiles = [block[at * stride : (at + places) * stride, :] for at in starts]
        for at, tile in zip(starts, reordered(order, tiles)):
            for head in range(heads):
                for j, result in enumerate((keys, values)):
                    line = (2 * head + j) * places
                    result[offset + at : offset + at + places, head * HD : (head + 1) * HD] = tile[
                        line : line + places
                    ]


ACROSS = (((1,), (1,)), ((), ()))


def unit_matrix(size):
    row = lax.broadcasted_iota(jnp.int32, (size, size), 0)
    column = lax.broadcasted_iota(jnp.int32, (size, size), 1)
    return jnp.where(row == column, 1.0, 0.0).astype(jnp.bfloat16)


def turned_over(unit, value):
    return lax.dot_general(unit, value, ACROSS, preferred_element_type=jnp.float32).astype(
        jnp.bfloat16
    )


def turn_heads(values, result):
    unit = unit_matrix(HD)
    for start in range(0, values.shape[1], HD):
        result[start : start + HD, :] = turned_over(unit, values[:, start : start + HD])


def part_kernel(*refs):
    *blocks, keys, turned, values = refs
    stride = keys.shape[1] * 2 // HD
    order = order_rows(stride, False)
    offset = 0
    for block in blocks:
        take_apart(block, order, keys, values, offset)
        offset += block.shape[0] // stride
    turn_heads(values, turned)


def part_keyval(blocks, width, name):
    count = sum(block.shape[0] for block in blocks) * HD // (2 * width)
    return pl.pallas_call(
        part_kernel,
        in_specs=[VMEM] * len(blocks),
        out_specs=[VMEM] * 2,
        out_shape=[
            jax.ShapeDtypeStruct((count, width), jnp.bfloat16),
            jax.ShapeDtypeStruct((width, count), jnp.bfloat16),
        ],
        scratch_shapes=[pltpu.VMEM((count, width), jnp.bfloat16)],
        compiler_params=params(16),
        cost_estimate=cost(2**10 * count * width, 8 * count * width),
        name=name,
    )(*blocks)


def query_kernel(*refs):
    *pieces, weight, cosine, sine, query, normed = refs
    columns = pieces[0].shape[1]
    index = lax.axis_index("tp")
    features = columns * len(pieces)
    values = [piece[...].astype(jnp.float32) for piece in pieces]
    mean = sum(jnp.sum(v, axis=1, keepdims=True) for v in values) / features
    values = [v - mean for v in values]
    spread = sum(jnp.sum(v * v, axis=1, keepdims=True) for v in values) / features
    inverse = lax.rsqrt(spread + 1e-05)
    for shift, v in enumerate(values):
        normed[:, lanes((index ^ shift) * columns, columns)] = (v * inverse).astype(jnp.bfloat16)
    width = weight.shape[1]
    wide = min(width, 2 * HD)
    for base in range(0, width, wide):
        product = jnp.dot(
            normed[...], weight[:, base : base + wide], preferred_element_type=jnp.float32
        )
        for start in range(0, wide, HD):
            query[:, base + start : base + start + HD] = rotated(
                product[:, start : start + HD], cosine[...], sine[...]
            ).astype(jnp.bfloat16)


def project_query(pieces, w_query, cosine, sine):
    rows, columns = pieces[0].shape
    depth, width = w_query.shape
    return pl.pallas_call(
        query_kernel,
        in_specs=[VMEM] * (len(pieces) + 3),
        out_specs=[VMEM] * 2,
        out_shape=[
            jax.ShapeDtypeStruct((rows, width), jnp.bfloat16),
            jax.ShapeDtypeStruct((rows, depth), jnp.bfloat16),
        ],
        compiler_params=params(20),
        cost_estimate=cost(2 * rows * depth * width, 2 * depth * width),
        name="project_query",
    )(*pieces, w_query, cosine, sine)


def weight_kernel(weight, result, near, arrived):
    slots, chunk = near.shape[:2]
    count = weight.shape[0] // chunk
    stride = result.shape[2] * 2 // HD
    copies = [
        pltpu.make_async_copy(
            weight.at[pl.ds(i * chunk, chunk)], near.at[i % slots], arrived.at[i]
        )
        for i in range(count)
    ]
    for copy in copies[:slots]:
        copy.start()
    order = order_rows(stride, False)
    for i, copy in enumerate(copies):
        copy.wait()
        take_apart(near.at[i % slots], order, result.at[0], result.at[1], i * chunk // stride)
        if i + slots < count:
            copies[i + slots].start()


def part_weights(w_keyval):
    depth, _, width = w_keyval.shape
    weight = viewed(w_keyval)
    count = max(depth // 256, 1)
    chunk = weight.shape[0] // count
    return pl.pallas_call(
        weight_kernel,
        in_specs=[HBM],
        out_specs=VMEM,
        out_shape=jax.ShapeDtypeStruct((2, depth, width), jnp.bfloat16),
        scratch_shapes=[
            pltpu.VMEM((count, chunk, HD), jnp.bfloat16),
            pltpu.SemaphoreType.DMA((count,)),
        ],
        compiler_params=params(38),
        cost_estimate=cost(2**10 * depth * width, 8 * depth * width),
        name="part_weights",
    )(weight)


def keyval_kernel(normed, weight, cosine, sine, keys, values, turned):
    heads = weight.shape[2] // HD
    for head in range(heads):
        span = slice(head * HD, (head + 1) * HD)
        product = jnp.dot(
            normed[...],
            jnp.concatenate([weight[0, :, span], weight[1, :, span]], axis=1),
            preferred_element_type=jnp.float32,
        )
        keys[:, span] = rotated(product[:, :HD], cosine[...], sine[...]).astype(jnp.bfloat16)
        values[:, span] = product[:, HD:].astype(jnp.bfloat16)
    turn_heads(values, turned)


def project_keyval(normed, weight, cosine, sine):
    rows, depth = normed.shape
    width = weight.shape[2]
    flat = jax.ShapeDtypeStruct((rows, width), jnp.bfloat16)
    return pl.pallas_call(
        keyval_kernel,
        in_specs=[VMEM] * 4,
        out_specs=[VMEM] * 3,
        out_shape=[flat, flat, jax.ShapeDtypeStruct((width, rows), jnp.bfloat16)],
        compiler_params=params(20),
        cost_estimate=cost(4 * rows * depth * width, 4 * depth * width),
        name="project_keyval",
    )(normed, weight, cosine, sine)


def weave_kernel(keys, values, *refs):
    cache, token = refs[-2:]
    token[...] = jnp.zeros_like(token)
    rows, width = keys.shape
    heads = width // HD
    stride = 2 * heads
    order = order_rows(stride, True)
    places = 2 * HD // stride
    for start in range(0, rows, 2 * places):
        starts = [at for at in (start, start + places) if at < rows]
        tiles = [
            jnp.concatenate(
                [
                    pair[at : at + places, head * HD : (head + 1) * HD]
                    for head in range(heads)
                    for pair in (keys, values)
                ],
                axis=0,
            )
            for at in starts
        ]
        for at, tile in zip(starts, reordered(order, tiles)):
            cache[at * stride : (at + places) * stride, :] = tile


def weave(keys, values, *earlier):
    rows, width = keys.shape
    heads = width // HD
    cache, token = pl.pallas_call(
        weave_kernel,
        in_specs=[VMEM] * (2 + len(earlier)),
        out_specs=[VMEM] * 2,
        out_shape=[
            jax.ShapeDtypeStruct((rows * heads * 2, HD), jnp.bfloat16),
            jax.ShapeDtypeStruct((8, HD), jnp.float32),
        ],
        compiler_params=params(16),
        cost_estimate=cost(2**10 * rows * width, 8 * rows * width),
        name="weave_cache",
    )(keys, values, *earlier)
    cache = cache.reshape(rows, heads, 2, HD).transpose(0, 2, 1, 3)
    return cache.reshape(rows, 2, width), token


def attend_kernel(spec, *refs):
    group, shifts, rings, slots, piece, parted, first, last, lowest, heads = spec
    fresh = slots > 0
    refs = list(refs)
    take = lambda count: [refs.pop(0) for _ in range(count)]
    lengths, shared, table = take(3)
    queries = take(len(shifts))
    if parted:
        blocks = take(2 * parted)
        sources = list(zip(blocks[::2], blocks[1::2]))
    else:
        raw = take(len(rings))
    if not first:
        old_mixes, old_extents = take(len(shifts)), take(len(shifts))
        skipped = lowest if old_mixes[0].shape[0] == queries[0].shape[1] else 0
    results = take(len(shifts))
    extents = [None if last and shift else take(1)[0] for shift in shifts]
    if not parted:
        sources = [tuple(take(2))]
    bias, first_scores, second_scores = take(3)
    extents = [take(1)[0] if extent is None else extent for extent in extents]
    if fresh:
        causal = take(1)[0]
    if not parted:
        values_here = take(1)[0]
        keys_here, turned_here = sources[0]
    rows, width = queries[0].shape
    stride = 2 * heads
    cycle = cycle_of(group)
    seq = lax.axis_index("seq")
    request, member = seq // group, seq % group
    place = pick(list(np.argsort(cycle)), request)
    edges = []
    count = 0
    for i in range(slots):
        wanted = seq * slots + i
        number = jnp.int32(0)
        for j in range(table.shape[0]):
            number = jnp.where(table[j, request] == wanted, jnp.int32(j), number)
        edges.append((count, BLK, number * BLK, lengths[request]))
        count += BLK
    for step, begin, size in rings:
        origin = pick(cycle, lax.rem(place + step + REQ, REQ))
        edges.append((count, size, (origin * group + member) * piece + begin, shared[0]))
        count += size
    for begin, size, start, length in edges:
        positions = start + lax.broadcasted_iota(jnp.int32, (size, HD), 0)
        lane = lax.broadcasted_iota(jnp.int32, (size, HD), 1)
        bias[begin : begin + size, :] = jnp.where(
            (positions >= length) & (lane == 0), NEGATIVE, 0.0
        ).astype(jnp.bfloat16)
    if fresh:
        bias[count : count + rows, :] = jnp.zeros((rows, HD), jnp.bfloat16)
        theirs = member * rows + lax.broadcasted_iota(jnp.int32, (rows, rows), 0)
        for i, shift in enumerate(shifts):
            mine = (member ^ shift) * rows + lax.broadcasted_iota(jnp.int32, (rows, rows), 1)
            causal[:, i * rows : (i + 1) * rows] = jnp.where(theirs <= mine, 0.0, NEGATIVE)
    if not parted:
        offset = 0
        order = order_rows(stride, False)
        for block in raw:
            take_apart(block, order, keys_here, values_here, offset)
            offset += block.shape[0] // stride
        turn_heads(values_here, turned_here)
    many = len(shifts) * rows
    unit = jnp.where(lax.broadcasted_iota(jnp.int32, (many, HD), 1) == 0, 1.0, 0.0)
    unit = unit.astype(jnp.bfloat16)
    chunks = []
    begin = 0
    for source in sources:
        length = source[0].shape[0]
        for start in range(0, length, 2 * HD):
            size = min(2 * HD, length - start)
            chunks.append((source, start, size, begin + start, fresh and begin == count))
        begin += length

    def beside(values, axis):
        return values[0] if len(values) == 1 else jnp.concatenate(values, axis=axis)

    def query_of(head):
        return jnp.concatenate([beside([q[:, lanes((lowest + head) * HD)] for q in queries], 0), unit], axis=1)

    def score(head, query, chunk, scores, top):
        (keys, _), start, size, at, masked = chunk
        head = head + (lowest if keys.shape[1] == width else 0)
        keys = keys[start : start + size, lanes(head * HD)]
        keys = jnp.concatenate([keys, bias[at : at + size, :]], axis=1)
        part = lax.dot_general(keys, query, ACROSS, preferred_element_type=jnp.float32)
        if masked:
            part = part + causal[start : start + size, :]
        scores[at : at + size, :] = part
        here = jnp.max(part, axis=0, keepdims=True)
        return here if top is None else jnp.maximum(top, here)

    def mix(head, chunk, scores, top, sums):
        (_, turned), start, size, at, _ = chunk
        head = head + (lowest if turned.shape[0] == width else 0)
        weights = jnp.exp2((scores[at : at + size, :] - top) * SCALE)
        here = jnp.sum(weights, axis=0, keepdims=True)
        product = jnp.dot(
            turned[lanes(head * HD), start : start + size],
            weights.astype(jnp.bfloat16),
            preferred_element_type=jnp.float32,
        )
        return (here, product) if sums is None else (sums[0] + here, sums[1] + product)

    together = min(heads // 2, 4 if count <= 256 else 1)

    def some_heads(base, scores, tops, following, next_scores):
        span = lambda k: lanes((base + k) * HD)
        line = lambda k: pl.ds(base + k, 1)
        each = range(together)
        if not first:
            olds = [
                beside([extent[line(skipped + k), :] for extent in old_extents], 1) for k in each
            ]
            tops = [jnp.maximum(top, old * (1.0 / SCALE)) for top, old in zip(tops, olds)]
        next_tops = [None] * together
        sums = [None] * together
        if following is not None:
            next_queries = [query_of(following + k) for k in each]
        for chunk in chunks:
            for k in each:
                if following is not None:
                    next_tops[k] = score(
                        following + k, next_queries[k], chunk, next_scores.at[k], next_tops[k]
                    )
                sums[k] = mix(base + k, chunk, scores.at[k], tops[k], sums[k])
        for k in each:
            summed, mixed = sums[k]
            if not first:
                factor = jnp.exp2(olds[k] - tops[k] * SCALE)
                summed = summed + factor
                old_mix = beside([old_mix[span(skipped + k), :] for old_mix in old_mixes], 1)
                mixed = mixed + old_mix * factor
            mixed = mixed * (1.0 / summed)
            extent = tops[k] * SCALE + jnp.log2(summed)
            for i, result in enumerate(results):
                columns = slice(i * rows, (i + 1) * rows)
                extents[i][line(k), :] = extent[:, columns]
                result[span(k), :] = mixed[:, columns].astype(result.dtype)
        return next_tops

    def two_parts(i, tops):
        base = 2 * together * i
        tops = some_heads(base, first_scores, tops, base + together, second_scores)
        following = jnp.minimum(base + 2 * together, heads - together)
        return some_heads(base + together, second_scores, tops, following, first_scores)

    tops = []
    for k in range(together):
        query, top = query_of(k), None
        for chunk in chunks:
            top = score(k, query, chunk, first_scores.at[k], top)
        tops.append(top)
    if heads == 2 * together:
        tops = some_heads(0, first_scores, tops, together, second_scores)
        some_heads(together, second_scores, tops, None, None)
    else:
        lax.fori_loop(0, heads // (2 * together), two_parts, tops)
    for i, shift in enumerate(shifts):
        if last and shift:
            line = extents[i][:heads, :]
            packed = []
            for _ in range(3):
                rounded = line.astype(jnp.bfloat16).astype(jnp.float32)
                packed.append(rounded)
                line = line - rounded
            gap = stat_rows(heads) - 3 * heads
            if gap:
                packed.append(jnp.zeros((gap, rows), jnp.float32))
            results[i][heads * HD :, :] = jnp.concatenate(packed, axis=0).astype(jnp.bfloat16)


def stat_rows(heads):
    return -(-3 * heads // 16) * 16


def attend(facts, queries, shifts, rings, slots, piece, blocks, parted, old, last, name, within=None):
    group = len(queries)
    queries = [queries[shift] for shift in shifts]
    rows, width = queries[0].shape
    lowest, heads = within or (0, width // HD)
    parted = len(blocks) // 2 if parted else 0
    operands = [*facts, *queries, *blocks]
    if old:
        operands += [old[shift][0] for shift in shifts] + [old[shift][1] for shift in shifts]
    count = sum(size for _, _, size in rings) + BLK * slots + (rows if slots else 0)
    many = len(shifts) * rows
    scratch = [pltpu.VMEM((count, HD), jnp.bfloat16)]
    together = min(heads // 2, 4 if count <= 256 else 1)
    scratch += [pltpu.VMEM((together, count, many), jnp.float32)] * 2
    lines = (max(heads, 8), rows)
    scratch += [pltpu.VMEM(lines, jnp.float32) for shift in shifts if last and shift]
    if slots:
        scratch.append(pltpu.VMEM((rows, many), jnp.float32))
    if not parted:
        scratch.append(pltpu.VMEM((count, heads * HD), jnp.bfloat16))
    mixes = [
        jax.ShapeDtypeStruct((heads * HD + stat_rows(heads), rows), jnp.bfloat16)
        if last and shift
        else jax.ShapeDtypeStruct((heads * HD, rows), jnp.float32)
        for shift in shifts
    ]
    extents = [
        jax.ShapeDtypeStruct(lines, jnp.float32) for shift in shifts if not (last and shift)
    ]
    scores = many * count * heads
    shapes = [*mixes, *extents]
    if not parted:
        shapes += [
            jax.ShapeDtypeStruct((count, heads * HD), jnp.bfloat16),
            jax.ShapeDtypeStruct((heads * HD, count), jnp.bfloat16),
        ]
    results = pl.pallas_call(
        functools.partial(
            attend_kernel,
            (group, shifts, rings, slots, piece, parted, not old, last, lowest, heads),
        ),
        in_specs=[SMEM] * 3 + [VMEM] * (len(operands) - 3),
        out_specs=[VMEM] * len(shapes),
        out_shape=shapes,
        scratch_shapes=scratch,
        compiler_params=params(24),
        cost_estimate=cost(4 * scores * HD, 4 * count * width, scores),
        name=name,
    )(*operands)
    mixes = results[: len(shifts)]
    extents = [*results[len(shifts) : len(shapes) - (0 if parted else 2)]]
    if last:
        extents = [extents.pop(0) if shift == 0 else None for shift in shifts]
    state = {shift: pair for shift, *pair in zip(shifts, mixes, extents)}
    return state, results[len(results) - 2 :]


def combine_kernel(pieces, *refs):
    *pairs, weight, _, attended, sent = refs
    results, own_extents, pairs = pairs[:pieces], pairs[pieces : 2 * pieces], pairs[2 * pieces :]
    rows = results[0].shape[1]
    heads = pieces * results[0].shape[0] // HD
    few = heads // pieces
    own = [extent[:few, :] for extent in own_extents]
    extents = [own[0] if pieces == 1 else jnp.concatenate(own, axis=0)]
    parts = [pairs[start : start + pieces] for start in range(0, len(pairs), pieces)]
    for part in parts:
        here = []
        for half in part:
            lines = half[few * HD :, :].astype(jnp.float32)
            here.append(sum(lines[i * few : (i + 1) * few] for i in range(3)))
        extents.append(here[0] if pieces == 1 else jnp.concatenate(here, axis=0))
    top = functools.reduce(jnp.maximum, extents)
    shares = [jnp.exp2(extent - top) for extent in extents]
    whole = sum(shares)
    shares = [share / whole for share in shares]
    unit = unit_matrix(rows)
    for head in range(heads):
        span = slice(head * HD, (head + 1) * HD)
        line = head % few * HD
        mixes = [results[head // few][line : line + HD, :]] + [
            part[head // few][line : line + HD, :].astype(jnp.float32) for part in parts
        ]
        mixed = sum(mix * share[head : head + 1] for mix, share in zip(mixes, shares))
        attended[:, span] = turned_over(unit, mixed.astype(jnp.bfloat16))
    index = lax.axis_index("tp")
    ways = sent.shape[0] + 1
    columns = weight.shape[1] // ways
    for shift in range(1, ways):
        sent[shift - 1] = jnp.dot(
            attended[...],
            weight[:, lanes((index ^ shift) * columns, columns)],
            preferred_element_type=jnp.float32,
        ).astype(jnp.bfloat16)


def combine(own, parts, w_out, token, ways):
    pieces = len(own)
    results, extents = [mix for mix, _ in own], [extent for _, extent in own]
    rows = results[0].shape[1]
    width = w_out.shape[0]
    columns = w_out.shape[1] // ways
    return pl.pallas_call(
        functools.partial(combine_kernel, pieces),
        in_specs=[VMEM] * (2 * pieces + len(parts) + 2),
        out_specs=[VMEM] * 2,
        out_shape=[
            jax.ShapeDtypeStruct((rows, width), jnp.bfloat16),
            jax.ShapeDtypeStruct((ways - 1, rows, columns), jnp.bfloat16),
        ],
        compiler_params=params(20),
        cost_estimate=cost(2 * rows * width * columns * (ways - 1), 2 * width * w_out.shape[1]),
        name="combine_send",
    )(*results, *extents, *parts, w_out, token)


def keep_kernel(attended, weight, hidden, kept):
    columns = hidden.shape[1]
    product = jnp.dot(
        attended[...],
        weight[:, lanes(lax.axis_index("tp") * columns, columns)],
        preferred_element_type=jnp.float32,
    )
    kept[...] = product + hidden[...].astype(jnp.float32)


def keep(attended, w_out, hidden):
    rows, width = attended.shape
    return pl.pallas_call(
        keep_kernel,
        in_specs=[VMEM] * 3,
        out_specs=VMEM,
        out_shape=jax.ShapeDtypeStruct(hidden.shape, jnp.float32),
        compiler_params=params(20),
        cost_estimate=cost(2 * rows * width * hidden.shape[1], 2 * width * w_out.shape[1]),
        name="keep_own",
    )(attended, w_out, hidden)


def local(
    hidden_in, w_query, w_keyval, w_out, prompt_cache, tail_cache, tail_table, tail_len, shared_len
):
    rows = hidden_in.shape[0]
    group = lax.axis_size("seq") // REQ
    ways = lax.axis_size("tp")
    cycle = cycle_of(group)
    half = REQ // 2
    piece = prompt_cache.shape[0]
    middle = piece // 2
    width = w_query.shape[1]
    stride = 2 * width // HD

    pieces = [hidden_in] + [swap(hidden_in, "tp", shift) for shift in range(1, ways)]
    prompt = viewed(prompt_cache)
    heads = width // HD
    pieces_out = 2 if heads >= 4 else 1
    few = heads // pieces_out
    every = list(range(pieces_out))
    ahead, behind = {part: [None] for part in every}, {part: [None] for part in every}
    nearest = []
    for blocks, way in ((ahead, 1), (behind, -1)):
        block = turn(prompt, cycle, group, way)
        nearest.append(block)
        split = block.reshape(piece, pieces_out, 2 * few, HD)
        for part in every:
            blocks[part].append(split[:, part].reshape(-1, HD))

    def step(part, *others):
        for blocks, way in ((ahead, 1), (behind, -1)):
            block = after(blocks[part][-1], *others)
            if len(blocks[part]) == half:
                cut = middle * 2 * few
                block = block[:cut] if way == 1 else block[cut:]
            blocks[part].append(turn(block, cycle, group, way))

    last_part = every[-1]
    two = pieces_out > 1
    weight = part_weights(w_keyval)
    cosine, sine = angles(after(tail_len, weight), shared_len, rows)
    pieces[0] = after(pieces[0], weight)
    query, normed = project_query(pieces, w_query, cosine, sine)
    queries = [query] + [swap(query, "seq", shift) for shift in range(1, group)]
    tail = viewed(tail_cache.reshape(-1, 2, tail_cache.shape[3]))
    slots = tail_cache.shape[0]
    step(0, weight, query)
    ready = after(cosine, *nearest)
    fresh_keys, fresh_values, fresh_turned = project_keyval(normed, weight, ready, sine)
    if two:
        step(1, fresh_keys)
    own_block = part_keyval([after(tail, fresh_keys), prompt], width, "part_own")
    near_block = part_keyval(nearest, width, "part_near")
    step(0, own_block[0], near_block[0])

    table = tail_table.T
    others = list(range(1, group))
    near_rings = [(0, 0, piece), (-1, 0, piece), (1, 0, piece)]
    near = [*own_block, *near_block]
    fresh = [fresh_keys, fresh_turned]
    facts = (tail_len, shared_len, table)
    theirs, _ = attend(
        facts,
        queries,
        others,
        near_rings,
        slots,
        piece,
        near + fresh,
        True,
        None,
        False,
        "attend_near_others",
    )
    new_cache, token = weave(fresh_keys, fresh_values, theirs[1][0])
    state = {part: theirs for part in every}
    rest = {part: [] for part in every}
    rest_rings = [(sign * hop, 0, piece) for hop in range(2, half) for sign in (-1, 1)]
    far_rings = [(-half, 0, middle), (half, middle, piece - middle)]

    def hop_others(facts, part, hop):
        last = hop == half
        rings = far_rings if last else [(-hop, 0, piece), (hop, 0, piece)]
        state[part], made = attend(
            facts,
            queries,
            others,
            rings,
            0,
            piece,
            [ahead[part][hop], behind[part][hop]],
            False,
            state[part],
            last,
            f"attend_hop{hop}_part{part}",
            (part * few, few),
        )
        rest[part] += made

    def attend_own(facts, part):
        made, _ = attend(
            facts,
            queries,
            [0],
            near_rings + rest_rings + far_rings,
            slots,
            piece,
            near + rest[part] + fresh,
            True,
            None,
            True,
            f"attend_own_part{part}",
            (part * few, few),
        )
        return made[0]

    own = {}
    received = {}
    hop_others(facts, 0, 2)
    if two:
        step(1, state[0][1][1], token)
    step(0, state[0][1][1], token)
    if two:
        hop_others(facts, 1, 2)
        facts = (after(tail_len, state[1][1][1]), shared_len, table)
    hop_others(facts, 0, 3)
    hop_others(facts, 0, 4)
    received[0] = [swap(state[0][shift][0], "seq", shift) for shift in others]
    if two:
        step(1, state[0][1][0])
        hop_others(facts, 1, 3)
        facts = (after(tail_len, received[0][0]), shared_len, table)
        hop_others(facts, 1, 4)
        received[1] = [swap(state[1][shift][0], "seq", shift) for shift in others]
    facts = (after(tail_len, state[last_part][1][0]), shared_len, table)
    for part in every:
        own[part] = attend_own(facts, part)
    parts = [received[part][i] for i in range(len(others)) for part in every]
    attended, sent = combine([own[part] for part in every], parts, w_out, token, ways)
    received = [swap(sent[shift - 1], "tp", shift) for shift in range(1, ways)]
    total = keep(attended, w_out, hidden_in)
    for part in received:
        total = total + part.astype(jnp.float32)
    return (total.astype(jnp.bfloat16), new_cache)


def solution(mesh):
    return jax.shard_map(
        local,
        mesh=mesh,
        in_specs=(
            P("seq", "tp"),
            P(None, "tp"),
            P(None, None, "tp"),
            P("tp", None),
            P("seq", None, "tp"),
            P("seq", None, None, "tp"),
            P(),
            P(),
            P(),
        ),
        out_specs=(P("seq", "tp"), P("seq", None, "tp")),
        check_vma=False,
    )
```

```python
import functools

import jax
import jax.numpy as jnp
import numpy as np
from jax import lax
from jax.experimental import pallas as pl
from jax.experimental.pallas import tpu as pltpu
from jax.sharding import PartitionSpec as P

HD = 128
REQ = 8
BLK = 128
NEGATIVE = -1e30
SCALE = float(HD**-0.5 * np.log2(np.e))


def params(mib=24):
    return pltpu.CompilerParams(vmem_limit_bytes=mib * 2**20)


def cost(flops, moved, exps=0):
    return pl.CostEstimate(flops=int(flops), bytes_accessed=int(moved), transcendentals=int(exps))


def cycle_of(group):
    if group == 2:
        return [0, 2, 4, 6, 7, 5, 3, 1]
    return list(range(REQ))


def pick(table, index):
    result = jnp.int32(table[0])
    for place, value in enumerate(table):
        result = jnp.where(index == place, jnp.int32(value), result)
    return result


def swap(value, axis, mask):
    pairs = [(source, source ^ mask) for source in range(lax.axis_size(axis))]
    return lax.ppermute(value, axis, pairs)


def turn(value, cycle, group, way):
    count = len(cycle)
    pairs = []
    for place in range(count):
        source, target = cycle[place], cycle[(place + way) % count]
        pairs += [(source * group + m, target * group + m) for m in range(group)]
    return lax.ppermute(value, "seq", pairs)


def rotated(vectors, cosine, sine):
    return vectors * cosine + pltpu.roll(vectors, HD // 2, 1) * sine


def position_kernel(lengths, shared, positions):
    rows = positions.shape[0]
    group = lax.axis_size("seq") // REQ
    seq = lax.axis_index("seq")
    start = shared[0] + lengths[seq // group] + (seq % group) * rows
    places = start + lax.broadcasted_iota(jnp.int32, positions.shape, 0)
    positions[...] = places.astype(jnp.float32)


def angles(tail_len, shared_len, rows):
    half = HD // 2
    positions = pl.pallas_call(
        position_kernel,
        in_specs=[SMEM] * 2,
        out_specs=VMEM,
        out_shape=jax.ShapeDtypeStruct((rows, HD), jnp.float32),
        compiler_params=params(8),
        cost_estimate=cost(rows * HD, 4 * rows * HD),
        name="positions",
    )(tail_len, shared_len)
    lane = jnp.arange(HD, dtype=jnp.int32)
    freqs = 10000.0 ** (-(lane % half).astype(jnp.float32) / half)
    angle = positions * freqs
    return jnp.cos(angle), jnp.sin(angle) * jnp.where(lane < half, -1.0, 1.0)


def lanes(start, count=HD):
    if isinstance(start, int):
        return pl.ds(start, count)
    return pl.ds(pl.multiple_of(start, HD), count)


def after(value, *others):
    return lax.optimization_barrier((value, *others))[0]


VMEM = pl.BlockSpec(memory_space=pltpu.VMEM)
HBM = pl.BlockSpec(memory_space=pltpu.HBM)
SMEM = pl.BlockSpec(memory_space=pltpu.SMEM)


def viewed(block):
    count, pair, width = block.shape
    heads = width // HD
    return block.reshape(count, pair, heads, HD).transpose(0, 2, 1, 3).reshape(-1, HD)


def order_rows(stride, back):
    rows = 2 * HD
    places = rows // stride
    row = lax.broadcasted_iota(jnp.int32, (rows, rows), 1 if back else 0)
    column = lax.broadcasted_iota(jnp.int32, (rows, rows), 0 if back else 1)
    source = lax.rem(row, places) * stride + lax.div(row, places)
    return jnp.where(column == source, 1.0, 0.0).astype(jnp.bfloat16)


def reordered(order, tiles):
    both = tiles[0] if len(tiles) == 1 else jnp.concatenate(tiles, axis=1)
    mixed = jnp.dot(order, both, preferred_element_type=jnp.float32).astype(jnp.bfloat16)
    return [mixed[:, i * HD : (i + 1) * HD] for i in range(len(tiles))]


def take_apart(block, order, keys, values, offset):
    heads = keys.shape[1] // HD
    stride = 2 * heads
    count = block.shape[0] // stride
    places = 2 * HD // stride
    for start in range(0, count, 2 * places):
        starts = [at for at in (start, start + places) if at < count]
        tiles = [block[at * stride : (at + places) * stride, :] for at in starts]
        for at, tile in zip(starts, reordered(order, tiles)):
            for head in range(heads):
                for j, result in enumerate((keys, values)):
                    line = (2 * head + j) * places
                    result[offset + at : offset + at + places, head * HD : (head + 1) * HD] = tile[
                        line : line + places
                    ]


ACROSS = (((1,), (1,)), ((), ()))


def unit_matrix(size):
    row = lax.broadcasted_iota(jnp.int32, (size, size), 0)
    column = lax.broadcasted_iota(jnp.int32, (size, size), 1)
    return jnp.where(row == column, 1.0, 0.0).astype(jnp.bfloat16)


def turned_over(unit, value):
    return lax.dot_general(unit, value, ACROSS, preferred_element_type=jnp.float32).astype(
        jnp.bfloat16
    )


def turn_heads(values, result):
    unit = unit_matrix(HD)
    for start in range(0, values.shape[1], HD):
        result[start : start + HD, :] = turned_over(unit, values[:, start : start + HD])


def part_kernel(*refs):
    *blocks, keys, turned, values = refs
    stride = keys.shape[1] * 2 // HD
    order = order_rows(stride, False)
    offset = 0
    for block in blocks:
        take_apart(block, order, keys, values, offset)
        offset += block.shape[0] // stride
    turn_heads(values, turned)


def part_keyval(blocks, width, name):
    count = sum(block.shape[0] for block in blocks) * HD // (2 * width)
    return pl.pallas_call(
        part_kernel,
        in_specs=[VMEM] * len(blocks),
        out_specs=[VMEM] * 2,
        out_shape=[
            jax.ShapeDtypeStruct((count, width), jnp.bfloat16),
            jax.ShapeDtypeStruct((width, count), jnp.bfloat16),
        ],
        scratch_shapes=[pltpu.VMEM((count, width), jnp.bfloat16)],
        compiler_params=params(16),
        cost_estimate=cost(2**10 * count * width, 8 * count * width),
        name=name,
    )(*blocks)


def query_kernel(*refs):
    *pieces, weight, cosine, sine, query, normed = refs
    columns = pieces[0].shape[1]
    index = lax.axis_index("tp")
    features = columns * len(pieces)
    values = [piece[...].astype(jnp.float32) for piece in pieces]
    mean = sum(jnp.sum(v, axis=1, keepdims=True) for v in values) / features
    values = [v - mean for v in values]
    spread = sum(jnp.sum(v * v, axis=1, keepdims=True) for v in values) / features
    inverse = lax.rsqrt(spread + 1e-05)
    for shift, v in enumerate(values):
        normed[:, lanes((index ^ shift) * columns, columns)] = (v * inverse).astype(jnp.bfloat16)
    width = weight.shape[1]
    wide = min(width, 2 * HD)
    for base in range(0, width, wide):
        product = jnp.dot(
            normed[...], weight[:, base : base + wide], preferred_element_type=jnp.float32
        )
        for start in range(0, wide, HD):
            query[:, base + start : base + start + HD] = rotated(
                product[:, start : start + HD], cosine[...], sine[...]
            ).astype(jnp.bfloat16)


def project_query(pieces, w_query, cosine, sine):
    rows, columns = pieces[0].shape
    depth, width = w_query.shape
    return pl.pallas_call(
        query_kernel,
        in_specs=[VMEM] * (len(pieces) + 3),
        out_specs=[VMEM] * 2,
        out_shape=[
            jax.ShapeDtypeStruct((rows, width), jnp.bfloat16),
            jax.ShapeDtypeStruct((rows, depth), jnp.bfloat16),
        ],
        compiler_params=params(20),
        cost_estimate=cost(2 * rows * depth * width, 2 * depth * width),
        name="project_query",
    )(*pieces, w_query, cosine, sine)


def weight_kernel(weight, result, near, arrived):
    slots, chunk = near.shape[:2]
    count = weight.shape[0] // chunk
    stride = result.shape[2] * 2 // HD
    copies = [
        pltpu.make_async_copy(
            weight.at[pl.ds(i * chunk, chunk)], near.at[i % slots], arrived.at[i]
        )
        for i in range(count)
    ]
    for copy in copies[:slots]:
        copy.start()
    order = order_rows(stride, False)
    for i, copy in enumerate(copies):
        copy.wait()
        take_apart(near.at[i % slots], order, result.at[0], result.at[1], i * chunk // stride)
        if i + slots < count:
            copies[i + slots].start()


def part_weights(w_keyval):
    depth, _, width = w_keyval.shape
    weight = viewed(w_keyval)
    count = max(depth // 256, 1)
    chunk = weight.shape[0] // count
    return pl.pallas_call(
        weight_kernel,
        in_specs=[HBM],
        out_specs=VMEM,
        out_shape=jax.ShapeDtypeStruct((2, depth, width), jnp.bfloat16),
        scratch_shapes=[
            pltpu.VMEM((count, chunk, HD), jnp.bfloat16),
            pltpu.SemaphoreType.DMA((count,)),
        ],
        compiler_params=params(38),
        cost_estimate=cost(2**10 * depth * width, 8 * depth * width),
        name="part_weights",
    )(weight)


def keyval_kernel(normed, weight, cosine, sine, keys, values, turned):
    heads = weight.shape[2] // HD
    for head in range(heads):
        span = slice(head * HD, (head + 1) * HD)
        product = jnp.dot(
            normed[...],
            jnp.concatenate([weight[0, :, span], weight[1, :, span]], axis=1),
            preferred_element_type=jnp.float32,
        )
        keys[:, span] = rotated(product[:, :HD], cosine[...], sine[...]).astype(jnp.bfloat16)
        values[:, span] = product[:, HD:].astype(jnp.bfloat16)
    turn_heads(values, turned)


def project_keyval(normed, weight, cosine, sine):
    rows, depth = normed.shape
    width = weight.shape[2]
    flat = jax.ShapeDtypeStruct((rows, width), jnp.bfloat16)
    return pl.pallas_call(
        keyval_kernel,
        in_specs=[VMEM] * 4,
        out_specs=[VMEM] * 3,
        out_shape=[flat, flat, jax.ShapeDtypeStruct((width, rows), jnp.bfloat16)],
        compiler_params=params(20),
        cost_estimate=cost(4 * rows * depth * width, 4 * depth * width),
        name="project_keyval",
    )(normed, weight, cosine, sine)


def weave_kernel(keys, values, *refs):
    cache, token = refs[-2:]
    token[...] = jnp.zeros_like(token)
    rows, width = keys.shape
    heads = width // HD
    stride = 2 * heads
    order = order_rows(stride, True)
    places = 2 * HD // stride
    for start in range(0, rows, 2 * places):
        starts = [at for at in (start, start + places) if at < rows]
        tiles = [
            jnp.concatenate(
                [
                    pair[at : at + places, head * HD : (head + 1) * HD]
                    for head in range(heads)
                    for pair in (keys, values)
                ],
                axis=0,
            )
            for at in starts
        ]
        for at, tile in zip(starts, reordered(order, tiles)):
            cache[at * stride : (at + places) * stride, :] = tile


def weave(keys, values, *earlier):
    rows, width = keys.shape
    heads = width // HD
    cache, token = pl.pallas_call(
        weave_kernel,
        in_specs=[VMEM] * (2 + len(earlier)),
        out_specs=[VMEM] * 2,
        out_shape=[
            jax.ShapeDtypeStruct((rows * heads * 2, HD), jnp.bfloat16),
            jax.ShapeDtypeStruct((8, HD), jnp.float32),
        ],
        compiler_params=params(16),
        cost_estimate=cost(2**10 * rows * width, 8 * rows * width),
        name="weave_cache",
    )(keys, values, *earlier)
    cache = cache.reshape(rows, heads, 2, HD).transpose(0, 2, 1, 3)
    return cache.reshape(rows, 2, width), token


def attend_kernel(spec, *refs):
    group, shifts, rings, slots, piece, parted, first, last, lowest, heads = spec
    fresh = slots > 0
    refs = list(refs)
    take = lambda count: [refs.pop(0) for _ in range(count)]
    lengths, shared, table = take(3)
    queries = take(len(shifts))
    if parted:
        blocks = take(2 * parted)
        sources = list(zip(blocks[::2], blocks[1::2]))
    else:
        raw = take(len(rings))
    if not first:
        old_mixes, old_extents = take(len(shifts)), take(len(shifts))
        skipped = lowest if old_mixes[0].shape[0] == queries[0].shape[1] else 0
    results = take(len(shifts))
    extents = [None if last and shift else take(1)[0] for shift in shifts]
    if not parted:
        sources = [tuple(take(2))]
    bias, first_scores, second_scores = take(3)
    extents = [take(1)[0] if extent is None else extent for extent in extents]
    if fresh:
        causal = take(1)[0]
    if not parted:
        values_here = take(1)[0]
        keys_here, turned_here = sources[0]
    rows, width = queries[0].shape
    stride = 2 * heads
    cycle = cycle_of(group)
    seq = lax.axis_index("seq")
    request, member = seq // group, seq % group
    place = pick(list(np.argsort(cycle)), request)
    edges = []
    count = 0
    for i in range(slots):
        wanted = seq * slots + i
        number = jnp.int32(0)
        for j in range(table.shape[0]):
            number = jnp.where(table[j, request] == wanted, jnp.int32(j), number)
        edges.append((count, BLK, number * BLK, lengths[request]))
        count += BLK
    for step, begin, size in rings:
        origin = pick(cycle, lax.rem(place + step + REQ, REQ))
        edges.append((count, size, (origin * group + member) * piece + begin, shared[0]))
        count += size
    for begin, size, start, length in edges:
        positions = start + lax.broadcasted_iota(jnp.int32, (size, HD), 0)
        lane = lax.broadcasted_iota(jnp.int32, (size, HD), 1)
        bias[begin : begin + size, :] = jnp.where(
            (positions >= length) & (lane == 0), NEGATIVE, 0.0
        ).astype(jnp.bfloat16)
    if fresh:
        bias[count : count + rows, :] = jnp.zeros((rows, HD), jnp.bfloat16)
        theirs = member * rows + lax.broadcasted_iota(jnp.int32, (rows, rows), 0)
        for i, shift in enumerate(shifts):
            mine = (member ^ shift) * rows + lax.broadcasted_iota(jnp.int32, (rows, rows), 1)
            causal[:, i * rows : (i + 1) * rows] = jnp.where(theirs <= mine, 0.0, NEGATIVE)
    if not parted:
        offset = 0
        order = order_rows(stride, False)
        for block in raw:
            take_apart(block, order, keys_here, values_here, offset)
            offset += block.shape[0] // stride
        turn_heads(values_here, turned_here)
    many = len(shifts) * rows
    unit = jnp.where(lax.broadcasted_iota(jnp.int32, (many, HD), 1) == 0, 1.0, 0.0)
    unit = unit.astype(jnp.bfloat16)
    chunks = []
    begin = 0
    for source in sources:
        length = source[0].shape[0]
        for start in range(0, length, 2 * HD):
            size = min(2 * HD, length - start)
            chunks.append((source, start, size, begin + start, fresh and begin == count))
        begin += length

    def beside(values, axis):
        return values[0] if len(values) == 1 else jnp.concatenate(values, axis=axis)

    def query_of(head):
        return jnp.concatenate([beside([q[:, lanes((lowest + head) * HD)] for q in queries], 0), unit], axis=1)

    def score(head, query, chunk, scores, top):
        (keys, _), start, size, at, masked = chunk
        head = head + (lowest if keys.shape[1] == width else 0)
        keys = keys[start : start + size, lanes(head * HD)]
        keys = jnp.concatenate([keys, bias[at : at + size, :]], axis=1)
        part = lax.dot_general(keys, query, ACROSS, preferred_element_type=jnp.float32)
        if masked:
            part = part + causal[start : start + size, :]
        scores[at : at + size, :] = part
        here = jnp.max(part, axis=0, keepdims=True)
        return here if top is None else jnp.maximum(top, here)

    def mix(head, chunk, scores, top, sums):
        (_, turned), start, size, at, _ = chunk
        head = head + (lowest if turned.shape[0] == width else 0)
        weights = jnp.exp2((scores[at : at + size, :] - top) * SCALE)
        here = jnp.sum(weights, axis=0, keepdims=True)
        product = jnp.dot(
            turned[lanes(head * HD), start : start + size],
            weights.astype(jnp.bfloat16),
            preferred_element_type=jnp.float32,
        )
        return (here, product) if sums is None else (sums[0] + here, sums[1] + product)

    together = min(heads // 2, 4 if count <= 256 else 1)

    def some_heads(base, scores, tops, following, next_scores):
        span = lambda k: lanes((base + k) * HD)
        line = lambda k: pl.ds(base + k, 1)
        each = range(together)
        if not first:
            olds = [
                beside([extent[line(skipped + k), :] for extent in old_extents], 1) for k in each
            ]
            tops = [jnp.maximum(top, old * (1.0 / SCALE)) for top, old in zip(tops, olds)]
        next_tops = [None] * together
        sums = [None] * together
        if following is not None:
            next_queries = [query_of(following + k) for k in each]
        for chunk in chunks:
            for k in each:
                if following is not None:
                    next_tops[k] = score(
                        following + k, next_queries[k], chunk, next_scores.at[k], next_tops[k]
                    )
                sums[k] = mix(base + k, chunk, scores.at[k], tops[k], sums[k])
        for k in each:
            summed, mixed = sums[k]
            if not first:
                factor = jnp.exp2(olds[k] - tops[k] * SCALE)
                summed = summed + factor
                old_mix = beside([old_mix[span(skipped + k), :] for old_mix in old_mixes], 1)
                mixed = mixed + old_mix * factor
            mixed = mixed * (1.0 / summed)
            extent = tops[k] * SCALE + jnp.log2(summed)
            for i, result in enumerate(results):
                columns = slice(i * rows, (i + 1) * rows)
                extents[i][line(k), :] = extent[:, columns]
                result[span(k), :] = mixed[:, columns].astype(result.dtype)
        return next_tops

    def two_parts(i, tops):
        base = 2 * together * i
        tops = some_heads(base, first_scores, tops, base + together, second_scores)
        following = jnp.minimum(base + 2 * together, heads - together)
        return some_heads(base + together, second_scores, tops, following, first_scores)

    tops = []
    for k in range(together):
        query, top = query_of(k), None
        for chunk in chunks:
            top = score(k, query, chunk, first_scores.at[k], top)
        tops.append(top)
    if heads == 2 * together:
        tops = some_heads(0, first_scores, tops, together, second_scores)
        some_heads(together, second_scores, tops, None, None)
    else:
        lax.fori_loop(0, heads // (2 * together), two_parts, tops)
    for i, shift in enumerate(shifts):
        if last and shift:
            line = extents[i][:heads, :]
            packed = []
            for _ in range(3):
                rounded = line.astype(jnp.bfloat16).astype(jnp.float32)
                packed.append(rounded)
                line = line - rounded
            gap = stat_rows(heads) - 3 * heads
            if gap:
                packed.append(jnp.zeros((gap, rows), jnp.float32))
            results[i][heads * HD :, :] = jnp.concatenate(packed, axis=0).astype(jnp.bfloat16)


def stat_rows(heads):
    return -(-3 * heads // 16) * 16


def attend(facts, queries, shifts, rings, slots, piece, blocks, parted, old, last, name, within=None):
    group = len(queries)
    queries = [queries[shift] for shift in shifts]
    rows, width = queries[0].shape
    lowest, heads = within or (0, width // HD)
    parted = len(blocks) // 2 if parted else 0
    operands = [*facts, *queries, *blocks]
    if old:
        operands += [old[shift][0] for shift in shifts] + [old[shift][1] for shift in shifts]
    count = sum(size for _, _, size in rings) + BLK * slots + (rows if slots else 0)
    many = len(shifts) * rows
    scratch = [pltpu.VMEM((count, HD), jnp.bfloat16)]
    together = min(heads // 2, 4 if count <= 256 else 1)
    scratch += [pltpu.VMEM((together, count, many), jnp.float32)] * 2
    lines = (max(heads, 8), rows)
    scratch += [pltpu.VMEM(lines, jnp.float32) for shift in shifts if last and shift]
    if slots:
        scratch.append(pltpu.VMEM((rows, many), jnp.float32))
    if not parted:
        scratch.append(pltpu.VMEM((count, heads * HD), jnp.bfloat16))
    mixes = [
        jax.ShapeDtypeStruct((heads * HD + stat_rows(heads), rows), jnp.bfloat16)
        if last and shift
        else jax.ShapeDtypeStruct((heads * HD, rows), jnp.float32)
        for shift in shifts
    ]
    extents = [
        jax.ShapeDtypeStruct(lines, jnp.float32) for shift in shifts if not (last and shift)
    ]
    scores = many * count * heads
    shapes = [*mixes, *extents]
    if not parted:
        shapes += [
            jax.ShapeDtypeStruct((count, heads * HD), jnp.bfloat16),
            jax.ShapeDtypeStruct((heads * HD, count), jnp.bfloat16),
        ]
    results = pl.pallas_call(
        functools.partial(
            attend_kernel,
            (group, shifts, rings, slots, piece, parted, not old, last, lowest, heads),
        ),
        in_specs=[SMEM] * 3 + [VMEM] * (len(operands) - 3),
        out_specs=[VMEM] * len(shapes),
        out_shape=shapes,
        scratch_shapes=scratch,
        compiler_params=params(24),
        cost_estimate=cost(4 * scores * HD, 4 * count * width, scores),
        name=name,
    )(*operands)
    mixes = results[: len(shifts)]
    extents = [*results[len(shifts) : len(shapes) - (0 if parted else 2)]]
    if last:
        extents = [extents.pop(0) if shift == 0 else None for shift in shifts]
    state = {shift: pair for shift, *pair in zip(shifts, mixes, extents)}
    return state, results[len(results) - 2 :]


def combine_kernel(pieces, *refs):
    *pairs, weight, _, attended, sent = refs
    results, own_extents, pairs = pairs[:pieces], pairs[pieces : 2 * pieces], pairs[2 * pieces :]
    rows = results[0].shape[1]
    heads = pieces * results[0].shape[0] // HD
    few = heads // pieces
    own = [extent[:few, :] for extent in own_extents]
    extents = [own[0] if pieces == 1 else jnp.concatenate(own, axis=0)]
    parts = [pairs[start : start + pieces] for start in range(0, len(pairs), pieces)]
    for part in parts:
        here = []
        for half in part:
            lines = half[few * HD :, :].astype(jnp.float32)
            here.append(sum(lines[i * few : (i + 1) * few] for i in range(3)))
        extents.append(here[0] if pieces == 1 else jnp.concatenate(here, axis=0))
    top = functools.reduce(jnp.maximum, extents)
    shares = [jnp.exp2(extent - top) for extent in extents]
    whole = sum(shares)
    shares = [share / whole for share in shares]
    unit = unit_matrix(rows)
    for head in range(heads):
        span = slice(head * HD, (head + 1) * HD)
        line = head % few * HD
        mixes = [results[head // few][line : line + HD, :]] + [
            part[head // few][line : line + HD, :].astype(jnp.float32) for part in parts
        ]
        mixed = sum(mix * share[head : head + 1] for mix, share in zip(mixes, shares))
        attended[:, span] = turned_over(unit, mixed.astype(jnp.bfloat16))
    index = lax.axis_index("tp")
    ways = sent.shape[0] + 1
    columns = weight.shape[1] // ways
    for shift in range(1, ways):
        sent[shift - 1] = jnp.dot(
            attended[...],
            weight[:, lanes((index ^ shift) * columns, columns)],
            preferred_element_type=jnp.float32,
        ).astype(jnp.bfloat16)


def combine(own, parts, w_out, token, ways):
    pieces = len(own)
    results, extents = [mix for mix, _ in own], [extent for _, extent in own]
    rows = results[0].shape[1]
    width = w_out.shape[0]
    columns = w_out.shape[1] // ways
    return pl.pallas_call(
        functools.partial(combine_kernel, pieces),
        in_specs=[VMEM] * (2 * pieces + len(parts) + 2),
        out_specs=[VMEM] * 2,
        out_shape=[
            jax.ShapeDtypeStruct((rows, width), jnp.bfloat16),
            jax.ShapeDtypeStruct((ways - 1, rows, columns), jnp.bfloat16),
        ],
        compiler_params=params(20),
        cost_estimate=cost(2 * rows * width * columns * (ways - 1), 2 * width * w_out.shape[1]),
        name="combine_send",
    )(*results, *extents, *parts, w_out, token)


def keep_kernel(attended, weight, hidden, kept):
    columns = hidden.shape[1]
    product = jnp.dot(
        attended[...],
        weight[:, lanes(lax.axis_index("tp") * columns, columns)],
        preferred_element_type=jnp.float32,
    )
    kept[...] = product + hidden[...].astype(jnp.float32)


def keep(attended, w_out, hidden):
    rows, width = attended.shape
    return pl.pallas_call(
        keep_kernel,
        in_specs=[VMEM] * 3,
        out_specs=VMEM,
        out_shape=jax.ShapeDtypeStruct(hidden.shape, jnp.float32),
        compiler_params=params(20),
        cost_estimate=cost(2 * rows * width * hidden.shape[1], 2 * width * w_out.shape[1]),
        name="keep_own",
    )(attended, w_out, hidden)


def local(
    hidden_in, w_query, w_keyval, w_out, prompt_cache, tail_cache, tail_table, tail_len, shared_len
):
    rows = hidden_in.shape[0]
    group = lax.axis_size("seq") // REQ
    ways = lax.axis_size("tp")
    cycle = cycle_of(group)
    half = REQ // 2
    piece = prompt_cache.shape[0]
    middle = piece // 2
    width = w_query.shape[1]
    stride = 2 * width // HD

    pieces = [hidden_in] + [swap(hidden_in, "tp", shift) for shift in range(1, ways)]
    prompt = viewed(prompt_cache)
    heads = width // HD
    pieces_out = 2 if heads >= 4 else 1
    few = heads // pieces_out
    every = list(range(pieces_out))
    ahead, behind = {part: [None] for part in every}, {part: [None] for part in every}
    nearest = []
    for blocks, way in ((ahead, 1), (behind, -1)):
        nearest.append(turn(prompt, cycle, group, way))

    def step(part, *others):
        for blocks, way in ((ahead, 1), (behind, -1)):
            block = after(blocks[part][-1], *others) if others else blocks[part][-1]
            if len(blocks[part]) == half:
                cut = middle * 2 * few
                block = block[:cut] if way == 1 else block[cut:]
            blocks[part].append(turn(block, cycle, group, way))

    last_part = every[-1]
    two = pieces_out > 1
    weight = part_weights(w_keyval)
    cosine, sine = angles(after(tail_len, weight), shared_len, rows)
    pieces[0] = after(pieces[0], weight)
    query, normed = project_query(pieces, w_query, cosine, sine)
    queries = [query] + [swap(query, "seq", shift) for shift in range(1, group)]
    tail = viewed(tail_cache.reshape(-1, 2, tail_cache.shape[3]))
    slots = tail_cache.shape[0]
    for blocks, block in zip((ahead, behind), nearest):
        split = after(block, weight, query).reshape(piece, pieces_out, 2 * few, HD)
        for part in every:
            blocks[part].append(split[:, part].reshape(-1, HD))
    step(0)
    ready = after(cosine, *nearest)
    fresh_keys, fresh_values, fresh_turned = project_keyval(normed, weight, ready, sine)
    if two:
        step(1, fresh_keys)
    own_block = part_keyval([after(tail, fresh_keys), prompt], width, "part_own")
    near_block = part_keyval(nearest, width, "part_near")
    step(0, own_block[0], near_block[0])

    table = tail_table.T
    others = list(range(1, group))
    near_rings = [(0, 0, piece), (-1, 0, piece), (1, 0, piece)]
    near = [*own_block, *near_block]
    fresh = [fresh_keys, fresh_turned]
    facts = (tail_len, shared_len, table)
    theirs, _ = attend(
        facts,
        queries,
        others,
        near_rings,
        slots,
        piece,
        near + fresh,
        True,
        None,
        False,
        "attend_near_others",
    )
    state = {part: theirs for part in every}
    rest = {part: [] for part in every}
    rest_rings = [(sign * hop, 0, piece) for hop in range(2, half) for sign in (-1, 1)]
    far_rings = [(-half, 0, middle), (half, middle, piece - middle)]

    def hop_others(facts, part, hop):
        last = hop == half
        rings = far_rings if last else [(-hop, 0, piece), (hop, 0, piece)]
        state[part], made = attend(
            facts,
            queries,
            others,
            rings,
            0,
            piece,
            [ahead[part][hop], behind[part][hop]],
            False,
            state[part],
            last,
            f"attend_hop{hop}_part{part}",
            (part * few, few),
        )
        rest[part] += made

    def attend_own(facts, part):
        made, _ = attend(
            facts,
            queries,
            [0],
            near_rings + rest_rings + far_rings,
            slots,
            piece,
            near + rest[part] + fresh,
            True,
            None,
            True,
            f"attend_own_part{part}",
            (part * few, few),
        )
        return made[0]

    own = {}
    received = {}
    hop_others(facts, 0, 2)
    step(0, state[0][1][1])
    hop_others(facts, 0, 3)
    if two:
        step(1, state[0][1][1])
    hop_others(facts, 0, 4)
    new_cache, token = weave(fresh_keys, fresh_values, state[0][1][0])
    if two:
        hop_others((after(tail_len, token), shared_len, table), 1, 2)
    received[0] = [swap(state[0][shift][0], "seq", shift) for shift in others]
    if two:
        step(1, state[1][1][1])
        hop_others(facts, 1, 3)
        facts = (after(tail_len, received[0][0]), shared_len, table)
        hop_others(facts, 1, 4)
        received[1] = [swap(state[1][shift][0], "seq", shift) for shift in others]
    facts = (after(tail_len, state[last_part][1][0]), shared_len, table)
    for part in every:
        own[part] = attend_own(facts, part)
    parts = [received[part][i] for i in range(len(others)) for part in every]
    attended, sent = combine([own[part] for part in every], parts, w_out, token, ways)
    received = [swap(sent[shift - 1], "tp", shift) for shift in range(1, ways)]
    total = keep(attended, w_out, hidden_in)
    for part in received:
        total = total + part.astype(jnp.float32)
    return (total.astype(jnp.bfloat16), new_cache)


def solution(mesh):
    return jax.shard_map(
        local,
        mesh=mesh,
        in_specs=(
            P("seq", "tp"),
            P(None, "tp"),
            P(None, None, "tp"),
            P("tp", None),
            P("seq", None, "tp"),
            P("seq", None, None, "tp"),
            P(),
            P(),
            P(),
        ),
        out_specs=(P("seq", "tp"), P("seq", None, "tp")),
        check_vma=False,
    )
```

```python
import functools

import jax
import jax.numpy as jnp
import numpy as np
from jax import lax
from jax.experimental import pallas as pl
from jax.experimental.pallas import tpu as pltpu
from jax.sharding import PartitionSpec as P

HD = 128
REQ = 8
BLK = 128
NEGATIVE = -1e30
SCALE = float(HD**-0.5 * np.log2(np.e))


def params(mib=24):
    return pltpu.CompilerParams(vmem_limit_bytes=mib * 2**20)


def cost(flops, moved, exps=0):
    return pl.CostEstimate(flops=int(flops), bytes_accessed=int(moved), transcendentals=int(exps))


def cycle_of(group):
    if group == 2:
        return [0, 2, 4, 6, 7, 5, 3, 1]
    return list(range(REQ))


def pick(table, index):
    result = jnp.int32(table[0])
    for place, value in enumerate(table):
        result = jnp.where(index == place, jnp.int32(value), result)
    return result


def swap(value, axis, mask):
    pairs = [(source, source ^ mask) for source in range(lax.axis_size(axis))]
    return lax.ppermute(value, axis, pairs)


def turn(value, cycle, group, way):
    count = len(cycle)
    pairs = []
    for place in range(count):
        source, target = cycle[place], cycle[(place + way) % count]
        pairs += [(source * group + m, target * group + m) for m in range(group)]
    return lax.ppermute(value, "seq", pairs)


def rotated(vectors, cosine, sine):
    return vectors * cosine + pltpu.roll(vectors, HD // 2, 1) * sine


def position_kernel(lengths, shared, positions):
    rows = positions.shape[0]
    group = lax.axis_size("seq") // REQ
    seq = lax.axis_index("seq")
    start = shared[0] + lengths[seq // group] + (seq % group) * rows
    places = start + lax.broadcasted_iota(jnp.int32, positions.shape, 0)
    positions[...] = places.astype(jnp.float32)


def angles(tail_len, shared_len, rows):
    half = HD // 2
    positions = pl.pallas_call(
        position_kernel,
        in_specs=[SMEM] * 2,
        out_specs=VMEM,
        out_shape=jax.ShapeDtypeStruct((rows, HD), jnp.float32),
        compiler_params=params(8),
        cost_estimate=cost(rows * HD, 4 * rows * HD),
        name="positions",
    )(tail_len, shared_len)
    lane = jnp.arange(HD, dtype=jnp.int32)
    freqs = 10000.0 ** (-(lane % half).astype(jnp.float32) / half)
    angle = positions * freqs
    return jnp.cos(angle), jnp.sin(angle) * jnp.where(lane < half, -1.0, 1.0)


def lanes(start, count=HD):
    if isinstance(start, int):
        return pl.ds(start, count)
    return pl.ds(pl.multiple_of(start, HD), count)


def after(value, *others):
    return lax.optimization_barrier((value, *others))[0]


VMEM = pl.BlockSpec(memory_space=pltpu.VMEM)
HBM = pl.BlockSpec(memory_space=pltpu.HBM)
SMEM = pl.BlockSpec(memory_space=pltpu.SMEM)


def viewed(block):
    count, pair, width = block.shape
    heads = width // HD
    return block.reshape(count, pair, heads, HD).transpose(0, 2, 1, 3).reshape(-1, HD)


def order_rows(stride, back):
    rows = 2 * HD
    places = rows // stride
    row = lax.broadcasted_iota(jnp.int32, (rows, rows), 1 if back else 0)
    column = lax.broadcasted_iota(jnp.int32, (rows, rows), 0 if back else 1)
    source = lax.rem(row, places) * stride + lax.div(row, places)
    return jnp.where(column == source, 1.0, 0.0).astype(jnp.bfloat16)


def reordered(order, tiles):
    both = tiles[0] if len(tiles) == 1 else jnp.concatenate(tiles, axis=1)
    mixed = jnp.dot(order, both, preferred_element_type=jnp.float32).astype(jnp.bfloat16)
    return [mixed[:, i * HD : (i + 1) * HD] for i in range(len(tiles))]


def take_apart(block, order, keys, values, offset):
    heads = keys.shape[1] // HD
    stride = 2 * heads
    count = block.shape[0] // stride
    places = 2 * HD // stride
    for start in range(0, count, 2 * places):
        starts = [at for at in (start, start + places) if at < count]
        tiles = [block[at * stride : (at + places) * stride, :] for at in starts]
        for at, tile in zip(starts, reordered(order, tiles)):
            for head in range(heads):
                for j, result in enumerate((keys, values)):
                    line = (2 * head + j) * places
                    result[offset + at : offset + at + places, head * HD : (head + 1) * HD] = tile[
                        line : line + places
                    ]


ACROSS = (((1,), (1,)), ((), ()))


def unit_matrix(size):
    row = lax.broadcasted_iota(jnp.int32, (size, size), 0)
    column = lax.broadcasted_iota(jnp.int32, (size, size), 1)
    return jnp.where(row == column, 1.0, 0.0).astype(jnp.bfloat16)


def turned_over(unit, value):
    return lax.dot_general(unit, value, ACROSS, preferred_element_type=jnp.float32).astype(
        jnp.bfloat16
    )


def turn_heads(values, result):
    unit = unit_matrix(HD)
    for start in range(0, values.shape[1], HD):
        result[start : start + HD, :] = turned_over(unit, values[:, start : start + HD])


def part_kernel(*refs):
    *blocks, keys, turned, values = refs
    stride = keys.shape[1] * 2 // HD
    order = order_rows(stride, False)
    offset = 0
    for block in blocks:
        take_apart(block, order, keys, values, offset)
        offset += block.shape[0] // stride
    turn_heads(values, turned)


def part_keyval(blocks, width, name):
    count = sum(block.shape[0] for block in blocks) * HD // (2 * width)
    return pl.pallas_call(
        part_kernel,
        in_specs=[VMEM] * len(blocks),
        out_specs=[VMEM] * 2,
        out_shape=[
            jax.ShapeDtypeStruct((count, width), jnp.bfloat16),
            jax.ShapeDtypeStruct((width, count), jnp.bfloat16),
        ],
        scratch_shapes=[pltpu.VMEM((count, width), jnp.bfloat16)],
        compiler_params=params(16),
        cost_estimate=cost(2**10 * count * width, 8 * count * width),
        name=name,
    )(*blocks)


def query_kernel(*refs):
    *pieces, weight, cosine, sine, query, normed = refs
    columns = pieces[0].shape[1]
    index = lax.axis_index("tp")
    features = columns * len(pieces)
    values = [piece[...].astype(jnp.float32) for piece in pieces]
    mean = sum(jnp.sum(v, axis=1, keepdims=True) for v in values) / features
    values = [v - mean for v in values]
    spread = sum(jnp.sum(v * v, axis=1, keepdims=True) for v in values) / features
    inverse = lax.rsqrt(spread + 1e-05)
    for shift, v in enumerate(values):
        normed[:, lanes((index ^ shift) * columns, columns)] = (v * inverse).astype(jnp.bfloat16)
    width = weight.shape[1]
    wide = min(width, 2 * HD)
    for base in range(0, width, wide):
        product = jnp.dot(
            normed[...], weight[:, base : base + wide], preferred_element_type=jnp.float32
        )
        for start in range(0, wide, HD):
            query[:, base + start : base + start + HD] = rotated(
                product[:, start : start + HD], cosine[...], sine[...]
            ).astype(jnp.bfloat16)


def project_query(pieces, w_query, cosine, sine):
    rows, columns = pieces[0].shape
    depth, width = w_query.shape
    return pl.pallas_call(
        query_kernel,
        in_specs=[VMEM] * (len(pieces) + 3),
        out_specs=[VMEM] * 2,
        out_shape=[
            jax.ShapeDtypeStruct((rows, width), jnp.bfloat16),
            jax.ShapeDtypeStruct((rows, depth), jnp.bfloat16),
        ],
        compiler_params=params(20),
        cost_estimate=cost(2 * rows * depth * width, 2 * depth * width),
        name="project_query",
    )(*pieces, w_query, cosine, sine)


def weight_kernel(weight, result, near, arrived):
    slots, chunk = near.shape[:2]
    count = weight.shape[0] // chunk
    stride = result.shape[2] * 2 // HD
    copies = [
        pltpu.make_async_copy(
            weight.at[pl.ds(i * chunk, chunk)], near.at[i % slots], arrived.at[i]
        )
        for i in range(count)
    ]
    for copy in copies[:slots]:
        copy.start()
    order = order_rows(stride, False)
    for i, copy in enumerate(copies):
        copy.wait()
        take_apart(near.at[i % slots], order, result.at[0], result.at[1], i * chunk // stride)
        if i + slots < count:
            copies[i + slots].start()


def part_weights(w_keyval):
    depth, _, width = w_keyval.shape
    weight = viewed(w_keyval)
    count = max(depth // 256, 1)
    chunk = weight.shape[0] // count
    return pl.pallas_call(
        weight_kernel,
        in_specs=[HBM],
        out_specs=VMEM,
        out_shape=jax.ShapeDtypeStruct((2, depth, width), jnp.bfloat16),
        scratch_shapes=[
            pltpu.VMEM((count, chunk, HD), jnp.bfloat16),
            pltpu.SemaphoreType.DMA((count,)),
        ],
        compiler_params=params(38),
        cost_estimate=cost(2**10 * depth * width, 8 * depth * width),
        name="part_weights",
    )(weight)


def keyval_kernel(normed, weight, cosine, sine, keys, values, turned):
    heads = weight.shape[2] // HD
    for head in range(heads):
        span = slice(head * HD, (head + 1) * HD)
        product = jnp.dot(
            normed[...],
            jnp.concatenate([weight[0, :, span], weight[1, :, span]], axis=1),
            preferred_element_type=jnp.float32,
        )
        keys[:, span] = rotated(product[:, :HD], cosine[...], sine[...]).astype(jnp.bfloat16)
        values[:, span] = product[:, HD:].astype(jnp.bfloat16)
    turn_heads(values, turned)


def project_keyval(normed, weight, cosine, sine):
    rows, depth = normed.shape
    width = weight.shape[2]
    flat = jax.ShapeDtypeStruct((rows, width), jnp.bfloat16)
    return pl.pallas_call(
        keyval_kernel,
        in_specs=[VMEM] * 4,
        out_specs=[VMEM] * 3,
        out_shape=[flat, flat, jax.ShapeDtypeStruct((width, rows), jnp.bfloat16)],
        compiler_params=params(20),
        cost_estimate=cost(4 * rows * depth * width, 4 * depth * width),
        name="project_keyval",
    )(normed, weight, cosine, sine)


def weave_kernel(keys, values, *refs):
    cache, token = refs[-2:]
    token[...] = jnp.zeros_like(token)
    rows, width = keys.shape
    heads = width // HD
    stride = 2 * heads
    order = order_rows(stride, True)
    places = 2 * HD // stride
    for start in range(0, rows, 2 * places):
        starts = [at for at in (start, start + places) if at < rows]
        tiles = [
            jnp.concatenate(
                [
                    pair[at : at + places, head * HD : (head + 1) * HD]
                    for head in range(heads)
                    for pair in (keys, values)
                ],
                axis=0,
            )
            for at in starts
        ]
        for at, tile in zip(starts, reordered(order, tiles)):
            cache[at * stride : (at + places) * stride, :] = tile


def weave(keys, values, *earlier):
    rows, width = keys.shape
    heads = width // HD
    cache, token = pl.pallas_call(
        weave_kernel,
        in_specs=[VMEM] * (2 + len(earlier)),
        out_specs=[VMEM] * 2,
        out_shape=[
            jax.ShapeDtypeStruct((rows * heads * 2, HD), jnp.bfloat16),
            jax.ShapeDtypeStruct((8, HD), jnp.float32),
        ],
        compiler_params=params(16),
        cost_estimate=cost(2**10 * rows * width, 8 * rows * width),
        name="weave_cache",
    )(keys, values, *earlier)
    cache = cache.reshape(rows, heads, 2, HD).transpose(0, 2, 1, 3)
    return cache.reshape(rows, 2, width), token


def attend_kernel(spec, *refs):
    group, shifts, rings, slots, piece, parted, first, last, lowest, heads = spec
    fresh = slots > 0
    refs = list(refs)
    take = lambda count: [refs.pop(0) for _ in range(count)]
    lengths, shared, table = take(3)
    queries = take(len(shifts))
    if parted:
        blocks = take(2 * parted)
        sources = list(zip(blocks[::2], blocks[1::2]))
    else:
        raw = take(len(rings))
    if not first:
        old_mixes, old_extents = take(len(shifts)), take(len(shifts))
    results = take(len(shifts))
    extents = [None if last and shift else take(1)[0] for shift in shifts]
    if not parted:
        sources = [tuple(take(2))]
    bias, first_scores, second_scores = take(3)
    extents = [take(1)[0] if extent is None else extent for extent in extents]
    if fresh:
        causal = take(1)[0]
    if not parted:
        values_here = take(1)[0]
        keys_here, turned_here = sources[0]
    rows, width = queries[0].shape
    stride = 2 * width // HD
    cycle = cycle_of(group)
    seq = lax.axis_index("seq")
    request, member = seq // group, seq % group
    place = pick(list(np.argsort(cycle)), request)
    edges = []
    count = 0
    for i in range(slots):
        wanted = seq * slots + i
        number = jnp.int32(0)
        for j in range(table.shape[0]):
            number = jnp.where(table[j, request] == wanted, jnp.int32(j), number)
        edges.append((count, BLK, number * BLK, lengths[request]))
        count += BLK
    for step, begin, size in rings:
        origin = pick(cycle, lax.rem(place + step + REQ, REQ))
        edges.append((count, size, (origin * group + member) * piece + begin, shared[0]))
        count += size
    for begin, size, start, length in edges:
        positions = start + lax.broadcasted_iota(jnp.int32, (size, HD), 0)
        lane = lax.broadcasted_iota(jnp.int32, (size, HD), 1)
        bias[begin : begin + size, :] = jnp.where(
            (positions >= length) & (lane == 0), NEGATIVE, 0.0
        ).astype(jnp.bfloat16)
    if fresh:
        bias[count : count + rows, :] = jnp.zeros((rows, HD), jnp.bfloat16)
        theirs = member * rows + lax.broadcasted_iota(jnp.int32, (rows, rows), 0)
        for i, shift in enumerate(shifts):
            mine = (member ^ shift) * rows + lax.broadcasted_iota(jnp.int32, (rows, rows), 1)
            causal[:, i * rows : (i + 1) * rows] = jnp.where(theirs <= mine, 0.0, NEGATIVE)
    if not parted:
        offset = 0
        order = order_rows(stride, False)
        for block in raw:
            take_apart(block, order, keys_here, values_here, offset)
            offset += block.shape[0] // stride
        turn_heads(values_here, turned_here)
    many = len(shifts) * rows
    unit = jnp.where(lax.broadcasted_iota(jnp.int32, (many, HD), 1) == 0, 1.0, 0.0)
    unit = unit.astype(jnp.bfloat16)
    chunks = []
    begin = 0
    for source in sources:
        length = source[0].shape[0]
        for start in range(0, length, 2 * HD):
            size = min(2 * HD, length - start)
            chunks.append((source, start, size, begin + start, fresh and begin == count))
        begin += length

    def beside(values, axis):
        return values[0] if len(values) == 1 else jnp.concatenate(values, axis=axis)

    def query_of(head):
        return jnp.concatenate([beside([q[:, lanes((lowest + head) * HD)] for q in queries], 0), unit], axis=1)

    def score(head, query, chunk, scores, top):
        (keys, _), start, size, at, masked = chunk
        keys = keys[start : start + size, lanes((lowest + head) * HD)]
        keys = jnp.concatenate([keys, bias[at : at + size, :]], axis=1)
        part = lax.dot_general(keys, query, ACROSS, preferred_element_type=jnp.float32)
        if masked:
            part = part + causal[start : start + size, :]
        scores[at : at + size, :] = part
        here = jnp.max(part, axis=0, keepdims=True)
        return here if top is None else jnp.maximum(top, here)

    def mix(head, chunk, scores, top, sums):
        (_, turned), start, size, at, _ = chunk
        weights = jnp.exp2((scores[at : at + size, :] - top) * SCALE)
        here = jnp.sum(weights, axis=0, keepdims=True)
        product = jnp.dot(
            turned[lanes((lowest + head) * HD), start : start + size],
            weights.astype(jnp.bfloat16),
            preferred_element_type=jnp.float32,
        )
        return (here, product) if sums is None else (sums[0] + here, sums[1] + product)

    together = min(heads // 2, 4 if count <= 256 else 1)

    def some_heads(base, scores, tops, following, next_scores):
        span = lambda k: lanes((base + k) * HD)
        line = lambda k: pl.ds(base + k, 1)
        each = range(together)
        if not first:
            olds = [beside([extent[line(lowest + k), :] for extent in old_extents], 1) for k in each]
            tops = [jnp.maximum(top, old * (1.0 / SCALE)) for top, old in zip(tops, olds)]
        next_tops = [None] * together
        sums = [None] * together
        if following is not None:
            next_queries = [query_of(following + k) for k in each]
        for chunk in chunks:
            for k in each:
                if following is not None:
                    next_tops[k] = score(
                        following + k, next_queries[k], chunk, next_scores.at[k], next_tops[k]
                    )
                sums[k] = mix(base + k, chunk, scores.at[k], tops[k], sums[k])
        for k in each:
            summed, mixed = sums[k]
            if not first:
                factor = jnp.exp2(olds[k] - tops[k] * SCALE)
                summed = summed + factor
                old_mix = beside([old_mix[span(lowest + k), :] for old_mix in old_mixes], 1)
                mixed = mixed + old_mix * factor
            mixed = mixed * (1.0 / summed)
            extent = tops[k] * SCALE + jnp.log2(summed)
            for i, result in enumerate(results):
                columns = slice(i * rows, (i + 1) * rows)
                extents[i][line(k), :] = extent[:, columns]
                result[span(k), :] = mixed[:, columns].astype(result.dtype)
        return next_tops

    def two_parts(i, tops):
        base = 2 * together * i
        tops = some_heads(base, first_scores, tops, base + together, second_scores)
        following = jnp.minimum(base + 2 * together, heads - together)
        return some_heads(base + together, second_scores, tops, following, first_scores)

    tops = []
    for k in range(together):
        query, top = query_of(k), None
        for chunk in chunks:
            top = score(k, query, chunk, first_scores.at[k], top)
        tops.append(top)
    if heads == 2 * together:
        tops = some_heads(0, first_scores, tops, together, second_scores)
        some_heads(together, second_scores, tops, None, None)
    else:
        lax.fori_loop(0, heads // (2 * together), two_parts, tops)
    for i, shift in enumerate(shifts):
        if last and shift:
            line = extents[i][:heads, :]
            packed = []
            for _ in range(3):
                rounded = line.astype(jnp.bfloat16).astype(jnp.float32)
                packed.append(rounded)
                line = line - rounded
            gap = stat_rows(heads) - 3 * heads
            if gap:
                packed.append(jnp.zeros((gap, rows), jnp.float32))
            results[i][heads * HD :, :] = jnp.concatenate(packed, axis=0).astype(jnp.bfloat16)


def stat_rows(heads):
    return -(-3 * heads // 16) * 16


def attend(facts, queries, shifts, rings, slots, piece, blocks, parted, old, last, name, within=None):
    group = len(queries)
    queries = [queries[shift] for shift in shifts]
    rows, width = queries[0].shape
    lowest, heads = within or (0, width // HD)
    parted = len(blocks) // 2 if parted else 0
    operands = [*facts, *queries, *blocks]
    if old:
        operands += [old[shift][0] for shift in shifts] + [old[shift][1] for shift in shifts]
    count = sum(size for _, _, size in rings) + BLK * slots + (rows if slots else 0)
    many = len(shifts) * rows
    scratch = [pltpu.VMEM((count, HD), jnp.bfloat16)]
    together = min(heads // 2, 4 if count <= 256 else 1)
    scratch += [pltpu.VMEM((together, count, many), jnp.float32)] * 2
    lines = (max(heads, 8), rows)
    scratch += [pltpu.VMEM(lines, jnp.float32) for shift in shifts if last and shift]
    if slots:
        scratch.append(pltpu.VMEM((rows, many), jnp.float32))
    if not parted:
        scratch.append(pltpu.VMEM((count, width), jnp.bfloat16))
    mixes = [
        jax.ShapeDtypeStruct((heads * HD + stat_rows(heads), rows), jnp.bfloat16)
        if last and shift
        else jax.ShapeDtypeStruct((heads * HD, rows), jnp.float32)
        for shift in shifts
    ]
    extents = [
        jax.ShapeDtypeStruct(lines, jnp.float32) for shift in shifts if not (last and shift)
    ]
    scores = many * count * heads
    shapes = [*mixes, *extents]
    if not parted:
        shapes += [
            jax.ShapeDtypeStruct((count, width), jnp.bfloat16),
            jax.ShapeDtypeStruct((width, count), jnp.bfloat16),
        ]
    results = pl.pallas_call(
        functools.partial(
            attend_kernel,
            (group, shifts, rings, slots, piece, parted, not old, last, lowest, heads),
        ),
        in_specs=[SMEM] * 3 + [VMEM] * (len(operands) - 3),
        out_specs=[VMEM] * len(shapes),
        out_shape=shapes,
        scratch_shapes=scratch,
        compiler_params=params(24),
        cost_estimate=cost(4 * scores * HD, 4 * count * width, scores),
        name=name,
    )(*operands)
    mixes = results[: len(shifts)]
    extents = [*results[len(shifts) : len(shapes) - (0 if parted else 2)]]
    if last:
        extents = [extents.pop(0) if shift == 0 else None for shift in shifts]
    state = {shift: pair for shift, *pair in zip(shifts, mixes, extents)}
    return state, results[len(results) - 2 :]


def combine_kernel(pieces, *refs):
    result, extent, *pairs, weight, _, attended, sent = refs
    width, rows = result.shape
    heads = width // HD
    extents = [extent[:heads, :]]
    few = heads // pieces
    parts = [pairs[start : start + pieces] for start in range(0, len(pairs), pieces)]
    for part in parts:
        here = []
        for half in part:
            lines = half[few * HD :, :].astype(jnp.float32)
            here.append(sum(lines[i * few : (i + 1) * few] for i in range(3)))
        extents.append(here[0] if pieces == 1 else jnp.concatenate(here, axis=0))
    top = functools.reduce(jnp.maximum, extents)
    shares = [jnp.exp2(extent - top) for extent in extents]
    whole = sum(shares)
    shares = [share / whole for share in shares]
    unit = unit_matrix(rows)
    for head in range(heads):
        span = slice(head * HD, (head + 1) * HD)
        line = head % few * HD
        mixes = [result[span, :]] + [
            part[head // few][line : line + HD, :].astype(jnp.float32) for part in parts
        ]
        mixed = sum(mix * share[head : head + 1] for mix, share in zip(mixes, shares))
        attended[:, span] = turned_over(unit, mixed.astype(jnp.bfloat16))
    index = lax.axis_index("tp")
    ways = sent.shape[0] + 1
    columns = weight.shape[1] // ways
    for shift in range(1, ways):
        sent[shift - 1] = jnp.dot(
            attended[...],
            weight[:, lanes((index ^ shift) * columns, columns)],
            preferred_element_type=jnp.float32,
        ).astype(jnp.bfloat16)


def combine(result, extent, parts, pieces, w_out, token, ways):
    width, rows = result.shape
    columns = w_out.shape[1] // ways
    return pl.pallas_call(
        functools.partial(combine_kernel, pieces),
        in_specs=[VMEM] * (4 + len(parts)),
        out_specs=[VMEM] * 2,
        out_shape=[
            jax.ShapeDtypeStruct((rows, width), jnp.bfloat16),
            jax.ShapeDtypeStruct((ways - 1, rows, columns), jnp.bfloat16),
        ],
        compiler_params=params(20),
        cost_estimate=cost(2 * rows * width * columns * (ways - 1), 2 * width * w_out.shape[1]),
        name="combine_send",
    )(result, extent, *parts, w_out, token)


def keep_kernel(attended, weight, hidden, kept):
    columns = hidden.shape[1]
    product = jnp.dot(
        attended[...],
        weight[:, lanes(lax.axis_index("tp") * columns, columns)],
        preferred_element_type=jnp.float32,
    )
    kept[...] = product + hidden[...].astype(jnp.float32)


def keep(attended, w_out, hidden):
    rows, width = attended.shape
    return pl.pallas_call(
        keep_kernel,
        in_specs=[VMEM] * 3,
        out_specs=VMEM,
        out_shape=jax.ShapeDtypeStruct(hidden.shape, jnp.float32),
        compiler_params=params(20),
        cost_estimate=cost(2 * rows * width * hidden.shape[1], 2 * width * w_out.shape[1]),
        name="keep_own",
    )(attended, w_out, hidden)


def local(
    hidden_in, w_query, w_keyval, w_out, prompt_cache, tail_cache, tail_table, tail_len, shared_len
):
    rows = hidden_in.shape[0]
    group = lax.axis_size("seq") // REQ
    ways = lax.axis_size("tp")
    cycle = cycle_of(group)
    half = REQ // 2
    piece = prompt_cache.shape[0]
    middle = piece // 2
    width = w_query.shape[1]
    stride = 2 * width // HD

    pieces = [hidden_in] + [swap(hidden_in, "tp", shift) for shift in range(1, ways)]
    prompt = viewed(prompt_cache)
    ahead, behind = {0: [None], 1: [None]}, {0: [None], 1: [None]}
    nearest = []
    for blocks, way in ((ahead, 1), (behind, -1)):
        block = turn(prompt, cycle, group, way)
        nearest.append(block)
        blocks[0].append(block[: middle * stride])
        blocks[1].append(block[middle * stride :])

    def step(which, *others):
        for blocks, part, way in ((ahead, which, 1), (behind, 1 - which, -1)):
            block = blocks[part][-1]
            if others:
                block = after(block, *others)
            blocks[part].append(turn(block, cycle, group, way))

    def arrived(hop):
        blocks = [way[part][hop] for way in (ahead, behind) for part in (0, 1)]
        rings = [(sign * hop, part * middle, middle) for sign in (-1, 1) for part in (0, 1)]
        return blocks, rings

    weight = part_weights(w_keyval)
    cosine, sine = angles(after(tail_len, weight), shared_len, rows)
    pieces[0] = after(pieces[0], weight)
    query, normed = project_query(pieces, w_query, cosine, sine)
    queries = [query] + [swap(query, "seq", shift) for shift in range(1, group)]
    tail = viewed(tail_cache.reshape(-1, 2, tail_cache.shape[3]))
    slots = tail_cache.shape[0]
    own_block = part_keyval([tail, prompt], width, "part_own")
    step(0, weight, query)
    step(1, query)
    ready = after(cosine, ahead[1][1], behind[0][1])
    fresh_keys, fresh_values, fresh_turned = project_keyval(normed, weight, ready, sine)
    step(0, fresh_keys)
    near_block = part_keyval(nearest, width, "part_near")
    step(1, near_block[0])

    table = tail_table.T
    others = list(range(1, group))
    near_rings = [(0, 0, piece), (-1, 0, piece), (1, 0, piece)]
    near = [*own_block, *near_block]
    fresh = [fresh_keys, fresh_turned]
    facts = (tail_len, shared_len, table)
    theirs, _ = attend(
        facts,
        queries,
        others,
        near_rings,
        slots,
        piece,
        near + fresh,
        True,
        None,
        False,
        "attend_near_others",
    )
    step(0, theirs[1][1])
    facts = (tail_len, shared_len, table)
    rest = []
    rest_rings = []
    for hop in range(2, half):
        blocks, rings = arrived(hop)
        name = f"attend_hop{hop}_others"
        theirs, parted = attend(
            facts, queries, others, rings, 0, piece, blocks, False, theirs, False, name
        )
        rest += parted
        rest_rings += rings
    rings = [(-half, 0, middle), (half, middle, piece - middle)]
    blocks = [ahead[0][half], behind[1][half]]
    heads = width // HD
    pieces_out = 2 if heads >= 4 else 1
    few = heads // pieces_out
    sending = []
    parted = False
    for lowest in range(0, heads, few):
        name = f"attend_far_others{lowest}"
        last, made = attend(
            facts,
            queries,
            others,
            rings,
            0,
            piece,
            parted or blocks,
            bool(parted),
            theirs,
            True,
            name,
            (lowest, few),
        )
        parted = parted or made
        sending.append([last[shift][0] for shift in others])
        facts = (after(tail_len, sending[-1][0]), shared_len, table)
    rest += parted
    rest_rings += rings
    own, _ = attend(
        facts,
        queries,
        [0],
        near_rings + rest_rings,
        slots,
        piece,
        near + rest + fresh,
        True,
        None,
        True,
        "attend_own",
    )
    arrivals = [
        [swap(part[i], "seq", shift) for i, shift in enumerate(others)] for part in sending
    ]
    parts = [part[i] for i in range(len(others)) for part in arrivals]
    new_cache, token = weave(fresh_keys, fresh_values, own[0][1], arrivals[0][0])
    attended, sent = combine(*own[0], parts, pieces_out, w_out, token, ways)
    received = [swap(sent[shift - 1], "tp", shift) for shift in range(1, ways)]
    total = keep(attended, w_out, hidden_in)
    for part in received:
        total = total + part.astype(jnp.float32)
    return (total.astype(jnp.bfloat16), new_cache)


def solution(mesh):
    return jax.shard_map(
        local,
        mesh=mesh,
        in_specs=(
            P("seq", "tp"),
            P(None, "tp"),
            P(None, None, "tp"),
            P("tp", None),
            P("seq", None, "tp"),
            P("seq", None, None, "tp"),
            P(),
            P(),
            P(),
        ),
        out_specs=(P("seq", "tp"), P("seq", None, "tp")),
        check_vma=False,
    )
```

```python
import functools

import jax
import jax.numpy as jnp
import numpy as np
from jax import lax
from jax.experimental import pallas as pl
from jax.experimental.pallas import tpu as pltpu
from jax.sharding import PartitionSpec as P

HD = 128
REQ = 8
BLK = 128
NEGATIVE = -1e30
SCALE = float(HD**-0.5 * np.log2(np.e))


def params(mib=24):
    return pltpu.CompilerParams(vmem_limit_bytes=mib * 2**20)


def cost(flops, moved, exps=0):
    return pl.CostEstimate(flops=int(flops), bytes_accessed=int(moved), transcendentals=int(exps))


def cycle_of(group):
    if group == 2:
        return [0, 2, 4, 6, 7, 5, 3, 1]
    return list(range(REQ))


def pick(table, index):
    result = jnp.int32(table[0])
    for place, value in enumerate(table):
        result = jnp.where(index == place, jnp.int32(value), result)
    return result


def swap(value, axis, mask):
    pairs = [(source, source ^ mask) for source in range(lax.axis_size(axis))]
    return lax.ppermute(value, axis, pairs)


def turn(value, cycle, group, way):
    count = len(cycle)
    pairs = []
    for place in range(count):
        source, target = cycle[place], cycle[(place + way) % count]
        pairs += [(source * group + m, target * group + m) for m in range(group)]
    return lax.ppermute(value, "seq", pairs)


def rotated(vectors, cosine, sine):
    return vectors * cosine + pltpu.roll(vectors, HD // 2, 1) * sine


def position_kernel(lengths, shared, positions):
    rows = positions.shape[0]
    group = lax.axis_size("seq") // REQ
    seq = lax.axis_index("seq")
    start = shared[0] + lengths[seq // group] + (seq % group) * rows
    places = start + lax.broadcasted_iota(jnp.int32, positions.shape, 0)
    positions[...] = places.astype(jnp.float32)


def angles(tail_len, shared_len, rows):
    half = HD // 2
    positions = pl.pallas_call(
        position_kernel,
        in_specs=[SMEM] * 2,
        out_specs=VMEM,
        out_shape=jax.ShapeDtypeStruct((rows, HD), jnp.float32),
        compiler_params=params(8),
        cost_estimate=cost(rows * HD, 4 * rows * HD),
        name="positions",
    )(tail_len, shared_len)
    lane = jnp.arange(HD, dtype=jnp.int32)
    freqs = 10000.0 ** (-(lane % half).astype(jnp.float32) / half)
    angle = positions * freqs
    return jnp.cos(angle), jnp.sin(angle) * jnp.where(lane < half, -1.0, 1.0)


def lanes(start, count=HD):
    if isinstance(start, int):
        return pl.ds(start, count)
    return pl.ds(pl.multiple_of(start, HD), count)


def after(value, *others):
    return lax.optimization_barrier((value, *others))[0]


VMEM = pl.BlockSpec(memory_space=pltpu.VMEM)
HBM = pl.BlockSpec(memory_space=pltpu.HBM)
SMEM = pl.BlockSpec(memory_space=pltpu.SMEM)


def viewed(block):
    count, pair, width = block.shape
    heads = width // HD
    return block.reshape(count, pair, heads, HD).transpose(0, 2, 1, 3).reshape(-1, HD)


def order_rows(stride, back):
    rows = 2 * HD
    places = rows // stride
    row = lax.broadcasted_iota(jnp.int32, (rows, rows), 1 if back else 0)
    column = lax.broadcasted_iota(jnp.int32, (rows, rows), 0 if back else 1)
    source = lax.rem(row, places) * stride + lax.div(row, places)
    return jnp.where(column == source, 1.0, 0.0).astype(jnp.bfloat16)


def reordered(order, tiles):
    both = tiles[0] if len(tiles) == 1 else jnp.concatenate(tiles, axis=1)
    mixed = jnp.dot(order, both, preferred_element_type=jnp.float32).astype(jnp.bfloat16)
    return [mixed[:, i * HD : (i + 1) * HD] for i in range(len(tiles))]


def take_apart(block, order, keys, values, offset):
    heads = keys.shape[1] // HD
    stride = 2 * heads
    count = block.shape[0] // stride
    places = 2 * HD // stride
    for start in range(0, count, 2 * places):
        starts = [at for at in (start, start + places) if at < count]
        tiles = [block[at * stride : (at + places) * stride, :] for at in starts]
        for at, tile in zip(starts, reordered(order, tiles)):
            for head in range(heads):
                for j, result in enumerate((keys, values)):
                    line = (2 * head + j) * places
                    result[offset + at : offset + at + places, head * HD : (head + 1) * HD] = tile[
                        line : line + places
                    ]


ACROSS = (((1,), (1,)), ((), ()))


def unit_matrix(size):
    row = lax.broadcasted_iota(jnp.int32, (size, size), 0)
    column = lax.broadcasted_iota(jnp.int32, (size, size), 1)
    return jnp.where(row == column, 1.0, 0.0).astype(jnp.bfloat16)


def turned_over(unit, value):
    return lax.dot_general(unit, value, ACROSS, preferred_element_type=jnp.float32).astype(
        jnp.bfloat16
    )


def turn_heads(values, result):
    unit = unit_matrix(HD)
    for start in range(0, values.shape[1], HD):
        result[start : start + HD, :] = turned_over(unit, values[:, start : start + HD])


def part_kernel(*refs):
    *blocks, keys, turned, values = refs
    stride = keys.shape[1] * 2 // HD
    order = order_rows(stride, False)
    offset = 0
    for block in blocks:
        take_apart(block, order, keys, values, offset)
        offset += block.shape[0] // stride
    turn_heads(values, turned)


def part_keyval(blocks, width, name):
    count = sum(block.shape[0] for block in blocks) * HD // (2 * width)
    return pl.pallas_call(
        part_kernel,
        in_specs=[VMEM] * len(blocks),
        out_specs=[VMEM] * 2,
        out_shape=[
            jax.ShapeDtypeStruct((count, width), jnp.bfloat16),
            jax.ShapeDtypeStruct((width, count), jnp.bfloat16),
        ],
        scratch_shapes=[pltpu.VMEM((count, width), jnp.bfloat16)],
        compiler_params=params(16),
        cost_estimate=cost(2**10 * count * width, 8 * count * width),
        name=name,
    )(*blocks)


def query_kernel(*refs):
    *pieces, weight, cosine, sine, query, normed = refs
    columns = pieces[0].shape[1]
    index = lax.axis_index("tp")
    features = columns * len(pieces)
    values = [piece[...].astype(jnp.float32) for piece in pieces]
    mean = sum(jnp.sum(v, axis=1, keepdims=True) for v in values) / features
    values = [v - mean for v in values]
    spread = sum(jnp.sum(v * v, axis=1, keepdims=True) for v in values) / features
    inverse = lax.rsqrt(spread + 1e-05)
    for shift, v in enumerate(values):
        normed[:, lanes((index ^ shift) * columns, columns)] = (v * inverse).astype(jnp.bfloat16)
    width = weight.shape[1]
    wide = min(width, 2 * HD)
    for base in range(0, width, wide):
        product = jnp.dot(
            normed[...], weight[:, base : base + wide], preferred_element_type=jnp.float32
        )
        for start in range(0, wide, HD):
            query[:, base + start : base + start + HD] = rotated(
                product[:, start : start + HD], cosine[...], sine[...]
            ).astype(jnp.bfloat16)


def project_query(pieces, w_query, cosine, sine):
    rows, columns = pieces[0].shape
    depth, width = w_query.shape
    return pl.pallas_call(
        query_kernel,
        in_specs=[VMEM] * (len(pieces) + 3),
        out_specs=[VMEM] * 2,
        out_shape=[
            jax.ShapeDtypeStruct((rows, width), jnp.bfloat16),
            jax.ShapeDtypeStruct((rows, depth), jnp.bfloat16),
        ],
        compiler_params=params(20),
        cost_estimate=cost(2 * rows * depth * width, 2 * depth * width),
        name="project_query",
    )(*pieces, w_query, cosine, sine)


def weight_kernel(weight, result, near, arrived):
    slots, chunk = near.shape[:2]
    count = weight.shape[0] // chunk
    stride = result.shape[2] * 2 // HD
    copies = [
        pltpu.make_async_copy(
            weight.at[pl.ds(i * chunk, chunk)], near.at[i % slots], arrived.at[i]
        )
        for i in range(count)
    ]
    for copy in copies[:slots]:
        copy.start()
    order = order_rows(stride, False)
    for i, copy in enumerate(copies):
        copy.wait()
        take_apart(near.at[i % slots], order, result.at[0], result.at[1], i * chunk // stride)
        if i + slots < count:
            copies[i + slots].start()


def part_weights(w_keyval):
    depth, _, width = w_keyval.shape
    weight = viewed(w_keyval)
    count = max(depth // 256, 1)
    chunk = weight.shape[0] // count
    return pl.pallas_call(
        weight_kernel,
        in_specs=[HBM],
        out_specs=VMEM,
        out_shape=jax.ShapeDtypeStruct((2, depth, width), jnp.bfloat16),
        scratch_shapes=[
            pltpu.VMEM((count, chunk, HD), jnp.bfloat16),
            pltpu.SemaphoreType.DMA((count,)),
        ],
        compiler_params=params(38),
        cost_estimate=cost(2**10 * depth * width, 8 * depth * width),
        name="part_weights",
    )(weight)


def keyval_kernel(normed, weight, cosine, sine, keys, values, turned):
    heads = weight.shape[2] // HD
    for head in range(heads):
        span = slice(head * HD, (head + 1) * HD)
        product = jnp.dot(
            normed[...],
            jnp.concatenate([weight[0, :, span], weight[1, :, span]], axis=1),
            preferred_element_type=jnp.float32,
        )
        keys[:, span] = rotated(product[:, :HD], cosine[...], sine[...]).astype(jnp.bfloat16)
        values[:, span] = product[:, HD:].astype(jnp.bfloat16)
    turn_heads(values, turned)


def project_keyval(normed, weight, cosine, sine):
    rows, depth = normed.shape
    width = weight.shape[2]
    flat = jax.ShapeDtypeStruct((rows, width), jnp.bfloat16)
    return pl.pallas_call(
        keyval_kernel,
        in_specs=[VMEM] * 4,
        out_specs=[VMEM] * 3,
        out_shape=[flat, flat, jax.ShapeDtypeStruct((width, rows), jnp.bfloat16)],
        compiler_params=params(20),
        cost_estimate=cost(4 * rows * depth * width, 4 * depth * width),
        name="project_keyval",
    )(normed, weight, cosine, sine)


def weave_kernel(keys, values, *refs):
    cache, token = refs[-2:]
    token[...] = jnp.zeros_like(token)
    rows, width = keys.shape
    heads = width // HD
    stride = 2 * heads
    order = order_rows(stride, True)
    places = 2 * HD // stride
    for start in range(0, rows, 2 * places):
        starts = [at for at in (start, start + places) if at < rows]
        tiles = [
            jnp.concatenate(
                [
                    pair[at : at + places, head * HD : (head + 1) * HD]
                    for head in range(heads)
                    for pair in (keys, values)
                ],
                axis=0,
            )
            for at in starts
        ]
        for at, tile in zip(starts, reordered(order, tiles)):
            cache[at * stride : (at + places) * stride, :] = tile


def weave(keys, values, *earlier):
    rows, width = keys.shape
    heads = width // HD
    cache, token = pl.pallas_call(
        weave_kernel,
        in_specs=[VMEM] * (2 + len(earlier)),
        out_specs=[VMEM] * 2,
        out_shape=[
            jax.ShapeDtypeStruct((rows * heads * 2, HD), jnp.bfloat16),
            jax.ShapeDtypeStruct((8, HD), jnp.float32),
        ],
        compiler_params=params(16),
        cost_estimate=cost(2**10 * rows * width, 8 * rows * width),
        name="weave_cache",
    )(keys, values, *earlier)
    cache = cache.reshape(rows, heads, 2, HD).transpose(0, 2, 1, 3)
    return cache.reshape(rows, 2, width), token


def attend_kernel(spec, *refs):
    group, shifts, rings, slots, piece, parted, first, last, lowest, heads = spec
    fresh = slots > 0
    refs = list(refs)
    take = lambda count: [refs.pop(0) for _ in range(count)]
    lengths, shared, table = take(3)
    queries = take(len(shifts))
    if parted:
        blocks = take(2 * parted)
        sources = list(zip(blocks[::2], blocks[1::2]))
    else:
        raw = take(len(rings))
    if not first:
        old_mixes, old_extents = take(len(shifts)), take(len(shifts))
    results = take(len(shifts))
    extents = [None if last and shift else take(1)[0] for shift in shifts]
    if not parted:
        sources = [tuple(take(2))]
    bias, first_scores, second_scores = take(3)
    extents = [take(1)[0] if extent is None else extent for extent in extents]
    if fresh:
        causal = take(1)[0]
    if not parted:
        values_here = take(1)[0]
        keys_here, turned_here = sources[0]
    rows, width = queries[0].shape
    stride = 2 * width // HD
    cycle = cycle_of(group)
    seq = lax.axis_index("seq")
    request, member = seq // group, seq % group
    place = pick(list(np.argsort(cycle)), request)
    edges = []
    count = 0
    for i in range(slots):
        wanted = seq * slots + i
        number = jnp.int32(0)
        for j in range(table.shape[0]):
            number = jnp.where(table[j, request] == wanted, jnp.int32(j), number)
        edges.append((count, BLK, number * BLK, lengths[request]))
        count += BLK
    for step, begin, size in rings:
        origin = pick(cycle, lax.rem(place + step + REQ, REQ))
        edges.append((count, size, (origin * group + member) * piece + begin, shared[0]))
        count += size
    for begin, size, start, length in edges:
        positions = start + lax.broadcasted_iota(jnp.int32, (size, HD), 0)
        lane = lax.broadcasted_iota(jnp.int32, (size, HD), 1)
        bias[begin : begin + size, :] = jnp.where(
            (positions >= length) & (lane == 0), NEGATIVE, 0.0
        ).astype(jnp.bfloat16)
    if fresh:
        bias[count : count + rows, :] = jnp.zeros((rows, HD), jnp.bfloat16)
        theirs = member * rows + lax.broadcasted_iota(jnp.int32, (rows, rows), 0)
        for i, shift in enumerate(shifts):
            mine = (member ^ shift) * rows + lax.broadcasted_iota(jnp.int32, (rows, rows), 1)
            causal[:, i * rows : (i + 1) * rows] = jnp.where(theirs <= mine, 0.0, NEGATIVE)
    if not parted:
        offset = 0
        order = order_rows(stride, False)
        for block in raw:
            take_apart(block, order, keys_here, values_here, offset)
            offset += block.shape[0] // stride
        turn_heads(values_here, turned_here)
    many = len(shifts) * rows
    unit = jnp.where(lax.broadcasted_iota(jnp.int32, (many, HD), 1) == 0, 1.0, 0.0)
    unit = unit.astype(jnp.bfloat16)
    chunks = []
    begin = 0
    for source in sources:
        length = source[0].shape[0]
        for start in range(0, length, 2 * HD):
            size = min(2 * HD, length - start)
            chunks.append((source, start, size, begin + start, fresh and begin == count))
        begin += length

    def beside(values, axis):
        return values[0] if len(values) == 1 else jnp.concatenate(values, axis=axis)

    def query_of(head):
        return jnp.concatenate([beside([q[:, lanes((lowest + head) * HD)] for q in queries], 0), unit], axis=1)

    def score(head, query, chunk, scores, top):
        (keys, _), start, size, at, masked = chunk
        keys = keys[start : start + size, lanes((lowest + head) * HD)]
        keys = jnp.concatenate([keys, bias[at : at + size, :]], axis=1)
        part = lax.dot_general(keys, query, ACROSS, preferred_element_type=jnp.float32)
        if masked:
            part = part + causal[start : start + size, :]
        scores[at : at + size, :] = part
        here = jnp.max(part, axis=0, keepdims=True)
        return here if top is None else jnp.maximum(top, here)

    def mix(head, chunk, scores, top, sums):
        (_, turned), start, size, at, _ = chunk
        weights = jnp.exp2((scores[at : at + size, :] - top) * SCALE)
        here = jnp.sum(weights, axis=0, keepdims=True)
        product = jnp.dot(
            turned[lanes((lowest + head) * HD), start : start + size],
            weights.astype(jnp.bfloat16),
            preferred_element_type=jnp.float32,
        )
        return (here, product) if sums is None else (sums[0] + here, sums[1] + product)

    together = min(heads // 2, 4 if count <= 256 else 1)

    def some_heads(base, scores, tops, following, next_scores):
        span = lambda k: lanes((base + k) * HD)
        line = lambda k: pl.ds(base + k, 1)
        each = range(together)
        if not first:
            olds = [beside([extent[line(lowest + k), :] for extent in old_extents], 1) for k in each]
            tops = [jnp.maximum(top, old * (1.0 / SCALE)) for top, old in zip(tops, olds)]
        next_tops = [None] * together
        sums = [None] * together
        if following is not None:
            next_queries = [query_of(following + k) for k in each]
        for chunk in chunks:
            for k in each:
                if following is not None:
                    next_tops[k] = score(
                        following + k, next_queries[k], chunk, next_scores.at[k], next_tops[k]
                    )
                sums[k] = mix(base + k, chunk, scores.at[k], tops[k], sums[k])
        for k in each:
            summed, mixed = sums[k]
            if not first:
                factor = jnp.exp2(olds[k] - tops[k] * SCALE)
                summed = summed + factor
                old_mix = beside([old_mix[span(lowest + k), :] for old_mix in old_mixes], 1)
                mixed = mixed + old_mix * factor
            mixed = mixed * (1.0 / summed)
            extent = tops[k] * SCALE + jnp.log2(summed)
            for i, result in enumerate(results):
                columns = slice(i * rows, (i + 1) * rows)
                extents[i][line(k), :] = extent[:, columns]
                result[span(k), :] = mixed[:, columns].astype(result.dtype)
        return next_tops

    def two_parts(i, tops):
        base = 2 * together * i
        tops = some_heads(base, first_scores, tops, base + together, second_scores)
        following = jnp.minimum(base + 2 * together, heads - together)
        return some_heads(base + together, second_scores, tops, following, first_scores)

    tops = []
    for k in range(together):
        query, top = query_of(k), None
        for chunk in chunks:
            top = score(k, query, chunk, first_scores.at[k], top)
        tops.append(top)
    if heads == 2 * together:
        tops = some_heads(0, first_scores, tops, together, second_scores)
        some_heads(together, second_scores, tops, None, None)
    else:
        lax.fori_loop(0, heads // (2 * together), two_parts, tops)
    for i, shift in enumerate(shifts):
        if last and shift:
            line = extents[i][:heads, :]
            packed = []
            for _ in range(3):
                rounded = line.astype(jnp.bfloat16).astype(jnp.float32)
                packed.append(rounded)
                line = line - rounded
            gap = stat_rows(heads) - 3 * heads
            if gap:
                packed.append(jnp.zeros((gap, rows), jnp.float32))
            results[i][heads * HD :, :] = jnp.concatenate(packed, axis=0).astype(jnp.bfloat16)


def stat_rows(heads):
    return -(-3 * heads // 16) * 16


def attend(facts, queries, shifts, rings, slots, piece, blocks, parted, old, last, name, within=None):
    group = len(queries)
    queries = [queries[shift] for shift in shifts]
    rows, width = queries[0].shape
    lowest, heads = within or (0, width // HD)
    parted = len(blocks) // 2 if parted else 0
    operands = [*facts, *queries, *blocks]
    if old:
        operands += [old[shift][0] for shift in shifts] + [old[shift][1] for shift in shifts]
    count = sum(size for _, _, size in rings) + BLK * slots + (rows if slots else 0)
    many = len(shifts) * rows
    scratch = [pltpu.VMEM((count, HD), jnp.bfloat16)]
    together = min(heads // 2, 4 if count <= 256 else 1)
    scratch += [pltpu.VMEM((together, count, many), jnp.float32)] * 2
    lines = (max(heads, 8), rows)
    scratch += [pltpu.VMEM(lines, jnp.float32) for shift in shifts if last and shift]
    if slots:
        scratch.append(pltpu.VMEM((rows, many), jnp.float32))
    if not parted:
        scratch.append(pltpu.VMEM((count, width), jnp.bfloat16))
    mixes = [
        jax.ShapeDtypeStruct((heads * HD + stat_rows(heads), rows), jnp.bfloat16)
        if last and shift
        else jax.ShapeDtypeStruct((heads * HD, rows), jnp.float32)
        for shift in shifts
    ]
    extents = [
        jax.ShapeDtypeStruct(lines, jnp.float32) for shift in shifts if not (last and shift)
    ]
    scores = many * count * heads
    shapes = [*mixes, *extents]
    if not parted:
        shapes += [
            jax.ShapeDtypeStruct((count, width), jnp.bfloat16),
            jax.ShapeDtypeStruct((width, count), jnp.bfloat16),
        ]
    results = pl.pallas_call(
        functools.partial(
            attend_kernel,
            (group, shifts, rings, slots, piece, parted, not old, last, lowest, heads),
        ),
        in_specs=[SMEM] * 3 + [VMEM] * (len(operands) - 3),
        out_specs=[VMEM] * len(shapes),
        out_shape=shapes,
        scratch_shapes=scratch,
        compiler_params=params(24),
        cost_estimate=cost(4 * scores * HD, 4 * count * width, scores),
        name=name,
    )(*operands)
    mixes = results[: len(shifts)]
    extents = [*results[len(shifts) : len(shapes) - (0 if parted else 2)]]
    if last:
        extents = [extents.pop(0) if shift == 0 else None for shift in shifts]
    state = {shift: pair for shift, *pair in zip(shifts, mixes, extents)}
    return state, results[len(results) - 2 :]


def combine_kernel(lowest, last, earlier, *refs):
    result, extent, *refs = refs
    *parts, weight = refs[: len(refs) - 2 - earlier]
    before = refs[len(refs) - 2 - earlier : len(refs) - 2]
    attended, sent = refs[-2:]
    rows, width = attended.shape
    few = width // HD
    extents = [extent[lowest : lowest + few, :]]
    for part in parts:
        lines = part[width:, :].astype(jnp.float32)
        extents.append(sum(lines[i * few : (i + 1) * few] for i in range(3)))
    top = functools.reduce(jnp.maximum, extents)
    shares = [jnp.exp2(extent - top) for extent in extents]
    whole = sum(shares)
    shares = [share / whole for share in shares]
    unit = unit_matrix(rows)
    for head in range(few):
        span = slice(head * HD, (head + 1) * HD)
        start = (lowest + head) * HD
        mixes = [result[start : start + HD, :]]
        mixes += [part[span, :].astype(jnp.float32) for part in parts]
        mixed = sum(mix * share[head : head + 1] for mix, share in zip(mixes, shares))
        attended[:, span] = turned_over(unit, mixed.astype(jnp.bfloat16))
    index = lax.axis_index("tp")
    ways = sent.shape[0] + 1
    columns = weight.shape[1] // ways
    for shift in range(1, ways):
        product = jnp.dot(
            attended[...],
            weight[lowest * HD : lowest * HD + width, lanes((index ^ shift) * columns, columns)],
            preferred_element_type=jnp.float32,
        )
        if len(before) > 1:
            product += before[0][shift - 1]
        sent[shift - 1] = product.astype(sent.dtype)


def combine(own, parts, lowest, few, w_out, earlier, last, ways):
    rows = own[0].shape[1]
    columns = w_out.shape[1] // ways
    kind = jnp.bfloat16 if last else jnp.float32
    return pl.pallas_call(
        functools.partial(combine_kernel, lowest, last, len(earlier)),
        in_specs=[VMEM] * (3 + len(parts) + len(earlier)),
        out_specs=[VMEM] * 2,
        out_shape=[
            jax.ShapeDtypeStruct((rows, few * HD), jnp.bfloat16),
            jax.ShapeDtypeStruct((ways - 1, rows, columns), kind),
        ],
        compiler_params=params(20),
        cost_estimate=cost(2 * rows * few * HD * columns * (ways - 1), 2 * few * HD * columns),
        name=f"combine_send{lowest}",
    )(*own, *parts, w_out, *earlier)


def keep_kernel(*refs):
    *pieces, weight, hidden, kept = refs
    columns = hidden.shape[1]
    attended = [piece[...] for piece in pieces]
    product = jnp.dot(
        attended[0] if len(pieces) == 1 else jnp.concatenate(attended, axis=1),
        weight[:, lanes(lax.axis_index("tp") * columns, columns)],
        preferred_element_type=jnp.float32,
    )
    kept[...] = product + hidden[...].astype(jnp.float32)


def keep(attended, w_out, hidden):
    rows, width = hidden.shape[0], w_out.shape[0]
    return pl.pallas_call(
        keep_kernel,
        in_specs=[VMEM] * (2 + len(attended)),
        out_specs=VMEM,
        out_shape=jax.ShapeDtypeStruct(hidden.shape, jnp.float32),
        compiler_params=params(20),
        cost_estimate=cost(2 * rows * width * hidden.shape[1], 2 * width * w_out.shape[1]),
        name="keep_own",
    )(*attended, w_out, hidden)


def local(
    hidden_in, w_query, w_keyval, w_out, prompt_cache, tail_cache, tail_table, tail_len, shared_len
):
    rows = hidden_in.shape[0]
    group = lax.axis_size("seq") // REQ
    ways = lax.axis_size("tp")
    cycle = cycle_of(group)
    half = REQ // 2
    piece = prompt_cache.shape[0]
    middle = piece // 2
    width = w_query.shape[1]
    stride = 2 * width // HD

    pieces = [hidden_in] + [swap(hidden_in, "tp", shift) for shift in range(1, ways)]
    prompt = viewed(prompt_cache)
    ahead, behind = {0: [None], 1: [None]}, {0: [None], 1: [None]}
    nearest = []
    for blocks, way in ((ahead, 1), (behind, -1)):
        block = turn(prompt, cycle, group, way)
        nearest.append(block)
        blocks[0].append(block[: middle * stride])
        blocks[1].append(block[middle * stride :])

    def step(which, *others):
        for blocks, part, way in ((ahead, which, 1), (behind, 1 - which, -1)):
            block = blocks[part][-1]
            if others:
                block = after(block, *others)
            blocks[part].append(turn(block, cycle, group, way))

    def arrived(hop):
        blocks = [way[part][hop] for way in (ahead, behind) for part in (0, 1)]
        rings = [(sign * hop, part * middle, middle) for sign in (-1, 1) for part in (0, 1)]
        return blocks, rings

    weight = part_weights(w_keyval)
    cosine, sine = angles(after(tail_len, weight), shared_len, rows)
    pieces[0] = after(pieces[0], weight)
    query, normed = project_query(pieces, w_query, cosine, sine)
    queries = [query] + [swap(query, "seq", shift) for shift in range(1, group)]
    tail = viewed(tail_cache.reshape(-1, 2, tail_cache.shape[3]))
    slots = tail_cache.shape[0]
    own_block = part_keyval([tail, prompt], width, "part_own")
    step(0, weight, query)
    step(1, query)
    ready = after(cosine, ahead[1][1], behind[0][1])
    fresh_keys, fresh_values, fresh_turned = project_keyval(normed, weight, ready, sine)
    step(0, fresh_keys)
    near_block = part_keyval(nearest, width, "part_near")
    step(1, near_block[0])

    table = tail_table.T
    others = list(range(1, group))
    near_rings = [(0, 0, piece), (-1, 0, piece), (1, 0, piece)]
    near = [*own_block, *near_block]
    fresh = [fresh_keys, fresh_turned]
    facts = (tail_len, shared_len, table)
    theirs, _ = attend(
        facts,
        queries,
        others,
        near_rings,
        slots,
        piece,
        near + fresh,
        True,
        None,
        False,
        "attend_near_others",
    )
    step(0, theirs[1][1])
    facts = (tail_len, shared_len, table)
    rest = []
    rest_rings = []
    for hop in range(2, half):
        blocks, rings = arrived(hop)
        name = f"attend_hop{hop}_others"
        theirs, parted = attend(
            facts, queries, others, rings, 0, piece, blocks, False, theirs, False, name
        )
        rest += parted
        rest_rings += rings
    rings = [(-half, 0, middle), (half, middle, piece - middle)]
    blocks = [ahead[0][half], behind[1][half]]
    heads = width // HD
    pieces_out = 2 if heads >= 4 else 1
    few = heads // pieces_out
    sending = []
    parted = False
    for lowest in range(0, heads, few):
        name = f"attend_far_others{lowest}"
        last, made = attend(
            facts,
            queries,
            others,
            rings,
            0,
            piece,
            parted or blocks,
            bool(parted),
            theirs,
            True,
            name,
            (lowest, few),
        )
        parted = parted or made
        sending.append([last[shift][0] for shift in others])
        facts = (after(tail_len, sending[-1][0]), shared_len, table)
    rest += parted
    rest_rings += rings
    own, _ = attend(
        facts,
        queries,
        [0],
        near_rings + rest_rings,
        slots,
        piece,
        near + rest + fresh,
        True,
        None,
        True,
        "attend_own",
    )
    arrivals = [
        [swap(part[i], "seq", shift) for i, shift in enumerate(others)] for part in sending
    ]
    new_cache, token = weave(fresh_keys, fresh_values, own[0][1], arrivals[0][0])
    attended = []
    earlier = [token]
    for piece_out, part in enumerate(arrivals):
        last = piece_out == pieces_out - 1
        made, sent = combine(own[0], part, piece_out * few, few, w_out, earlier, last, ways)
        attended.append(made)
        earlier = [sent, token]
    received = [swap(sent[shift - 1], "tp", shift) for shift in range(1, ways)]
    total = keep(attended, w_out, hidden_in)
    for part in received:
        total = total + part.astype(jnp.float32)
    return (total.astype(jnp.bfloat16), new_cache)


def solution(mesh):
    return jax.shard_map(
        local,
        mesh=mesh,
        in_specs=(
            P("seq", "tp"),
            P(None, "tp"),
            P(None, None, "tp"),
            P("tp", None),
            P("seq", None, "tp"),
            P("seq", None, None, "tp"),
            P(),
            P(),
            P(),
        ),
        out_specs=(P("seq", "tp"), P("seq", None, "tp")),
        check_vma=False,
    )
```

```python
import functools

import jax
import jax.numpy as jnp
import numpy as np
from jax import lax
from jax.experimental import pallas as pl
from jax.experimental.pallas import tpu as pltpu
from jax.sharding import PartitionSpec as P

HD = 128
REQ = 8
BLK = 128
NEGATIVE = -1e30
SCALE = float(HD**-0.5 * np.log2(np.e))


def params(mib=24):
    return pltpu.CompilerParams(vmem_limit_bytes=mib * 2**20)


def cost(flops, moved, exps=0):
    return pl.CostEstimate(flops=int(flops), bytes_accessed=int(moved), transcendentals=int(exps))


def cycle_of(group):
    if group == 2:
        return [0, 2, 4, 6, 7, 5, 3, 1]
    return list(range(REQ))


def pick(table, index):
    result = jnp.int32(table[0])
    for place, value in enumerate(table):
        result = jnp.where(index == place, jnp.int32(value), result)
    return result


def swap(value, axis, mask):
    pairs = [(source, source ^ mask) for source in range(lax.axis_size(axis))]
    return lax.ppermute(value, axis, pairs)


def turn(value, cycle, group, way):
    count = len(cycle)
    pairs = []
    for place in range(count):
        source, target = cycle[place], cycle[(place + way) % count]
        pairs += [(source * group + m, target * group + m) for m in range(group)]
    return lax.ppermute(value, "seq", pairs)


def rotated(vectors, cosine, sine):
    return vectors * cosine + pltpu.roll(vectors, HD // 2, 1) * sine


def position_kernel(lengths, shared, positions):
    rows = positions.shape[0]
    group = lax.axis_size("seq") // REQ
    seq = lax.axis_index("seq")
    start = shared[0] + lengths[seq // group] + (seq % group) * rows
    places = start + lax.broadcasted_iota(jnp.int32, positions.shape, 0)
    positions[...] = places.astype(jnp.float32)


def angles(tail_len, shared_len, rows):
    half = HD // 2
    positions = pl.pallas_call(
        position_kernel,
        in_specs=[SMEM] * 2,
        out_specs=VMEM,
        out_shape=jax.ShapeDtypeStruct((rows, HD), jnp.float32),
        compiler_params=params(8),
        cost_estimate=cost(rows * HD, 4 * rows * HD),
        name="positions",
    )(tail_len, shared_len)
    lane = jnp.arange(HD, dtype=jnp.int32)
    freqs = 10000.0 ** (-(lane % half).astype(jnp.float32) / half)
    angle = positions * freqs
    return jnp.cos(angle), jnp.sin(angle) * jnp.where(lane < half, -1.0, 1.0)


def lanes(start, count=HD):
    if isinstance(start, int):
        return pl.ds(start, count)
    return pl.ds(pl.multiple_of(start, HD), count)


def after(value, *others):
    return lax.optimization_barrier((value, *others))[0]


VMEM = pl.BlockSpec(memory_space=pltpu.VMEM)
HBM = pl.BlockSpec(memory_space=pltpu.HBM)
SMEM = pl.BlockSpec(memory_space=pltpu.SMEM)


def viewed(block):
    count, pair, width = block.shape
    heads = width // HD
    return block.reshape(count, pair, heads, HD).transpose(0, 2, 1, 3).reshape(-1, HD)


def order_rows(stride, back):
    rows = 2 * HD
    places = rows // stride
    row = lax.broadcasted_iota(jnp.int32, (rows, rows), 1 if back else 0)
    column = lax.broadcasted_iota(jnp.int32, (rows, rows), 0 if back else 1)
    source = lax.rem(row, places) * stride + lax.div(row, places)
    return jnp.where(column == source, 1.0, 0.0).astype(jnp.bfloat16)


def reordered(order, tiles):
    both = tiles[0] if len(tiles) == 1 else jnp.concatenate(tiles, axis=1)
    mixed = jnp.dot(order, both, preferred_element_type=jnp.float32).astype(jnp.bfloat16)
    return [mixed[:, i * HD : (i + 1) * HD] for i in range(len(tiles))]


def take_apart(block, order, keys, values, offset):
    heads = keys.shape[1] // HD
    stride = 2 * heads
    count = block.shape[0] // stride
    places = 2 * HD // stride
    for start in range(0, count, 2 * places):
        starts = [at for at in (start, start + places) if at < count]
        tiles = [block[at * stride : (at + places) * stride, :] for at in starts]
        for at, tile in zip(starts, reordered(order, tiles)):
            for head in range(heads):
                for j, result in enumerate((keys, values)):
                    line = (2 * head + j) * places
                    result[offset + at : offset + at + places, head * HD : (head + 1) * HD] = tile[
                        line : line + places
                    ]


ACROSS = (((1,), (1,)), ((), ()))


def unit_matrix(size):
    row = lax.broadcasted_iota(jnp.int32, (size, size), 0)
    column = lax.broadcasted_iota(jnp.int32, (size, size), 1)
    return jnp.where(row == column, 1.0, 0.0).astype(jnp.bfloat16)


def turned_over(unit, value):
    return lax.dot_general(unit, value, ACROSS, preferred_element_type=jnp.float32).astype(
        jnp.bfloat16
    )


def turn_heads(values, result):
    unit = unit_matrix(HD)
    for start in range(0, values.shape[1], HD):
        result[start : start + HD, :] = turned_over(unit, values[:, start : start + HD])


def part_kernel(*refs):
    *blocks, keys, turned, values = refs
    stride = keys.shape[1] * 2 // HD
    order = order_rows(stride, False)
    offset = 0
    for block in blocks:
        take_apart(block, order, keys, values, offset)
        offset += block.shape[0] // stride
    turn_heads(values, turned)


def part_keyval(blocks, width, name):
    count = sum(block.shape[0] for block in blocks) * HD // (2 * width)
    return pl.pallas_call(
        part_kernel,
        in_specs=[VMEM] * len(blocks),
        out_specs=[VMEM] * 2,
        out_shape=[
            jax.ShapeDtypeStruct((count, width), jnp.bfloat16),
            jax.ShapeDtypeStruct((width, count), jnp.bfloat16),
        ],
        scratch_shapes=[pltpu.VMEM((count, width), jnp.bfloat16)],
        compiler_params=params(16),
        cost_estimate=cost(2**10 * count * width, 8 * count * width),
        name=name,
    )(*blocks)


def query_kernel(*refs):
    *pieces, weight, cosine, sine, query, normed = refs
    columns = pieces[0].shape[1]
    index = lax.axis_index("tp")
    features = columns * len(pieces)
    values = [piece[...].astype(jnp.float32) for piece in pieces]
    mean = sum(jnp.sum(v, axis=1, keepdims=True) for v in values) / features
    values = [v - mean for v in values]
    spread = sum(jnp.sum(v * v, axis=1, keepdims=True) for v in values) / features
    inverse = lax.rsqrt(spread + 1e-05)
    for shift, v in enumerate(values):
        normed[:, lanes((index ^ shift) * columns, columns)] = (v * inverse).astype(jnp.bfloat16)
    width = weight.shape[1]
    wide = min(width, 2 * HD)
    for base in range(0, width, wide):
        product = jnp.dot(
            normed[...], weight[:, base : base + wide], preferred_element_type=jnp.float32
        )
        for start in range(0, wide, HD):
            query[:, base + start : base + start + HD] = rotated(
                product[:, start : start + HD], cosine[...], sine[...]
            ).astype(jnp.bfloat16)


def project_query(pieces, w_query, cosine, sine):
    rows, columns = pieces[0].shape
    depth, width = w_query.shape
    return pl.pallas_call(
        query_kernel,
        in_specs=[VMEM] * (len(pieces) + 3),
        out_specs=[VMEM] * 2,
        out_shape=[
            jax.ShapeDtypeStruct((rows, width), jnp.bfloat16),
            jax.ShapeDtypeStruct((rows, depth), jnp.bfloat16),
        ],
        compiler_params=params(20),
        cost_estimate=cost(2 * rows * depth * width, 2 * depth * width),
        name="project_query",
    )(*pieces, w_query, cosine, sine)


def weight_kernel(weight, result, near, arrived):
    slots, chunk = near.shape[:2]
    count = weight.shape[0] // chunk
    stride = result.shape[2] * 2 // HD
    copies = [
        pltpu.make_async_copy(
            weight.at[pl.ds(i * chunk, chunk)], near.at[i % slots], arrived.at[i]
        )
        for i in range(count)
    ]
    for copy in copies[:slots]:
        copy.start()
    order = order_rows(stride, False)
    for i, copy in enumerate(copies):
        copy.wait()
        take_apart(near.at[i % slots], order, result.at[0], result.at[1], i * chunk // stride)
        if i + slots < count:
            copies[i + slots].start()


def part_weights(w_keyval):
    depth, _, width = w_keyval.shape
    weight = viewed(w_keyval)
    count = max(depth // 256, 1)
    chunk = weight.shape[0] // count
    return pl.pallas_call(
        weight_kernel,
        in_specs=[HBM],
        out_specs=VMEM,
        out_shape=jax.ShapeDtypeStruct((2, depth, width), jnp.bfloat16),
        scratch_shapes=[
            pltpu.VMEM((count, chunk, HD), jnp.bfloat16),
            pltpu.SemaphoreType.DMA((count,)),
        ],
        compiler_params=params(38),
        cost_estimate=cost(2**10 * depth * width, 8 * depth * width),
        name="part_weights",
    )(weight)


def keyval_kernel(normed, weight, cosine, sine, keys, values, turned):
    heads = weight.shape[2] // HD
    for head in range(heads):
        span = slice(head * HD, (head + 1) * HD)
        product = jnp.dot(
            normed[...],
            jnp.concatenate([weight[0, :, span], weight[1, :, span]], axis=1),
            preferred_element_type=jnp.float32,
        )
        keys[:, span] = rotated(product[:, :HD], cosine[...], sine[...]).astype(jnp.bfloat16)
        values[:, span] = product[:, HD:].astype(jnp.bfloat16)
    turn_heads(values, turned)


def project_keyval(normed, weight, cosine, sine):
    rows, depth = normed.shape
    width = weight.shape[2]
    flat = jax.ShapeDtypeStruct((rows, width), jnp.bfloat16)
    return pl.pallas_call(
        keyval_kernel,
        in_specs=[VMEM] * 4,
        out_specs=[VMEM] * 3,
        out_shape=[flat, flat, jax.ShapeDtypeStruct((width, rows), jnp.bfloat16)],
        compiler_params=params(20),
        cost_estimate=cost(4 * rows * depth * width, 4 * depth * width),
        name="project_keyval",
    )(normed, weight, cosine, sine)


def weave_kernel(keys, values, *refs):
    cache, token = refs[-2:]
    token[...] = jnp.zeros_like(token)
    rows, width = keys.shape
    heads = width // HD
    stride = 2 * heads
    order = order_rows(stride, True)
    places = 2 * HD // stride
    for start in range(0, rows, 2 * places):
        starts = [at for at in (start, start + places) if at < rows]
        tiles = [
            jnp.concatenate(
                [
                    pair[at : at + places, head * HD : (head + 1) * HD]
                    for head in range(heads)
                    for pair in (keys, values)
                ],
                axis=0,
            )
            for at in starts
        ]
        for at, tile in zip(starts, reordered(order, tiles)):
            cache[at * stride : (at + places) * stride, :] = tile


def weave(keys, values, *earlier):
    rows, width = keys.shape
    heads = width // HD
    cache, token = pl.pallas_call(
        weave_kernel,
        in_specs=[VMEM] * (2 + len(earlier)),
        out_specs=[VMEM] * 2,
        out_shape=[
            jax.ShapeDtypeStruct((rows * heads * 2, HD), jnp.bfloat16),
            jax.ShapeDtypeStruct((8, HD), jnp.float32),
        ],
        compiler_params=params(16),
        cost_estimate=cost(2**10 * rows * width, 8 * rows * width),
        name="weave_cache",
    )(keys, values, *earlier)
    cache = cache.reshape(rows, heads, 2, HD).transpose(0, 2, 1, 3)
    return cache.reshape(rows, 2, width), token


def attend_kernel(spec, *refs):
    group, shifts, rings, slots, piece, parted, first, last, lowest, heads = spec
    fresh = slots > 0
    refs = list(refs)
    take = lambda count: [refs.pop(0) for _ in range(count)]
    lengths, shared, table = take(3)
    queries = take(len(shifts))
    if parted:
        blocks = take(2 * parted)
        sources = list(zip(blocks[::2], blocks[1::2]))
    else:
        raw = take(len(rings))
    if not first:
        old_mixes, old_extents = take(len(shifts)), take(len(shifts))
    results = take(len(shifts))
    extents = [None if last and shift else take(1)[0] for shift in shifts]
    if not parted:
        sources = [tuple(take(2))]
    bias, first_scores, second_scores = take(3)
    extents = [take(1)[0] if extent is None else extent for extent in extents]
    if fresh:
        causal = take(1)[0]
    if not parted:
        values_here = take(1)[0]
        keys_here, turned_here = sources[0]
    rows, width = queries[0].shape
    stride = 2 * width // HD
    cycle = cycle_of(group)
    seq = lax.axis_index("seq")
    request, member = seq // group, seq % group
    place = pick(list(np.argsort(cycle)), request)
    edges = []
    count = 0
    for i in range(slots):
        wanted = seq * slots + i
        number = jnp.int32(0)
        for j in range(table.shape[0]):
            number = jnp.where(table[j, request] == wanted, jnp.int32(j), number)
        edges.append((count, BLK, number * BLK, lengths[request]))
        count += BLK
    for step, begin, size in rings:
        origin = pick(cycle, lax.rem(place + step + REQ, REQ))
        edges.append((count, size, (origin * group + member) * piece + begin, shared[0]))
        count += size
    for begin, size, start, length in edges:
        positions = start + lax.broadcasted_iota(jnp.int32, (size, HD), 0)
        lane = lax.broadcasted_iota(jnp.int32, (size, HD), 1)
        bias[begin : begin + size, :] = jnp.where(
            (positions >= length) & (lane == 0), NEGATIVE, 0.0
        ).astype(jnp.bfloat16)
    if fresh:
        bias[count : count + rows, :] = jnp.zeros((rows, HD), jnp.bfloat16)
        theirs = member * rows + lax.broadcasted_iota(jnp.int32, (rows, rows), 0)
        for i, shift in enumerate(shifts):
            mine = (member ^ shift) * rows + lax.broadcasted_iota(jnp.int32, (rows, rows), 1)
            causal[:, i * rows : (i + 1) * rows] = jnp.where(theirs <= mine, 0.0, NEGATIVE)
    if not parted:
        offset = 0
        order = order_rows(stride, False)
        for block in raw:
            take_apart(block, order, keys_here, values_here, offset)
            offset += block.shape[0] // stride
        turn_heads(values_here, turned_here)
    many = len(shifts) * rows
    unit = jnp.where(lax.broadcasted_iota(jnp.int32, (many, HD), 1) == 0, 1.0, 0.0)
    unit = unit.astype(jnp.bfloat16)
    chunks = []
    begin = 0
    for source in sources:
        length = source[0].shape[0]
        for start in range(0, length, 2 * HD):
            size = min(2 * HD, length - start)
            chunks.append((source, start, size, begin + start, fresh and begin == count))
        begin += length

    def beside(values, axis):
        return values[0] if len(values) == 1 else jnp.concatenate(values, axis=axis)

    def query_of(head):
        return jnp.concatenate([beside([q[:, lanes((lowest + head) * HD)] for q in queries], 0), unit], axis=1)

    def score(head, query, chunk, scores, top):
        (keys, _), start, size, at, masked = chunk
        keys = keys[start : start + size, lanes((lowest + head) * HD)]
        keys = jnp.concatenate([keys, bias[at : at + size, :]], axis=1)
        part = lax.dot_general(keys, query, ACROSS, preferred_element_type=jnp.float32)
        if masked:
            part = part + causal[start : start + size, :]
        scores[at : at + size, :] = part
        here = jnp.max(part, axis=0, keepdims=True)
        return here if top is None else jnp.maximum(top, here)

    def mix(head, chunk, scores, top, sums):
        (_, turned), start, size, at, _ = chunk
        weights = jnp.exp2((scores[at : at + size, :] - top) * SCALE)
        here = jnp.sum(weights, axis=0, keepdims=True)
        product = jnp.dot(
            turned[lanes((lowest + head) * HD), start : start + size],
            weights.astype(jnp.bfloat16),
            preferred_element_type=jnp.float32,
        )
        return (here, product) if sums is None else (sums[0] + here, sums[1] + product)

    together = min(heads // 2, 4 if count <= 256 else 1)

    def some_heads(base, scores, tops, following, next_scores):
        span = lambda k: lanes((base + k) * HD)
        line = lambda k: pl.ds(base + k, 1)
        each = range(together)
        if not first:
            olds = [beside([extent[line(lowest + k), :] for extent in old_extents], 1) for k in each]
            tops = [jnp.maximum(top, old * (1.0 / SCALE)) for top, old in zip(tops, olds)]
        next_tops = [None] * together
        sums = [None] * together
        if following is not None:
            next_queries = [query_of(following + k) for k in each]
        for chunk in chunks:
            for k in each:
                if following is not None:
                    next_tops[k] = score(
                        following + k, next_queries[k], chunk, next_scores.at[k], next_tops[k]
                    )
                sums[k] = mix(base + k, chunk, scores.at[k], tops[k], sums[k])
        for k in each:
            summed, mixed = sums[k]
            if not first:
                factor = jnp.exp2(olds[k] - tops[k] * SCALE)
                summed = summed + factor
                old_mix = beside([old_mix[span(lowest + k), :] for old_mix in old_mixes], 1)
                mixed = mixed + old_mix * factor
            mixed = mixed * (1.0 / summed)
            extent = tops[k] * SCALE + jnp.log2(summed)
            for i, result in enumerate(results):
                columns = slice(i * rows, (i + 1) * rows)
                extents[i][line(k), :] = extent[:, columns]
                result[span(k), :] = mixed[:, columns].astype(result.dtype)
        return next_tops

    def two_parts(i, tops):
        base = 2 * together * i
        tops = some_heads(base, first_scores, tops, base + together, second_scores)
        following = jnp.minimum(base + 2 * together, heads - together)
        return some_heads(base + together, second_scores, tops, following, first_scores)

    tops = []
    for k in range(together):
        query, top = query_of(k), None
        for chunk in chunks:
            top = score(k, query, chunk, first_scores.at[k], top)
        tops.append(top)
    if heads == 2 * together:
        tops = some_heads(0, first_scores, tops, together, second_scores)
        some_heads(together, second_scores, tops, None, None)
    else:
        lax.fori_loop(0, heads // (2 * together), two_parts, tops)
    for i, shift in enumerate(shifts):
        if last and shift:
            line = extents[i][:heads, :]
            packed = []
            for _ in range(3):
                rounded = line.astype(jnp.bfloat16).astype(jnp.float32)
                packed.append(rounded)
                line = line - rounded
            gap = stat_rows(heads) - 3 * heads
            if gap:
                packed.append(jnp.zeros((gap, rows), jnp.float32))
            results[i][heads * HD :, :] = jnp.concatenate(packed, axis=0).astype(jnp.bfloat16)


def stat_rows(heads):
    return -(-3 * heads // 16) * 16


def attend(facts, queries, shifts, rings, slots, piece, blocks, parted, old, last, name, within=None):
    group = len(queries)
    queries = [queries[shift] for shift in shifts]
    rows, width = queries[0].shape
    lowest, heads = within or (0, width // HD)
    parted = len(blocks) // 2 if parted else 0
    operands = [*facts, *queries, *blocks]
    if old:
        operands += [old[shift][0] for shift in shifts] + [old[shift][1] for shift in shifts]
    count = sum(size for _, _, size in rings) + BLK * slots + (rows if slots else 0)
    many = len(shifts) * rows
    scratch = [pltpu.VMEM((count, HD), jnp.bfloat16)]
    together = min(heads // 2, 4 if count <= 256 else 1)
    scratch += [pltpu.VMEM((together, count, many), jnp.float32)] * 2
    lines = (max(heads, 8), rows)
    scratch += [pltpu.VMEM(lines, jnp.float32) for shift in shifts if last and shift]
    if slots:
        scratch.append(pltpu.VMEM((rows, many), jnp.float32))
    if not parted:
        scratch.append(pltpu.VMEM((count, width), jnp.bfloat16))
    mixes = [
        jax.ShapeDtypeStruct((heads * HD + stat_rows(heads), rows), jnp.bfloat16)
        if last and shift
        else jax.ShapeDtypeStruct((heads * HD, rows), jnp.float32)
        for shift in shifts
    ]
    extents = [
        jax.ShapeDtypeStruct(lines, jnp.float32) for shift in shifts if not (last and shift)
    ]
    scores = many * count * heads
    shapes = [*mixes, *extents]
    if not parted:
        shapes += [
            jax.ShapeDtypeStruct((count, width), jnp.bfloat16),
            jax.ShapeDtypeStruct((width, count), jnp.bfloat16),
        ]
    results = pl.pallas_call(
        functools.partial(
            attend_kernel,
            (group, shifts, rings, slots, piece, parted, not old, last, lowest, heads),
        ),
        in_specs=[SMEM] * 3 + [VMEM] * (len(operands) - 3),
        out_specs=[VMEM] * len(shapes),
        out_shape=shapes,
        scratch_shapes=scratch,
        compiler_params=params(24),
        cost_estimate=cost(4 * scores * HD, 4 * count * width, scores),
        name=name,
    )(*operands)
    mixes = results[: len(shifts)]
    extents = [*results[len(shifts) : len(shapes) - (0 if parted else 2)]]
    if last:
        extents = [extents.pop(0) if shift == 0 else None for shift in shifts]
    state = {shift: pair for shift, *pair in zip(shifts, mixes, extents)}
    return state, results[len(results) - 2 :]


def combine_kernel(lowest, last, earlier, *refs):
    result, extent, *refs = refs
    *parts, weight = refs[: len(refs) - 2 - earlier]
    before = refs[len(refs) - 2 - earlier : len(refs) - 2]
    attended, sent = refs[-2:]
    rows, width = attended.shape
    few = width // HD
    extents = [extent[lowest : lowest + few, :]]
    for part in parts:
        lines = part[width:, :].astype(jnp.float32)
        extents.append(sum(lines[i * few : (i + 1) * few] for i in range(3)))
    top = functools.reduce(jnp.maximum, extents)
    shares = [jnp.exp2(extent - top) for extent in extents]
    whole = sum(shares)
    shares = [share / whole for share in shares]
    unit = unit_matrix(rows)
    for head in range(few):
        span = slice(head * HD, (head + 1) * HD)
        start = (lowest + head) * HD
        mixes = [result[start : start + HD, :]]
        mixes += [part[span, :].astype(jnp.float32) for part in parts]
        mixed = sum(mix * share[head : head + 1] for mix, share in zip(mixes, shares))
        attended[:, span] = turned_over(unit, mixed.astype(jnp.bfloat16))
    index = lax.axis_index("tp")
    ways = sent.shape[0] + 1
    columns = weight.shape[1] // ways
    for shift in range(1, ways):
        product = jnp.dot(
            attended[...],
            weight[lowest * HD : lowest * HD + width, lanes((index ^ shift) * columns, columns)],
            preferred_element_type=jnp.float32,
        )
        if len(before) > 1:
            product += before[0][shift - 1]
        sent[shift - 1] = product.astype(sent.dtype)


def combine(own, parts, lowest, few, w_out, earlier, last, ways):
    rows = own[0].shape[1]
    columns = w_out.shape[1] // ways
    kind = jnp.bfloat16 if last else jnp.float32
    return pl.pallas_call(
        functools.partial(combine_kernel, lowest, last, len(earlier)),
        in_specs=[VMEM] * (3 + len(parts) + len(earlier)),
        out_specs=[VMEM] * 2,
        out_shape=[
            jax.ShapeDtypeStruct((rows, few * HD), jnp.bfloat16),
            jax.ShapeDtypeStruct((ways - 1, rows, columns), kind),
        ],
        compiler_params=params(20),
        cost_estimate=cost(2 * rows * few * HD * columns * (ways - 1), 2 * few * HD * columns),
        name=f"combine_send{lowest}",
    )(*own, *parts, w_out, *earlier)


def keep_kernel(*refs):
    *pieces, weight, hidden, kept = refs
    columns = hidden.shape[1]
    attended = [piece[...] for piece in pieces]
    product = jnp.dot(
        attended[0] if len(pieces) == 1 else jnp.concatenate(attended, axis=1),
        weight[:, lanes(lax.axis_index("tp") * columns, columns)],
        preferred_element_type=jnp.float32,
    )
    kept[...] = product + hidden[...].astype(jnp.float32)


def keep(attended, w_out, hidden):
    rows, width = hidden.shape[0], w_out.shape[0]
    return pl.pallas_call(
        keep_kernel,
        in_specs=[VMEM] * (2 + len(attended)),
        out_specs=VMEM,
        out_shape=jax.ShapeDtypeStruct(hidden.shape, jnp.float32),
        compiler_params=params(20),
        cost_estimate=cost(2 * rows * width * hidden.shape[1], 2 * width * w_out.shape[1]),
        name="keep_own",
    )(*attended, w_out, hidden)


def finish_kernel(*refs):
    kept, *received, result = refs
    rows = 64 if kept.shape[0] % 64 == 0 else kept.shape[0]
    for start in range(0, kept.shape[0], rows):
        span = slice(start, start + rows)
        total = kept[span, :]
        for part in received:
            total = total + part[span, :].astype(jnp.float32)
        result[span, :] = total.astype(jnp.bfloat16)


def finish(kept, received):
    return pl.pallas_call(
        finish_kernel,
        in_specs=[VMEM] * (1 + len(received)),
        out_specs=VMEM,
        out_shape=jax.ShapeDtypeStruct(kept.shape, jnp.bfloat16),
        compiler_params=params(16),
        cost_estimate=cost(kept.size * len(received), 8 * kept.size),
        name="finish",
    )(kept, *received)


def local(
    hidden_in, w_query, w_keyval, w_out, prompt_cache, tail_cache, tail_table, tail_len, shared_len
):
    rows = hidden_in.shape[0]
    group = lax.axis_size("seq") // REQ
    ways = lax.axis_size("tp")
    cycle = cycle_of(group)
    half = REQ // 2
    piece = prompt_cache.shape[0]
    middle = piece // 2
    width = w_query.shape[1]
    stride = 2 * width // HD

    pieces = [hidden_in] + [swap(hidden_in, "tp", shift) for shift in range(1, ways)]
    prompt = viewed(prompt_cache)
    ahead, behind = {0: [None], 1: [None]}, {0: [None], 1: [None]}
    nearest = []
    for blocks, way in ((ahead, 1), (behind, -1)):
        block = turn(prompt, cycle, group, way)
        nearest.append(block)
        blocks[0].append(block[: middle * stride])
        blocks[1].append(block[middle * stride :])

    def step(which, *others):
        for blocks, part, way in ((ahead, which, 1), (behind, 1 - which, -1)):
            block = blocks[part][-1]
            if others:
                block = after(block, *others)
            blocks[part].append(turn(block, cycle, group, way))

    def arrived(hop):
        blocks = [way[part][hop] for way in (ahead, behind) for part in (0, 1)]
        rings = [(sign * hop, part * middle, middle) for sign in (-1, 1) for part in (0, 1)]
        return blocks, rings

    weight = part_weights(w_keyval)
    cosine, sine = angles(after(tail_len, weight), shared_len, rows)
    pieces[0] = after(pieces[0], weight)
    query, normed = project_query(pieces, w_query, cosine, sine)
    queries = [query] + [swap(query, "seq", shift) for shift in range(1, group)]
    tail = viewed(tail_cache.reshape(-1, 2, tail_cache.shape[3]))
    slots = tail_cache.shape[0]
    own_block = part_keyval([tail, prompt], width, "part_own")
    step(0, weight, query)
    step(1, query)
    ready = after(cosine, ahead[1][1], behind[0][1])
    fresh_keys, fresh_values, fresh_turned = project_keyval(normed, weight, ready, sine)
    step(0, fresh_keys)
    near_block = part_keyval(nearest, width, "part_near")
    step(1, near_block[0])

    table = tail_table.T
    others = list(range(1, group))
    near_rings = [(0, 0, piece), (-1, 0, piece), (1, 0, piece)]
    near = [*own_block, *near_block]
    fresh = [fresh_keys, fresh_turned]
    facts = (tail_len, shared_len, table)
    theirs, _ = attend(
        facts,
        queries,
        others,
        near_rings,
        slots,
        piece,
        near + fresh,
        True,
        None,
        False,
        "attend_near_others",
    )
    step(0, theirs[1][1])
    facts = (tail_len, shared_len, table)
    rest = []
    rest_rings = []
    for hop in range(2, half):
        blocks, rings = arrived(hop)
        name = f"attend_hop{hop}_others"
        theirs, parted = attend(
            facts, queries, others, rings, 0, piece, blocks, False, theirs, False, name
        )
        rest += parted
        rest_rings += rings
    rings = [(-half, 0, middle), (half, middle, piece - middle)]
    blocks = [ahead[0][half], behind[1][half]]
    heads = width // HD
    pieces_out = 2 if heads >= 4 else 1
    few = heads // pieces_out
    sending = []
    parted = False
    for lowest in range(0, heads, few):
        name = f"attend_far_others{lowest}"
        last, made = attend(
            facts,
            queries,
            others,
            rings,
            0,
            piece,
            parted or blocks,
            bool(parted),
            theirs,
            True,
            name,
            (lowest, few),
        )
        parted = parted or made
        sending.append([last[shift][0] for shift in others])
        facts = (after(tail_len, sending[-1][0]), shared_len, table)
    rest += parted
    rest_rings += rings
    own, _ = attend(
        facts,
        queries,
        [0],
        near_rings + rest_rings,
        slots,
        piece,
        near + rest + fresh,
        True,
        None,
        True,
        "attend_own",
    )
    arrivals = [
        [swap(part[i], "seq", shift) for i, shift in enumerate(others)] for part in sending
    ]
    new_cache, token = weave(fresh_keys, fresh_values, own[0][1], arrivals[0][0])
    attended = []
    earlier = [token]
    for piece_out, part in enumerate(arrivals):
        last = piece_out == pieces_out - 1
        made, sent = combine(own[0], part, piece_out * few, few, w_out, earlier, last, ways)
        attended.append(made)
        earlier = [sent, token]
    received = [swap(sent[shift - 1], "tp", shift) for shift in range(1, ways)]
    hidden_out = finish(keep(attended, w_out, hidden_in), received)
    return (hidden_out, new_cache)


def solution(mesh):
    return jax.shard_map(
        local,
        mesh=mesh,
        in_specs=(
            P("seq", "tp"),
            P(None, "tp"),
            P(None, None, "tp"),
            P("tp", None),
            P("seq", None, "tp"),
            P("seq", None, None, "tp"),
            P(),
            P(),
            P(),
        ),
        out_specs=(P("seq", "tp"), P("seq", None, "tp")),
        check_vma=False,
    )
```
